32 devices in a mesh: section: 2 (over core), dp: 16 (over z, y, x).
Axes of the slice: x: 2, y: 2, z: 4, core: 2. Of those that a mesh axis runs over, the one named last changes fastest.
Arguments:
- inputs: bfloat16 [2, 1024, 4096], P(None, 'dp'), may hold values from -6 to 6
- cotangent: bfloat16 [2, 1024, 4096], P(None, 'dp'), may hold values from -6 to 6
- doc_lengths: int32 [2, 16, 2], P(None, 'dp'), may hold values from 1 to 48, 64 in all within a row
- norm_gain: bfloat16 [2, 4096], P('section'), may hold values from 0.25 to 1.75
- w_qkv: bfloat16 [2, 4096, 192], P('section', 'dp'), may hold values from -0.09375 to 0.09375
- w_out: bfloat16 [2, 64, 4096], P('section', None, 'dp'), may hold values from -0.75 to 0.75
Outputs:
- grad_qkv: float32 [2, 4096, 192], P('section', 'dp')
- grad_out: float32 [2, 64, 4096], P('section', None, 'dp')
The draws below stay inside these ranges and needn't reach their ends.
Inputs may be any that keep to these rules, and one draw needn't show every extreme that they name: `doc_lengths`: each row's 2 lengths add up to 64.
All inputs are finite; a program needn't handle non-finite values.
Results may differ from the reference program's by a relative error of at most 0.025.
Values may be sent and summed in bfloat16 or wider, within the bound.
No kernel may reach another device: no remote copies, remote signals or barrier semaphores. Data moves between devices by JAX's collectives and lax.ppermute only.
A program may use at most 64 MiB of HBM per device.

```python
import math
import jax
import jax.numpy as jnp
import numpy as np
from jax import lax

D = 4096
HD = 64
MBTOK = 64
MB = 2
DOCS = 2
SECTIONS = 2
TOKENS = 1024
N_SECTION = 2
N_DP = 16


def steps_of(stream_key, extent, shards, least, largest):
    level, own = 1.0, jax.random.fold_in(stream_key, 6)
    for axis_at, blocks in shards:
        draws = jnp.exp(jax.random.uniform(jax.random.fold_in(own, axis_at), (blocks,), jnp.float32, least / len(shards), largest / len(shards)))
        level = level * jnp.repeat(draws, extent[axis_at] // blocks).reshape([-1 if axis == axis_at else 1 for axis in range(len(extent))])
    return level


def profile(count, total, limit, lean):
    loads = [(1 << 20) // math.isqrt(grade ** lean) + 1 for grade in range(2, count + 1)]
    rest, given = total - limit - (count - 1), [1] * (count - 1)
    while rest > 0:
        free = [i for i in range(count - 1) if given[i] < limit]
        mass, left = sum([loads[i] for i in free]), rest
        for i in free:
            more = min(limit - given[i], max(1, left * loads[i] // mass), rest)
            given[i] = given[i] + more
            rest = rest - more
    return np.array([limit] + given)


def ragged(stream_key, count, total, bound, slope):
    if count == 2:
        one = jax.random.randint(stream_key, (), max(1, total - bound), min(bound, total - 1) + 1)
        return jnp.stack([one, total - one])
    sizes = jnp.asarray(profile(count, total, bound, slope), jnp.int32)
    pairs = (count - 1) // 2
    source_of, sink = sizes[1:1 + 2 * pairs:2], sizes[2:2 + 2 * pairs:2]
    margin = jnp.minimum(source_of - 1, bound - sink)
    moved = jax.random.randint(jax.random.fold_in(stream_key, 1), (pairs,), 0, 1 << 20) % (margin + 1)
    sizes = sizes.at[1:1 + 2 * pairs:2].set(source_of - moved).at[2:2 + 2 * pairs:2].set(sink + moved)
    return sizes[jax.random.permutation(jax.random.fold_in(stream_key, 2), count)]


def bell_draw(rng, extent, width, reach, pieces=(), kind=jnp.bfloat16):
    values = width * jax.random.normal(rng, extent, jnp.float32)
    if pieces:
        values = values * steps_of(rng, extent, pieces, -0.22, 0.18)
    return jnp.clip(values, -reach, reach).astype(kind)


def setup_inputs(seed: int = 0) -> dict:
    streams_of = jax.random.split(jax.random.key(seed), 7)
    inputs = bell_draw(streams_of[0], (MB, TOKENS, D), 1.0, 6.0, ((1, 16),))
    cotangent = bell_draw(streams_of[1], (MB, TOKENS, D), 1.0, 6.0, ((1, 16),))
    doc_lengths = jax.vmap(lambda own: ragged(own, DOCS, MBTOK, MBTOK * 3 // 4, 2))(jax.random.split(streams_of[2], MB * N_DP)).reshape((MB, N_DP, DOCS)).astype(jnp.int32)
    norm_gain = jnp.clip(1.0 + 0.15 * jax.random.normal(streams_of[3], (SECTIONS, D), jnp.float32), 0.25, 1.75).astype(jnp.bfloat16)
    w_qkv = bell_draw(streams_of[4], (SECTIONS, D, 3 * HD), D ** -0.5, 0.09375, ((0, 2), (1, 16)))
    w_out = bell_draw(streams_of[5], (SECTIONS, HD, D), HD ** -0.5, 0.75, ((0, 2), (2, 16)))
    return dict(inputs=inputs, cotangent=cotangent, doc_lengths=doc_lengths, norm_gain=norm_gain, w_qkv=w_qkv, w_out=w_out)


def segments_of(lengths, count):
    ends = jnp.cumsum(lengths).astype(jnp.int32)
    position = jnp.arange(count, dtype=jnp.int32)
    return lax.optimization_barrier(jnp.sum((position[:, None] >= ends[None, :]).astype(jnp.int32), axis=1)).astype(jnp.int32)

def layer(x, gain, w_qkv, w_out, seg):
    head = w_out.shape[0]
    x_wide = x.astype(jnp.float32)
    scale = lax.rsqrt(lax.optimization_barrier(jnp.mean(x_wide * x_wide, axis=-1, keepdims=True)) + 1e-05)
    normed = (x_wide * scale * gain.astype(jnp.float32)).astype(jnp.bfloat16)
    qkv = jnp.dot(normed, w_qkv, preferred_element_type=jnp.float32).astype(jnp.bfloat16)
    query = qkv[:, :head]
    keys = qkv[:, head:2 * head]
    values = qkv[:, 2 * head:]
    scores = jnp.dot(query, keys.T, preferred_element_type=jnp.float32) * head ** (-0.5)
    rows = jnp.arange(x.shape[0], dtype=jnp.int32)
    allowed = (seg[:, None] == seg[None, :]) & (rows[:, None] >= rows[None, :])
    scores = jnp.where(allowed, scores, -1e+30)
    probs = jax.nn.softmax(scores, axis=-1).astype(jnp.bfloat16)
    attended = jnp.dot(probs, values, preferred_element_type=jnp.float32).astype(jnp.bfloat16)
    return (x_wide + jnp.dot(attended, w_out, preferred_element_type=jnp.float32)).astype(jnp.bfloat16)

def reference(inputs, cotangent, doc_lengths, norm_gain, w_qkv, w_out):
    blocks = inputs.reshape(MB, N_DP, MBTOK, D)
    cot_blocks = cotangent.reshape(MB, N_DP, MBTOK, D)
    segs = jax.vmap(jax.vmap(lambda lens: segments_of(lens, MBTOK)))(doc_lengths)

    def run(x, cot, seg):
        saved = []
        for level in range(N_SECTION):
            saved.append(x)
            x = layer(x, norm_gain[level], w_qkv[level], w_out[level], seg)
        grad_in = cot
        qkv_list = []
        out_list = []
        for level in reversed(range(N_SECTION)):
            gain = norm_gain[level]
            _, pull = jax.vjp(lambda a, b, c: layer(a, gain, b, c, seg), saved[level], w_qkv[level], w_out[level])
            grad_in, grad_q, grad_o = pull(grad_in)
            qkv_list.insert(0, grad_q)
            out_list.insert(0, grad_o)
        return (jnp.stack(qkv_list), jnp.stack(out_list))
    total_qkv = jnp.zeros(w_qkv.shape, jnp.float32)
    total_out = jnp.zeros(w_out.shape, jnp.float32)
    for micro in range(MB):
        grad_q, grad_o = jax.vmap(run)(blocks[micro], cot_blocks[micro], segs[micro])
        total_qkv = total_qkv + lax.optimization_barrier(jnp.sum(grad_q.astype(jnp.float32), axis=0))
        total_out = total_out + lax.optimization_barrier(jnp.sum(grad_o.astype(jnp.float32), axis=0))
    return (total_qkv, total_out)
```

```python
import functools

import jax
import jax.numpy as jnp
from jax import lax
from jax.experimental import pallas as pl
from jax.experimental.pallas import tpu as pltpu
from jax.sharding import PartitionSpec as P

F32 = jnp.float32
BF16 = jnp.bfloat16
PLANE = 4
STATS = 16
VMEM_LIMIT = 32 * 1024 * 1024


def passed_along(block, axis, distance):
    devices = range(lax.axis_size(axis))
    route = [(i - distance, i) for i in devices if i - distance in devices]
    return lax.ppermute(block, axis, route)


def segments_of(lengths, count):
    ends = jnp.cumsum(lengths)
    position = jnp.arange(count, dtype=jnp.int32)
    return jnp.sum((position[:, None] >= ends[None, :]).astype(jnp.int32), axis=1)


def layer(x, gain, w_qkv, w_out, seg):
    head = w_out.shape[0]
    x_wide = x.astype(jnp.float32)
    scale = lax.rsqrt(jnp.mean(x_wide * x_wide, axis=-1, keepdims=True) + 1e-05)
    normed = (x_wide * scale * gain.astype(jnp.float32)).astype(jnp.bfloat16)
    qkv = jnp.dot(normed, w_qkv, preferred_element_type=jnp.float32).astype(jnp.bfloat16)
    query = qkv[:, :head]
    keys = qkv[:, head : 2 * head]
    values = qkv[:, 2 * head :]
    scores = jnp.dot(query, keys.T, preferred_element_type=jnp.float32) * head ** (-0.5)
    rows = jnp.arange(x.shape[0], dtype=jnp.int32)
    allowed = (seg[:, None] == seg[None, :]) & (rows[:, None] >= rows[None, :])
    scores = jnp.where(allowed, scores, -1e30)
    probs = jax.nn.softmax(scores, axis=-1).astype(jnp.bfloat16)
    attended = jnp.dot(probs, values, preferred_element_type=jnp.float32).astype(jnp.bfloat16)
    return (x_wide + jnp.dot(attended, w_out, preferred_element_type=jnp.float32)).astype(
        jnp.bfloat16
    )


def pipelined(inputs, cotangent, doc_lengths, norm_gain, w_qkv, w_out):
    sections = lax.axis_size("section")
    section = lax.axis_index("section")
    micro = inputs.shape[0]
    count = inputs.shape[1]
    segs = jax.vmap(lambda lens: segments_of(lens, count))(doc_lengths[:, 0, :])
    gain = norm_gain[0]
    full_qkv, full_out = (
        lax.all_gather(w_qkv[0], "dp", axis=0, tiled=True),
        lax.all_gather(w_out[0], "dp", axis=1, tiled=True),
    )
    total_steps = micro + sections - 1
    empty = jnp.zeros(inputs.shape[1:], inputs.dtype)

    def forward_at(step, incoming, saved):
        index = step - section
        live = (index >= 0) & (index < micro)
        slot = jnp.clip(index, 0, micro - 1)
        first = lax.dynamic_index_in_dim(inputs, slot, 0, keepdims=False)
        x = jnp.where(section == 0, first, incoming)
        seg = lax.dynamic_index_in_dim(segs, slot, 0, keepdims=False)
        out = layer(x, gain, full_qkv, full_out, seg)
        old = lax.dynamic_index_in_dim(saved, slot, 0, keepdims=False)
        saved = lax.dynamic_update_index_in_dim(saved, jnp.where(live, x, old), slot, 0)
        return (out, saved)

    def forward_step(carry, step):
        incoming, saved = carry
        out, saved = forward_at(step, incoming, saved)
        incoming = passed_along(out, "section", 1)
        return ((incoming, saved), None)

    start_saved = jnp.zeros(inputs.shape, inputs.dtype)
    (incoming, saved), _ = lax.scan(
        forward_step, (empty, start_saved), jnp.arange(total_steps - 1, dtype=jnp.int32)
    )
    _, saved = forward_at(jnp.int32(total_steps - 1), incoming, saved)

    def backward_at(step, incoming, sum_qkv, sum_out):
        index = step - (sections - 1 - section)
        live = (index >= 0) & (index < micro)
        slot = jnp.clip(index, 0, micro - 1)
        last = lax.dynamic_index_in_dim(cotangent, slot, 0, keepdims=False)
        grad_y = jnp.where(section == sections - 1, last, incoming)
        x = lax.dynamic_index_in_dim(saved, slot, 0, keepdims=False)
        seg = lax.dynamic_index_in_dim(segs, slot, 0, keepdims=False)
        _, pull = jax.vjp(lambda a, b, c: layer(a, gain, b, c, seg), x, full_qkv, full_out)
        grad_x, grad_q, grad_o = pull(grad_y)
        sum_qkv = sum_qkv + jnp.where(live, grad_q.astype(jnp.float32), 0.0)
        sum_out = sum_out + jnp.where(live, grad_o.astype(jnp.float32), 0.0)
        return (grad_x, sum_qkv, sum_out)

    def backward_step(carry, step):
        incoming, sum_qkv, sum_out = carry
        grad_x, sum_qkv, sum_out = backward_at(step, incoming, sum_qkv, sum_out)
        incoming = passed_along(grad_x, "section", -1)
        return ((incoming, sum_qkv, sum_out), None)

    zero_qkv = jnp.zeros(full_qkv.shape, jnp.float32)
    zero_out = jnp.zeros(full_out.shape, jnp.float32)
    (incoming, sum_qkv, sum_out), _ = lax.scan(
        backward_step, (empty, zero_qkv, zero_out), jnp.arange(total_steps - 1, dtype=jnp.int32)
    )
    _, sum_qkv, sum_out = backward_at(jnp.int32(total_steps - 1), incoming, sum_qkv, sum_out)
    share_qkv, share_out = (
        lax.psum_scatter(sum_qkv, "dp", scatter_dimension=0, tiled=True),
        lax.psum_scatter(sum_out, "dp", scatter_dimension=1, tiled=True),
    )
    return (share_qkv[None], share_out[None])


def nn(a, b):
    return lax.dot_general(a, b, (((1,), (0,)), ((), ())), preferred_element_type=F32)


def nt(a, b):
    return lax.dot_general(a, b, (((1,), (1,)), ((), ())), preferred_element_type=F32)


def prepare_kernel(planes, index, x_ref, c_ref, xs_ref, cs_ref):
    width = xs_ref.shape[-1] // planes
    for z in range(planes):
        for p in range(PLANE):
            here = slice((z * PLANE + p) * width, (z * PLANE + p + 1) * width)
            there = slice(z * width, (z + 1) * width)
            xs_ref[p, :, there] = x_ref[0, :, here]
            cs_ref[p, :, there] = c_ref[0, :, here]


def gain_of(w_ref, z, wide):
    return w_ref[z, wide : wide + STATS, :].astype(F32)[0:1, :]


def partial_qkv(x_of, w_ref, qkv_rows, out_rows):
    total = None
    squares = None
    for z in range(w_ref.shape[0]):
        x = x_of(z)
        gained = (x * gain_of(w_ref, z, qkv_rows + out_rows)).astype(BF16)
        part = nt(w_ref[z, :qkv_rows, :], gained)
        square = jnp.sum(x * x, axis=1, keepdims=True)
        total = part if total is None else total + part
        squares = square if squares is None else squares + square
    return total, squares


def stat_rows(squares, extra):
    rows = squares.shape[0]
    row = jnp.transpose(jnp.broadcast_to(squares, (rows, 128)))[0:STATS, :]
    at = lax.broadcasted_iota(jnp.int32, (STATS, rows), 0)
    high = row.astype(BF16).astype(F32)
    low = row - high
    out = jnp.where(at == 0, high, jnp.where(at == 1, low, 0.0))
    if extra is not None:
        out = jnp.where(at == 2, extra, out)
    return out.astype(BF16)


def spread(out_ref, at, value):
    for p in range(PLANE):
        out_ref[p, at : at + value.shape[0], :] = value


def first_kernel(planes, heads, index, docs, x_ref, *refs):
    own, other = refs[:planes], refs[planes : 2 * planes]
    w0_ref, w1_ref, out_ref = refs[2 * planes :]
    qkv_rows, out_rows = 3 * heads, heads
    section, z, p = index[0], index[1], index[2]
    for k in range(planes):
        mine, theirs = own[k][...], other[k][...]
        w0_ref[z ^ k] = jnp.where(section == 0, mine, theirs)
        w1_ref[z ^ k] = jnp.where(section == 0, theirs, mine)
    width = x_ref.shape[-1] // planes
    rows = x_ref.shape[0] * x_ref.shape[1]

    def x_of(z):
        x = x_ref[:, :, z * width : (z + 1) * width]
        return x.reshape(rows, width).astype(F32)

    total, squares = partial_qkv(x_of, w0_ref, qkv_rows, out_rows)
    spread(out_ref, 0, total.astype(BF16))
    position = lax.broadcasted_iota(jnp.int32, (STATS, rows), 1)
    block = rows // PLANE
    local = position - p * block
    ends = docs[0]
    seg = (local >= ends).astype(F32)
    for i in range(1, docs.shape[0]):
        ends = ends + docs[i]
        seg = seg + (local >= ends).astype(F32)
    seg = jnp.where((local >= 0) & (local < block), seg, 0.0)
    spread(out_ref, qkv_rows, stat_rows(squares, seg))


def attention(qkv_t, codes_row, codes_col, heads):
    rows = qkv_t.shape[1]
    narrow = qkv_t.astype(BF16)
    keys = jnp.transpose(qkv_t[heads : 2 * heads]).astype(BF16)
    scores = nn(keys, narrow[:heads]) * heads ** (-0.5)
    key_at = lax.broadcasted_iota(jnp.int32, (rows, rows), 0)
    query_at = lax.broadcasted_iota(jnp.int32, (rows, rows), 1)
    allowed = (codes_row == codes_col) & (query_at >= key_at)
    scores = jnp.where(allowed, scores, -1e30)
    top = jnp.max(scores, axis=0, keepdims=True)
    raised = jnp.exp(scores - top)
    probs = raised / jnp.sum(raised, axis=0, keepdims=True)
    attended = nn(narrow[2 * heads :], probs.astype(BF16)).astype(BF16)
    return probs, attended


def attention_grad(qkv_t, probs, d_att_t, heads):
    narrow = qkv_t.astype(BF16)
    values = jnp.transpose(qkv_t[2 * heads :]).astype(BF16)
    d_values = nt(d_att_t, probs.astype(BF16))
    d_probs = nn(values, d_att_t).astype(BF16).astype(F32)
    inner = jnp.sum(probs * d_probs, axis=0, keepdims=True)
    d_scores = (probs * (d_probs - inner) * heads ** (-0.5)).astype(BF16)
    d_query = nn(narrow[heads : 2 * heads], d_scores)
    d_keys = nt(narrow[:heads], d_scores)
    return jnp.concatenate([d_query, d_keys, d_values], axis=0).astype(BF16)


def summed(parts_ref, start, stop):
    total = parts_ref[0, start:stop, :].astype(F32)
    for p in range(1, PLANE):
        total = total + parts_ref[p, start:stop, :].astype(F32)
    return total


def scaled(parts_ref, qkv_rows, features):
    stats = summed(parts_ref, qkv_rows, qkv_rows + STATS)
    scale = lax.rsqrt((stats[0:1, :] + stats[1:2, :]) / features + 1e-05)
    qkv_t = (summed(parts_ref, 0, qkv_rows) * scale).astype(BF16).astype(F32)
    return qkv_t, scale, stats


def column(row):
    count = row.shape[1]
    return jnp.transpose(jnp.broadcast_to(row, (128, count)))[:, 0:1]


def second_kernel(
    features, heads, parts_ref, x_ref, c_ref, w0_ref, w1_ref, out_ref, y_ref, qkv_ref, probs_ref, att_ref, stat_ref
):
    planes = w0_ref.shape[0]
    qkv_rows, out_rows = 3 * heads, heads
    width = x_ref.shape[-1] // planes
    rows = x_ref.shape[0] * x_ref.shape[1]
    qkv_t, scale, stats = scaled(parts_ref, qkv_rows, features)
    block = lax.broadcasted_iota(jnp.int32, (1, rows), 1) // (rows // PLANE)
    codes = stats[2:3, :] + (block * rows).astype(F32)
    probs, att_t = attention(qkv_t, codes, column(codes), heads)
    qkv_ref[...] = qkv_t
    probs_ref[...] = probs
    att_ref[...] = att_t
    at = lax.broadcasted_iota(jnp.int32, stat_ref.shape, 0)
    stat_ref[...] = jnp.where(at == 0, scale, codes)
    att = jnp.transpose(att_t.astype(F32)).astype(BF16)
    d_att = None
    for z in range(planes):
        cols = slice(z * width, (z + 1) * width)
        x = x_ref[:, :, cols].reshape(rows, width).astype(F32)
        y_ref[:, cols] = (x + nn(att, w0_ref[z, qkv_rows : qkv_rows + out_rows, :])).astype(BF16)
        c = c_ref[:, :, cols].reshape(rows, width)
        part = nt(w1_ref[z, qkv_rows : qkv_rows + out_rows, :], c)
        d_att = part if d_att is None else d_att + part
    total, squares = partial_qkv(
        lambda z: y_ref[:, z * width : (z + 1) * width].astype(F32), w1_ref, qkv_rows, out_rows
    )
    spread(out_ref, 0, total.astype(BF16))
    spread(out_ref, qkv_rows, stat_rows(squares, None))
    spread(out_ref, qkv_rows + STATS, d_att.astype(BF16))


def third_kernel(
    features, heads, parts_ref, c_ref, y_ref, att_ref, stat_ref, w0_ref, w1_ref, out_ref, g0_ref, g1_ref
):
    planes = w0_ref.shape[0]
    qkv_rows, out_rows = 3 * heads, heads
    width = y_ref.shape[-1] // planes
    rows = y_ref.shape[0]
    qkv_t, scale, _ = scaled(parts_ref, qkv_rows, features)
    d_att_t = summed(parts_ref, qkv_rows + STATS, qkv_rows + STATS + heads).astype(BF16)
    codes = stat_ref[1:2, :]
    probs, att_t = attention(qkv_t, codes, column(codes), heads)
    d_qkv_t = attention_grad(qkv_t, probs, d_att_t, heads)
    wide = d_qkv_t.astype(F32)
    inner = jnp.sum(wide * qkv_t, axis=0, keepdims=True) * scale * scale / features
    d_qkv = jnp.transpose(wide).astype(BF16)
    scale_col, inner_col = column(scale), column(inner)
    att0_t = att_ref[...]
    d_att = None
    for z in range(planes):
        cols = slice(z * width, (z + 1) * width)
        gain = gain_of(w1_ref, z, qkv_rows + out_rows)
        c = c_ref[:, :, cols].reshape(rows, width)
        y = y_ref[:, cols].astype(F32)
        normed = (y * scale_col * gain).astype(BF16)
        g1_ref[z, :qkv_rows, :] = nn(d_qkv_t, normed).astype(g1_ref.dtype)
        g1_ref[z, qkv_rows:, :] = nn(att_t, c).astype(g1_ref.dtype)
        d_normed = nn(d_qkv, w1_ref[z, :qkv_rows, :])
        d_y = (c.astype(F32) + scale_col * gain * d_normed - y * inner_col).astype(BF16)
        g0_ref[z] = nn(att0_t, d_y).astype(g0_ref.dtype)
        part = nt(w0_ref[z, qkv_rows : qkv_rows + out_rows, :], d_y)
        d_att = part if d_att is None else d_att + part
    spread(out_ref, 0, d_att.astype(BF16))


def fourth_kernel(
    heads, index, parts_ref, x_ref, qkv_ref, probs_ref, stat_ref, w0_ref, g0_ref, g1_ref, keep_ref, send_ref
):
    planes = w0_ref.shape[0]
    qkv_rows, out_rows = 3 * heads, heads
    width = x_ref.shape[-1] // planes
    rows = x_ref.shape[0] * x_ref.shape[1]
    section, place = index[0], index[1]
    d_att_t = summed(parts_ref, 0, heads).astype(BF16)
    d_qkv_t = attention_grad(qkv_ref[...], probs_ref[...], d_att_t, heads)
    scale_col = column(stat_ref[0:1, :])
    for z in range(planes):
        cols = slice(z * width, (z + 1) * width)
        x = x_ref[:, :, cols].reshape(rows, width).astype(F32)
        normed = (x * scale_col * gain_of(w0_ref, z, qkv_rows + out_rows)).astype(BF16)
        zero = nn(d_qkv_t, normed)
        one = g1_ref[z, :qkv_rows, :]
        keep_ref[z, :qkv_rows, :] = jnp.where(section == 0, zero, one)
        send_ref[z, :qkv_rows, :] = jnp.where(section == 0, one, zero).astype(BF16)
        zero, one = g0_ref[z], g1_ref[z, qkv_rows:, :]
        keep_ref[z, qkv_rows:, :] = jnp.where(section == 0, zero, one)
        send_ref[z, qkv_rows:, :] = jnp.where(section == 0, one, zero).astype(BF16)


def merge_kernel(index, keep_ref, come_ref, *out_refs):
    place = index[1]
    out_refs[0][...] = keep_ref[place] + come_ref[place].astype(F32)
    for k in range(1, len(out_refs)):
        out_refs[k][...] = (keep_ref[place ^ k] + come_ref[place ^ k].astype(F32)).astype(BF16)


def last_kernel(qkv_rows, keep_ref, *refs):
    parts, (qkv_ref, out_ref) = refs[:-2], refs[-2:]
    total = keep_ref[...]
    for part in parts:
        total = total + part[...].astype(F32)
    qkv_ref[...] = total[:qkv_rows]
    out_ref[...] = total[qkv_rows:]


def call(kernel, outs, *args, scalars=0):
    smem = pl.BlockSpec(memory_space=pltpu.SMEM)
    vmem = pl.BlockSpec(memory_space=pltpu.VMEM)
    return pl.pallas_call(
        kernel,
        out_shape=[jax.ShapeDtypeStruct(shape, dtype) for shape, dtype in outs],
        in_specs=[smem] * scalars + [vmem] * (len(args) - scalars),
        out_specs=[vmem] * len(outs),
        compiler_params=pltpu.CompilerParams(vmem_limit_bytes=VMEM_LIMIT),
    )(*args)


def planar(inputs, cotangent, doc_lengths, norm_gain, w_qkv, w_out):
    shards = lax.axis_size("dp")
    planes = shards // PLANE
    section, place = lax.axis_index("section"), lax.axis_index("dp")
    z, p = place // PLANE, place % PLANE
    index = jnp.stack([section, z, p]).astype(jnp.int32)
    block, features = inputs.shape[1:]
    rows = PLANE * block
    heads, width = w_out.shape[1:]
    qkv_rows = w_qkv.shape[2]
    cols = planes * width
    in_plane = [[a * PLANE + b for b in range(PLANE)] for a in range(planes)]

    def along_z(value, k):
        route = [(a * PLANE + b, (a ^ k) * PLANE + b) for a in range(planes) for b in range(PLANE)]
        return lax.ppermute(value, "dp", route)

    def to_sibling(value):
        return lax.ppermute(value, "section", [(0, 1), (1, 0)])

    def exchange(value):
        return lax.all_to_all(value, "dp", 0, 0, axis_index_groups=in_plane, tiled=True)

    gain = lax.dynamic_slice(norm_gain, (0, place * width), (1, width))
    pack = jnp.concatenate(
        [w_qkv[0].T, w_out[0], jnp.pad(gain, ((0, STATS - 1), (0, 0)))], axis=0
    )
    own = [pack] + [along_z(pack, k) for k in range(1, planes)]

    one_batch = pl.BlockSpec((1, block, features), lambda i, index: (index[0], 0, 0))
    split = pl.BlockSpec((PLANE, block, cols), lambda i, index: (0, 0, 0))
    xs, cs = pl.pallas_call(
        functools.partial(prepare_kernel, planes),
        grid_spec=pltpu.PrefetchScalarGridSpec(
            num_scalar_prefetch=1,
            grid=(1,),
            in_specs=[one_batch, one_batch],
            out_specs=[split, split],
        ),
        out_shape=[jax.ShapeDtypeStruct((PLANE, block, cols), BF16)] * 2,
        compiler_params=pltpu.CompilerParams(vmem_limit_bytes=VMEM_LIMIT),
    )(index, inputs, cotangent)
    x = exchange(xs)
    c = exchange(cs)
    other = [to_sibling(piece) for piece in own]

    docs = lax.dynamic_index_in_dim(doc_lengths, section, 0, keepdims=False)[0]
    weights = ((planes,) + pack.shape, BF16)
    w0, w1, sent = call(
        functools.partial(first_kernel, planes, heads),
        [weights, weights, ((PLANE, qkv_rows + STATS, rows), BF16)],
        index, docs, x, *own, *other, scalars=2,
    )
    y, qkv, probs, att, stats = None, None, None, None, None
    sent, y, qkv, probs, att, stats = call(
        functools.partial(second_kernel, features, heads),
        [
            ((PLANE, qkv_rows + STATS + heads, rows), BF16),
            ((rows, cols), BF16),
            ((qkv_rows, rows), F32),
            ((rows, rows), F32),
            ((heads, rows), BF16),
            ((8, rows), F32),
        ],
        exchange(sent), x, c, w0, w1,
    )
    sent, g0, g1 = call(
        functools.partial(third_kernel, features, heads),
        [
            ((PLANE, heads, rows), BF16),
            ((planes, heads, width), F32),
            ((planes, qkv_rows + heads, width), F32),
        ],
        exchange(sent), c, y, att, stats, w0, w1,
    )
    grads = (planes, qkv_rows + heads, width)
    keep, send = call(
        functools.partial(fourth_kernel, heads),
        [(grads, F32), (grads, BF16)],
        index, exchange(sent), x, qkv, probs, stats, w0, g0, g1, scalars=1,
    )
    merged = call(
        merge_kernel,
        [(grads[1:], F32)] + [(grads[1:], BF16)] * (planes - 1),
        index, keep, to_sibling(send), scalars=1,
    )
    parts = [along_z(merged[k], k) for k in range(1, planes)]
    grad_qkv, grad_out = call(
        functools.partial(last_kernel, qkv_rows),
        [((qkv_rows, width), F32), ((heads, width), F32)],
        merged[0], *parts,
    )
    return (grad_qkv.T[None], grad_out[None])


def solution(mesh):
    sections, shards = mesh.shape["section"], mesh.shape["dp"]
    planes = shards // PLANE

    def body(inputs, *rest):
        fits = shards % PLANE == 0 and planes & (planes - 1) == 0
        if sections == 2 and inputs.shape[0] == 2 and fits:
            return planar(inputs, *rest)
        return pipelined(inputs, *rest)

    return jax.shard_map(
        body,
        mesh=mesh,
        in_specs=(
            P(None, "dp", None),
            P(None, "dp", None),
            P(None, "dp", None),
            P("section", None),
            P("section", "dp", None),
            P("section", None, "dp"),
        ),
        out_specs=(P("section", "dp", None), P("section", None, "dp")),
        check_vma=False,
    )
```

```python
import functools

import jax
import jax.numpy as jnp
from jax import lax
from jax.experimental import pallas as pl
from jax.experimental.pallas import tpu as pltpu
from jax.sharding import PartitionSpec as P

F32 = jnp.float32
BF16 = jnp.bfloat16
PLANE = 4
STATS = 16
VMEM_LIMIT = 16 * 1024 * 1024


def passed_along(block, axis, distance):
    devices = range(lax.axis_size(axis))
    route = [(i - distance, i) for i in devices if i - distance in devices]
    return lax.ppermute(block, axis, route)


def segments_of(lengths, count):
    ends = jnp.cumsum(lengths)
    position = jnp.arange(count, dtype=jnp.int32)
    return jnp.sum((position[:, None] >= ends[None, :]).astype(jnp.int32), axis=1)


def layer(x, gain, w_qkv, w_out, seg):
    head = w_out.shape[0]
    x_wide = x.astype(jnp.float32)
    scale = lax.rsqrt(jnp.mean(x_wide * x_wide, axis=-1, keepdims=True) + 1e-05)
    normed = (x_wide * scale * gain.astype(jnp.float32)).astype(jnp.bfloat16)
    qkv = jnp.dot(normed, w_qkv, preferred_element_type=jnp.float32).astype(jnp.bfloat16)
    query = qkv[:, :head]
    keys = qkv[:, head : 2 * head]
    values = qkv[:, 2 * head :]
    scores = jnp.dot(query, keys.T, preferred_element_type=jnp.float32) * head ** (-0.5)
    rows = jnp.arange(x.shape[0], dtype=jnp.int32)
    allowed = (seg[:, None] == seg[None, :]) & (rows[:, None] >= rows[None, :])
    scores = jnp.where(allowed, scores, -1e30)
    probs = jax.nn.softmax(scores, axis=-1).astype(jnp.bfloat16)
    attended = jnp.dot(probs, values, preferred_element_type=jnp.float32).astype(jnp.bfloat16)
    return (x_wide + jnp.dot(attended, w_out, preferred_element_type=jnp.float32)).astype(
        jnp.bfloat16
    )


def pipelined(inputs, cotangent, doc_lengths, norm_gain, w_qkv, w_out):
    sections = lax.axis_size("section")
    section = lax.axis_index("section")
    micro = inputs.shape[0]
    count = inputs.shape[1]
    segs = jax.vmap(lambda lens: segments_of(lens, count))(doc_lengths[:, 0, :])
    gain = norm_gain[0]
    full_qkv, full_out = (
        lax.all_gather(w_qkv[0], "dp", axis=0, tiled=True),
        lax.all_gather(w_out[0], "dp", axis=1, tiled=True),
    )
    total_steps = micro + sections - 1
    empty = jnp.zeros(inputs.shape[1:], inputs.dtype)

    def forward_at(step, incoming, saved):
        index = step - section
        live = (index >= 0) & (index < micro)
        slot = jnp.clip(index, 0, micro - 1)
        first = lax.dynamic_index_in_dim(inputs, slot, 0, keepdims=False)
        x = jnp.where(section == 0, first, incoming)
        seg = lax.dynamic_index_in_dim(segs, slot, 0, keepdims=False)
        out = layer(x, gain, full_qkv, full_out, seg)
        old = lax.dynamic_index_in_dim(saved, slot, 0, keepdims=False)
        saved = lax.dynamic_update_index_in_dim(saved, jnp.where(live, x, old), slot, 0)
        return (out, saved)

    def forward_step(carry, step):
        incoming, saved = carry
        out, saved = forward_at(step, incoming, saved)
        incoming = passed_along(out, "section", 1)
        return ((incoming, saved), None)

    start_saved = jnp.zeros(inputs.shape, inputs.dtype)
    (incoming, saved), _ = lax.scan(
        forward_step, (empty, start_saved), jnp.arange(total_steps - 1, dtype=jnp.int32)
    )
    _, saved = forward_at(jnp.int32(total_steps - 1), incoming, saved)

    def backward_at(step, incoming, sum_qkv, sum_out):
        index = step - (sections - 1 - section)
        live = (index >= 0) & (index < micro)
        slot = jnp.clip(index, 0, micro - 1)
        last = lax.dynamic_index_in_dim(cotangent, slot, 0, keepdims=False)
        grad_y = jnp.where(section == sections - 1, last, incoming)
        x = lax.dynamic_index_in_dim(saved, slot, 0, keepdims=False)
        seg = lax.dynamic_index_in_dim(segs, slot, 0, keepdims=False)
        _, pull = jax.vjp(lambda a, b, c: layer(a, gain, b, c, seg), x, full_qkv, full_out)
        grad_x, grad_q, grad_o = pull(grad_y)
        sum_qkv = sum_qkv + jnp.where(live, grad_q.astype(jnp.float32), 0.0)
        sum_out = sum_out + jnp.where(live, grad_o.astype(jnp.float32), 0.0)
        return (grad_x, sum_qkv, sum_out)

    def backward_step(carry, step):
        incoming, sum_qkv, sum_out = carry
        grad_x, sum_qkv, sum_out = backward_at(step, incoming, sum_qkv, sum_out)
        incoming = passed_along(grad_x, "section", -1)
        return ((incoming, sum_qkv, sum_out), None)

    zero_qkv = jnp.zeros(full_qkv.shape, jnp.float32)
    zero_out = jnp.zeros(full_out.shape, jnp.float32)
    (incoming, sum_qkv, sum_out), _ = lax.scan(
        backward_step, (empty, zero_qkv, zero_out), jnp.arange(total_steps - 1, dtype=jnp.int32)
    )
    _, sum_qkv, sum_out = backward_at(jnp.int32(total_steps - 1), incoming, sum_qkv, sum_out)
    share_qkv, share_out = (
        lax.psum_scatter(sum_qkv, "dp", scatter_dimension=0, tiled=True),
        lax.psum_scatter(sum_out, "dp", scatter_dimension=1, tiled=True),
    )
    return (share_qkv[None], share_out[None])


def nn(a, b):
    return lax.dot_general(a, b, (((1,), (0,)), ((), ())), preferred_element_type=F32)


def nt(a, b):
    return lax.dot_general(a, b, (((1,), (1,)), ((), ())), preferred_element_type=F32)


def blocks_kernel(planes, index, x_ref, c_ref, *refs):
    out_refs, sems = refs[:PLANE], refs[PLANE]
    width = x_ref.shape[-1] // (planes * PLANE)
    section, p = index[0], index[2]
    copies = []
    for k in range(PLANE):
        for z in range(planes):
            at = pl.multiple_of((z * PLANE + (p ^ k)) * width, width)
            for half, ref in enumerate((x_ref, c_ref)):
                copies.append(
                    pltpu.make_async_copy(
                        ref.at[section, :, pl.ds(at, width)],
                        out_refs[k].at[half, :, pl.ds(z * width, width)],
                        sems.at[len(copies)],
                    )
                )
    for copy in copies:
        copy.start()
    for copy in copies:
        copy.wait()


def gain_of(w_ref, z, wide):
    return w_ref[z, wide : wide + STATS, :].astype(F32)[0:1, :]


def partial_qkv(x_of, w_ref, qkv_rows, out_rows):
    total = None
    squares = None
    for z in range(w_ref.shape[0]):
        x = x_of(z)
        gained = (x * gain_of(w_ref, z, qkv_rows + out_rows)).astype(BF16)
        part = nt(w_ref[z, :qkv_rows, :], gained)
        square = jnp.sum(x * x, axis=1, keepdims=True)
        total = part if total is None else total + part
        squares = square if squares is None else squares + square
    return total, squares


def stat_rows(squares, extra):
    rows = squares.shape[0]
    row = jnp.transpose(jnp.broadcast_to(squares, (rows, 128)))[0:STATS, :]
    at = lax.broadcasted_iota(jnp.int32, (STATS, rows), 0)
    high = row.astype(BF16).astype(F32)
    low = row - high
    out = jnp.where(at == 0, high, jnp.where(at == 1, low, 0.0))
    if extra is not None:
        out = jnp.where(at == 2, extra, out)
    return out.astype(BF16)


def first_kernel(planes, heads, index, docs, *refs):
    blocks, own, other = refs[:PLANE], refs[PLANE : PLANE + planes], refs[PLANE + planes : PLANE + 2 * planes]
    x_ref, c_ref, w0_ref, w1_ref, out_ref = refs[PLANE + 2 * planes :]
    qkv_rows, out_rows = 3 * heads, heads
    section, z, p = index[0], index[1], index[2]
    for k in range(planes):
        mine, theirs = own[k][...], other[k][...]
        w0_ref[z ^ k] = jnp.where(section == 0, mine, theirs)
        w1_ref[z ^ k] = jnp.where(section == 0, theirs, mine)
    for k in range(PLANE):
        x_ref[p ^ k] = blocks[k][0]
        c_ref[p ^ k] = blocks[k][1]
    width = x_ref.shape[-1] // planes
    rows = x_ref.shape[0] * x_ref.shape[1]

    def x_of(z):
        x = x_ref[:, :, z * width : (z + 1) * width]
        return x.reshape(rows, width).astype(F32)

    total, squares = partial_qkv(x_of, w0_ref, qkv_rows, out_rows)
    out_ref[:qkv_rows, :] = total.astype(BF16)
    position = lax.broadcasted_iota(jnp.int32, (STATS, rows), 1)
    block = rows // PLANE
    local = position - p * block
    ends = docs[section, 0, 0]
    seg = (local >= ends).astype(F32)
    for i in range(1, docs.shape[2]):
        ends = ends + docs[section, 0, i]
        seg = seg + (local >= ends).astype(F32)
    seg = jnp.where((local >= 0) & (local < block), seg, 0.0)
    out_ref[qkv_rows:, :] = stat_rows(squares, seg)


def attention(qkv_t, codes_row, codes_col, heads):
    rows = qkv_t.shape[1]
    narrow = qkv_t.astype(BF16)
    keys = jnp.transpose(qkv_t[heads : 2 * heads]).astype(BF16)
    scores = nn(keys, narrow[:heads]) * heads ** (-0.5)
    key_at = lax.broadcasted_iota(jnp.int32, (rows, rows), 0)
    query_at = lax.broadcasted_iota(jnp.int32, (rows, rows), 1)
    allowed = (codes_row == codes_col) & (query_at >= key_at)
    scores = jnp.where(allowed, scores, -1e30)
    top = jnp.max(scores, axis=0, keepdims=True)
    raised = jnp.exp(scores - top)
    probs = raised / jnp.sum(raised, axis=0, keepdims=True)
    attended = nn(narrow[2 * heads :], probs.astype(BF16)).astype(BF16)
    return probs, attended


def attention_grad(qkv_t, probs, d_att_t, heads):
    narrow = qkv_t.astype(BF16)
    values = jnp.transpose(qkv_t[2 * heads :]).astype(BF16)
    d_values = nt(d_att_t, probs.astype(BF16))
    d_probs = nn(values, d_att_t).astype(BF16).astype(F32)
    inner = jnp.sum(probs * d_probs, axis=0, keepdims=True)
    d_scores = (probs * (d_probs - inner) * heads ** (-0.5)).astype(BF16)
    d_query = nn(narrow[heads : 2 * heads], d_scores)
    d_keys = nt(narrow[:heads], d_scores)
    return jnp.concatenate([d_query, d_keys, d_values], axis=0).astype(BF16)


def summed(parts, start, stop):
    total = parts[0][start:stop, :].astype(F32)
    for part in parts[1:]:
        total = total + part[start:stop, :].astype(F32)
    return total


def scaled(parts, qkv_rows, features):
    stats = summed(parts, qkv_rows, qkv_rows + STATS)
    scale = lax.rsqrt((stats[0:1, :] + stats[1:2, :]) / features + 1e-05)
    qkv_t = (summed(parts, 0, qkv_rows) * scale).astype(BF16).astype(F32)
    return qkv_t, scale, stats


def column(row):
    count = row.shape[1]
    return jnp.transpose(jnp.broadcast_to(row, (128, count)))[:, 0:1]


def second_kernel(features, heads, *refs):
    parts, (x_ref, c_ref, w0_ref, w1_ref) = refs[:PLANE], refs[PLANE : PLANE + 4]
    out_ref, y_ref, qkv_ref, probs_ref, att_ref, stat_ref = refs[PLANE + 4 :]
    planes = w0_ref.shape[0]
    qkv_rows, out_rows = 3 * heads, heads
    width = x_ref.shape[-1] // planes
    rows = x_ref.shape[0] * x_ref.shape[1]
    qkv_t, scale, stats = scaled(parts, qkv_rows, features)
    block = lax.broadcasted_iota(jnp.int32, (1, rows), 1) // (rows // PLANE)
    codes = stats[2:3, :] + (block * rows).astype(F32)
    probs, att_t = attention(qkv_t, codes, column(codes), heads)
    qkv_ref[...] = qkv_t
    probs_ref[...] = probs
    att_ref[...] = att_t
    at = lax.broadcasted_iota(jnp.int32, stat_ref.shape, 0)
    stat_ref[...] = jnp.where(at == 0, scale, codes)
    att = jnp.transpose(att_t.astype(F32)).astype(BF16)
    d_att = None
    for z in range(planes):
        cols = slice(z * width, (z + 1) * width)
        x = x_ref[:, :, cols].reshape(rows, width).astype(F32)
        y_ref[:, cols] = (x + nn(att, w0_ref[z, qkv_rows : qkv_rows + out_rows, :])).astype(BF16)
        c = c_ref[:, :, cols].reshape(rows, width)
        part = nt(w1_ref[z, qkv_rows : qkv_rows + out_rows, :], c)
        d_att = part if d_att is None else d_att + part
    total, squares = partial_qkv(
        lambda z: y_ref[:, z * width : (z + 1) * width].astype(F32), w1_ref, qkv_rows, out_rows
    )
    out_ref[:qkv_rows, :] = total.astype(BF16)
    out_ref[qkv_rows : qkv_rows + STATS, :] = stat_rows(squares, None)
    out_ref[qkv_rows + STATS :, :] = d_att.astype(BF16)


def third_kernel(features, heads, *refs):
    parts, (c_ref, y_ref, att_ref, stat_ref, w0_ref, w1_ref) = refs[:PLANE], refs[PLANE : PLANE + 6]
    out_ref, g0_ref, g1_ref = refs[PLANE + 6 :]
    planes = w0_ref.shape[0]
    qkv_rows, out_rows = 3 * heads, heads
    width = y_ref.shape[-1] // planes
    rows = y_ref.shape[0]
    qkv_t, scale, _ = scaled(parts, qkv_rows, features)
    d_att_t = summed(parts, qkv_rows + STATS, qkv_rows + STATS + heads).astype(BF16)
    codes = stat_ref[1:2, :]
    probs, att_t = attention(qkv_t, codes, column(codes), heads)
    d_qkv_t = attention_grad(qkv_t, probs, d_att_t, heads)
    wide = d_qkv_t.astype(F32)
    inner = jnp.sum(wide * qkv_t, axis=0, keepdims=True) * scale * scale / features
    d_qkv = jnp.transpose(wide).astype(BF16)
    scale_col, inner_col = column(scale), column(inner)
    att0_t = att_ref[...]
    d_att = None
    for z in range(planes):
        cols = slice(z * width, (z + 1) * width)
        gain = gain_of(w1_ref, z, qkv_rows + out_rows)
        c = c_ref[:, :, cols].reshape(rows, width)
        y = y_ref[:, cols].astype(F32)
        normed = (y * scale_col * gain).astype(BF16)
        g1_ref[z, :qkv_rows, :] = nn(d_qkv_t, normed).astype(g1_ref.dtype)
        g1_ref[z, qkv_rows:, :] = nn(att_t, c).astype(g1_ref.dtype)
        d_normed = nn(d_qkv, w1_ref[z, :qkv_rows, :])
        d_y = (c.astype(F32) + scale_col * gain * d_normed - y * inner_col).astype(BF16)
        g0_ref[z] = nn(att0_t, d_y).astype(g0_ref.dtype)
        part = nt(w0_ref[z, qkv_rows : qkv_rows + out_rows, :], d_y)
        d_att = part if d_att is None else d_att + part
    out_ref[...] = d_att.astype(BF16)


def fourth_kernel(heads, index, *refs):
    parts, (x_ref, qkv_ref, probs_ref, stat_ref, w0_ref, g0_ref, g1_ref) = refs[:PLANE], refs[PLANE : PLANE + 7]
    keep_ref, send_ref = refs[PLANE + 7 :]
    planes = w0_ref.shape[0]
    qkv_rows, out_rows = 3 * heads, heads
    width = x_ref.shape[-1] // planes
    rows = x_ref.shape[0] * x_ref.shape[1]
    section = index[0]
    d_att_t = summed(parts, 0, heads).astype(BF16)
    d_qkv_t = attention_grad(qkv_ref[...], probs_ref[...], d_att_t, heads)
    scale_col = column(stat_ref[0:1, :])
    for z in range(planes):
        cols = slice(z * width, (z + 1) * width)
        x = x_ref[:, :, cols].reshape(rows, width).astype(F32)
        normed = (x * scale_col * gain_of(w0_ref, z, qkv_rows + out_rows)).astype(BF16)
        zero = nn(d_qkv_t, normed)
        one = g1_ref[z, :qkv_rows, :]
        keep_ref[z, :qkv_rows, :] = jnp.where(section == 0, zero, one)
        send_ref[z, :qkv_rows, :] = jnp.where(section == 0, one, zero).astype(BF16)
        zero, one = g0_ref[z], g1_ref[z, qkv_rows:, :]
        keep_ref[z, qkv_rows:, :] = jnp.where(section == 0, zero, one)
        send_ref[z, qkv_rows:, :] = jnp.where(section == 0, one, zero).astype(BF16)


def merge_kernel(index, keep_ref, come_ref, *out_refs):
    place = index[1]
    out_refs[0][...] = keep_ref[place] + come_ref[place].astype(F32)
    for k in range(1, len(out_refs)):
        out_refs[k][...] = (keep_ref[place ^ k] + come_ref[place ^ k].astype(F32)).astype(BF16)


def last_kernel(qkv_rows, keep_ref, *refs):
    parts, (qkv_ref, out_ref) = refs[:-2], refs[-2:]
    total = keep_ref[...]
    for part in parts:
        total = total + part[...].astype(F32)
    qkv_ref[...] = total[:qkv_rows]
    out_ref[...] = total[qkv_rows:]


def call(kernel, outs, *args, scalars=0):
    smem = pl.BlockSpec(memory_space=pltpu.SMEM)
    vmem = pl.BlockSpec(memory_space=pltpu.VMEM)
    return pl.pallas_call(
        kernel,
        out_shape=[jax.ShapeDtypeStruct(shape, dtype) for shape, dtype in outs],
        in_specs=[smem] * scalars + [vmem] * (len(args) - scalars),
        out_specs=[vmem] * len(outs),
        compiler_params=pltpu.CompilerParams(vmem_limit_bytes=VMEM_LIMIT),
    )(*args)


def planar(inputs, cotangent, doc_lengths, norm_gain, w_qkv, w_out):
    shards = lax.axis_size("dp")
    planes = shards // PLANE
    section, place = lax.axis_index("section"), lax.axis_index("dp")
    z, p = place // PLANE, place % PLANE
    index = jnp.stack([section, z, p]).astype(jnp.int32)
    block, features = inputs.shape[1:]
    rows = PLANE * block
    heads, width = w_out.shape[1:]
    qkv_rows = w_qkv.shape[2]
    cols = planes * width
    def along_z(value, k):
        route = [(a * PLANE + b, (a ^ k) * PLANE + b) for a in range(planes) for b in range(PLANE)]
        return lax.ppermute(value, "dp", route)

    def to_sibling(value):
        return lax.ppermute(value, "section", [(0, 1), (1, 0)])

    def along_plane(value, k):
        route = [(a * PLANE + b, a * PLANE + (b ^ k)) for a in range(planes) for b in range(PLANE)]
        return lax.ppermute(value, "dp", route)

    def exchange(value):
        return [value] + [along_plane(value, k) for k in range(1, PLANE)]

    gain = lax.dynamic_slice(norm_gain, (0, place * width), (1, width))
    pack = jnp.concatenate(
        [w_qkv[0].T, w_out[0], jnp.pad(gain, ((0, STATS - 1), (0, 0)))], axis=0
    )
    own = [pack] + [along_z(pack, k) for k in range(1, planes)]

    blocks = pl.pallas_call(
        functools.partial(blocks_kernel, planes),
        out_shape=[jax.ShapeDtypeStruct((2, block, cols), BF16)] * PLANE,
        in_specs=[pl.BlockSpec(memory_space=pltpu.SMEM)] + [pl.BlockSpec(memory_space=pltpu.HBM)] * 2,
        out_specs=[pl.BlockSpec(memory_space=pltpu.VMEM)] * PLANE,
        scratch_shapes=[pltpu.SemaphoreType.DMA((2 * PLANE * planes,))],
        compiler_params=pltpu.CompilerParams(vmem_limit_bytes=VMEM_LIMIT),
    )(index, inputs, cotangent)
    blocks = [blocks[0]] + [along_plane(blocks[k], k) for k in range(1, PLANE)]
    other = [to_sibling(piece) for piece in own]

    weights = ((planes,) + pack.shape, BF16)
    split = ((PLANE, block, cols), BF16)
    x, c, w0, w1, sent = call(
        functools.partial(first_kernel, planes, heads),
        [split, split, weights, weights, ((qkv_rows + STATS, rows), BF16)],
        index, doc_lengths, *blocks, *own, *other, scalars=2,
    )
    sent, y, qkv, probs, att, stats = call(
        functools.partial(second_kernel, features, heads),
        [
            ((qkv_rows + STATS + heads, rows), BF16),
            ((rows, cols), BF16),
            ((qkv_rows, rows), F32),
            ((rows, rows), F32),
            ((heads, rows), BF16),
            ((8, rows), F32),
        ],
        *exchange(sent), x, c, w0, w1,
    )
    sent, g0, g1 = call(
        functools.partial(third_kernel, features, heads),
        [
            ((heads, rows), BF16),
            ((planes, heads, width), F32),
            ((planes, qkv_rows + heads, width), F32),
        ],
        *exchange(sent), c, y, att, stats, w0, w1,
    )
    grads = (planes, qkv_rows + heads, width)
    keep, send = call(
        functools.partial(fourth_kernel, heads),
        [(grads, F32), (grads, BF16)],
        index, *exchange(sent), x, qkv, probs, stats, w0, g0, g1, scalars=1,
    )
    merged = call(
        merge_kernel,
        [(grads[1:], F32)] + [(grads[1:], BF16)] * (planes - 1),
        index, keep, to_sibling(send), scalars=1,
    )
    parts = [along_z(merged[k], k) for k in range(1, planes)]
    grad_qkv, grad_out = call(
        functools.partial(last_kernel, qkv_rows),
        [((qkv_rows, width), F32), ((heads, width), F32)],
        merged[0], *parts,
    )
    return (grad_qkv.T[None], grad_out[None])


def solution(mesh):
    sections, shards = mesh.shape["section"], mesh.shape["dp"]
    planes = shards // PLANE

    def body(inputs, *rest):
        fits = shards % PLANE == 0 and planes & (planes - 1) == 0
        if sections == 2 and inputs.shape[0] == 2 and fits:
            return planar(inputs, *rest)
        return pipelined(inputs, *rest)

    return jax.shard_map(
        body,
        mesh=mesh,
        in_specs=(
            P(None, "dp", None),
            P(None, "dp", None),
            P(None, "dp", None),
            P("section", None),
            P("section", "dp", None),
            P("section", None, "dp"),
        ),
        out_specs=(P("section", "dp", None), P("section", None, "dp")),
        check_vma=False,
    )
```

```python
import functools

import jax
import jax.numpy as jnp
from jax import lax
from jax.experimental import pallas as pl
from jax.experimental.pallas import tpu as pltpu
from jax.sharding import PartitionSpec as P

F32 = jnp.float32
BF16 = jnp.bfloat16
PLANE = 4
STATS = 16
VMEM_LIMIT = 16 * 1024 * 1024


def passed_along(block, axis, distance):
    devices = range(lax.axis_size(axis))
    route = [(i - distance, i) for i in devices if i - distance in devices]
    return lax.ppermute(block, axis, route)


def segments_of(lengths, count):
    ends = jnp.cumsum(lengths)
    position = jnp.arange(count, dtype=jnp.int32)
    return jnp.sum((position[:, None] >= ends[None, :]).astype(jnp.int32), axis=1)


def layer(x, gain, w_qkv, w_out, seg):
    head = w_out.shape[0]
    x_wide = x.astype(jnp.float32)
    scale = lax.rsqrt(jnp.mean(x_wide * x_wide, axis=-1, keepdims=True) + 1e-05)
    normed = (x_wide * scale * gain.astype(jnp.float32)).astype(jnp.bfloat16)
    qkv = jnp.dot(normed, w_qkv, preferred_element_type=jnp.float32).astype(jnp.bfloat16)
    query = qkv[:, :head]
    keys = qkv[:, head : 2 * head]
    values = qkv[:, 2 * head :]
    scores = jnp.dot(query, keys.T, preferred_element_type=jnp.float32) * head ** (-0.5)
    rows = jnp.arange(x.shape[0], dtype=jnp.int32)
    allowed = (seg[:, None] == seg[None, :]) & (rows[:, None] >= rows[None, :])
    scores = jnp.where(allowed, scores, -1e30)
    probs = jax.nn.softmax(scores, axis=-1).astype(jnp.bfloat16)
    attended = jnp.dot(probs, values, preferred_element_type=jnp.float32).astype(jnp.bfloat16)
    return (x_wide + jnp.dot(attended, w_out, preferred_element_type=jnp.float32)).astype(
        jnp.bfloat16
    )


def pipelined(inputs, cotangent, doc_lengths, norm_gain, w_qkv, w_out):
    sections = lax.axis_size("section")
    section = lax.axis_index("section")
    micro = inputs.shape[0]
    count = inputs.shape[1]
    segs = jax.vmap(lambda lens: segments_of(lens, count))(doc_lengths[:, 0, :])
    gain = norm_gain[0]
    full_qkv, full_out = (
        lax.all_gather(w_qkv[0], "dp", axis=0, tiled=True),
        lax.all_gather(w_out[0], "dp", axis=1, tiled=True),
    )
    total_steps = micro + sections - 1
    empty = jnp.zeros(inputs.shape[1:], inputs.dtype)

    def forward_at(step, incoming, saved):
        index = step - section
        live = (index >= 0) & (index < micro)
        slot = jnp.clip(index, 0, micro - 1)
        first = lax.dynamic_index_in_dim(inputs, slot, 0, keepdims=False)
        x = jnp.where(section == 0, first, incoming)
        seg = lax.dynamic_index_in_dim(segs, slot, 0, keepdims=False)
        out = layer(x, gain, full_qkv, full_out, seg)
        old = lax.dynamic_index_in_dim(saved, slot, 0, keepdims=False)
        saved = lax.dynamic_update_index_in_dim(saved, jnp.where(live, x, old), slot, 0)
        return (out, saved)

    def forward_step(carry, step):
        incoming, saved = carry
        out, saved = forward_at(step, incoming, saved)
        incoming = passed_along(out, "section", 1)
        return ((incoming, saved), None)

    start_saved = jnp.zeros(inputs.shape, inputs.dtype)
    (incoming, saved), _ = lax.scan(
        forward_step, (empty, start_saved), jnp.arange(total_steps - 1, dtype=jnp.int32)
    )
    _, saved = forward_at(jnp.int32(total_steps - 1), incoming, saved)

    def backward_at(step, incoming, sum_qkv, sum_out):
        index = step - (sections - 1 - section)
        live = (index >= 0) & (index < micro)
        slot = jnp.clip(index, 0, micro - 1)
        last = lax.dynamic_index_in_dim(cotangent, slot, 0, keepdims=False)
        grad_y = jnp.where(section == sections - 1, last, incoming)
        x = lax.dynamic_index_in_dim(saved, slot, 0, keepdims=False)
        seg = lax.dynamic_index_in_dim(segs, slot, 0, keepdims=False)
        _, pull = jax.vjp(lambda a, b, c: layer(a, gain, b, c, seg), x, full_qkv, full_out)
        grad_x, grad_q, grad_o = pull(grad_y)
        sum_qkv = sum_qkv + jnp.where(live, grad_q.astype(jnp.float32), 0.0)
        sum_out = sum_out + jnp.where(live, grad_o.astype(jnp.float32), 0.0)
        return (grad_x, sum_qkv, sum_out)

    def backward_step(carry, step):
        incoming, sum_qkv, sum_out = carry
        grad_x, sum_qkv, sum_out = backward_at(step, incoming, sum_qkv, sum_out)
        incoming = passed_along(grad_x, "section", -1)
        return ((incoming, sum_qkv, sum_out), None)

    zero_qkv = jnp.zeros(full_qkv.shape, jnp.float32)
    zero_out = jnp.zeros(full_out.shape, jnp.float32)
    (incoming, sum_qkv, sum_out), _ = lax.scan(
        backward_step, (empty, zero_qkv, zero_out), jnp.arange(total_steps - 1, dtype=jnp.int32)
    )
    _, sum_qkv, sum_out = backward_at(jnp.int32(total_steps - 1), incoming, sum_qkv, sum_out)
    share_qkv, share_out = (
        lax.psum_scatter(sum_qkv, "dp", scatter_dimension=0, tiled=True),
        lax.psum_scatter(sum_out, "dp", scatter_dimension=1, tiled=True),
    )
    return (share_qkv[None], share_out[None])


def nn(a, b):
    return lax.dot_general(a, b, (((1,), (0,)), ((), ())), preferred_element_type=F32)


def nt(a, b):
    return lax.dot_general(a, b, (((1,), (1,)), ((), ())), preferred_element_type=F32)


def blocks_kernel(planes, index, gain_ref, qkv_ref, wout_ref, x_ref, c_ref, pack_ref, *refs):
    out_refs, sems = refs[:PLANE], refs[PLANE]
    qkv_rows, heads = qkv_ref.shape[0], wout_ref.shape[0]
    width = x_ref.shape[-1] // (planes * PLANE)
    section, p = index[0], index[2]
    copies = [
        pltpu.make_async_copy(qkv_ref, pack_ref.at[:qkv_rows], sems.at[0]),
        pltpu.make_async_copy(wout_ref, pack_ref.at[qkv_rows : qkv_rows + heads], sems.at[1]),
    ]
    for k in range(PLANE):
        for z in range(planes):
            at = pl.multiple_of((z * PLANE + (p ^ k)) * width, width)
            for half, ref in enumerate((x_ref, c_ref)):
                copies.append(
                    pltpu.make_async_copy(
                        ref.at[section, :, pl.ds(at, width)],
                        out_refs[k].at[half, :, pl.ds(z * width, width)],
                        sems.at[len(copies)],
                    )
                )
    for copy in copies:
        copy.start()
    pack_ref[qkv_rows + heads :, :] = jnp.broadcast_to(gain_ref[...].astype(F32), (STATS, width)).astype(BF16)
    for copy in copies:
        copy.wait()


def gain_of(w_ref, z, wide):
    return w_ref[z, wide : wide + STATS, :].astype(F32)[0:1, :]


def partial_qkv(x_of, w_ref, qkv_rows, out_rows):
    total = None
    squares = None
    for z in range(w_ref.shape[0]):
        x = x_of(z)
        gained = (x * gain_of(w_ref, z, qkv_rows + out_rows)).astype(BF16)
        part = nt(w_ref[z, :qkv_rows, :], gained)
        square = jnp.sum(x * x, axis=1, keepdims=True)
        total = part if total is None else total + part
        squares = square if squares is None else squares + square
    return total, squares


def stat_rows(squares, extra):
    rows = squares.shape[0]
    row = jnp.transpose(jnp.broadcast_to(squares, (rows, 128)))[0:STATS, :]
    at = lax.broadcasted_iota(jnp.int32, (STATS, rows), 0)
    high = row.astype(BF16).astype(F32)
    low = row - high
    out = jnp.where(at == 0, high, jnp.where(at == 1, low, 0.0))
    if extra is not None:
        out = jnp.where(at == 2, extra, out)
    return out.astype(BF16)


def first_kernel(planes, heads, index, docs, *refs):
    blocks, own, other = refs[:PLANE], refs[PLANE : PLANE + planes], refs[PLANE + planes : PLANE + 2 * planes]
    x_ref, c_ref, w0_ref, w1_ref, out_ref = refs[PLANE + 2 * planes :]
    qkv_rows, out_rows = 3 * heads, heads
    section, z, p = index[0], index[1], index[2]
    for k in range(planes):
        mine, theirs = own[k][...], other[k][...]
        w0_ref[z ^ k] = jnp.where(section == 0, mine, theirs)
        w1_ref[z ^ k] = jnp.where(section == 0, theirs, mine)
    for k in range(PLANE):
        x_ref[p ^ k] = blocks[k][0]
        c_ref[p ^ k] = blocks[k][1]
    width = x_ref.shape[-1] // planes
    rows = x_ref.shape[0] * x_ref.shape[1]

    def x_of(z):
        x = x_ref[:, :, z * width : (z + 1) * width]
        return x.reshape(rows, width).astype(F32)

    total, squares = partial_qkv(x_of, w0_ref, qkv_rows, out_rows)
    out_ref[:qkv_rows, :] = total.astype(BF16)
    position = lax.broadcasted_iota(jnp.int32, (STATS, rows), 1)
    block = rows // PLANE
    local = position - p * block
    ends = docs[section, 0, 0]
    seg = (local >= ends).astype(F32)
    for i in range(1, docs.shape[2]):
        ends = ends + docs[section, 0, i]
        seg = seg + (local >= ends).astype(F32)
    seg = jnp.where((local >= 0) & (local < block), seg, 0.0)
    out_ref[qkv_rows:, :] = stat_rows(squares, seg)


def attention(qkv_t, codes_row, codes_col, heads):
    rows = qkv_t.shape[1]
    narrow = qkv_t.astype(BF16)
    keys = jnp.transpose(qkv_t[heads : 2 * heads]).astype(BF16)
    scores = nn(keys, narrow[:heads]) * heads ** (-0.5)
    key_at = lax.broadcasted_iota(jnp.int32, (rows, rows), 0)
    query_at = lax.broadcasted_iota(jnp.int32, (rows, rows), 1)
    allowed = (codes_row == codes_col) & (query_at >= key_at)
    scores = jnp.where(allowed, scores, -1e30)
    top = jnp.max(scores, axis=0, keepdims=True)
    raised = jnp.exp(scores - top)
    probs = raised / jnp.sum(raised, axis=0, keepdims=True)
    attended = nn(narrow[2 * heads :], probs.astype(BF16)).astype(BF16)
    return probs, attended


def attention_grad(qkv_t, probs, d_att_t, heads):
    narrow = qkv_t.astype(BF16)
    values = jnp.transpose(qkv_t[2 * heads :]).astype(BF16)
    d_values = nt(d_att_t, probs.astype(BF16))
    d_probs = nn(values, d_att_t).astype(BF16).astype(F32)
    inner = jnp.sum(probs * d_probs, axis=0, keepdims=True)
    d_scores = (probs * (d_probs - inner) * heads ** (-0.5)).astype(BF16)
    d_query = nn(narrow[heads : 2 * heads], d_scores)
    d_keys = nt(narrow[:heads], d_scores)
    return jnp.concatenate([d_query, d_keys, d_values], axis=0).astype(BF16)


def summed(parts, start, stop):
    total = parts[0][start:stop, :].astype(F32)
    for part in parts[1:]:
        total = total + part[start:stop, :].astype(F32)
    return total


def scaled(parts, qkv_rows, features):
    stats = summed(parts, qkv_rows, qkv_rows + STATS)
    scale = lax.rsqrt((stats[0:1, :] + stats[1:2, :]) / features + 1e-05)
    qkv_t = (summed(parts, 0, qkv_rows) * scale).astype(BF16).astype(F32)
    return qkv_t, scale, stats


def column(row):
    count = row.shape[1]
    return jnp.transpose(jnp.broadcast_to(row, (128, count)))[:, 0:1]


def second_kernel(features, heads, *refs):
    parts, (x_ref, c_ref, w0_ref, w1_ref) = refs[:PLANE], refs[PLANE : PLANE + 4]
    out_ref, y_ref, qkv_ref, probs_ref, att_ref, stat_ref = refs[PLANE + 4 :]
    planes = w0_ref.shape[0]
    qkv_rows, out_rows = 3 * heads, heads
    width = x_ref.shape[-1] // planes
    rows = x_ref.shape[0] * x_ref.shape[1]
    qkv_t, scale, stats = scaled(parts, qkv_rows, features)
    block = lax.broadcasted_iota(jnp.int32, (1, rows), 1) // (rows // PLANE)
    codes = stats[2:3, :] + (block * rows).astype(F32)
    probs, att_t = attention(qkv_t, codes, column(codes), heads)
    qkv_ref[...] = qkv_t
    probs_ref[...] = probs
    att_ref[...] = att_t
    at = lax.broadcasted_iota(jnp.int32, stat_ref.shape, 0)
    stat_ref[...] = jnp.where(at == 0, scale, codes)
    att = jnp.transpose(att_t.astype(F32)).astype(BF16)
    d_att = None
    for z in range(planes):
        cols = slice(z * width, (z + 1) * width)
        x = x_ref[:, :, cols].reshape(rows, width).astype(F32)
        y_ref[:, cols] = (x + nn(att, w0_ref[z, qkv_rows : qkv_rows + out_rows, :])).astype(BF16)
        c = c_ref[:, :, cols].reshape(rows, width)
        part = nt(w1_ref[z, qkv_rows : qkv_rows + out_rows, :], c)
        d_att = part if d_att is None else d_att + part
    total, squares = partial_qkv(
        lambda z: y_ref[:, z * width : (z + 1) * width].astype(F32), w1_ref, qkv_rows, out_rows
    )
    out_ref[:qkv_rows, :] = total.astype(BF16)
    out_ref[qkv_rows : qkv_rows + STATS, :] = stat_rows(squares, None)
    out_ref[qkv_rows + STATS :, :] = d_att.astype(BF16)


def third_kernel(features, heads, *refs):
    parts, (c_ref, y_ref, att_ref, stat_ref, w0_ref, w1_ref) = refs[:PLANE], refs[PLANE : PLANE + 6]
    out_ref, g0_ref, g1_ref = refs[PLANE + 6 :]
    planes = w0_ref.shape[0]
    qkv_rows, out_rows = 3 * heads, heads
    width = y_ref.shape[-1] // planes
    rows = y_ref.shape[0]
    qkv_t, scale, _ = scaled(parts, qkv_rows, features)
    d_att_t = summed(parts, qkv_rows + STATS, qkv_rows + STATS + heads).astype(BF16)
    codes = stat_ref[1:2, :]
    probs, att_t = attention(qkv_t, codes, column(codes), heads)
    d_qkv_t = attention_grad(qkv_t, probs, d_att_t, heads)
    wide = d_qkv_t.astype(F32)
    inner = jnp.sum(wide * qkv_t, axis=0, keepdims=True) * scale * scale / features
    d_qkv = jnp.transpose(wide).astype(BF16)
    scale_col, inner_col = column(scale), column(inner)
    att0_t = att_ref[...]
    d_att = None
    for z in range(planes):
        cols = slice(z * width, (z + 1) * width)
        gain = gain_of(w1_ref, z, qkv_rows + out_rows)
        c = c_ref[:, :, cols].reshape(rows, width)
        y = y_ref[:, cols].astype(F32)
        normed = (y * scale_col * gain).astype(BF16)
        g1_ref[z, :qkv_rows, :] = nn(d_qkv_t, normed).astype(g1_ref.dtype)
        g1_ref[z, qkv_rows:, :] = nn(att_t, c).astype(g1_ref.dtype)
        d_normed = nn(d_qkv, w1_ref[z, :qkv_rows, :])
        d_y = (c.astype(F32) + scale_col * gain * d_normed - y * inner_col).astype(BF16)
        g0_ref[z] = nn(att0_t, d_y).astype(g0_ref.dtype)
        part = nt(w0_ref[z, qkv_rows : qkv_rows + out_rows, :], d_y)
        d_att = part if d_att is None else d_att + part
    out_ref[...] = d_att.astype(BF16)


def fourth_kernel(heads, index, *refs):
    parts, (x_ref, qkv_ref, probs_ref, stat_ref, w0_ref, g0_ref, g1_ref) = refs[:PLANE], refs[PLANE : PLANE + 7]
    keep_ref, send_ref = refs[PLANE + 7 :]
    planes = w0_ref.shape[0]
    qkv_rows, out_rows = 3 * heads, heads
    width = x_ref.shape[-1] // planes
    rows = x_ref.shape[0] * x_ref.shape[1]
    section = index[0]
    d_att_t = summed(parts, 0, heads).astype(BF16)
    d_qkv_t = attention_grad(qkv_ref[...], probs_ref[...], d_att_t, heads)
    scale_col = column(stat_ref[0:1, :])
    for z in range(planes):
        cols = slice(z * width, (z + 1) * width)
        x = x_ref[:, :, cols].reshape(rows, width).astype(F32)
        normed = (x * scale_col * gain_of(w0_ref, z, qkv_rows + out_rows)).astype(BF16)
        zero = nn(d_qkv_t, normed)
        one = g1_ref[z, :qkv_rows, :]
        keep_ref[z, :qkv_rows, :] = jnp.where(section == 0, zero, one)
        send_ref[z, :qkv_rows, :] = jnp.where(section == 0, one, zero).astype(BF16)
        zero, one = g0_ref[z], g1_ref[z, qkv_rows:, :]
        keep_ref[z, qkv_rows:, :] = jnp.where(section == 0, zero, one)
        send_ref[z, qkv_rows:, :] = jnp.where(section == 0, one, zero).astype(BF16)


def merge_kernel(index, keep_ref, come_ref, *out_refs):
    place = index[1]
    out_refs[0][...] = keep_ref[place] + come_ref[place].astype(F32)
    for k in range(1, len(out_refs)):
        out_refs[k][...] = (keep_ref[place ^ k] + come_ref[place ^ k].astype(F32)).astype(BF16)


def last_kernel(qkv_rows, keep_ref, *refs):
    parts, (qkv_ref, out_ref) = refs[:-2], refs[-2:]
    total = keep_ref[...]
    for part in parts:
        total = total + part[...].astype(F32)
    qkv_ref[...] = total[:qkv_rows]
    out_ref[...] = total[qkv_rows:]


def far_first(value, count, send):
    of = lambda k: value[k] if isinstance(value, (list, tuple)) else value
    got = {k: send(of(k), k) for k in reversed(range(1, count))}
    return [of(0)] + [got[k] for k in range(1, count)]


def call(kernel, outs, *args, scalars=0):
    smem = pl.BlockSpec(memory_space=pltpu.SMEM)
    vmem = pl.BlockSpec(memory_space=pltpu.VMEM)
    return pl.pallas_call(
        kernel,
        out_shape=[jax.ShapeDtypeStruct(shape, dtype) for shape, dtype in outs],
        in_specs=[smem] * scalars + [vmem] * (len(args) - scalars),
        out_specs=[vmem] * len(outs),
        compiler_params=pltpu.CompilerParams(vmem_limit_bytes=VMEM_LIMIT),
    )(*args)


def planar(inputs, cotangent, doc_lengths, norm_gain, w_qkv, w_out):
    shards = lax.axis_size("dp")
    planes = shards // PLANE
    section, place = lax.axis_index("section"), lax.axis_index("dp")
    z, p = place // PLANE, place % PLANE
    index = jnp.stack([section, z, p]).astype(jnp.int32)
    block, features = inputs.shape[1:]
    rows = PLANE * block
    heads, width = w_out.shape[1:]
    qkv_rows = w_qkv.shape[2]
    cols = planes * width
    def along_z(value, k):
        route = [(a * PLANE + b, (a ^ k) * PLANE + b) for a in range(planes) for b in range(PLANE)]
        return lax.ppermute(value, "dp", route)

    def to_sibling(value):
        return lax.ppermute(value, "section", [(0, 1), (1, 0)])

    def along_plane(value, k):
        route = [(a * PLANE + b, a * PLANE + (b ^ k)) for a in range(planes) for b in range(PLANE)]
        return lax.ppermute(value, "dp", route)

    def exchange(value):
        return far_first(value, PLANE, along_plane)

    gain = lax.dynamic_slice(norm_gain, (0, place * width), (1, width))
    smem, vmem = pl.BlockSpec(memory_space=pltpu.SMEM), pl.BlockSpec(memory_space=pltpu.VMEM)
    hbm = pl.BlockSpec(memory_space=pltpu.HBM)
    in_hbm = [
        pltpu.with_memory_space_constraint(value, pltpu.HBM)
        for value in (w_qkv[0].T, w_out[0], inputs, cotangent)
    ]
    pack, *blocks = pl.pallas_call(
        functools.partial(blocks_kernel, planes),
        out_shape=[jax.ShapeDtypeStruct((qkv_rows + heads + STATS, width), BF16)]
        + [jax.ShapeDtypeStruct((2, block, cols), BF16)] * PLANE,
        in_specs=[smem, vmem] + [hbm] * 4,
        out_specs=[vmem] * (1 + PLANE),
        scratch_shapes=[pltpu.SemaphoreType.DMA((2 + 2 * PLANE * planes,))],
        compiler_params=pltpu.CompilerParams(vmem_limit_bytes=VMEM_LIMIT),
    )(index, gain, *in_hbm)
    own = far_first(pack, planes, along_z)
    blocks = [blocks[0]] + far_first(blocks, PLANE, along_plane)[1:]
    other = [to_sibling(piece) for piece in own]

    weights = ((planes,) + pack.shape, BF16)
    split = ((PLANE, block, cols), BF16)
    x, c, w0, w1, sent = call(
        functools.partial(first_kernel, planes, heads),
        [split, split, weights, weights, ((qkv_rows + STATS, rows), BF16)],
        index, doc_lengths, *blocks, *own, *other, scalars=2,
    )
    sent, y, qkv, probs, att, stats = call(
        functools.partial(second_kernel, features, heads),
        [
            ((qkv_rows + STATS + heads, rows), BF16),
            ((rows, cols), BF16),
            ((qkv_rows, rows), F32),
            ((rows, rows), F32),
            ((heads, rows), BF16),
            ((8, rows), F32),
        ],
        *exchange(sent), x, c, w0, w1,
    )
    sent, g0, g1 = call(
        functools.partial(third_kernel, features, heads),
        [
            ((heads, rows), BF16),
            ((planes, heads, width), F32),
            ((planes, qkv_rows + heads, width), F32),
        ],
        *exchange(sent), c, y, att, stats, w0, w1,
    )
    grads = (planes, qkv_rows + heads, width)
    keep, send = call(
        functools.partial(fourth_kernel, heads),
        [(grads, F32), (grads, BF16)],
        index, *exchange(sent), x, qkv, probs, stats, w0, g0, g1, scalars=1,
    )
    merged = call(
        merge_kernel,
        [(grads[1:], F32)] + [(grads[1:], BF16)] * (planes - 1),
        index, keep, to_sibling(send), scalars=1,
    )
    parts = far_first(merged, planes, along_z)[1:]
    grad_qkv, grad_out = call(
        functools.partial(last_kernel, qkv_rows),
        [((qkv_rows, width), F32), ((heads, width), F32)],
        merged[0], *parts,
    )
    return (grad_qkv.T[None], grad_out[None])


def solution(mesh):
    sections, shards = mesh.shape["section"], mesh.shape["dp"]
    planes = shards // PLANE

    def body(inputs, *rest):
        fits = shards % PLANE == 0 and planes & (planes - 1) == 0
        if sections == 2 and inputs.shape[0] == 2 and fits:
            return planar(inputs, *rest)
        return pipelined(inputs, *rest)

    return jax.shard_map(
        body,
        mesh=mesh,
        in_specs=(
            P(None, "dp", None),
            P(None, "dp", None),
            P(None, "dp", None),
            P("section", None),
            P("section", "dp", None),
            P("section", None, "dp"),
        ),
        out_specs=(P("section", "dp", None), P("section", None, "dp")),
        check_vma=False,
    )
```

```python
import functools

import jax
import jax.numpy as jnp
from jax import lax
from jax.experimental import pallas as pl
from jax.experimental.pallas import tpu as pltpu
from jax.sharding import PartitionSpec as P

F32 = jnp.float32
BF16 = jnp.bfloat16
PLANE = 4
STATS = 16
VMEM_LIMIT = 16 * 1024 * 1024


def passed_along(block, axis, distance):
    devices = range(lax.axis_size(axis))
    route = [(i - distance, i) for i in devices if i - distance in devices]
    return lax.ppermute(block, axis, route)


def segments_of(lengths, count):
    ends = jnp.cumsum(lengths)
    position = jnp.arange(count, dtype=jnp.int32)
    return jnp.sum((position[:, None] >= ends[None, :]).astype(jnp.int32), axis=1)


def layer(x, gain, w_qkv, w_out, seg):
    head = w_out.shape[0]
    x_wide = x.astype(jnp.float32)
    scale = lax.rsqrt(jnp.mean(x_wide * x_wide, axis=-1, keepdims=True) + 1e-05)
    normed = (x_wide * scale * gain.astype(jnp.float32)).astype(jnp.bfloat16)
    qkv = jnp.dot(normed, w_qkv, preferred_element_type=jnp.float32).astype(jnp.bfloat16)
    query = qkv[:, :head]
    keys = qkv[:, head : 2 * head]
    values = qkv[:, 2 * head :]
    scores = jnp.dot(query, keys.T, preferred_element_type=jnp.float32) * head ** (-0.5)
    rows = jnp.arange(x.shape[0], dtype=jnp.int32)
    allowed = (seg[:, None] == seg[None, :]) & (rows[:, None] >= rows[None, :])
    scores = jnp.where(allowed, scores, -1e30)
    probs = jax.nn.softmax(scores, axis=-1).astype(jnp.bfloat16)
    attended = jnp.dot(probs, values, preferred_element_type=jnp.float32).astype(jnp.bfloat16)
    return (x_wide + jnp.dot(attended, w_out, preferred_element_type=jnp.float32)).astype(
        jnp.bfloat16
    )


def pipelined(inputs, cotangent, doc_lengths, norm_gain, w_qkv, w_out):
    sections = lax.axis_size("section")
    section = lax.axis_index("section")
    micro = inputs.shape[0]
    count = inputs.shape[1]
    segs = jax.vmap(lambda lens: segments_of(lens, count))(doc_lengths[:, 0, :])
    gain = norm_gain[0]
    full_qkv, full_out = (
        lax.all_gather(w_qkv[0], "dp", axis=0, tiled=True),
        lax.all_gather(w_out[0], "dp", axis=1, tiled=True),
    )
    total_steps = micro + sections - 1
    empty = jnp.zeros(inputs.shape[1:], inputs.dtype)

    def forward_at(step, incoming, saved):
        index = step - section
        live = (index >= 0) & (index < micro)
        slot = jnp.clip(index, 0, micro - 1)
        first = lax.dynamic_index_in_dim(inputs, slot, 0, keepdims=False)
        x = jnp.where(section == 0, first, incoming)
        seg = lax.dynamic_index_in_dim(segs, slot, 0, keepdims=False)
        out = layer(x, gain, full_qkv, full_out, seg)
        old = lax.dynamic_index_in_dim(saved, slot, 0, keepdims=False)
        saved = lax.dynamic_update_index_in_dim(saved, jnp.where(live, x, old), slot, 0)
        return (out, saved)

    def forward_step(carry, step):
        incoming, saved = carry
        out, saved = forward_at(step, incoming, saved)
        incoming = passed_along(out, "section", 1)
        return ((incoming, saved), None)

    start_saved = jnp.zeros(inputs.shape, inputs.dtype)
    (incoming, saved), _ = lax.scan(
        forward_step, (empty, start_saved), jnp.arange(total_steps - 1, dtype=jnp.int32)
    )
    _, saved = forward_at(jnp.int32(total_steps - 1), incoming, saved)

    def backward_at(step, incoming, sum_qkv, sum_out):
        index = step - (sections - 1 - section)
        live = (index >= 0) & (index < micro)
        slot = jnp.clip(index, 0, micro - 1)
        last = lax.dynamic_index_in_dim(cotangent, slot, 0, keepdims=False)
        grad_y = jnp.where(section == sections - 1, last, incoming)
        x = lax.dynamic_index_in_dim(saved, slot, 0, keepdims=False)
        seg = lax.dynamic_index_in_dim(segs, slot, 0, keepdims=False)
        _, pull = jax.vjp(lambda a, b, c: layer(a, gain, b, c, seg), x, full_qkv, full_out)
        grad_x, grad_q, grad_o = pull(grad_y)
        sum_qkv = sum_qkv + jnp.where(live, grad_q.astype(jnp.float32), 0.0)
        sum_out = sum_out + jnp.where(live, grad_o.astype(jnp.float32), 0.0)
        return (grad_x, sum_qkv, sum_out)

    def backward_step(carry, step):
        incoming, sum_qkv, sum_out = carry
        grad_x, sum_qkv, sum_out = backward_at(step, incoming, sum_qkv, sum_out)
        incoming = passed_along(grad_x, "section", -1)
        return ((incoming, sum_qkv, sum_out), None)

    zero_qkv = jnp.zeros(full_qkv.shape, jnp.float32)
    zero_out = jnp.zeros(full_out.shape, jnp.float32)
    (incoming, sum_qkv, sum_out), _ = lax.scan(
        backward_step, (empty, zero_qkv, zero_out), jnp.arange(total_steps - 1, dtype=jnp.int32)
    )
    _, sum_qkv, sum_out = backward_at(jnp.int32(total_steps - 1), incoming, sum_qkv, sum_out)
    share_qkv, share_out = (
        lax.psum_scatter(sum_qkv, "dp", scatter_dimension=0, tiled=True),
        lax.psum_scatter(sum_out, "dp", scatter_dimension=1, tiled=True),
    )
    return (share_qkv[None], share_out[None])


def nn(a, b):
    return lax.dot_general(a, b, (((1,), (0,)), ((), ())), preferred_element_type=F32)


def nt(a, b):
    return lax.dot_general(a, b, (((1,), (1,)), ((), ())), preferred_element_type=F32)


def blocks_kernel(planes, index, gain_ref, qkv_ref, wout_ref, x_ref, c_ref, pack_ref, *refs):
    out_refs, sems = refs[:PLANE], refs[PLANE]
    qkv_rows, heads = qkv_ref.shape[0], wout_ref.shape[0]
    width = x_ref.shape[-1] // (planes * PLANE)
    section, p = index[0], index[2]
    copies = [
        pltpu.make_async_copy(qkv_ref, pack_ref.at[:qkv_rows], sems.at[0]),
        pltpu.make_async_copy(wout_ref, pack_ref.at[qkv_rows : qkv_rows + heads], sems.at[1]),
    ]
    for k in range(PLANE):
        for z in range(planes):
            at = pl.multiple_of((z * PLANE + (p ^ k)) * width, width)
            for half, ref in enumerate((x_ref, c_ref)):
                copies.append(
                    pltpu.make_async_copy(
                        ref.at[section, :, pl.ds(at, width)],
                        out_refs[k].at[half, :, pl.ds(z * width, width)],
                        sems.at[len(copies)],
                    )
                )
    for copy in copies:
        copy.start()
    pack_ref[qkv_rows + heads :, :] = jnp.broadcast_to(gain_ref[...].astype(F32), (STATS, width)).astype(BF16)
    for copy in copies:
        copy.wait()


def project_kernel(planes, heads, index, *refs):
    blocks, own, other = refs[:PLANE], refs[PLANE : PLANE + planes], refs[PLANE + planes : PLANE + 2 * planes]
    x_ref, c_ref, vx_ref, gain_ref = refs[PLANE + 2 * planes : PLANE + 2 * planes + 4]
    out_refs = refs[PLANE + 2 * planes + 4 : -2]
    vc_ref, sum_ref = refs[-2:]
    qkv, width = 3 * heads, vx_ref.shape[-1]
    section, z, p = index[0], index[1], index[2]
    for k in range(planes):
        at = z ^ k
        zero = jnp.where(section == 0, own[k][...], other[k][...])
        one = jnp.where(section == 0, other[k][...], own[k][...])
        gains = [w[qkv + heads :].astype(F32)[0:1] for w in (zero, one)]
        gain_ref[at, 0:1, :] = gains[0]
        gain_ref[at, 1:2, :] = gains[1]
        empty = jnp.zeros((heads, width), BF16)
        vx_ref[at, :qkv, :] = (zero[:qkv].astype(F32) * gains[0]).astype(BF16)
        vx_ref[at, qkv : qkv + heads, :] = zero[qkv : qkv + heads]
        vx_ref[at, qkv + heads : 2 * qkv + heads, :] = (one[:qkv].astype(F32) * gains[1]).astype(BF16)
        vx_ref[at, 2 * qkv + heads :, :] = empty
        vc_ref[at, :heads, :] = empty
        vc_ref[at, heads : 2 * heads, :] = one[qkv : qkv + heads]
        vc_ref[at, 2 * heads : 3 * heads, :] = zero[qkv : qkv + heads]
        vc_ref[at, 3 * heads :, :] = empty
    for k in range(PLANE):
        x_ref[p ^ k] = blocks[k][0]
        c_ref[p ^ k] = blocks[k][1]
    rows = x_ref.shape[0] * x_ref.shape[1]
    with_x = with_c = squares = products = None
    for z in range(planes):
        cols = slice(z * width, (z + 1) * width)
        x = x_ref[:, :, cols].reshape(rows, width)
        c = c_ref[:, :, cols].reshape(rows, width)
        wide = x.astype(F32)
        out = vx_ref[z, qkv : qkv + heads, :]
        right = jnp.concatenate([vx_ref[z, qkv + heads : 2 * qkv + heads, :], out], axis=0)
        new = nt(x, vx_ref[z]), nt(c, vc_ref[z]), jnp.sum(wide * wide, axis=1, keepdims=True), nt(out, right)
        if with_x is None:
            with_x, with_c, squares, products = new
        else:
            with_x, with_c = with_x + new[0], with_c + new[1]
            squares, products = squares + new[2], products + new[3]
    half = 2 * heads
    lane = lax.broadcasted_iota(jnp.int32, (rows, half), 1)
    high = squares.astype(BF16).astype(F32)
    last = jnp.where(lane == heads, high, jnp.where(lane == heads + 1, squares - high, with_c[:, half:]))
    sum_ref[:, : 3 * half] = with_x[:, : 3 * half].astype(BF16)
    sum_ref[:, 3 * half : 4 * half] = (with_x[:, 3 * half :] + with_c[:, :half]).astype(BF16)
    sum_ref[:, 4 * half :] = last.astype(BF16)
    block = rows // PLANE
    for k in range(PLANE):
        start = pl.multiple_of((p ^ k) * block, block)
        out_refs[k][:, : 5 * half] = sum_ref[pl.ds(start, block), :]
        out_refs[k][:, 5 * half :] = products.astype(BF16)


def exact(a, b, dims):
    return lax.dot_general(
        a, b, (dims, ((), ())), precision=lax.Precision.HIGHEST, preferred_element_type=F32
    )


def attention(qkv, allowed, heads):
    query, keys, values = (qkv[:, i * heads : (i + 1) * heads].astype(BF16) for i in range(3))
    scores = jnp.where(allowed, nt(query, keys) * heads ** (-0.5), -1e30)
    raised = jnp.exp(scores - jnp.max(scores, axis=1, keepdims=True))
    probs = raised / jnp.sum(raised, axis=1, keepdims=True)
    return probs, nn(probs.astype(BF16), values).astype(BF16)


def attention_grad(qkv, probs, d_att, heads):
    query, keys, values = (qkv[:, i * heads : (i + 1) * heads].astype(BF16) for i in range(3))
    d_values = nn(jnp.transpose(probs).astype(BF16), d_att)
    d_probs = nt(d_att, values).astype(BF16).astype(F32)
    inner = jnp.sum(probs * d_probs, axis=1, keepdims=True)
    d_scores = probs * (d_probs - inner) * heads ** (-0.5)
    d_query = nn(d_scores.astype(BF16), keys)
    d_keys = nn(jnp.transpose(d_scores).astype(BF16), query)
    return jnp.concatenate([d_query, d_keys, d_values], axis=1).astype(BF16).astype(F32)


def chain_kernel(features, heads, index, docs, *refs):
    parts, out_ref = refs[:-1], refs[-1]
    qkv, half = 3 * heads, 2 * heads
    total = parts[0][...].astype(F32)
    for part in parts[1:]:
        total = total + part[...].astype(F32)
    rows = total.shape[0]
    section = index[0]
    query_at = lax.broadcasted_iota(jnp.int32, (rows, rows), 0)
    key_at = lax.broadcasted_iota(jnp.int32, (rows, rows), 1)
    allowed = query_at >= key_at
    end = 0
    for i in range(docs.shape[2]):
        end = end + docs[section, 0, i]
        allowed = allowed & ((query_at >= end) == (key_at >= end))
    x_out = total[:, qkv : 2 * half]
    x_one = total[:, 2 * half : 2 * half + qkv]
    c_one = total[:, 4 * half - heads : 4 * half].astype(BF16)
    tail = total[:, 4 * half : 5 * half]
    c_zero = tail[:, :heads]
    lane = lax.broadcasted_iota(jnp.int32, tail.shape, 1)
    squares = jnp.sum(jnp.where((lane == heads) | (lane == heads + 1), tail, 0.0), axis=1, keepdims=True)
    mixed = total[:, 5 * half : 5 * half + qkv]
    gram = total[:, 5 * half + qkv :]

    scale0 = lax.rsqrt(squares / features + 1e-05)
    qkv0 = (total[:, :qkv] * scale0).astype(BF16).astype(F32)
    probs0, att0 = attention(qkv0, allowed, heads)
    wide0 = att0.astype(F32)
    y_out = x_out + exact(wide0, gram, ((1,), (0,)))
    squares = squares + jnp.sum(wide0 * (x_out + y_out), axis=1, keepdims=True)
    scale1 = lax.rsqrt(jnp.maximum(squares, 0.0) / features + 1e-05)
    qkv1 = ((x_one + exact(wide0, mixed, ((1,), (0,)))) * scale1).astype(BF16).astype(F32)
    probs1, att1 = attention(qkv1, allowed, heads)
    d_qkv1 = attention_grad(qkv1, probs1, c_one, heads)
    inner = jnp.sum(d_qkv1 * qkv1, axis=1, keepdims=True) * scale1 * scale1 / features
    e1 = d_qkv1 * scale1
    d_att0 = c_zero + exact(e1, mixed, ((1,), (1,))) - inner * y_out
    e0 = attention_grad(qkv0, probs0, d_att0.astype(BF16), heads) * scale0
    factors = [e0, wide0, e1, wide0 * inner, att1.astype(F32), jnp.zeros((rows, heads), F32)]
    out_ref[...] = jnp.concatenate(factors, axis=1).astype(BF16)


def grads_kernel(planes, heads, index, *refs):
    factors, (x_ref, c_ref, vx_ref, gain_ref) = refs[:PLANE], refs[PLANE : PLANE + 4]
    keep_ref, send_ref, all_ref = refs[PLANE + 4 :]
    qkv, half, width = 3 * heads, 2 * heads, vx_ref.shape[-1]
    section, p = index[0], index[2]
    for k in range(PLANE):
        all_ref[p ^ k] = factors[k][...]
    rows = x_ref.shape[0] * x_ref.shape[1]
    turned = jnp.transpose(all_ref[...].astype(F32).reshape(rows, 5 * half)).astype(BF16)
    att0, att1 = turned[qkv : qkv + heads], turned[4 * half : 4 * half + heads]
    right = turned[2 * half : 4 * half]
    small = nt(right, att0).astype(BF16)
    small_t = nt(att0, right[:qkv]).astype(BF16)
    for z in range(planes):
        cols = slice(z * width, (z + 1) * width)
        x = x_ref[:, :, cols].reshape(rows, width)
        c = c_ref[:, :, cols].reshape(rows, width)
        out = vx_ref[z, qkv : qkv + heads, :]
        with_x = nn(turned[: 4 * half], x)
        left = with_x[2 * half :] + nn(small, out)
        zero = with_x[:qkv] * gain_ref[z, 0:1, :]
        one = left[:qkv] * gain_ref[z, 1:2, :]
        keep_ref[z, :qkv, :] = jnp.where(section == 0, zero, one)
        send_ref[z, :qkv, :] = jnp.where(section == 0, one, zero).astype(BF16)
        zero = nn(att0, c) + nn(small_t, vx_ref[z, qkv + heads : 2 * qkv + heads, :]) - left[qkv:]
        one = nn(att1, c)
        keep_ref[z, qkv:, :] = jnp.where(section == 0, zero, one)
        send_ref[z, qkv:, :] = jnp.where(section == 0, one, zero).astype(BF16)


def merge_kernel(index, keep_ref, come_ref, *out_refs):
    place = index[1]
    out_refs[0][...] = keep_ref[place] + come_ref[place].astype(F32)
    for k in range(1, len(out_refs)):
        out_refs[k][...] = (keep_ref[place ^ k] + come_ref[place ^ k].astype(F32)).astype(BF16)


def last_kernel(qkv_rows, keep_ref, *refs):
    parts, (qkv_ref, out_ref) = refs[:-2], refs[-2:]
    total = keep_ref[...]
    for part in parts:
        total = total + part[...].astype(F32)
    qkv_ref[...] = total[:qkv_rows]
    out_ref[...] = total[qkv_rows:]


def far_first(value, count, send):
    of = lambda k: value[k] if isinstance(value, (list, tuple)) else value
    got = {k: send(of(k), k) for k in reversed(range(1, count))}
    return [of(0)] + [got[k] for k in range(1, count)]


def call(kernel, outs, *args, scalars=0, scratch=()):
    smem = pl.BlockSpec(memory_space=pltpu.SMEM)
    vmem = pl.BlockSpec(memory_space=pltpu.VMEM)
    return pl.pallas_call(
        kernel,
        out_shape=[jax.ShapeDtypeStruct(shape, dtype) for shape, dtype in outs],
        in_specs=[smem] * scalars + [vmem] * (len(args) - scalars),
        out_specs=[vmem] * len(outs),
        scratch_shapes=[pltpu.VMEM(shape, dtype) for shape, dtype in scratch],
        compiler_params=pltpu.CompilerParams(vmem_limit_bytes=VMEM_LIMIT),
    )(*args)


def planar(inputs, cotangent, doc_lengths, norm_gain, w_qkv, w_out):
    shards = lax.axis_size("dp")
    planes = shards // PLANE
    section, place = lax.axis_index("section"), lax.axis_index("dp")
    z, p = place // PLANE, place % PLANE
    index = jnp.stack([section, z, p]).astype(jnp.int32)
    block, features = inputs.shape[1:]
    rows = PLANE * block
    heads, width = w_out.shape[1:]
    qkv_rows = w_qkv.shape[2]
    cols = planes * width
    def along_z(value, k):
        route = [(a * PLANE + b, (a ^ k) * PLANE + b) for a in range(planes) for b in range(PLANE)]
        return lax.ppermute(value, "dp", route)

    def to_sibling(value):
        return lax.ppermute(value, "section", [(0, 1), (1, 0)])

    def along_plane(value, k):
        route = [(a * PLANE + b, a * PLANE + (b ^ k)) for a in range(planes) for b in range(PLANE)]
        return lax.ppermute(value, "dp", route)

    def exchange(value):
        return far_first(value, PLANE, along_plane)

    gain = lax.dynamic_slice(norm_gain, (0, place * width), (1, width))
    smem, vmem = pl.BlockSpec(memory_space=pltpu.SMEM), pl.BlockSpec(memory_space=pltpu.VMEM)
    hbm = pl.BlockSpec(memory_space=pltpu.HBM)
    in_hbm = [
        pltpu.with_memory_space_constraint(value, pltpu.HBM)
        for value in (w_qkv[0].T, w_out[0], inputs, cotangent)
    ]
    pack, *blocks = pl.pallas_call(
        functools.partial(blocks_kernel, planes),
        out_shape=[jax.ShapeDtypeStruct((qkv_rows + heads + STATS, width), BF16)]
        + [jax.ShapeDtypeStruct((2, block, cols), BF16)] * PLANE,
        in_specs=[smem, vmem] + [hbm] * 4,
        out_specs=[vmem] * (1 + PLANE),
        scratch_shapes=[pltpu.SemaphoreType.DMA((2 + 2 * PLANE * planes,))],
        compiler_params=pltpu.CompilerParams(vmem_limit_bytes=VMEM_LIMIT),
    )(index, gain, *in_hbm)
    own = far_first(pack, planes, along_z)
    blocks = [blocks[0]] + far_first(blocks, PLANE, along_plane)[1:]
    other = [to_sibling(piece) for piece in own]

    split = ((PLANE, block, cols), BF16)
    half = 2 * heads
    x, c, vx, gains, *sent = call(
        functools.partial(project_kernel, planes, heads),
        [split, split, ((planes, 4 * half, width), BF16), ((planes, 8, width), F32)]
        + [((block, 7 * half), BF16)] * PLANE,
        index, *blocks, *own, *other, scalars=1,
        scratch=[((planes, 2 * half, width), BF16), ((rows, 5 * half), BF16)],
    )
    (factors,) = call(
        functools.partial(chain_kernel, features, heads),
        [((block, 5 * half), BF16)],
        index, doc_lengths, *exchange(sent), scalars=2,
    )
    grads = (planes, qkv_rows + heads, width)
    keep, send = call(
        functools.partial(grads_kernel, planes, heads),
        [(grads, F32), (grads, BF16)],
        index, *exchange(factors), x, c, vx, gains, scalars=1,
        scratch=[((PLANE, block, 5 * half), BF16)],
    )
    merged = call(
        merge_kernel,
        [(grads[1:], F32)] + [(grads[1:], BF16)] * (planes - 1),
        index, keep, to_sibling(send), scalars=1,
    )
    parts = far_first(merged, planes, along_z)[1:]
    grad_qkv, grad_out = call(
        functools.partial(last_kernel, qkv_rows),
        [((qkv_rows, width), F32), ((heads, width), F32)],
        merged[0], *parts,
    )
    return (grad_qkv.T[None], grad_out[None])


def solution(mesh):
    sections, shards = mesh.shape["section"], mesh.shape["dp"]
    planes = shards // PLANE

    def body(inputs, *rest):
        fits = shards % PLANE == 0 and planes & (planes - 1) == 0
        if sections == 2 and inputs.shape[0] == 2 and fits:
            return planar(inputs, *rest)
        return pipelined(inputs, *rest)

    return jax.shard_map(
        body,
        mesh=mesh,
        in_specs=(
            P(None, "dp", None),
            P(None, "dp", None),
            P(None, "dp", None),
            P("section", None),
            P("section", "dp", None),
            P("section", None, "dp"),
        ),
        out_specs=(P("section", "dp", None), P("section", None, "dp")),
        check_vma=False,
    )
```

```python
import functools

import jax
import jax.numpy as jnp
from jax import lax
from jax.experimental import pallas as pl
from jax.experimental.pallas import tpu as pltpu
from jax.sharding import PartitionSpec as P

F32 = jnp.float32
BF16 = jnp.bfloat16
PLANE = 4
STATS = 16
VMEM_LIMIT = 16 * 1024 * 1024


def passed_along(block, axis, distance):
    devices = range(lax.axis_size(axis))
    route = [(i - distance, i) for i in devices if i - distance in devices]
    return lax.ppermute(block, axis, route)


def segments_of(lengths, count):
    ends = jnp.cumsum(lengths)
    position = jnp.arange(count, dtype=jnp.int32)
    return jnp.sum((position[:, None] >= ends[None, :]).astype(jnp.int32), axis=1)


def layer(x, gain, w_qkv, w_out, seg):
    head = w_out.shape[0]
    x_wide = x.astype(jnp.float32)
    scale = lax.rsqrt(jnp.mean(x_wide * x_wide, axis=-1, keepdims=True) + 1e-05)
    normed = (x_wide * scale * gain.astype(jnp.float32)).astype(jnp.bfloat16)
    qkv = jnp.dot(normed, w_qkv, preferred_element_type=jnp.float32).astype(jnp.bfloat16)
    query = qkv[:, :head]
    keys = qkv[:, head : 2 * head]
    values = qkv[:, 2 * head :]
    scores = jnp.dot(query, keys.T, preferred_element_type=jnp.float32) * head ** (-0.5)
    rows = jnp.arange(x.shape[0], dtype=jnp.int32)
    allowed = (seg[:, None] == seg[None, :]) & (rows[:, None] >= rows[None, :])
    scores = jnp.where(allowed, scores, -1e30)
    probs = jax.nn.softmax(scores, axis=-1).astype(jnp.bfloat16)
    attended = jnp.dot(probs, values, preferred_element_type=jnp.float32).astype(jnp.bfloat16)
    return (x_wide + jnp.dot(attended, w_out, preferred_element_type=jnp.float32)).astype(
        jnp.bfloat16
    )


def pipelined(inputs, cotangent, doc_lengths, norm_gain, w_qkv, w_out):
    sections = lax.axis_size("section")
    section = lax.axis_index("section")
    micro = inputs.shape[0]
    count = inputs.shape[1]
    segs = jax.vmap(lambda lens: segments_of(lens, count))(doc_lengths[:, 0, :])
    gain = norm_gain[0]
    full_qkv, full_out = (
        lax.all_gather(w_qkv[0], "dp", axis=0, tiled=True),
        lax.all_gather(w_out[0], "dp", axis=1, tiled=True),
    )
    total_steps = micro + sections - 1
    empty = jnp.zeros(inputs.shape[1:], inputs.dtype)

    def forward_at(step, incoming, saved):
        index = step - section
        live = (index >= 0) & (index < micro)
        slot = jnp.clip(index, 0, micro - 1)
        first = lax.dynamic_index_in_dim(inputs, slot, 0, keepdims=False)
        x = jnp.where(section == 0, first, incoming)
        seg = lax.dynamic_index_in_dim(segs, slot, 0, keepdims=False)
        out = layer(x, gain, full_qkv, full_out, seg)
        old = lax.dynamic_index_in_dim(saved, slot, 0, keepdims=False)
        saved = lax.dynamic_update_index_in_dim(saved, jnp.where(live, x, old), slot, 0)
        return (out, saved)

    def forward_step(carry, step):
        incoming, saved = carry
        out, saved = forward_at(step, incoming, saved)
        incoming = passed_along(out, "section", 1)
        return ((incoming, saved), None)

    start_saved = jnp.zeros(inputs.shape, inputs.dtype)
    (incoming, saved), _ = lax.scan(
        forward_step, (empty, start_saved), jnp.arange(total_steps - 1, dtype=jnp.int32)
    )
    _, saved = forward_at(jnp.int32(total_steps - 1), incoming, saved)

    def backward_at(step, incoming, sum_qkv, sum_out):
        index = step - (sections - 1 - section)
        live = (index >= 0) & (index < micro)
        slot = jnp.clip(index, 0, micro - 1)
        last = lax.dynamic_index_in_dim(cotangent, slot, 0, keepdims=False)
        grad_y = jnp.where(section == sections - 1, last, incoming)
        x = lax.dynamic_index_in_dim(saved, slot, 0, keepdims=False)
        seg = lax.dynamic_index_in_dim(segs, slot, 0, keepdims=False)
        _, pull = jax.vjp(lambda a, b, c: layer(a, gain, b, c, seg), x, full_qkv, full_out)
        grad_x, grad_q, grad_o = pull(grad_y)
        sum_qkv = sum_qkv + jnp.where(live, grad_q.astype(jnp.float32), 0.0)
        sum_out = sum_out + jnp.where(live, grad_o.astype(jnp.float32), 0.0)
        return (grad_x, sum_qkv, sum_out)

    def backward_step(carry, step):
        incoming, sum_qkv, sum_out = carry
        grad_x, sum_qkv, sum_out = backward_at(step, incoming, sum_qkv, sum_out)
        incoming = passed_along(grad_x, "section", -1)
        return ((incoming, sum_qkv, sum_out), None)

    zero_qkv = jnp.zeros(full_qkv.shape, jnp.float32)
    zero_out = jnp.zeros(full_out.shape, jnp.float32)
    (incoming, sum_qkv, sum_out), _ = lax.scan(
        backward_step, (empty, zero_qkv, zero_out), jnp.arange(total_steps - 1, dtype=jnp.int32)
    )
    _, sum_qkv, sum_out = backward_at(jnp.int32(total_steps - 1), incoming, sum_qkv, sum_out)
    share_qkv, share_out = (
        lax.psum_scatter(sum_qkv, "dp", scatter_dimension=0, tiled=True),
        lax.psum_scatter(sum_out, "dp", scatter_dimension=1, tiled=True),
    )
    return (share_qkv[None], share_out[None])


def nn(a, b):
    return lax.dot_general(a, b, (((1,), (0,)), ((), ())), preferred_element_type=F32)


def nt(a, b):
    return lax.dot_general(a, b, (((1,), (1,)), ((), ())), preferred_element_type=F32)


def blocks_kernel(planes, index, gain_ref, qkv_ref, wout_ref, x_ref, c_ref, pack_ref, *refs):
    out_refs, sems = refs[:PLANE], refs[PLANE]
    qkv_rows, heads = qkv_ref.shape[0], wout_ref.shape[0]
    width = x_ref.shape[-1] // (planes * PLANE)
    section, p = index[0], index[2]
    copies = [
        pltpu.make_async_copy(qkv_ref, pack_ref.at[:qkv_rows], sems.at[0]),
        pltpu.make_async_copy(wout_ref, pack_ref.at[qkv_rows : qkv_rows + heads], sems.at[1]),
    ]
    for k in range(PLANE):
        for z in range(planes):
            at = pl.multiple_of((z * PLANE + (p ^ k)) * width, width)
            for half, ref in enumerate((x_ref, c_ref)):
                copies.append(
                    pltpu.make_async_copy(
                        ref.at[section, :, pl.ds(at, width)],
                        out_refs[k].at[half, :, pl.ds(z * width, width)],
                        sems.at[len(copies)],
                    )
                )
    for copy in copies:
        copy.start()
    pack_ref[qkv_rows + heads :, :] = jnp.broadcast_to(gain_ref[...].astype(F32), (STATS, width)).astype(BF16)
    for copy in copies:
        copy.wait()


def project_kernel(planes, heads, index, *refs):
    blocks, (own, other) = refs[:PLANE], refs[PLANE : PLANE + 2]
    x_ref, c_ref, vx_ref, gain_ref = refs[PLANE + 2 : PLANE + 6]
    out_refs = refs[PLANE + 6 : -2]
    vc_ref, sum_ref = refs[-2:]
    qkv, width = 3 * heads, vx_ref.shape[-1]
    section, p = index[0], index[2]
    for at in range(planes):
        zero = jnp.where(section == 0, own[at], other[at])
        one = jnp.where(section == 0, other[at], own[at])
        gains = [w[qkv + heads :].astype(F32)[0:1] for w in (zero, one)]
        gain_ref[at, 0:1, :] = gains[0]
        gain_ref[at, 1:2, :] = gains[1]
        empty = jnp.zeros((heads, width), BF16)
        vx_ref[at, :qkv, :] = (zero[:qkv].astype(F32) * gains[0]).astype(BF16)
        vx_ref[at, qkv : qkv + heads, :] = zero[qkv : qkv + heads]
        vx_ref[at, qkv + heads : 2 * qkv + heads, :] = (one[:qkv].astype(F32) * gains[1]).astype(BF16)
        vx_ref[at, 2 * qkv + heads :, :] = empty
        vc_ref[at, :heads, :] = empty
        vc_ref[at, heads : 2 * heads, :] = one[qkv : qkv + heads]
        vc_ref[at, 2 * heads : 3 * heads, :] = zero[qkv : qkv + heads]
        vc_ref[at, 3 * heads :, :] = empty
    for k in range(PLANE):
        x_ref[p ^ k] = blocks[k][0]
        c_ref[p ^ k] = blocks[k][1]
    rows = x_ref.shape[0] * x_ref.shape[1]
    with_x = with_c = squares = products = None
    for z in range(planes):
        cols = slice(z * width, (z + 1) * width)
        x = x_ref[:, :, cols].reshape(rows, width)
        c = c_ref[:, :, cols].reshape(rows, width)
        wide = x.astype(F32)
        out = vx_ref[z, qkv : qkv + heads, :]
        right = jnp.concatenate([vx_ref[z, qkv + heads : 2 * qkv + heads, :], out], axis=0)
        new = nt(x, vx_ref[z]), nt(c, vc_ref[z]), jnp.sum(wide * wide, axis=1, keepdims=True), nt(out, right)
        if with_x is None:
            with_x, with_c, squares, products = new
        else:
            with_x, with_c = with_x + new[0], with_c + new[1]
            squares, products = squares + new[2], products + new[3]
    half = 2 * heads
    lane = lax.broadcasted_iota(jnp.int32, (rows, half), 1)
    high = squares.astype(BF16).astype(F32)
    last = jnp.where(lane == heads, high, jnp.where(lane == heads + 1, squares - high, with_c[:, half:]))
    sum_ref[:, : 3 * half] = with_x[:, : 3 * half].astype(BF16)
    sum_ref[:, 3 * half : 4 * half] = (with_x[:, 3 * half :] + with_c[:, :half]).astype(BF16)
    sum_ref[:, 4 * half :] = last.astype(BF16)
    block = rows // PLANE
    for k in range(PLANE):
        start = pl.multiple_of((p ^ k) * block, block)
        out_refs[k][:, : 5 * half] = sum_ref[pl.ds(start, block), :]
        out_refs[k][:, 5 * half :] = products.astype(BF16)


def exact(a, b, dims):
    return lax.dot_general(
        a, b, (dims, ((), ())), precision=lax.Precision.HIGHEST, preferred_element_type=F32
    )


def attention(qkv, allowed, heads):
    query, keys, values = (qkv[:, i * heads : (i + 1) * heads].astype(BF16) for i in range(3))
    scores = jnp.where(allowed, nt(query, keys) * heads ** (-0.5), -1e30)
    raised = jnp.exp(scores - jnp.max(scores, axis=1, keepdims=True))
    probs = raised / jnp.sum(raised, axis=1, keepdims=True)
    return probs, nn(probs.astype(BF16), values).astype(BF16)


def attention_grad(qkv, probs, d_att, heads):
    query, keys, values = (qkv[:, i * heads : (i + 1) * heads].astype(BF16) for i in range(3))
    d_values = nn(jnp.transpose(probs).astype(BF16), d_att)
    d_probs = nt(d_att, values).astype(BF16).astype(F32)
    inner = jnp.sum(probs * d_probs, axis=1, keepdims=True)
    d_scores = probs * (d_probs - inner) * heads ** (-0.5)
    d_query = nn(d_scores.astype(BF16), keys)
    d_keys = nn(jnp.transpose(d_scores).astype(BF16), query)
    return jnp.concatenate([d_query, d_keys, d_values], axis=1).astype(BF16).astype(F32)


def chain_kernel(features, heads, index, docs, *refs):
    parts, out_ref = refs[:-1], refs[-1]
    qkv, half = 3 * heads, 2 * heads
    total = parts[0][...].astype(F32)
    for part in parts[1:]:
        total = total + part[...].astype(F32)
    rows = total.shape[0]
    section = index[0]
    query_at = lax.broadcasted_iota(jnp.int32, (rows, rows), 0)
    key_at = lax.broadcasted_iota(jnp.int32, (rows, rows), 1)
    allowed = query_at >= key_at
    end = 0
    for i in range(docs.shape[2]):
        end = end + docs[section, 0, i]
        allowed = allowed & ((query_at >= end) == (key_at >= end))
    x_out = total[:, qkv : 2 * half]
    x_one = total[:, 2 * half : 2 * half + qkv]
    c_one = total[:, 4 * half - heads : 4 * half].astype(BF16)
    tail = total[:, 4 * half : 5 * half]
    c_zero = tail[:, :heads]
    lane = lax.broadcasted_iota(jnp.int32, tail.shape, 1)
    squares = jnp.sum(jnp.where((lane == heads) | (lane == heads + 1), tail, 0.0), axis=1, keepdims=True)
    mixed = total[:, 5 * half : 5 * half + qkv]
    gram = total[:, 5 * half + qkv :]

    scale0 = lax.rsqrt(squares / features + 1e-05)
    qkv0 = (total[:, :qkv] * scale0).astype(BF16).astype(F32)
    probs0, att0 = attention(qkv0, allowed, heads)
    wide0 = att0.astype(F32)
    y_out = x_out + exact(wide0, gram, ((1,), (0,)))
    squares = squares + jnp.sum(wide0 * (x_out + y_out), axis=1, keepdims=True)
    scale1 = lax.rsqrt(jnp.maximum(squares, 0.0) / features + 1e-05)
    qkv1 = ((x_one + exact(wide0, mixed, ((1,), (0,)))) * scale1).astype(BF16).astype(F32)
    probs1, att1 = attention(qkv1, allowed, heads)
    d_qkv1 = attention_grad(qkv1, probs1, c_one, heads)
    inner = jnp.sum(d_qkv1 * qkv1, axis=1, keepdims=True) * scale1 * scale1 / features
    e1 = d_qkv1 * scale1
    d_att0 = c_zero + exact(e1, mixed, ((1,), (1,))) - inner * y_out
    e0 = attention_grad(qkv0, probs0, d_att0.astype(BF16), heads) * scale0
    factors = [e0, wide0, e1, wide0 * inner, att1.astype(F32), jnp.zeros((rows, heads), F32)]
    out_ref[...] = jnp.concatenate(factors, axis=1).astype(BF16)


def grads_kernel(planes, heads, index, *refs):
    factors, (x_ref, c_ref, vx_ref, gain_ref) = refs[:PLANE], refs[PLANE : PLANE + 4]
    keep_ref, send_ref, all_ref = refs[PLANE + 4 :]
    qkv, half, width = 3 * heads, 2 * heads, vx_ref.shape[-1]
    section, p = index[0], index[2]
    for k in range(PLANE):
        all_ref[p ^ k] = factors[k][...]
    rows = x_ref.shape[0] * x_ref.shape[1]
    turned = jnp.transpose(all_ref[...].astype(F32).reshape(rows, 5 * half)).astype(BF16)
    att0, att1 = turned[qkv : qkv + heads], turned[4 * half : 4 * half + heads]
    right = turned[2 * half : 4 * half]
    small = nt(right, att0).astype(BF16)
    small_t = nt(att0, right[:qkv]).astype(BF16)
    for z in range(planes):
        cols = slice(z * width, (z + 1) * width)
        x = x_ref[:, :, cols].reshape(rows, width)
        c = c_ref[:, :, cols].reshape(rows, width)
        out = vx_ref[z, qkv : qkv + heads, :]
        with_x = nn(turned[: 4 * half], x)
        left = with_x[2 * half :] + nn(small, out)
        zero = with_x[:qkv] * gain_ref[z, 0:1, :]
        one = left[:qkv] * gain_ref[z, 1:2, :]
        keep_ref[z, :qkv, :] = jnp.where(section == 0, zero, one)
        send_ref[z, :qkv, :] = jnp.where(section == 0, one, zero).astype(BF16)
        zero = nn(att0, c) + nn(small_t, vx_ref[z, qkv + heads : 2 * qkv + heads, :]) - left[qkv:]
        one = nn(att1, c)
        keep_ref[z, qkv:, :] = jnp.where(section == 0, zero, one)
        send_ref[z, qkv:, :] = jnp.where(section == 0, one, zero).astype(BF16)


def merge_kernel(index, keep_ref, come_ref, *out_refs):
    place = index[1]
    out_refs[0][...] = keep_ref[place] + come_ref[place].astype(F32)
    for k in range(1, len(out_refs)):
        out_refs[k][...] = (keep_ref[place ^ k] + come_ref[place ^ k].astype(F32)).astype(BF16)


def last_kernel(qkv_rows, keep_ref, *refs):
    parts, (qkv_ref, out_ref) = refs[:-2], refs[-2:]
    total = keep_ref[...]
    for part in parts:
        total = total + part[...].astype(F32)
    qkv_ref[...] = total[:qkv_rows]
    out_ref[...] = total[qkv_rows:]


def far_first(value, count, send):
    of = lambda k: value[k] if isinstance(value, (list, tuple)) else value
    got = {k: send(of(k), k) for k in reversed(range(1, count))}
    return [of(0)] + [got[k] for k in range(1, count)]


def call(kernel, outs, *args, scalars=0, scratch=()):
    smem = pl.BlockSpec(memory_space=pltpu.SMEM)
    vmem = pl.BlockSpec(memory_space=pltpu.VMEM)
    return pl.pallas_call(
        kernel,
        out_shape=[jax.ShapeDtypeStruct(shape, dtype) for shape, dtype in outs],
        in_specs=[smem] * scalars + [vmem] * (len(args) - scalars),
        out_specs=[vmem] * len(outs),
        scratch_shapes=[pltpu.VMEM(shape, dtype) for shape, dtype in scratch],
        compiler_params=pltpu.CompilerParams(vmem_limit_bytes=VMEM_LIMIT),
    )(*args)


def planar(inputs, cotangent, doc_lengths, norm_gain, w_qkv, w_out):
    shards = lax.axis_size("dp")
    planes = shards // PLANE
    section, place = lax.axis_index("section"), lax.axis_index("dp")
    z, p = place // PLANE, place % PLANE
    index = jnp.stack([section, z, p]).astype(jnp.int32)
    block, features = inputs.shape[1:]
    rows = PLANE * block
    heads, width = w_out.shape[1:]
    qkv_rows = w_qkv.shape[2]
    cols = planes * width
    def along_z(value, k):
        route = [(a * PLANE + b, (a ^ k) * PLANE + b) for a in range(planes) for b in range(PLANE)]
        return lax.ppermute(value, "dp", route)

    def to_sibling(value):
        return lax.ppermute(value, "section", [(0, 1), (1, 0)])

    def along_plane(value, k):
        route = [(a * PLANE + b, a * PLANE + (b ^ k)) for a in range(planes) for b in range(PLANE)]
        return lax.ppermute(value, "dp", route)

    def exchange(value):
        return far_first(value, PLANE, along_plane)

    gain = lax.dynamic_slice(norm_gain, (0, place * width), (1, width))
    smem, vmem = pl.BlockSpec(memory_space=pltpu.SMEM), pl.BlockSpec(memory_space=pltpu.VMEM)
    hbm = pl.BlockSpec(memory_space=pltpu.HBM)
    in_hbm = [
        pltpu.with_memory_space_constraint(value, pltpu.HBM)
        for value in (w_qkv[0].T, w_out[0], inputs, cotangent)
    ]
    pack, *blocks = pl.pallas_call(
        functools.partial(blocks_kernel, planes),
        out_shape=[jax.ShapeDtypeStruct((qkv_rows + heads + STATS, width), BF16)]
        + [jax.ShapeDtypeStruct((2, block, cols), BF16)] * PLANE,
        in_specs=[smem, vmem] + [hbm] * 4,
        out_specs=[vmem] * (1 + PLANE),
        scratch_shapes=[pltpu.SemaphoreType.DMA((2 + 2 * PLANE * planes,))],
        compiler_params=pltpu.CompilerParams(vmem_limit_bytes=VMEM_LIMIT),
    )(index, gain, *in_hbm)
    in_column = [[a * PLANE + b for a in range(planes)] for b in range(PLANE)]
    own = lax.all_gather(pack, "dp", axis=0, axis_index_groups=in_column)
    blocks = [blocks[0]] + far_first(blocks, PLANE, along_plane)[1:]
    other = to_sibling(own)

    split = ((PLANE, block, cols), BF16)
    half = 2 * heads
    x, c, vx, gains, *sent = call(
        functools.partial(project_kernel, planes, heads),
        [split, split, ((planes, 4 * half, width), BF16), ((planes, 8, width), F32)]
        + [((block, 7 * half), BF16)] * PLANE,
        index, *blocks, own, other, scalars=1,
        scratch=[((planes, 2 * half, width), BF16), ((rows, 5 * half), BF16)],
    )
    (factors,) = call(
        functools.partial(chain_kernel, features, heads),
        [((block, 5 * half), BF16)],
        index, doc_lengths, *exchange(sent), scalars=2,
    )
    grads = (planes, qkv_rows + heads, width)
    keep, send = call(
        functools.partial(grads_kernel, planes, heads),
        [(grads, F32), (grads, BF16)],
        index, *exchange(factors), x, c, vx, gains, scalars=1,
        scratch=[((PLANE, block, 5 * half), BF16)],
    )
    merged = call(
        merge_kernel,
        [(grads[1:], F32)] + [(grads[1:], BF16)] * (planes - 1),
        index, keep, to_sibling(send), scalars=1,
    )
    parts = far_first(merged, planes, along_z)[1:]
    grad_qkv, grad_out = call(
        functools.partial(last_kernel, qkv_rows),
        [((qkv_rows, width), F32), ((heads, width), F32)],
        merged[0], *parts,
    )
    return (grad_qkv.T[None], grad_out[None])


def solution(mesh):
    sections, shards = mesh.shape["section"], mesh.shape["dp"]
    planes = shards // PLANE

    def body(inputs, *rest):
        fits = shards % PLANE == 0 and planes & (planes - 1) == 0
        if sections == 2 and inputs.shape[0] == 2 and fits:
            return planar(inputs, *rest)
        return pipelined(inputs, *rest)

    return jax.shard_map(
        body,
        mesh=mesh,
        in_specs=(
            P(None, "dp", None),
            P(None, "dp", None),
            P(None, "dp", None),
            P("section", None),
            P("section", "dp", None),
            P("section", None, "dp"),
        ),
        out_specs=(P("section", "dp", None), P("section", None, "dp")),
        check_vma=False,
    )
```

```python
import functools

import jax
import jax.numpy as jnp
from jax import lax
from jax.experimental import pallas as pl
from jax.experimental.pallas import tpu as pltpu
from jax.sharding import PartitionSpec as P

F32 = jnp.float32
BF16 = jnp.bfloat16
PLANE = 4
STATS = 16
VMEM_LIMIT = 16 * 1024 * 1024


def passed_along(block, axis, distance):
    devices = range(lax.axis_size(axis))
    route = [(i - distance, i) for i in devices if i - distance in devices]
    return lax.ppermute(block, axis, route)


def segments_of(lengths, count):
    ends = jnp.cumsum(lengths)
    position = jnp.arange(count, dtype=jnp.int32)
    return jnp.sum((position[:, None] >= ends[None, :]).astype(jnp.int32), axis=1)


def layer(x, gain, w_qkv, w_out, seg):
    head = w_out.shape[0]
    x_wide = x.astype(jnp.float32)
    scale = lax.rsqrt(jnp.mean(x_wide * x_wide, axis=-1, keepdims=True) + 1e-05)
    normed = (x_wide * scale * gain.astype(jnp.float32)).astype(jnp.bfloat16)
    qkv = jnp.dot(normed, w_qkv, preferred_element_type=jnp.float32).astype(jnp.bfloat16)
    query = qkv[:, :head]
    keys = qkv[:, head : 2 * head]
    values = qkv[:, 2 * head :]
    scores = jnp.dot(query, keys.T, preferred_element_type=jnp.float32) * head ** (-0.5)
    rows = jnp.arange(x.shape[0], dtype=jnp.int32)
    allowed = (seg[:, None] == seg[None, :]) & (rows[:, None] >= rows[None, :])
    scores = jnp.where(allowed, scores, -1e30)
    probs = jax.nn.softmax(scores, axis=-1).astype(jnp.bfloat16)
    attended = jnp.dot(probs, values, preferred_element_type=jnp.float32).astype(jnp.bfloat16)
    return (x_wide + jnp.dot(attended, w_out, preferred_element_type=jnp.float32)).astype(
        jnp.bfloat16
    )


def pipelined(inputs, cotangent, doc_lengths, norm_gain, w_qkv, w_out):
    sections = lax.axis_size("section")
    section = lax.axis_index("section")
    micro = inputs.shape[0]
    count = inputs.shape[1]
    segs = jax.vmap(lambda lens: segments_of(lens, count))(doc_lengths[:, 0, :])
    gain = norm_gain[0]
    full_qkv, full_out = (
        lax.all_gather(w_qkv[0], "dp", axis=0, tiled=True),
        lax.all_gather(w_out[0], "dp", axis=1, tiled=True),
    )
    total_steps = micro + sections - 1
    empty = jnp.zeros(inputs.shape[1:], inputs.dtype)

    def forward_at(step, incoming, saved):
        index = step - section
        live = (index >= 0) & (index < micro)
        slot = jnp.clip(index, 0, micro - 1)
        first = lax.dynamic_index_in_dim(inputs, slot, 0, keepdims=False)
        x = jnp.where(section == 0, first, incoming)
        seg = lax.dynamic_index_in_dim(segs, slot, 0, keepdims=False)
        out = layer(x, gain, full_qkv, full_out, seg)
        old = lax.dynamic_index_in_dim(saved, slot, 0, keepdims=False)
        saved = lax.dynamic_update_index_in_dim(saved, jnp.where(live, x, old), slot, 0)
        return (out, saved)

    def forward_step(carry, step):
        incoming, saved = carry
        out, saved = forward_at(step, incoming, saved)
        incoming = passed_along(out, "section", 1)
        return ((incoming, saved), None)

    start_saved = jnp.zeros(inputs.shape, inputs.dtype)
    (incoming, saved), _ = lax.scan(
        forward_step, (empty, start_saved), jnp.arange(total_steps - 1, dtype=jnp.int32)
    )
    _, saved = forward_at(jnp.int32(total_steps - 1), incoming, saved)

    def backward_at(step, incoming, sum_qkv, sum_out):
        index = step - (sections - 1 - section)
        live = (index >= 0) & (index < micro)
        slot = jnp.clip(index, 0, micro - 1)
        last = lax.dynamic_index_in_dim(cotangent, slot, 0, keepdims=False)
        grad_y = jnp.where(section == sections - 1, last, incoming)
        x = lax.dynamic_index_in_dim(saved, slot, 0, keepdims=False)
        seg = lax.dynamic_index_in_dim(segs, slot, 0, keepdims=False)
        _, pull = jax.vjp(lambda a, b, c: layer(a, gain, b, c, seg), x, full_qkv, full_out)
        grad_x, grad_q, grad_o = pull(grad_y)
        sum_qkv = sum_qkv + jnp.where(live, grad_q.astype(jnp.float32), 0.0)
        sum_out = sum_out + jnp.where(live, grad_o.astype(jnp.float32), 0.0)
        return (grad_x, sum_qkv, sum_out)

    def backward_step(carry, step):
        incoming, sum_qkv, sum_out = carry
        grad_x, sum_qkv, sum_out = backward_at(step, incoming, sum_qkv, sum_out)
        incoming = passed_along(grad_x, "section", -1)
        return ((incoming, sum_qkv, sum_out), None)

    zero_qkv = jnp.zeros(full_qkv.shape, jnp.float32)
    zero_out = jnp.zeros(full_out.shape, jnp.float32)
    (incoming, sum_qkv, sum_out), _ = lax.scan(
        backward_step, (empty, zero_qkv, zero_out), jnp.arange(total_steps - 1, dtype=jnp.int32)
    )
    _, sum_qkv, sum_out = backward_at(jnp.int32(total_steps - 1), incoming, sum_qkv, sum_out)
    share_qkv, share_out = (
        lax.psum_scatter(sum_qkv, "dp", scatter_dimension=0, tiled=True),
        lax.psum_scatter(sum_out, "dp", scatter_dimension=1, tiled=True),
    )
    return (share_qkv[None], share_out[None])


def nn(a, b):
    return lax.dot_general(a, b, (((1,), (0,)), ((), ())), preferred_element_type=F32)


def nt(a, b):
    return lax.dot_general(a, b, (((1,), (1,)), ((), ())), preferred_element_type=F32)


def pack_kernel(index, gain_ref, qkv_ref, wout_ref, pack_ref, row_ref, sems):
    qkv_rows, heads, width = qkv_ref.shape[0], wout_ref.shape[0], qkv_ref.shape[1]
    at = pl.multiple_of((index[1] * PLANE + index[2]) * width, width)
    copies = [
        pltpu.make_async_copy(gain_ref.at[:, pl.ds(at, width)], row_ref, sems.at[0]),
        pltpu.make_async_copy(qkv_ref, pack_ref.at[:qkv_rows], sems.at[1]),
        pltpu.make_async_copy(wout_ref, pack_ref.at[qkv_rows : qkv_rows + heads], sems.at[2]),
    ]
    for copy in copies:
        copy.start()
    copies[0].wait()
    pack_ref[qkv_rows + heads :, :] = jnp.broadcast_to(row_ref[...].astype(F32), (STATS, width)).astype(BF16)
    copies[1].wait()
    copies[2].wait()


def blocks_kernel(planes, index, x_ref, c_ref, *refs):
    out_refs, sems = refs[:PLANE], refs[PLANE]
    width = x_ref.shape[-1] // (planes * PLANE)
    section, p = index[0], index[2]
    copies = []
    for k in range(PLANE):
        for z in range(planes):
            at = pl.multiple_of((z * PLANE + (p ^ k)) * width, width)
            for half, ref in enumerate((x_ref, c_ref)):
                copies.append(
                    pltpu.make_async_copy(
                        ref.at[section, :, pl.ds(at, width)],
                        out_refs[k].at[half, :, pl.ds(z * width, width)],
                        sems.at[len(copies)],
                    )
                )
    for copy in copies:
        copy.start()
    for copy in copies:
        copy.wait()


def project_kernel(planes, heads, index, *refs):
    blocks, own, other = refs[:PLANE], refs[PLANE : PLANE + planes], refs[PLANE + planes : PLANE + 2 * planes]
    x_ref, c_ref, vx_ref, gain_ref = refs[PLANE + 2 * planes : PLANE + 2 * planes + 4]
    out_refs = refs[PLANE + 2 * planes + 4 : -2]
    vc_ref, sum_ref = refs[-2:]
    qkv, width = 3 * heads, vx_ref.shape[-1]
    section, z, p = index[0], index[1], index[2]
    for k in range(planes):
        at = z ^ k
        zero = jnp.where(section == 0, own[k][...], other[k][...])
        one = jnp.where(section == 0, other[k][...], own[k][...])
        gains = [w[qkv + heads :].astype(F32)[0:1] for w in (zero, one)]
        gain_ref[at, 0:1, :] = gains[0]
        gain_ref[at, 1:2, :] = gains[1]
        empty = jnp.zeros((heads, width), BF16)
        vx_ref[at, :qkv, :] = (zero[:qkv].astype(F32) * gains[0]).astype(BF16)
        vx_ref[at, qkv : qkv + heads, :] = zero[qkv : qkv + heads]
        vx_ref[at, qkv + heads : 2 * qkv + heads, :] = (one[:qkv].astype(F32) * gains[1]).astype(BF16)
        vx_ref[at, 2 * qkv + heads :, :] = empty
        vc_ref[at, :heads, :] = empty
        vc_ref[at, heads : 2 * heads, :] = one[qkv : qkv + heads]
        vc_ref[at, 2 * heads : 3 * heads, :] = zero[qkv : qkv + heads]
        vc_ref[at, 3 * heads :, :] = empty
    for k in range(PLANE):
        x_ref[p ^ k] = blocks[-k][0]
        c_ref[p ^ k] = blocks[-k][1]
    rows = x_ref.shape[0] * x_ref.shape[1]
    with_x = with_c = squares = products = None
    for z in range(planes):
        cols = slice(z * width, (z + 1) * width)
        x = x_ref[:, :, cols].reshape(rows, width)
        c = c_ref[:, :, cols].reshape(rows, width)
        wide = x.astype(F32)
        out = vx_ref[z, qkv : qkv + heads, :]
        right = jnp.concatenate([vx_ref[z, qkv + heads : 2 * qkv + heads, :], out], axis=0)
        new = nt(x, vx_ref[z]), nt(c, vc_ref[z]), jnp.sum(wide * wide, axis=1, keepdims=True), nt(out, right)
        if with_x is None:
            with_x, with_c, squares, products = new
        else:
            with_x, with_c = with_x + new[0], with_c + new[1]
            squares, products = squares + new[2], products + new[3]
    half = 2 * heads
    lane = lax.broadcasted_iota(jnp.int32, (rows, half), 1)
    high = squares.astype(BF16).astype(F32)
    last = jnp.where(lane == heads, high, jnp.where(lane == heads + 1, squares - high, with_c[:, half:]))
    sum_ref[:, : 3 * half] = with_x[:, : 3 * half].astype(BF16)
    sum_ref[:, 3 * half : 4 * half] = (with_x[:, 3 * half :] + with_c[:, :half]).astype(BF16)
    sum_ref[:, 4 * half :] = last.astype(BF16)
    block = rows // PLANE
    for k in range(PLANE):
        start = pl.multiple_of((p ^ k) * block, block)
        out_refs[k][:, : 5 * half] = sum_ref[pl.ds(start, block), :]
        out_refs[k][:, 5 * half :] = products.astype(BF16)


def exact(a, b, dims):
    return lax.dot_general(
        a, b, (dims, ((), ())), precision=lax.Precision.HIGHEST, preferred_element_type=F32
    )


def attention(qkv, allowed, heads):
    query, keys, values = (qkv[:, i * heads : (i + 1) * heads].astype(BF16) for i in range(3))
    scores = jnp.where(allowed, nt(query, keys) * heads ** (-0.5), -1e30)
    raised = jnp.exp(scores - jnp.max(scores, axis=1, keepdims=True))
    probs = raised / jnp.sum(raised, axis=1, keepdims=True)
    return probs, nn(probs.astype(BF16), values).astype(BF16)


def attention_grad(qkv, probs, d_att, heads):
    query, keys, values = (qkv[:, i * heads : (i + 1) * heads].astype(BF16) for i in range(3))
    d_values = nn(jnp.transpose(probs).astype(BF16), d_att)
    d_probs = nt(d_att, values).astype(BF16).astype(F32)
    inner = jnp.sum(probs * d_probs, axis=1, keepdims=True)
    d_scores = probs * (d_probs - inner) * heads ** (-0.5)
    d_query = nn(d_scores.astype(BF16), keys)
    d_keys = nn(jnp.transpose(d_scores).astype(BF16), query)
    return jnp.concatenate([d_query, d_keys, d_values], axis=1).astype(BF16).astype(F32)


def chain_kernel(features, heads, index, docs, *refs):
    parts, out_ref = refs[:-1], refs[-1]
    qkv, half = 3 * heads, 2 * heads
    total = parts[0][...].astype(F32)
    for part in parts[1:]:
        total = total + part[...].astype(F32)
    rows = total.shape[0]
    section = index[0]
    query_at = lax.broadcasted_iota(jnp.int32, (rows, rows), 0)
    key_at = lax.broadcasted_iota(jnp.int32, (rows, rows), 1)
    allowed = query_at >= key_at
    end = 0
    for i in range(docs.shape[2]):
        end = end + docs[section, 0, i]
        allowed = allowed & ((query_at >= end) == (key_at >= end))
    x_out = total[:, qkv : 2 * half]
    x_one = total[:, 2 * half : 2 * half + qkv]
    c_one = total[:, 4 * half - heads : 4 * half].astype(BF16)
    tail = total[:, 4 * half : 5 * half]
    c_zero = tail[:, :heads]
    lane = lax.broadcasted_iota(jnp.int32, tail.shape, 1)
    squares = jnp.sum(jnp.where((lane == heads) | (lane == heads + 1), tail, 0.0), axis=1, keepdims=True)
    mixed = total[:, 5 * half : 5 * half + qkv]
    gram = total[:, 5 * half + qkv :]

    scale0 = lax.rsqrt(squares / features + 1e-05)
    qkv0 = (total[:, :qkv] * scale0).astype(BF16).astype(F32)
    probs0, att0 = attention(qkv0, allowed, heads)
    wide0 = att0.astype(F32)
    y_out = x_out + exact(wide0, gram, ((1,), (0,)))
    squares = squares + jnp.sum(wide0 * (x_out + y_out), axis=1, keepdims=True)
    scale1 = lax.rsqrt(jnp.maximum(squares, 0.0) / features + 1e-05)
    qkv1 = ((x_one + exact(wide0, mixed, ((1,), (0,)))) * scale1).astype(BF16).astype(F32)
    probs1, att1 = attention(qkv1, allowed, heads)
    d_qkv1 = attention_grad(qkv1, probs1, c_one, heads)
    inner = jnp.sum(d_qkv1 * qkv1, axis=1, keepdims=True) * scale1 * scale1 / features
    e1 = d_qkv1 * scale1
    d_att0 = c_zero + exact(e1, mixed, ((1,), (1,))) - inner * y_out
    e0 = attention_grad(qkv0, probs0, d_att0.astype(BF16), heads) * scale0
    factors = [e0, wide0, e1, wide0 * inner, att1.astype(F32), jnp.zeros((rows, heads), F32)]
    out_ref[...] = jnp.concatenate(factors, axis=1).astype(BF16)


def grads_kernel(planes, heads, index, *refs):
    factors, (x_ref, c_ref, vx_ref, gain_ref) = refs[:PLANE], refs[PLANE : PLANE + 4]
    keep_ref, send_ref, all_ref = refs[PLANE + 4 :]
    qkv, half, width = 3 * heads, 2 * heads, vx_ref.shape[-1]
    section, p = index[0], index[2]
    for k in range(PLANE):
        all_ref[p ^ k] = factors[k][...]
    rows = x_ref.shape[0] * x_ref.shape[1]
    turned = jnp.transpose(all_ref[...].astype(F32).reshape(rows, 5 * half)).astype(BF16)
    att0, att1 = turned[qkv : qkv + heads], turned[4 * half : 4 * half + heads]
    right = turned[2 * half : 4 * half]
    small = nt(right, att0).astype(BF16)
    small_t = nt(att0, right[:qkv]).astype(BF16)
    for z in range(planes):
        cols = slice(z * width, (z + 1) * width)
        x = x_ref[:, :, cols].reshape(rows, width)
        c = c_ref[:, :, cols].reshape(rows, width)
        out = vx_ref[z, qkv : qkv + heads, :]
        with_x = nn(turned[: 4 * half], x)
        left = with_x[2 * half :] + nn(small, out)
        zero = with_x[:qkv] * gain_ref[z, 0:1, :]
        one = left[:qkv] * gain_ref[z, 1:2, :]
        keep_ref[z, :qkv, :] = jnp.where(section == 0, zero, one)
        send_ref[z, :qkv, :] = jnp.where(section == 0, one, zero).astype(BF16)
        zero = nn(att0, c) + nn(small_t, vx_ref[z, qkv + heads : 2 * qkv + heads, :]) - left[qkv:]
        one = nn(att1, c)
        keep_ref[z, qkv:, :] = jnp.where(section == 0, zero, one)
        send_ref[z, qkv:, :] = jnp.where(section == 0, one, zero).astype(BF16)


def merge_kernel(index, keep_ref, come_ref, *out_refs):
    place = index[1]
    out_refs[0][...] = keep_ref[place] + come_ref[place].astype(F32)
    for k in range(1, len(out_refs)):
        out_refs[k][...] = (keep_ref[place ^ k] + come_ref[place ^ k].astype(F32)).astype(BF16)


def last_kernel(qkv_rows, keep_ref, *refs):
    parts, (qkv_ref, out_ref) = refs[:-2], refs[-2:]
    total = keep_ref[...]
    for part in parts:
        total = total + part[...].astype(F32)
    qkv_ref[...] = total[:qkv_rows]
    out_ref[...] = total[qkv_rows:]


def far_first(value, count, send):
    of = lambda k: value[k] if isinstance(value, (list, tuple)) else value
    got = {k: send(of(k), k) for k in reversed(range(1, count))}
    return [of(0)] + [got[k] for k in range(1, count)]


def call(kernel, outs, *args, scalars=0, scratch=()):
    smem = pl.BlockSpec(memory_space=pltpu.SMEM)
    vmem = pl.BlockSpec(memory_space=pltpu.VMEM)
    return pl.pallas_call(
        kernel,
        out_shape=[jax.ShapeDtypeStruct(shape, dtype) for shape, dtype in outs],
        in_specs=[smem] * scalars + [vmem] * (len(args) - scalars),
        out_specs=[vmem] * len(outs),
        scratch_shapes=[pltpu.VMEM(shape, dtype) for shape, dtype in scratch],
        compiler_params=pltpu.CompilerParams(vmem_limit_bytes=VMEM_LIMIT),
    )(*args)


def planar(inputs, cotangent, doc_lengths, norm_gain, w_qkv, w_out):
    shards = lax.axis_size("dp")
    planes = shards // PLANE
    section, place = lax.axis_index("section"), lax.axis_index("dp")
    z, p = place // PLANE, place % PLANE
    index = jnp.stack([section, z, p]).astype(jnp.int32)
    block, features = inputs.shape[1:]
    rows = PLANE * block
    heads, width = w_out.shape[1:]
    qkv_rows = w_qkv.shape[2]
    cols = planes * width
    def along_z(value, k):
        route = [(a * PLANE + b, (a ^ k) * PLANE + b) for a in range(planes) for b in range(PLANE)]
        return lax.ppermute(value, "dp", route)

    def to_sibling(value):
        return lax.ppermute(value, "section", [(0, 1), (1, 0)])

    def along_plane(value, k):
        route = [(a * PLANE + b, a * PLANE + (b ^ k)) for a in range(planes) for b in range(PLANE)]
        return lax.ppermute(value, "dp", route)

    def exchange(value):
        return far_first(value, PLANE, along_plane)

    smem, vmem = pl.BlockSpec(memory_space=pltpu.SMEM), pl.BlockSpec(memory_space=pltpu.VMEM)
    hbm = pl.BlockSpec(memory_space=pltpu.HBM)
    params = pltpu.CompilerParams(vmem_limit_bytes=VMEM_LIMIT)
    gain, qkv_in, out_in, x_in, c_in = [
        pltpu.with_memory_space_constraint(value, pltpu.HBM)
        for value in (norm_gain, w_qkv[0].T, w_out[0], inputs, cotangent)
    ]
    pack = pl.pallas_call(
        pack_kernel,
        out_shape=jax.ShapeDtypeStruct((qkv_rows + heads + STATS, width), BF16),
        in_specs=[smem] + [hbm] * 3,
        out_specs=vmem,
        scratch_shapes=[pltpu.VMEM((1, width), BF16), pltpu.SemaphoreType.DMA((3,))],
        compiler_params=params,
    )(index, gain, qkv_in, out_in)
    blocks = pl.pallas_call(
        functools.partial(blocks_kernel, planes),
        out_shape=[jax.ShapeDtypeStruct((2, block, cols), BF16)] * PLANE,
        in_specs=[smem] + [hbm] * 2,
        out_specs=[vmem] * PLANE,
        scratch_shapes=[pltpu.SemaphoreType.DMA((2 * PLANE * planes,))],
        compiler_params=params,
    )(index, x_in, c_in)
    blocks = [blocks[0]] + far_first(blocks, PLANE, along_plane)[1:]
    far = {k: along_z(pack, k) for k in reversed(range(2, planes))}
    later, _ = lax.optimization_barrier((pack, far[planes - 1] if far else pack))
    near = [along_z(later, 1)] if planes > 1 else []
    own = [later] + near + [far[k] for k in range(2, planes)]
    other = [to_sibling(piece) for piece in own]

    split = ((PLANE, block, cols), BF16)
    half = 2 * heads
    x, c, vx, gains, *sent = call(
        functools.partial(project_kernel, planes, heads),
        [split, split, ((planes, 4 * half, width), BF16), ((planes, 8, width), F32)]
        + [((block, 7 * half), BF16)] * PLANE,
        index, blocks[0], *blocks[:0:-1], *own, *other, scalars=1,
        scratch=[((planes, 2 * half, width), BF16), ((rows, 5 * half), BF16)],
    )
    (factors,) = call(
        functools.partial(chain_kernel, features, heads),
        [((block, 5 * half), BF16)],
        index, doc_lengths, *exchange(sent)[::-1], scalars=2,
    )
    grads = (planes, qkv_rows + heads, width)
    keep, send = call(
        functools.partial(grads_kernel, planes, heads),
        [(grads, F32), (grads, BF16)],
        index, *exchange(factors), x, c, vx, gains, scalars=1,
        scratch=[((PLANE, block, 5 * half), BF16)],
    )
    merged = call(
        merge_kernel,
        [(grads[1:], F32)] + [(grads[1:], BF16)] * (planes - 1),
        index, keep, to_sibling(send), scalars=1,
    )
    parts = far_first(merged, planes, along_z)[1:]
    grad_qkv, grad_out = call(
        functools.partial(last_kernel, qkv_rows),
        [((qkv_rows, width), F32), ((heads, width), F32)],
        merged[0], *parts[::-1],
    )
    return (grad_qkv.T[None], grad_out[None])


def solution(mesh):
    sections, shards = mesh.shape["section"], mesh.shape["dp"]
    planes = shards // PLANE

    def body(inputs, *rest):
        fits = shards % PLANE == 0 and planes & (planes - 1) == 0
        if sections == 2 and inputs.shape[0] == 2 and fits:
            return planar(inputs, *rest)
        return pipelined(inputs, *rest)

    return jax.shard_map(
        body,
        mesh=mesh,
        in_specs=(
            P(None, "dp", None),
            P(None, "dp", None),
            P(None, "dp", None),
            P("section", None),
            P("section", "dp", None),
            P("section", None, "dp"),
        ),
        out_specs=(P("section", "dp", None), P("section", None, "dp")),
        check_vma=False,
    )
```

```python
import functools

import jax
import jax.numpy as jnp
from jax import lax
from jax.experimental import pallas as pl
from jax.experimental.pallas import tpu as pltpu
from jax.sharding import PartitionSpec as P

F32 = jnp.float32
BF16 = jnp.bfloat16
PLANE = 4
NEAR = 2
STATS = 16
VMEM_LIMIT = 16 * 1024 * 1024


def passed_along(block, axis, distance):
    devices = range(lax.axis_size(axis))
    route = [(i - distance, i) for i in devices if i - distance in devices]
    return lax.ppermute(block, axis, route)


def segments_of(lengths, count):
    ends = jnp.cumsum(lengths)
    position = jnp.arange(count, dtype=jnp.int32)
    return jnp.sum((position[:, None] >= ends[None, :]).astype(jnp.int32), axis=1)


def layer(x, gain, w_qkv, w_out, seg):
    head = w_out.shape[0]
    x_wide = x.astype(jnp.float32)
    scale = lax.rsqrt(jnp.mean(x_wide * x_wide, axis=-1, keepdims=True) + 1e-05)
    normed = (x_wide * scale * gain.astype(jnp.float32)).astype(jnp.bfloat16)
    qkv = jnp.dot(normed, w_qkv, preferred_element_type=jnp.float32).astype(jnp.bfloat16)
    query = qkv[:, :head]
    keys = qkv[:, head : 2 * head]
    values = qkv[:, 2 * head :]
    scores = jnp.dot(query, keys.T, preferred_element_type=jnp.float32) * head ** (-0.5)
    rows = jnp.arange(x.shape[0], dtype=jnp.int32)
    allowed = (seg[:, None] == seg[None, :]) & (rows[:, None] >= rows[None, :])
    scores = jnp.where(allowed, scores, -1e30)
    probs = jax.nn.softmax(scores, axis=-1).astype(jnp.bfloat16)
    attended = jnp.dot(probs, values, preferred_element_type=jnp.float32).astype(jnp.bfloat16)
    return (x_wide + jnp.dot(attended, w_out, preferred_element_type=jnp.float32)).astype(
        jnp.bfloat16
    )


def pipelined(inputs, cotangent, doc_lengths, norm_gain, w_qkv, w_out):
    sections = lax.axis_size("section")
    section = lax.axis_index("section")
    micro = inputs.shape[0]
    count = inputs.shape[1]
    segs = jax.vmap(lambda lens: segments_of(lens, count))(doc_lengths[:, 0, :])
    gain = norm_gain[0]
    full_qkv, full_out = (
        lax.all_gather(w_qkv[0], "dp", axis=0, tiled=True),
        lax.all_gather(w_out[0], "dp", axis=1, tiled=True),
    )
    total_steps = micro + sections - 1
    empty = jnp.zeros(inputs.shape[1:], inputs.dtype)

    def forward_at(step, incoming, saved):
        index = step - section
        live = (index >= 0) & (index < micro)
        slot = jnp.clip(index, 0, micro - 1)
        first = lax.dynamic_index_in_dim(inputs, slot, 0, keepdims=False)
        x = jnp.where(section == 0, first, incoming)
        seg = lax.dynamic_index_in_dim(segs, slot, 0, keepdims=False)
        out = layer(x, gain, full_qkv, full_out, seg)
        old = lax.dynamic_index_in_dim(saved, slot, 0, keepdims=False)
        saved = lax.dynamic_update_index_in_dim(saved, jnp.where(live, x, old), slot, 0)
        return (out, saved)

    def forward_step(carry, step):
        incoming, saved = carry
        out, saved = forward_at(step, incoming, saved)
        incoming = passed_along(out, "section", 1)
        return ((incoming, saved), None)

    start_saved = jnp.zeros(inputs.shape, inputs.dtype)
    (incoming, saved), _ = lax.scan(
        forward_step, (empty, start_saved), jnp.arange(total_steps - 1, dtype=jnp.int32)
    )
    _, saved = forward_at(jnp.int32(total_steps - 1), incoming, saved)

    def backward_at(step, incoming, sum_qkv, sum_out):
        index = step - (sections - 1 - section)
        live = (index >= 0) & (index < micro)
        slot = jnp.clip(index, 0, micro - 1)
        last = lax.dynamic_index_in_dim(cotangent, slot, 0, keepdims=False)
        grad_y = jnp.where(section == sections - 1, last, incoming)
        x = lax.dynamic_index_in_dim(saved, slot, 0, keepdims=False)
        seg = lax.dynamic_index_in_dim(segs, slot, 0, keepdims=False)
        _, pull = jax.vjp(lambda a, b, c: layer(a, gain, b, c, seg), x, full_qkv, full_out)
        grad_x, grad_q, grad_o = pull(grad_y)
        sum_qkv = sum_qkv + jnp.where(live, grad_q.astype(jnp.float32), 0.0)
        sum_out = sum_out + jnp.where(live, grad_o.astype(jnp.float32), 0.0)
        return (grad_x, sum_qkv, sum_out)

    def backward_step(carry, step):
        incoming, sum_qkv, sum_out = carry
        grad_x, sum_qkv, sum_out = backward_at(step, incoming, sum_qkv, sum_out)
        incoming = passed_along(grad_x, "section", -1)
        return ((incoming, sum_qkv, sum_out), None)

    zero_qkv = jnp.zeros(full_qkv.shape, jnp.float32)
    zero_out = jnp.zeros(full_out.shape, jnp.float32)
    (incoming, sum_qkv, sum_out), _ = lax.scan(
        backward_step, (empty, zero_qkv, zero_out), jnp.arange(total_steps - 1, dtype=jnp.int32)
    )
    _, sum_qkv, sum_out = backward_at(jnp.int32(total_steps - 1), incoming, sum_qkv, sum_out)
    share_qkv, share_out = (
        lax.psum_scatter(sum_qkv, "dp", scatter_dimension=0, tiled=True),
        lax.psum_scatter(sum_out, "dp", scatter_dimension=1, tiled=True),
    )
    return (share_qkv[None], share_out[None])


def nn(a, b):
    return lax.dot_general(a, b, (((1,), (0,)), ((), ())), preferred_element_type=F32)


def nt(a, b):
    return lax.dot_general(a, b, (((1,), (1,)), ((), ())), preferred_element_type=F32)


def pack_kernel(index, gain_ref, qkv_ref, wout_ref, pack_ref, row_ref, sems):
    qkv_rows, heads, width = qkv_ref.shape[0], wout_ref.shape[0], qkv_ref.shape[1]
    at = pl.multiple_of((index[1] * PLANE + index[2]) * width, width)
    copies = [
        pltpu.make_async_copy(gain_ref.at[:, pl.ds(at, width)], row_ref, sems.at[0]),
        pltpu.make_async_copy(qkv_ref, pack_ref.at[:qkv_rows], sems.at[1]),
        pltpu.make_async_copy(wout_ref, pack_ref.at[qkv_rows : qkv_rows + heads], sems.at[2]),
    ]
    for copy in copies:
        copy.start()
    copies[0].wait()
    pack_ref[qkv_rows + heads :, :] = jnp.broadcast_to(row_ref[...].astype(F32), (STATS, width)).astype(BF16)
    copies[1].wait()
    copies[2].wait()


def blocks_kernel(planes, index, x_ref, c_ref, *refs):
    out_refs, sems = refs[:PLANE], refs[PLANE]
    width = x_ref.shape[-1] // (planes * PLANE)
    section, p = index[0], index[2]
    copies = []
    for k in range(PLANE):
        for z in range(planes):
            at = pl.multiple_of((z * PLANE + (p ^ k)) * width, width)
            for half, ref in enumerate((x_ref, c_ref)):
                copies.append(
                    pltpu.make_async_copy(
                        ref.at[section, :, pl.ds(at, width)],
                        out_refs[k].at[half, :, pl.ds(z * width, width)],
                        sems.at[len(copies)],
                    )
                )
    for copy in copies:
        copy.start()
    for copy in copies:
        copy.wait()


def project_kernel(planes, heads, index, *refs):
    blocks, own, other = refs[:PLANE], refs[PLANE : PLANE + planes], refs[PLANE + planes : PLANE + 2 * planes]
    vx_ref, gain_ref, mine_ref, near_ref = refs[PLANE + 2 * planes : PLANE + 2 * planes + 4]
    out_refs = refs[PLANE + 2 * planes + 4 : -4]
    x_ref, c_ref, vc_ref, sum_ref = refs[-4:]
    qkv, width = 3 * heads, vx_ref.shape[-1]
    section, place, p = index[0], index[1], index[2]
    for k in range(planes):
        at = place ^ k
        zero = jnp.where(section == 0, own[k][...], other[k][...])
        one = jnp.where(section == 0, other[k][...], own[k][...])
        gains = [w[qkv + heads :].astype(F32)[0:1] for w in (zero, one)]
        gain_ref[at, 0:1, :] = gains[0]
        gain_ref[at, 1:2, :] = gains[1]
        empty = jnp.zeros((heads, width), BF16)
        vx_ref[at, :qkv, :] = (zero[:qkv].astype(F32) * gains[0]).astype(BF16)
        vx_ref[at, qkv : qkv + heads, :] = zero[qkv : qkv + heads]
        vx_ref[at, qkv + heads : 2 * qkv + heads, :] = (one[:qkv].astype(F32) * gains[1]).astype(BF16)
        vx_ref[at, 2 * qkv + heads :, :] = empty
        vc_ref[at, :heads, :] = empty
        vc_ref[at, heads : 2 * heads, :] = one[qkv : qkv + heads]
        vc_ref[at, 2 * heads : 3 * heads, :] = zero[qkv : qkv + heads]
        vc_ref[at, 3 * heads :, :] = empty
    for k in range(PLANE):
        x_ref[p ^ k] = blocks[-k][0]
        c_ref[p ^ k] = blocks[-k][1]
    rows = x_ref.shape[0] * x_ref.shape[1]
    with_x = with_c = squares = products = None
    for z in range(planes):
        cols = slice(z * width, (z + 1) * width)
        x = x_ref[:, :, cols].reshape(rows, width)
        c = c_ref[:, :, cols].reshape(rows, width)
        wide = x.astype(F32)
        out = vx_ref[z, qkv : qkv + heads, :]
        right = jnp.concatenate([vx_ref[z, qkv + heads : 2 * qkv + heads, :], out], axis=0)
        new = nt(x, vx_ref[z]), nt(c, vc_ref[z]), jnp.sum(wide * wide, axis=1, keepdims=True), nt(out, right)
        if with_x is None:
            with_x, with_c, squares, products = new
        else:
            with_x, with_c = with_x + new[0], with_c + new[1]
            squares, products = squares + new[2], products + new[3]
    half = 2 * heads
    lane = lax.broadcasted_iota(jnp.int32, (rows, half), 1)
    high = squares.astype(BF16).astype(F32)
    last = jnp.where(lane == heads, high, jnp.where(lane == heads + 1, squares - high, with_c[:, half:]))
    sum_ref[:, : 3 * half] = with_x[:, : 3 * half].astype(BF16)
    sum_ref[:, 3 * half : 4 * half] = (with_x[:, 3 * half :] + with_c[:, :half]).astype(BF16)
    sum_ref[:, 4 * half :] = last.astype(BF16)
    block = rows // PLANE
    for k in range(PLANE):
        start = pl.multiple_of((p ^ k) * block, block)
        out_refs[k][:, : 5 * half] = sum_ref[pl.ds(start, block), :]
        out_refs[k][:, 5 * half :] = products.astype(BF16)
    for h in range(planes // NEAR):
        for to_ref, low in ((mine_ref, place & (NEAR - 1)), (near_ref, (place ^ 1) & (NEAR - 1))):
            cols = pl.ds(pl.multiple_of((h * NEAR + low) * width, width), width)
            to_ref[0, h] = x_ref[:, :, cols].reshape(rows, width)
            to_ref[1, h] = c_ref[:, :, cols].reshape(rows, width)


def exact(a, b, dims):
    return lax.dot_general(
        a, b, (dims, ((), ())), precision=lax.Precision.HIGHEST, preferred_element_type=F32
    )


def attention(qkv, allowed, heads):
    query, keys, values = (qkv[:, i * heads : (i + 1) * heads].astype(BF16) for i in range(3))
    scores = jnp.where(allowed, nt(query, keys) * heads ** (-0.5), -1e30)
    raised = jnp.exp(scores - jnp.max(scores, axis=1, keepdims=True))
    probs = raised / jnp.sum(raised, axis=1, keepdims=True)
    return probs, nn(probs.astype(BF16), values).astype(BF16)


def attention_grad(qkv, probs, d_att, heads):
    query, keys, values = (qkv[:, i * heads : (i + 1) * heads].astype(BF16) for i in range(3))
    d_values = nn(jnp.transpose(probs).astype(BF16), d_att)
    d_probs = nt(d_att, values).astype(BF16).astype(F32)
    inner = jnp.sum(probs * d_probs, axis=1, keepdims=True)
    d_scores = probs * (d_probs - inner) * heads ** (-0.5)
    d_query = nn(d_scores.astype(BF16), keys)
    d_keys = nn(jnp.transpose(d_scores).astype(BF16), query)
    return jnp.concatenate([d_query, d_keys, d_values], axis=1).astype(BF16).astype(F32)


def chain_kernel(features, heads, index, docs, *refs):
    parts, out_ref = refs[:-1], refs[-1]
    qkv, half = 3 * heads, 2 * heads
    total = parts[0][...].astype(F32)
    for part in parts[1:]:
        total = total + part[...].astype(F32)
    rows = total.shape[0]
    section = index[0]
    query_at = lax.broadcasted_iota(jnp.int32, (rows, rows), 0)
    key_at = lax.broadcasted_iota(jnp.int32, (rows, rows), 1)
    allowed = query_at >= key_at
    end = 0
    for i in range(docs.shape[2]):
        end = end + docs[section, 0, i]
        allowed = allowed & ((query_at >= end) == (key_at >= end))
    x_out = total[:, qkv : 2 * half]
    x_one = total[:, 2 * half : 2 * half + qkv]
    c_one = total[:, 4 * half - heads : 4 * half].astype(BF16)
    tail = total[:, 4 * half : 5 * half]
    c_zero = tail[:, :heads]
    lane = lax.broadcasted_iota(jnp.int32, tail.shape, 1)
    squares = jnp.sum(jnp.where((lane == heads) | (lane == heads + 1), tail, 0.0), axis=1, keepdims=True)
    mixed = total[:, 5 * half : 5 * half + qkv]
    gram = total[:, 5 * half + qkv :]

    scale0 = lax.rsqrt(squares / features + 1e-05)
    qkv0 = (total[:, :qkv] * scale0).astype(BF16).astype(F32)
    probs0, att0 = attention(qkv0, allowed, heads)
    wide0 = att0.astype(F32)
    y_out = x_out + exact(wide0, gram, ((1,), (0,)))
    squares = squares + jnp.sum(wide0 * (x_out + y_out), axis=1, keepdims=True)
    scale1 = lax.rsqrt(jnp.maximum(squares, 0.0) / features + 1e-05)
    qkv1 = ((x_one + exact(wide0, mixed, ((1,), (0,)))) * scale1).astype(BF16).astype(F32)
    probs1, att1 = attention(qkv1, allowed, heads)
    d_qkv1 = attention_grad(qkv1, probs1, c_one, heads)
    inner = jnp.sum(d_qkv1 * qkv1, axis=1, keepdims=True) * scale1 * scale1 / features
    e1 = d_qkv1 * scale1
    d_att0 = c_zero + exact(e1, mixed, ((1,), (1,))) - inner * y_out
    e0 = attention_grad(qkv0, probs0, d_att0.astype(BF16), heads) * scale0
    factors = [e0, wide0, e1, wide0 * inner, att1.astype(F32), jnp.zeros((rows, heads), F32)]
    out_ref[...] = jnp.concatenate(factors, axis=1).astype(BF16)


def grads_kernel(planes, heads, index, *refs):
    groups = refs[:PLANE], refs[PLANE : NEAR * PLANE]
    wide_refs, (vx_ref, gain_ref) = refs[NEAR * PLANE : NEAR * PLANE + NEAR], refs[NEAR * (PLANE + 1) : -3]
    keep_ref, send_ref, all_ref = refs[-3:]
    qkv, half = 3 * heads, 2 * heads
    section, z, p = index[0], index[1], index[2]
    for g, group in enumerate(groups):
        for k in range(PLANE):
            all_ref[g, p ^ k] = group[k][...]
    rows = wide_refs[0].shape[2]
    turned = jnp.transpose(all_ref[...].astype(F32).reshape(NEAR * rows, 5 * half)).astype(BF16)
    att0, att1 = turned[qkv : qkv + heads], turned[4 * half : 4 * half + heads]
    right = turned[2 * half : 4 * half]
    small = nt(right, att0).astype(BF16)
    small_t = nt(att0, right[:qkv]).astype(BF16)
    for h in range(planes // NEAR):
        at = h * NEAR + (z & (NEAR - 1))
        x = jnp.concatenate([ref[0, h] for ref in wide_refs], axis=0)
        c = jnp.concatenate([ref[1, h] for ref in wide_refs], axis=0)
        out = vx_ref[at, qkv : qkv + heads, :]
        with_x = nn(turned[: 4 * half], x)
        left = with_x[2 * half :] + nn(small, out)
        zero = with_x[:qkv] * gain_ref[at, 0:1, :]
        one = left[:qkv] * gain_ref[at, 1:2, :]
        keep_ref[h, :qkv, :] = jnp.where(section == 0, zero, one)
        send_ref[h, :qkv, :] = jnp.where(section == 0, one, zero).astype(BF16)
        zero = nn(att0, c) + nn(small_t, vx_ref[at, qkv + heads : 2 * qkv + heads, :]) - left[qkv:]
        one = nn(att1, c)
        keep_ref[h, qkv:, :] = jnp.where(section == 0, zero, one)
        send_ref[h, qkv:, :] = jnp.where(section == 0, one, zero).astype(BF16)


def merge_kernel(index, keep_ref, come_ref, *out_refs):
    place = index[1] >> (NEAR.bit_length() - 1)
    out_refs[0][...] = keep_ref[place] + come_ref[place].astype(F32)
    for k in range(1, len(out_refs)):
        out_refs[k][...] = (keep_ref[place ^ k] + come_ref[place ^ k].astype(F32)).astype(BF16)


def last_kernel(qkv_rows, keep_ref, *refs):
    parts, (qkv_ref, out_ref) = refs[:-2], refs[-2:]
    total = keep_ref[...]
    for part in parts:
        total = total + part[...].astype(F32)
    qkv_ref[...] = total[:qkv_rows]
    out_ref[...] = total[qkv_rows:]


def far_first(value, count, send):
    of = lambda k: value[k] if isinstance(value, (list, tuple)) else value
    got = {k: send(of(k), k) for k in reversed(range(1, count))}
    return [of(0)] + [got[k] for k in range(1, count)]


def call(kernel, outs, *args, scalars=0, scratch=()):
    smem = pl.BlockSpec(memory_space=pltpu.SMEM)
    vmem = pl.BlockSpec(memory_space=pltpu.VMEM)
    return pl.pallas_call(
        kernel,
        out_shape=[jax.ShapeDtypeStruct(shape, dtype) for shape, dtype in outs],
        in_specs=[smem] * scalars + [vmem] * (len(args) - scalars),
        out_specs=[vmem] * len(outs),
        scratch_shapes=[pltpu.VMEM(shape, dtype) for shape, dtype in scratch],
        compiler_params=pltpu.CompilerParams(vmem_limit_bytes=VMEM_LIMIT),
    )(*args)


def planar(inputs, cotangent, doc_lengths, norm_gain, w_qkv, w_out):
    shards = lax.axis_size("dp")
    planes = shards // PLANE
    section, place = lax.axis_index("section"), lax.axis_index("dp")
    z, p = place // PLANE, place % PLANE
    index = jnp.stack([section, z, p]).astype(jnp.int32)
    block, features = inputs.shape[1:]
    rows = PLANE * block
    heads, width = w_out.shape[1:]
    qkv_rows = w_qkv.shape[2]
    cols = planes * width
    def along_z(value, k):
        route = [(a * PLANE + b, (a ^ k) * PLANE + b) for a in range(planes) for b in range(PLANE)]
        return lax.ppermute(value, "dp", route)

    def to_sibling(value):
        return lax.ppermute(value, "section", [(0, 1), (1, 0)])

    def along_plane(value, k, up=0):
        route = [(a * PLANE + b, (a ^ up) * PLANE + (b ^ k)) for a in range(planes) for b in range(PLANE)]
        return lax.ppermute(value, "dp", route)

    def exchange(value):
        return far_first(value, PLANE, along_plane)

    smem, vmem = pl.BlockSpec(memory_space=pltpu.SMEM), pl.BlockSpec(memory_space=pltpu.VMEM)
    hbm = pl.BlockSpec(memory_space=pltpu.HBM)
    params = pltpu.CompilerParams(vmem_limit_bytes=VMEM_LIMIT)
    gain, qkv_in, out_in, x_in, c_in = [
        pltpu.with_memory_space_constraint(value, pltpu.HBM)
        for value in (norm_gain, w_qkv[0].T, w_out[0], inputs, cotangent)
    ]
    pack = pl.pallas_call(
        pack_kernel,
        out_shape=jax.ShapeDtypeStruct((qkv_rows + heads + STATS, width), BF16),
        in_specs=[smem] + [hbm] * 3,
        out_specs=vmem,
        scratch_shapes=[pltpu.VMEM((1, width), BF16), pltpu.SemaphoreType.DMA((3,))],
        compiler_params=params,
    )(index, gain, qkv_in, out_in)
    blocks = pl.pallas_call(
        functools.partial(blocks_kernel, planes),
        out_shape=[jax.ShapeDtypeStruct((2, block, cols), BF16)] * PLANE,
        in_specs=[smem] + [hbm] * 2,
        out_specs=[vmem] * PLANE,
        scratch_shapes=[pltpu.SemaphoreType.DMA((2 * PLANE * planes,))],
        compiler_params=params,
    )(index, x_in, c_in)
    blocks = [blocks[0]] + far_first(blocks, PLANE, along_plane)[1:]
    far = {k: along_z(pack, k) for k in reversed(range(2, planes))}
    later, _ = lax.optimization_barrier((pack, far[planes - 1] if far else pack))
    near = [along_z(later, 1)] if planes > 1 else []
    own = [later] + near + [far[k] for k in range(2, planes)]
    other = [to_sibling(piece) for piece in own]

    split = ((PLANE, block, cols), BF16)
    half, highs = 2 * heads, planes // NEAR
    columns = ((2, highs, rows, width), BF16)
    vx, gains, mine, near, *sent = call(
        functools.partial(project_kernel, planes, heads),
        [((planes, 4 * half, width), BF16), ((planes, 8, width), F32), columns, columns]
        + [((block, 7 * half), BF16)] * PLANE,
        index, blocks[0], *blocks[:0:-1], *own, *other, scalars=1,
        scratch=[split, split, ((planes, 2 * half, width), BF16), ((rows, 5 * half), BF16)],
    )
    (factors,) = call(
        functools.partial(chain_kernel, features, heads),
        [((block, 5 * half), BF16)],
        index, doc_lengths, *exchange(sent)[::-1], scalars=2,
    )
    near = along_z(near, 1)
    gathered = [along_plane(factors, k, up) for up in range(NEAR) for k in range(PLANE) if up or k]
    grads = (highs, qkv_rows + heads, width)
    keep, send = call(
        functools.partial(grads_kernel, planes, heads),
        [(grads, F32), (grads, BF16)],
        index, factors, *gathered, mine, near, vx, gains, scalars=1,
        scratch=[((NEAR, PLANE, block, 5 * half), BF16)],
    )
    merged = call(
        merge_kernel,
        [(grads[1:], F32)] + [(grads[1:], BF16)] * (highs - 1),
        index, keep, to_sibling(send), scalars=1,
    )
    parts = [along_z(merged[k], k * NEAR) for k in range(1, highs)]
    grad_qkv, grad_out = call(
        functools.partial(last_kernel, qkv_rows),
        [((qkv_rows, width), F32), ((heads, width), F32)],
        merged[0], *parts,
    )
    return (grad_qkv.T[None], grad_out[None])


def solution(mesh):
    sections, shards = mesh.shape["section"], mesh.shape["dp"]
    planes = shards // PLANE

    def body(inputs, *rest):
        fits = shards % (PLANE * NEAR) == 0 and planes & (planes - 1) == 0
        if sections == 2 and inputs.shape[0] == 2 and fits:
            return planar(inputs, *rest)
        return pipelined(inputs, *rest)

    return jax.shard_map(
        body,
        mesh=mesh,
        in_specs=(
            P(None, "dp", None),
            P(None, "dp", None),
            P(None, "dp", None),
            P("section", None),
            P("section", "dp", None),
            P("section", None, "dp"),
        ),
        out_specs=(P("section", "dp", None), P("section", None, "dp")),
        check_vma=False,
    )
```

```python
import functools

import jax
import jax.numpy as jnp
from jax import lax
from jax.experimental import pallas as pl
from jax.experimental.pallas import tpu as pltpu
from jax.sharding import PartitionSpec as P

F32 = jnp.float32
BF16 = jnp.bfloat16
PLANE = 4
RING = (0, 1, 3, 2)
STATS = 16
VMEM_LIMIT = 16 * 1024 * 1024


def passed_along(block, axis, distance):
    devices = range(lax.axis_size(axis))
    route = [(i - distance, i) for i in devices if i - distance in devices]
    return lax.ppermute(block, axis, route)


def segments_of(lengths, count):
    ends = jnp.cumsum(lengths)
    position = jnp.arange(count, dtype=jnp.int32)
    return jnp.sum((position[:, None] >= ends[None, :]).astype(jnp.int32), axis=1)


def layer(x, gain, w_qkv, w_out, seg):
    head = w_out.shape[0]
    x_wide = x.astype(jnp.float32)
    scale = lax.rsqrt(jnp.mean(x_wide * x_wide, axis=-1, keepdims=True) + 1e-05)
    normed = (x_wide * scale * gain.astype(jnp.float32)).astype(jnp.bfloat16)
    qkv = jnp.dot(normed, w_qkv, preferred_element_type=jnp.float32).astype(jnp.bfloat16)
    query = qkv[:, :head]
    keys = qkv[:, head : 2 * head]
    values = qkv[:, 2 * head :]
    scores = jnp.dot(query, keys.T, preferred_element_type=jnp.float32) * head ** (-0.5)
    rows = jnp.arange(x.shape[0], dtype=jnp.int32)
    allowed = (seg[:, None] == seg[None, :]) & (rows[:, None] >= rows[None, :])
    scores = jnp.where(allowed, scores, -1e30)
    probs = jax.nn.softmax(scores, axis=-1).astype(jnp.bfloat16)
    attended = jnp.dot(probs, values, preferred_element_type=jnp.float32).astype(jnp.bfloat16)
    return (x_wide + jnp.dot(attended, w_out, preferred_element_type=jnp.float32)).astype(
        jnp.bfloat16
    )


def pipelined(inputs, cotangent, doc_lengths, norm_gain, w_qkv, w_out):
    sections = lax.axis_size("section")
    section = lax.axis_index("section")
    micro = inputs.shape[0]
    count = inputs.shape[1]
    segs = jax.vmap(lambda lens: segments_of(lens, count))(doc_lengths[:, 0, :])
    gain = norm_gain[0]
    full_qkv, full_out = (
        lax.all_gather(w_qkv[0], "dp", axis=0, tiled=True),
        lax.all_gather(w_out[0], "dp", axis=1, tiled=True),
    )
    total_steps = micro + sections - 1
    empty = jnp.zeros(inputs.shape[1:], inputs.dtype)

    def forward_at(step, incoming, saved):
        index = step - section
        live = (index >= 0) & (index < micro)
        slot = jnp.clip(index, 0, micro - 1)
        first = lax.dynamic_index_in_dim(inputs, slot, 0, keepdims=False)
        x = jnp.where(section == 0, first, incoming)
        seg = lax.dynamic_index_in_dim(segs, slot, 0, keepdims=False)
        out = layer(x, gain, full_qkv, full_out, seg)
        old = lax.dynamic_index_in_dim(saved, slot, 0, keepdims=False)
        saved = lax.dynamic_update_index_in_dim(saved, jnp.where(live, x, old), slot, 0)
        return (out, saved)

    def forward_step(carry, step):
        incoming, saved = carry
        out, saved = forward_at(step, incoming, saved)
        incoming = passed_along(out, "section", 1)
        return ((incoming, saved), None)

    start_saved = jnp.zeros(inputs.shape, inputs.dtype)
    (incoming, saved), _ = lax.scan(
        forward_step, (empty, start_saved), jnp.arange(total_steps - 1, dtype=jnp.int32)
    )
    _, saved = forward_at(jnp.int32(total_steps - 1), incoming, saved)

    def backward_at(step, incoming, sum_qkv, sum_out):
        index = step - (sections - 1 - section)
        live = (index >= 0) & (index < micro)
        slot = jnp.clip(index, 0, micro - 1)
        last = lax.dynamic_index_in_dim(cotangent, slot, 0, keepdims=False)
        grad_y = jnp.where(section == sections - 1, last, incoming)
        x = lax.dynamic_index_in_dim(saved, slot, 0, keepdims=False)
        seg = lax.dynamic_index_in_dim(segs, slot, 0, keepdims=False)
        _, pull = jax.vjp(lambda a, b, c: layer(a, gain, b, c, seg), x, full_qkv, full_out)
        grad_x, grad_q, grad_o = pull(grad_y)
        sum_qkv = sum_qkv + jnp.where(live, grad_q.astype(jnp.float32), 0.0)
        sum_out = sum_out + jnp.where(live, grad_o.astype(jnp.float32), 0.0)
        return (grad_x, sum_qkv, sum_out)

    def backward_step(carry, step):
        incoming, sum_qkv, sum_out = carry
        grad_x, sum_qkv, sum_out = backward_at(step, incoming, sum_qkv, sum_out)
        incoming = passed_along(grad_x, "section", -1)
        return ((incoming, sum_qkv, sum_out), None)

    zero_qkv = jnp.zeros(full_qkv.shape, jnp.float32)
    zero_out = jnp.zeros(full_out.shape, jnp.float32)
    (incoming, sum_qkv, sum_out), _ = lax.scan(
        backward_step, (empty, zero_qkv, zero_out), jnp.arange(total_steps - 1, dtype=jnp.int32)
    )
    _, sum_qkv, sum_out = backward_at(jnp.int32(total_steps - 1), incoming, sum_qkv, sum_out)
    share_qkv, share_out = (
        lax.psum_scatter(sum_qkv, "dp", scatter_dimension=0, tiled=True),
        lax.psum_scatter(sum_out, "dp", scatter_dimension=1, tiled=True),
    )
    return (share_qkv[None], share_out[None])


def nn(a, b):
    return lax.dot_general(a, b, (((1,), (0,)), ((), ())), preferred_element_type=F32)


def nt(a, b):
    return lax.dot_general(a, b, (((1,), (1,)), ((), ())), preferred_element_type=F32)


def pack_kernel(index, gain_ref, qkv_ref, wout_ref, pack_ref, row_ref, sems):
    qkv_rows, heads, width = qkv_ref.shape[0], wout_ref.shape[0], qkv_ref.shape[1]
    at = pl.multiple_of((index[1] * PLANE + index[2]) * width, width)
    copies = [
        pltpu.make_async_copy(gain_ref.at[:, pl.ds(at, width)], row_ref, sems.at[0]),
        pltpu.make_async_copy(qkv_ref, pack_ref.at[:qkv_rows], sems.at[1]),
        pltpu.make_async_copy(wout_ref, pack_ref.at[qkv_rows : qkv_rows + heads], sems.at[2]),
    ]
    for copy in copies:
        copy.start()
    copies[0].wait()
    pack_ref[qkv_rows + heads :, :] = jnp.broadcast_to(row_ref[...].astype(F32), (STATS, width)).astype(BF16)
    copies[1].wait()
    copies[2].wait()


def blocks_kernel(planes, index, x_ref, c_ref, *refs):
    out_refs, sems = refs[:PLANE], refs[PLANE]
    width = x_ref.shape[-1] // (planes * PLANE)
    section, p = index[0], index[2]
    copies = []
    for k in range(PLANE):
        for z in range(planes):
            at = pl.multiple_of((z * PLANE + (p ^ k)) * width, width)
            for half, ref in enumerate((x_ref, c_ref)):
                copies.append(
                    pltpu.make_async_copy(
                        ref.at[section, :, pl.ds(at, width)],
                        out_refs[k].at[half, :, pl.ds(z * width, width)],
                        sems.at[len(copies)],
                    )
                )
    for copy in copies:
        copy.start()
    for copy in copies:
        copy.wait()


def project_kernel(planes, heads, index, *refs):
    blocks, own, other = refs[:PLANE], refs[PLANE : PLANE + planes], refs[PLANE + planes : PLANE + 2 * planes]
    x_ref, c_ref, vx_ref, gain_ref = refs[PLANE + 2 * planes : PLANE + 2 * planes + 4]
    out_refs = refs[PLANE + 2 * planes + 4 : -2]
    vc_ref, sum_ref = refs[-2:]
    qkv, width = 3 * heads, vx_ref.shape[-1]
    section, z, p = index[0], index[1], index[2]
    for k in range(planes):
        at = z ^ k
        zero = jnp.where(section == 0, own[k][...], other[k][...])
        one = jnp.where(section == 0, other[k][...], own[k][...])
        gains = [w[qkv + heads :].astype(F32)[0:1] for w in (zero, one)]
        gain_ref[at, 0:1, :] = gains[0]
        gain_ref[at, 1:2, :] = gains[1]
        empty = jnp.zeros((heads, width), BF16)
        vx_ref[at, :qkv, :] = (zero[:qkv].astype(F32) * gains[0]).astype(BF16)
        vx_ref[at, qkv : qkv + heads, :] = zero[qkv : qkv + heads]
        vx_ref[at, qkv + heads : 2 * qkv + heads, :] = (one[:qkv].astype(F32) * gains[1]).astype(BF16)
        vx_ref[at, 2 * qkv + heads :, :] = empty
        vc_ref[at, :heads, :] = empty
        vc_ref[at, heads : 2 * heads, :] = one[qkv : qkv + heads]
        vc_ref[at, 2 * heads : 3 * heads, :] = zero[qkv : qkv + heads]
        vc_ref[at, 3 * heads :, :] = empty
    for k in range(PLANE):
        x_ref[p ^ k] = blocks[-k][0]
        c_ref[p ^ k] = blocks[-k][1]
    rows = x_ref.shape[0] * x_ref.shape[1]
    with_x = with_c = squares = products = None
    for z in range(planes):
        cols = slice(z * width, (z + 1) * width)
        x = x_ref[:, :, cols].reshape(rows, width)
        c = c_ref[:, :, cols].reshape(rows, width)
        wide = x.astype(F32)
        out = vx_ref[z, qkv : qkv + heads, :]
        right = jnp.concatenate([vx_ref[z, qkv + heads : 2 * qkv + heads, :], out], axis=0)
        new = nt(x, vx_ref[z]), nt(c, vc_ref[z]), jnp.sum(wide * wide, axis=1, keepdims=True), nt(out, right)
        if with_x is None:
            with_x, with_c, squares, products = new
        else:
            with_x, with_c = with_x + new[0], with_c + new[1]
            squares, products = squares + new[2], products + new[3]
    half = 2 * heads
    lane = lax.broadcasted_iota(jnp.int32, (rows, half), 1)
    high = squares.astype(BF16).astype(F32)
    last = jnp.where(lane == heads, high, jnp.where(lane == heads + 1, squares - high, with_c[:, half:]))
    sum_ref[:, : 3 * half] = with_x[:, : 3 * half].astype(BF16)
    sum_ref[:, 3 * half : 4 * half] = (with_x[:, 3 * half :] + with_c[:, :half]).astype(BF16)
    sum_ref[:, 4 * half :] = last.astype(BF16)
    block = rows // PLANE
    for k in range(PLANE):
        start = pl.multiple_of((p ^ k) * block, block)
        out_refs[k][:, : 5 * half] = sum_ref[pl.ds(start, block), :]
        out_refs[k][:, 5 * half :] = products.astype(BF16)


def exact(a, b, dims):
    return lax.dot_general(
        a, b, (dims, ((), ())), precision=lax.Precision.HIGHEST, preferred_element_type=F32
    )


def attention(qkv, allowed, heads):
    query, keys, values = (qkv[:, i * heads : (i + 1) * heads].astype(BF16) for i in range(3))
    scores = jnp.where(allowed, nt(query, keys) * heads ** (-0.5), -1e30)
    raised = jnp.exp(scores - jnp.max(scores, axis=1, keepdims=True))
    probs = raised / jnp.sum(raised, axis=1, keepdims=True)
    return probs, nn(probs.astype(BF16), values).astype(BF16)


def attention_grad(qkv, probs, d_att, heads):
    query, keys, values = (qkv[:, i * heads : (i + 1) * heads].astype(BF16) for i in range(3))
    d_values = nn(jnp.transpose(probs).astype(BF16), d_att)
    d_probs = nt(d_att, values).astype(BF16).astype(F32)
    inner = jnp.sum(probs * d_probs, axis=1, keepdims=True)
    d_scores = probs * (d_probs - inner) * heads ** (-0.5)
    d_query = nn(d_scores.astype(BF16), keys)
    d_keys = nn(jnp.transpose(d_scores).astype(BF16), query)
    return jnp.concatenate([d_query, d_keys, d_values], axis=1).astype(BF16).astype(F32)


def chain_kernel(features, heads, index, docs, *refs):
    parts, out_ref = refs[:-1], refs[-1]
    qkv, half = 3 * heads, 2 * heads
    total = parts[0][...].astype(F32)
    for part in parts[1:]:
        total = total + part[...].astype(F32)
    rows = total.shape[0]
    section = index[0]
    query_at = lax.broadcasted_iota(jnp.int32, (rows, rows), 0)
    key_at = lax.broadcasted_iota(jnp.int32, (rows, rows), 1)
    allowed = query_at >= key_at
    end = 0
    for i in range(docs.shape[2]):
        end = end + docs[section, 0, i]
        allowed = allowed & ((query_at >= end) == (key_at >= end))
    x_out = total[:, qkv : 2 * half]
    x_one = total[:, 2 * half : 2 * half + qkv]
    c_one = total[:, 4 * half - heads : 4 * half].astype(BF16)
    tail = total[:, 4 * half : 5 * half]
    c_zero = tail[:, :heads]
    lane = lax.broadcasted_iota(jnp.int32, tail.shape, 1)
    squares = jnp.sum(jnp.where((lane == heads) | (lane == heads + 1), tail, 0.0), axis=1, keepdims=True)
    mixed = total[:, 5 * half : 5 * half + qkv]
    gram = total[:, 5 * half + qkv :]

    scale0 = lax.rsqrt(squares / features + 1e-05)
    qkv0 = (total[:, :qkv] * scale0).astype(BF16).astype(F32)
    probs0, att0 = attention(qkv0, allowed, heads)
    wide0 = att0.astype(F32)
    y_out = x_out + exact(wide0, gram, ((1,), (0,)))
    squares = squares + jnp.sum(wide0 * (x_out + y_out), axis=1, keepdims=True)
    scale1 = lax.rsqrt(jnp.maximum(squares, 0.0) / features + 1e-05)
    qkv1 = ((x_one + exact(wide0, mixed, ((1,), (0,)))) * scale1).astype(BF16).astype(F32)
    probs1, att1 = attention(qkv1, allowed, heads)
    d_qkv1 = attention_grad(qkv1, probs1, c_one, heads)
    inner = jnp.sum(d_qkv1 * qkv1, axis=1, keepdims=True) * scale1 * scale1 / features
    e1 = d_qkv1 * scale1
    d_att0 = c_zero + exact(e1, mixed, ((1,), (1,))) - inner * y_out
    e0 = attention_grad(qkv0, probs0, d_att0.astype(BF16), heads) * scale0
    factors = [e0, wide0, e1, wide0 * inner, att1.astype(F32), jnp.zeros((rows, heads), F32)]
    out_ref[...] = jnp.concatenate(factors, axis=1).astype(BF16)


def grads_kernel(planes, heads, index, *refs):
    ring_ref, x_ref, c_ref, vx_ref, gain_ref, keep_ref, send_ref = refs
    qkv, half, width = 3 * heads, 2 * heads, vx_ref.shape[-1]
    section = index[0]
    rows = x_ref.shape[0] * x_ref.shape[1]
    in_order = jnp.concatenate([ring_ref[RING.index(b)] for b in range(PLANE)], axis=0)
    turned = jnp.transpose(in_order.astype(F32)).astype(BF16)
    att0, att1 = turned[qkv : qkv + heads], turned[4 * half : 4 * half + heads]
    right = turned[2 * half : 4 * half]
    small = nt(right, att0).astype(BF16)
    small_t = nt(att0, right[:qkv]).astype(BF16)
    for z in range(planes):
        cols = slice(z * width, (z + 1) * width)
        x = x_ref[:, :, cols].reshape(rows, width)
        c = c_ref[:, :, cols].reshape(rows, width)
        out = vx_ref[z, qkv : qkv + heads, :]
        with_x = nn(turned[: 4 * half], x)
        left = with_x[2 * half :] + nn(small, out)
        zero = with_x[:qkv] * gain_ref[z, 0:1, :]
        one = left[:qkv] * gain_ref[z, 1:2, :]
        keep_ref[z, :qkv, :] = jnp.where(section == 0, zero, one)
        send_ref[z, :qkv, :] = jnp.where(section == 0, one, zero).astype(BF16)
        zero = nn(att0, c) + nn(small_t, vx_ref[z, qkv + heads : 2 * qkv + heads, :]) - left[qkv:]
        one = nn(att1, c)
        keep_ref[z, qkv:, :] = jnp.where(section == 0, zero, one)
        send_ref[z, qkv:, :] = jnp.where(section == 0, one, zero).astype(BF16)


def merge_kernel(index, keep_ref, come_ref, *out_refs):
    place = index[1]
    out_refs[0][...] = keep_ref[place] + come_ref[place].astype(F32)
    for k in range(1, len(out_refs)):
        out_refs[k][...] = (keep_ref[place ^ k] + come_ref[place ^ k].astype(F32)).astype(BF16)


def last_kernel(qkv_rows, keep_ref, *refs):
    parts, (qkv_ref, out_ref) = refs[:-2], refs[-2:]
    total = keep_ref[...]
    for part in parts:
        total = total + part[...].astype(F32)
    qkv_ref[...] = total[:qkv_rows]
    out_ref[...] = total[qkv_rows:]


def far_first(value, count, send):
    of = lambda k: value[k] if isinstance(value, (list, tuple)) else value
    got = {k: send(of(k), k) for k in reversed(range(1, count))}
    return [of(0)] + [got[k] for k in range(1, count)]


def call(kernel, outs, *args, scalars=0, scratch=()):
    smem = pl.BlockSpec(memory_space=pltpu.SMEM)
    vmem = pl.BlockSpec(memory_space=pltpu.VMEM)
    return pl.pallas_call(
        kernel,
        out_shape=[jax.ShapeDtypeStruct(shape, dtype) for shape, dtype in outs],
        in_specs=[smem] * scalars + [vmem] * (len(args) - scalars),
        out_specs=[vmem] * len(outs),
        scratch_shapes=[pltpu.VMEM(shape, dtype) for shape, dtype in scratch],
        compiler_params=pltpu.CompilerParams(vmem_limit_bytes=VMEM_LIMIT),
    )(*args)


def planar(inputs, cotangent, doc_lengths, norm_gain, w_qkv, w_out):
    shards = lax.axis_size("dp")
    planes = shards // PLANE
    section, place = lax.axis_index("section"), lax.axis_index("dp")
    z, p = place // PLANE, place % PLANE
    index = jnp.stack([section, z, p]).astype(jnp.int32)
    block, features = inputs.shape[1:]
    rows = PLANE * block
    heads, width = w_out.shape[1:]
    qkv_rows = w_qkv.shape[2]
    cols = planes * width
    def along_z(value, k):
        route = [(a * PLANE + b, (a ^ k) * PLANE + b) for a in range(planes) for b in range(PLANE)]
        return lax.ppermute(value, "dp", route)

    def to_sibling(value):
        return lax.ppermute(value, "section", [(0, 1), (1, 0)])

    def along_plane(value, k):
        route = [(a * PLANE + b, a * PLANE + (b ^ k)) for a in range(planes) for b in range(PLANE)]
        return lax.ppermute(value, "dp", route)

    in_ring = [[a * PLANE + b for b in RING] for a in range(planes)]

    def exchange(value):
        return far_first(value, PLANE, along_plane)

    smem, vmem = pl.BlockSpec(memory_space=pltpu.SMEM), pl.BlockSpec(memory_space=pltpu.VMEM)
    hbm = pl.BlockSpec(memory_space=pltpu.HBM)
    params = pltpu.CompilerParams(vmem_limit_bytes=VMEM_LIMIT)
    gain, qkv_in, out_in, x_in, c_in = [
        pltpu.with_memory_space_constraint(value, pltpu.HBM)
        for value in (norm_gain, w_qkv[0].T, w_out[0], inputs, cotangent)
    ]
    pack = pl.pallas_call(
        pack_kernel,
        out_shape=jax.ShapeDtypeStruct((qkv_rows + heads + STATS, width), BF16),
        in_specs=[smem] + [hbm] * 3,
        out_specs=vmem,
        scratch_shapes=[pltpu.VMEM((1, width), BF16), pltpu.SemaphoreType.DMA((3,))],
        compiler_params=params,
    )(index, gain, qkv_in, out_in)
    blocks = pl.pallas_call(
        functools.partial(blocks_kernel, planes),
        out_shape=[jax.ShapeDtypeStruct((2, block, cols), BF16)] * PLANE,
        in_specs=[smem] + [hbm] * 2,
        out_specs=[vmem] * PLANE,
        scratch_shapes=[pltpu.SemaphoreType.DMA((2 * PLANE * planes,))],
        compiler_params=params,
    )(index, x_in, c_in)
    blocks = [blocks[0]] + far_first(blocks, PLANE, along_plane)[1:]
    far = {k: along_z(pack, k) for k in reversed(range(2, planes))}
    later, _ = lax.optimization_barrier((pack, far[planes - 1] if far else pack))
    near = [along_z(later, 1)] if planes > 1 else []
    own = [later] + near + [far[k] for k in range(2, planes)]
    other = [to_sibling(piece) for piece in own]

    split = ((PLANE, block, cols), BF16)
    half = 2 * heads
    x, c, vx, gains, *sent = call(
        functools.partial(project_kernel, planes, heads),
        [split, split, ((planes, 4 * half, width), BF16), ((planes, 8, width), F32)]
        + [((block, 7 * half), BF16)] * PLANE,
        index, blocks[0], *blocks[:0:-1], *own, *other, scalars=1,
        scratch=[((planes, 2 * half, width), BF16), ((rows, 5 * half), BF16)],
    )
    (factors,) = call(
        functools.partial(chain_kernel, features, heads),
        [((block, 5 * half), BF16)],
        index, doc_lengths, *exchange(sent)[::-1], scalars=2,
    )
    grads = (planes, qkv_rows + heads, width)
    keep, send = call(
        functools.partial(grads_kernel, planes, heads),
        [(grads, F32), (grads, BF16)],
        index, lax.all_gather(factors, "dp", axis=0, axis_index_groups=in_ring), x, c, vx, gains, scalars=1,
    )
    merged = call(
        merge_kernel,
        [(grads[1:], F32)] + [(grads[1:], BF16)] * (planes - 1),
        index, keep, to_sibling(send), scalars=1,
    )
    parts = far_first(merged, planes, along_z)[1:]
    grad_qkv, grad_out = call(
        functools.partial(last_kernel, qkv_rows),
        [((qkv_rows, width), F32), ((heads, width), F32)],
        merged[0], *parts[::-1],
    )
    return (grad_qkv.T[None], grad_out[None])


def solution(mesh):
    sections, shards = mesh.shape["section"], mesh.shape["dp"]
    planes = shards // PLANE

    def body(inputs, *rest):
        fits = shards % PLANE == 0 and planes & (planes - 1) == 0
        if sections == 2 and inputs.shape[0] == 2 and fits:
            return planar(inputs, *rest)
        return pipelined(inputs, *rest)

    return jax.shard_map(
        body,
        mesh=mesh,
        in_specs=(
            P(None, "dp", None),
            P(None, "dp", None),
            P(None, "dp", None),
            P("section", None),
            P("section", "dp", None),
            P("section", None, "dp"),
        ),
        out_specs=(P("section", "dp", None), P("section", None, "dp")),
        check_vma=False,
    )
```

```python
import functools

import jax
import jax.numpy as jnp
from jax import lax
from jax.experimental import pallas as pl
from jax.experimental.pallas import tpu as pltpu
from jax.sharding import PartitionSpec as P

F32 = jnp.float32
BF16 = jnp.bfloat16
PLANE = 4
STATS = 16
VMEM_LIMIT = 16 * 1024 * 1024


def passed_along(block, axis, distance):
    devices = range(lax.axis_size(axis))
    route = [(i - distance, i) for i in devices if i - distance in devices]
    return lax.ppermute(block, axis, route)


def segments_of(lengths, count):
    ends = jnp.cumsum(lengths)
    position = jnp.arange(count, dtype=jnp.int32)
    return jnp.sum((position[:, None] >= ends[None, :]).astype(jnp.int32), axis=1)


def layer(x, gain, w_qkv, w_out, seg):
    head = w_out.shape[0]
    x_wide = x.astype(jnp.float32)
    scale = lax.rsqrt(jnp.mean(x_wide * x_wide, axis=-1, keepdims=True) + 1e-05)
    normed = (x_wide * scale * gain.astype(jnp.float32)).astype(jnp.bfloat16)
    qkv = jnp.dot(normed, w_qkv, preferred_element_type=jnp.float32).astype(jnp.bfloat16)
    query = qkv[:, :head]
    keys = qkv[:, head : 2 * head]
    values = qkv[:, 2 * head :]
    scores = jnp.dot(query, keys.T, preferred_element_type=jnp.float32) * head ** (-0.5)
    rows = jnp.arange(x.shape[0], dtype=jnp.int32)
    allowed = (seg[:, None] == seg[None, :]) & (rows[:, None] >= rows[None, :])
    scores = jnp.where(allowed, scores, -1e30)
    probs = jax.nn.softmax(scores, axis=-1).astype(jnp.bfloat16)
    attended = jnp.dot(probs, values, preferred_element_type=jnp.float32).astype(jnp.bfloat16)
    return (x_wide + jnp.dot(attended, w_out, preferred_element_type=jnp.float32)).astype(
        jnp.bfloat16
    )


def pipelined(inputs, cotangent, doc_lengths, norm_gain, w_qkv, w_out):
    sections = lax.axis_size("section")
    section = lax.axis_index("section")
    micro = inputs.shape[0]
    count = inputs.shape[1]
    segs = jax.vmap(lambda lens: segments_of(lens, count))(doc_lengths[:, 0, :])
    gain = norm_gain[0]
    full_qkv, full_out = (
        lax.all_gather(w_qkv[0], "dp", axis=0, tiled=True),
        lax.all_gather(w_out[0], "dp", axis=1, tiled=True),
    )
    total_steps = micro + sections - 1
    empty = jnp.zeros(inputs.shape[1:], inputs.dtype)

    def forward_at(step, incoming, saved):
        index = step - section
        live = (index >= 0) & (index < micro)
        slot = jnp.clip(index, 0, micro - 1)
        first = lax.dynamic_index_in_dim(inputs, slot, 0, keepdims=False)
        x = jnp.where(section == 0, first, incoming)
        seg = lax.dynamic_index_in_dim(segs, slot, 0, keepdims=False)
        out = layer(x, gain, full_qkv, full_out, seg)
        old = lax.dynamic_index_in_dim(saved, slot, 0, keepdims=False)
        saved = lax.dynamic_update_index_in_dim(saved, jnp.where(live, x, old), slot, 0)
        return (out, saved)

    def forward_step(carry, step):
        incoming, saved = carry
        out, saved = forward_at(step, incoming, saved)
        incoming = passed_along(out, "section", 1)
        return ((incoming, saved), None)

    start_saved = jnp.zeros(inputs.shape, inputs.dtype)
    (incoming, saved), _ = lax.scan(
        forward_step, (empty, start_saved), jnp.arange(total_steps - 1, dtype=jnp.int32)
    )
    _, saved = forward_at(jnp.int32(total_steps - 1), incoming, saved)

    def backward_at(step, incoming, sum_qkv, sum_out):
        index = step - (sections - 1 - section)
        live = (index >= 0) & (index < micro)
        slot = jnp.clip(index, 0, micro - 1)
        last = lax.dynamic_index_in_dim(cotangent, slot, 0, keepdims=False)
        grad_y = jnp.where(section == sections - 1, last, incoming)
        x = lax.dynamic_index_in_dim(saved, slot, 0, keepdims=False)
        seg = lax.dynamic_index_in_dim(segs, slot, 0, keepdims=False)
        _, pull = jax.vjp(lambda a, b, c: layer(a, gain, b, c, seg), x, full_qkv, full_out)
        grad_x, grad_q, grad_o = pull(grad_y)
        sum_qkv = sum_qkv + jnp.where(live, grad_q.astype(jnp.float32), 0.0)
        sum_out = sum_out + jnp.where(live, grad_o.astype(jnp.float32), 0.0)
        return (grad_x, sum_qkv, sum_out)

    def backward_step(carry, step):
        incoming, sum_qkv, sum_out = carry
        grad_x, sum_qkv, sum_out = backward_at(step, incoming, sum_qkv, sum_out)
        incoming = passed_along(grad_x, "section", -1)
        return ((incoming, sum_qkv, sum_out), None)

    zero_qkv = jnp.zeros(full_qkv.shape, jnp.float32)
    zero_out = jnp.zeros(full_out.shape, jnp.float32)
    (incoming, sum_qkv, sum_out), _ = lax.scan(
        backward_step, (empty, zero_qkv, zero_out), jnp.arange(total_steps - 1, dtype=jnp.int32)
    )
    _, sum_qkv, sum_out = backward_at(jnp.int32(total_steps - 1), incoming, sum_qkv, sum_out)
    share_qkv, share_out = (
        lax.psum_scatter(sum_qkv, "dp", scatter_dimension=0, tiled=True),
        lax.psum_scatter(sum_out, "dp", scatter_dimension=1, tiled=True),
    )
    return (share_qkv[None], share_out[None])


def nn(a, b):
    return lax.dot_general(a, b, (((1,), (0,)), ((), ())), preferred_element_type=F32)


def nt(a, b):
    return lax.dot_general(a, b, (((1,), (1,)), ((), ())), preferred_element_type=F32)


def pack_kernel(qkv_ref, wout_ref, pack_ref, sems):
    qkv_rows = qkv_ref.shape[0]
    copies = [
        pltpu.make_async_copy(qkv_ref, pack_ref.at[:qkv_rows], sems.at[0]),
        pltpu.make_async_copy(wout_ref, pack_ref.at[qkv_rows:], sems.at[1]),
    ]
    for copy in copies:
        copy.start()
    for copy in copies:
        copy.wait()


def blocks_kernel(planes, index, x_ref, *refs):
    out_refs, sems = refs[:PLANE], refs[PLANE]
    width = x_ref.shape[-1] // (planes * PLANE)
    section, p = index[0], index[2]
    copies = []
    for k in range(PLANE):
        for z in range(planes):
            at = pl.multiple_of((z * PLANE + (p ^ k)) * width, width)
            copies.append(
                pltpu.make_async_copy(
                    x_ref.at[section, :, pl.ds(at, width)],
                    out_refs[k].at[:, pl.ds(z * width, width)],
                    sems.at[len(copies)],
                )
            )
    for copy in copies:
        copy.start()
    for copy in copies:
        copy.wait()


def project_kernel(planes, heads, index, *refs):
    blocks, own, other = refs[:PLANE], refs[PLANE : PLANE + planes], refs[PLANE + planes : PLANE + 2 * planes]
    gain_refs = refs[PLANE + 2 * planes : PLANE + 2 * planes + 2]
    x_ref, vx_ref, vc_ref, gain_ref = refs[PLANE + 2 * planes + 2 : PLANE + 2 * planes + 6]
    out_refs, sum_ref = refs[PLANE + 2 * planes + 6 : -1], refs[-1]
    qkv, width = 3 * heads, vx_ref.shape[-1]
    section, place, p = index[0], index[1], index[2]
    for z in range(planes):
        mine, theirs = (ref[pl.ds(z * PLANE + p, 1), :] for ref in gain_refs)
        gain_ref[z, 0:1, :] = jnp.where(section == 0, mine, theirs)
        gain_ref[z, 1:2, :] = jnp.where(section == 0, theirs, mine)
    for k in range(planes):
        at = place ^ k
        zero = jnp.where(section == 0, own[k][...], other[k][...])
        one = jnp.where(section == 0, other[k][...], own[k][...])
        vx_ref[at, :qkv, :] = (zero[:qkv].astype(F32) * gain_ref[at, 0:1, :]).astype(BF16)
        vx_ref[at, qkv : qkv + heads, :] = zero[qkv:]
        vx_ref[at, qkv + heads : 2 * qkv + heads, :] = (one[:qkv].astype(F32) * gain_ref[at, 1:2, :]).astype(BF16)
        vx_ref[at, 2 * qkv + heads :, :] = jnp.zeros((heads, width), BF16)
        vc_ref[at, :heads, :] = one[qkv:]
        vc_ref[at, heads:, :] = zero[qkv:]
    for k in range(PLANE):
        x_ref[p ^ k] = blocks[-k][...]
    rows = x_ref.shape[0] * x_ref.shape[1]
    with_x = squares = products = None
    for z in range(planes):
        x = x_ref[:, :, z * width : (z + 1) * width].reshape(rows, width)
        wide = x.astype(F32)
        out = vx_ref[z, qkv : qkv + heads, :]
        right = jnp.concatenate([vx_ref[z, qkv + heads : 2 * qkv + heads, :], out], axis=0)
        new = nt(x, vx_ref[z]), jnp.sum(wide * wide, axis=1, keepdims=True), nt(out, right)
        if with_x is None:
            with_x, squares, products = new
        else:
            with_x, squares, products = with_x + new[0], squares + new[1], products + new[2]
    half = 2 * heads
    lane = lax.broadcasted_iota(jnp.int32, (rows, half), 1)
    high = squares.astype(BF16).astype(F32)
    last = jnp.where(lane == heads, high, jnp.where(lane == heads + 1, squares - high, with_x[:, 3 * half :]))
    sum_ref[:, : 3 * half] = with_x[:, : 3 * half].astype(BF16)
    sum_ref[:, 3 * half :] = last.astype(BF16)
    block = rows // PLANE
    for k in range(PLANE):
        start = pl.multiple_of((p ^ k) * block, block)
        out_refs[k][:, : 4 * half] = sum_ref[pl.ds(start, block), :]
        out_refs[k][:, 4 * half :] = products.astype(BF16)


def cotangent_kernel(planes, index, *refs):
    blocks, vc_ref, c_ref = refs[:PLANE], refs[PLANE], refs[PLANE + 1]
    out_refs, sum_ref = refs[PLANE + 2 : -1], refs[-1]
    p, width = index[2], vc_ref.shape[-1]
    for k in range(PLANE):
        c_ref[p ^ k] = blocks[-k][...]
    rows = c_ref.shape[0] * c_ref.shape[1]
    total = None
    for z in range(planes):
        part = nt(c_ref[:, :, z * width : (z + 1) * width].reshape(rows, width), vc_ref[z])
        total = part if total is None else total + part
    sum_ref[...] = total.astype(BF16)
    block = rows // PLANE
    for k in range(PLANE):
        out_refs[k][...] = sum_ref[pl.ds(pl.multiple_of((p ^ k) * block, block), block), :]


def attention(qkv, allowed, heads):
    query, keys, values = (qkv[:, i * heads : (i + 1) * heads].astype(BF16) for i in range(3))
    scores = jnp.where(allowed, nt(query, keys) * heads ** (-0.5), -1e30)
    raised = jnp.exp(scores - jnp.max(scores, axis=1, keepdims=True))
    probs = raised / jnp.sum(raised, axis=1, keepdims=True)
    return probs, nn(probs.astype(BF16), values).astype(BF16)


def attention_grad(qkv, probs, att, d_att, heads):
    query, keys, values = (qkv[:, i * heads : (i + 1) * heads].astype(BF16) for i in range(3))
    inner = jnp.sum(att.astype(F32) * d_att.astype(F32), axis=1, keepdims=True)
    d_values = nn(jnp.transpose(probs).astype(BF16), d_att)
    d_scores = probs * (nt(d_att, values) - inner) * heads ** (-0.5)
    d_query = nn(d_scores.astype(BF16), keys)
    d_keys = nn(jnp.transpose(d_scores).astype(BF16), query)
    return jnp.concatenate([d_query, d_keys, d_values], axis=1).astype(BF16).astype(F32)


def summed(parts):
    total = parts[0][...].astype(F32)
    for part in parts[1:]:
        total = total + part[...].astype(F32)
    return total


def chain_kernel(features, heads, index, docs, *refs):
    out_ref = refs[-1]
    qkv, half = 3 * heads, 2 * heads
    total, from_c = summed(refs[:PLANE]), summed(refs[PLANE:-1])
    rows = total.shape[0]
    section = index[0]
    query_at = lax.broadcasted_iota(jnp.int32, (rows, rows), 0)
    key_at = lax.broadcasted_iota(jnp.int32, (rows, rows), 1)
    allowed = query_at >= key_at
    end = 0
    for i in range(docs.shape[2]):
        end = end + docs[section, 0, i]
        allowed = allowed & ((query_at >= end) == (key_at >= end))
    x_out = total[:, qkv : 2 * half]
    x_one = total[:, 2 * half : 2 * half + qkv]
    tail = total[:, 3 * half : 4 * half]
    lane = lax.broadcasted_iota(jnp.int32, tail.shape, 1)
    squares = jnp.sum(jnp.where((lane == heads) | (lane == heads + 1), tail, 0.0), axis=1, keepdims=True)
    mixed = total[:, 4 * half : 4 * half + qkv].astype(BF16)
    gram = total[:, 4 * half + qkv :].astype(BF16)
    c_one, c_zero = from_c[:, :heads].astype(BF16), from_c[:, heads:]

    scale0 = lax.rsqrt(squares / features + 1e-05)
    qkv0 = (total[:, :qkv] * scale0).astype(BF16).astype(F32)
    probs0, att0 = attention(qkv0, allowed, heads)
    wide0 = att0.astype(F32)
    y_out = x_out + nn(att0, gram)
    squares = squares + jnp.sum(wide0 * (x_out + y_out), axis=1, keepdims=True)
    scale1 = lax.rsqrt(jnp.maximum(squares, 0.0) / features + 1e-05)
    qkv1 = ((x_one + nn(att0, mixed)) * scale1).astype(BF16).astype(F32)
    probs1, att1 = attention(qkv1, allowed, heads)
    d_qkv1 = attention_grad(qkv1, probs1, att1, c_one, heads)
    inner = jnp.sum(d_qkv1 * qkv1, axis=1, keepdims=True) * scale1 * scale1 / features
    e1 = d_qkv1 * scale1
    d_att0 = c_zero + nt(e1.astype(BF16), mixed) - inner * y_out
    e0 = attention_grad(qkv0, probs0, att0, d_att0.astype(BF16), heads) * scale0
    factors = [e0, wide0, e1, wide0 * inner, att1.astype(F32), jnp.zeros((rows, heads), F32)]
    out_ref[...] = jnp.concatenate(factors, axis=1).astype(BF16)


def grads_kernel(planes, heads, index, *refs):
    factors, (x_ref, c_ref, vx_ref, gain_ref) = refs[:PLANE], refs[PLANE : PLANE + 4]
    keep_ref, send_ref, all_ref = refs[PLANE + 4 :]
    qkv, half, width = 3 * heads, 2 * heads, vx_ref.shape[-1]
    section, p = index[0], index[2]
    for k in range(PLANE):
        all_ref[p ^ k] = factors[k][...]
    rows = x_ref.shape[0] * x_ref.shape[1]
    turned = jnp.transpose(all_ref[...].astype(F32).reshape(rows, 5 * half)).astype(BF16)
    att0, att1 = turned[qkv : qkv + heads], turned[4 * half : 4 * half + heads]
    right = turned[2 * half : 4 * half]
    small = nt(right, att0).astype(BF16)
    small_t = nt(att0, right[:qkv]).astype(BF16)
    for z in range(planes):
        cols = slice(z * width, (z + 1) * width)
        x = x_ref[:, :, cols].reshape(rows, width)
        c = c_ref[:, :, cols].reshape(rows, width)
        out = vx_ref[z, qkv : qkv + heads, :]
        with_x = nn(turned[: 4 * half], x)
        left = with_x[2 * half :] + nn(small, out)
        zero = with_x[:qkv] * gain_ref[z, 0:1, :]
        one = left[:qkv] * gain_ref[z, 1:2, :]
        keep_ref[z, :qkv, :] = jnp.where(section == 0, zero, one)
        send_ref[z, :qkv, :] = jnp.where(section == 0, one, zero).astype(BF16)
        zero = nn(att0, c) + nn(small_t, vx_ref[z, qkv + heads : 2 * qkv + heads, :]) - left[qkv:]
        one = nn(att1, c)
        keep_ref[z, qkv:, :] = jnp.where(section == 0, zero, one)
        send_ref[z, qkv:, :] = jnp.where(section == 0, one, zero).astype(BF16)


def merge_kernel(index, keep_ref, come_ref, *out_refs):
    place = index[1]
    out_refs[0][...] = keep_ref[place] + come_ref[place].astype(F32)
    for k in range(1, len(out_refs)):
        out_refs[k][...] = (keep_ref[place ^ k] + come_ref[place ^ k].astype(F32)).astype(BF16)


def last_kernel(qkv_rows, keep_ref, *refs):
    parts, (qkv_ref, out_ref) = refs[:-2], refs[-2:]
    total = keep_ref[...]
    for part in parts:
        total = total + part[...].astype(F32)
    qkv_ref[...] = total[:qkv_rows]
    out_ref[...] = total[qkv_rows:]


def far_first(value, count, send):
    of = lambda k: value[k] if isinstance(value, (list, tuple)) else value
    got = {k: send(of(k), k) for k in reversed(range(1, count))}
    return [of(0)] + [got[k] for k in range(1, count)]


def call(kernel, outs, *args, scalars=0, scratch=()):
    smem = pl.BlockSpec(memory_space=pltpu.SMEM)
    vmem = pl.BlockSpec(memory_space=pltpu.VMEM)
    return pl.pallas_call(
        kernel,
        out_shape=[jax.ShapeDtypeStruct(shape, dtype) for shape, dtype in outs],
        in_specs=[smem] * scalars + [vmem] * (len(args) - scalars),
        out_specs=[vmem] * len(outs),
        scratch_shapes=[pltpu.VMEM(shape, dtype) for shape, dtype in scratch],
        compiler_params=pltpu.CompilerParams(vmem_limit_bytes=VMEM_LIMIT),
    )(*args)


def planar(inputs, cotangent, doc_lengths, norm_gain, w_qkv, w_out):
    shards = lax.axis_size("dp")
    planes = shards // PLANE
    section, place = lax.axis_index("section"), lax.axis_index("dp")
    z, p = place // PLANE, place % PLANE
    index = jnp.stack([section, z, p]).astype(jnp.int32)
    block, features = inputs.shape[1:]
    rows = PLANE * block
    heads, width = w_out.shape[1:]
    qkv_rows = w_qkv.shape[2]
    cols = planes * width
    def along_z(value, k):
        route = [(a * PLANE + b, (a ^ k) * PLANE + b) for a in range(planes) for b in range(PLANE)]
        return lax.ppermute(value, "dp", route)

    def to_sibling(value):
        return lax.ppermute(value, "section", [(0, 1), (1, 0)])

    def along_plane(value, k):
        route = [(a * PLANE + b, a * PLANE + (b ^ k)) for a in range(planes) for b in range(PLANE)]
        return lax.ppermute(value, "dp", route)

    def exchange(value):
        return far_first(value, PLANE, along_plane)

    smem, vmem = pl.BlockSpec(memory_space=pltpu.SMEM), pl.BlockSpec(memory_space=pltpu.VMEM)
    hbm = pl.BlockSpec(memory_space=pltpu.HBM)
    params = pltpu.CompilerParams(vmem_limit_bytes=VMEM_LIMIT)
    qkv_in, out_in, x_in, c_in = [
        pltpu.with_memory_space_constraint(value, pltpu.HBM)
        for value in (w_qkv[0].T, w_out[0], inputs, cotangent)
    ]
    pack = pl.pallas_call(
        pack_kernel,
        out_shape=jax.ShapeDtypeStruct((qkv_rows + heads, width), BF16),
        in_specs=[hbm] * 2,
        out_specs=vmem,
        scratch_shapes=[pltpu.SemaphoreType.DMA((2,))],
        compiler_params=params,
    )(qkv_in, out_in)
    split_blocks = pl.pallas_call(
        functools.partial(blocks_kernel, planes),
        out_shape=[jax.ShapeDtypeStruct((block, cols), BF16)] * PLANE,
        in_specs=[smem, hbm],
        out_specs=[vmem] * PLANE,
        scratch_shapes=[pltpu.SemaphoreType.DMA((PLANE * planes,))],
        compiler_params=params,
    )

    def swapped(value):
        out = split_blocks(index, value)
        return [out[0]] + far_first(out, PLANE, along_plane)[:0:-1]

    far = {k: along_z(pack, k) for k in reversed(range(2, planes))}
    x_blocks, c_blocks = swapped(x_in), swapped(c_in)
    later, late_gain, _ = lax.optimization_barrier((pack, norm_gain, far[planes - 1] if far else pack))
    near = [along_z(later, 1)] if planes > 1 else []
    own = [pack] + near + [far[k] for k in range(2, planes)]
    other = [to_sibling(piece) for piece in [later] + own[1:]]
    gains = [value[0].reshape(shards, width).astype(F32) for value in (norm_gain, to_sibling(late_gain))]

    split = ((PLANE, block, cols), BF16)
    half = 2 * heads
    x, vx, vc, gains, *sent = call(
        functools.partial(project_kernel, planes, heads),
        [split, ((planes, 4 * half, width), BF16), ((planes, half, width), BF16), ((planes, 8, width), F32)]
        + [((block, 6 * half), BF16)] * PLANE,
        index, *x_blocks, *own, *other, *gains, scalars=1,
        scratch=[((rows, 4 * half), BF16)],
    )
    first = exchange(sent)[::-1]
    c, *sent = call(
        functools.partial(cotangent_kernel, planes),
        [split] + [((block, half), BF16)] * PLANE,
        index, *c_blocks, vc, scalars=1,
        scratch=[((rows, half), BF16)],
    )
    (factors,) = call(
        functools.partial(chain_kernel, features, heads),
        [((block, 5 * half), BF16)],
        index, doc_lengths, *first, *exchange(sent)[::-1], scalars=2,
    )
    grads = (planes, qkv_rows + heads, width)
    keep, send = call(
        functools.partial(grads_kernel, planes, heads),
        [(grads, F32), (grads, BF16)],
        index, *exchange(factors), x, c, vx, gains, scalars=1,
        scratch=[((PLANE, block, 5 * half), BF16)],
    )
    merged = call(
        merge_kernel,
        [(grads[1:], F32)] + [(grads[1:], BF16)] * (planes - 1),
        index, keep, to_sibling(send), scalars=1,
    )
    parts = far_first(merged, planes, along_z)[1:]
    grad_qkv, grad_out = call(
        functools.partial(last_kernel, qkv_rows),
        [((qkv_rows, width), F32), ((heads, width), F32)],
        merged[0], *parts[::-1],
    )
    return (grad_qkv.T[None], grad_out[None])


def solution(mesh):
    sections, shards = mesh.shape["section"], mesh.shape["dp"]
    planes = shards // PLANE

    def body(inputs, *rest):
        fits = shards % PLANE == 0 and planes & (planes - 1) == 0
        if sections == 2 and inputs.shape[0] == 2 and fits:
            return planar(inputs, *rest)
        return pipelined(inputs, *rest)

    return jax.shard_map(
        body,
        mesh=mesh,
        in_specs=(
            P(None, "dp", None),
            P(None, "dp", None),
            P(None, "dp", None),
            P("section", None),
            P("section", "dp", None),
            P("section", None, "dp"),
        ),
        out_specs=(P("section", "dp", None), P("section", None, "dp")),
        check_vma=False,
    )
```

```python
import functools

import jax
import jax.numpy as jnp
from jax import lax
from jax.experimental import pallas as pl
from jax.experimental.pallas import tpu as pltpu
from jax.sharding import PartitionSpec as P

F32 = jnp.float32
BF16 = jnp.bfloat16
PLANE = 4
VMEM_LIMIT = 16 * 1024 * 1024


def passed_along(block, axis, distance):
    devices = range(lax.axis_size(axis))
    route = [(i - distance, i) for i in devices if i - distance in devices]
    return lax.ppermute(block, axis, route)


def segments_of(lengths, count):
    ends = jnp.cumsum(lengths)
    position = jnp.arange(count, dtype=jnp.int32)
    return jnp.sum((position[:, None] >= ends[None, :]).astype(jnp.int32), axis=1)


def layer(x, gain, w_qkv, w_out, seg):
    head = w_out.shape[0]
    x_wide = x.astype(jnp.float32)
    scale = lax.rsqrt(jnp.mean(x_wide * x_wide, axis=-1, keepdims=True) + 1e-05)
    normed = (x_wide * scale * gain.astype(jnp.float32)).astype(jnp.bfloat16)
    qkv = jnp.dot(normed, w_qkv, preferred_element_type=jnp.float32).astype(jnp.bfloat16)
    query = qkv[:, :head]
    keys = qkv[:, head : 2 * head]
    values = qkv[:, 2 * head :]
    scores = jnp.dot(query, keys.T, preferred_element_type=jnp.float32) * head ** (-0.5)
    rows = jnp.arange(x.shape[0], dtype=jnp.int32)
    allowed = (seg[:, None] == seg[None, :]) & (rows[:, None] >= rows[None, :])
    scores = jnp.where(allowed, scores, -1e30)
    probs = jax.nn.softmax(scores, axis=-1).astype(jnp.bfloat16)
    attended = jnp.dot(probs, values, preferred_element_type=jnp.float32).astype(jnp.bfloat16)
    return (x_wide + jnp.dot(attended, w_out, preferred_element_type=jnp.float32)).astype(
        jnp.bfloat16
    )


def pipelined(inputs, cotangent, doc_lengths, norm_gain, w_qkv, w_out):
    sections = lax.axis_size("section")
    section = lax.axis_index("section")
    micro = inputs.shape[0]
    count = inputs.shape[1]
    segs = jax.vmap(lambda lens: segments_of(lens, count))(doc_lengths[:, 0, :])
    gain = norm_gain[0]
    full_qkv, full_out = (
        lax.all_gather(w_qkv[0], "dp", axis=0, tiled=True),
        lax.all_gather(w_out[0], "dp", axis=1, tiled=True),
    )
    total_steps = micro + sections - 1
    empty = jnp.zeros(inputs.shape[1:], inputs.dtype)

    def forward_at(step, incoming, saved):
        index = step - section
        live = (index >= 0) & (index < micro)
        slot = jnp.clip(index, 0, micro - 1)
        first = lax.dynamic_index_in_dim(inputs, slot, 0, keepdims=False)
        x = jnp.where(section == 0, first, incoming)
        seg = lax.dynamic_index_in_dim(segs, slot, 0, keepdims=False)
        out = layer(x, gain, full_qkv, full_out, seg)
        old = lax.dynamic_index_in_dim(saved, slot, 0, keepdims=False)
        saved = lax.dynamic_update_index_in_dim(saved, jnp.where(live, x, old), slot, 0)
        return (out, saved)

    def forward_step(carry, step):
        incoming, saved = carry
        out, saved = forward_at(step, incoming, saved)
        incoming = passed_along(out, "section", 1)
        return ((incoming, saved), None)

    start_saved = jnp.zeros(inputs.shape, inputs.dtype)
    (incoming, saved), _ = lax.scan(
        forward_step, (empty, start_saved), jnp.arange(total_steps - 1, dtype=jnp.int32)
    )
    _, saved = forward_at(jnp.int32(total_steps - 1), incoming, saved)

    def backward_at(step, incoming, sum_qkv, sum_out):
        index = step - (sections - 1 - section)
        live = (index >= 0) & (index < micro)
        slot = jnp.clip(index, 0, micro - 1)
        last = lax.dynamic_index_in_dim(cotangent, slot, 0, keepdims=False)
        grad_y = jnp.where(section == sections - 1, last, incoming)
        x = lax.dynamic_index_in_dim(saved, slot, 0, keepdims=False)
        seg = lax.dynamic_index_in_dim(segs, slot, 0, keepdims=False)
        _, pull = jax.vjp(lambda a, b, c: layer(a, gain, b, c, seg), x, full_qkv, full_out)
        grad_x, grad_q, grad_o = pull(grad_y)
        sum_qkv = sum_qkv + jnp.where(live, grad_q.astype(jnp.float32), 0.0)
        sum_out = sum_out + jnp.where(live, grad_o.astype(jnp.float32), 0.0)
        return (grad_x, sum_qkv, sum_out)

    def backward_step(carry, step):
        incoming, sum_qkv, sum_out = carry
        grad_x, sum_qkv, sum_out = backward_at(step, incoming, sum_qkv, sum_out)
        incoming = passed_along(grad_x, "section", -1)
        return ((incoming, sum_qkv, sum_out), None)

    zero_qkv = jnp.zeros(full_qkv.shape, jnp.float32)
    zero_out = jnp.zeros(full_out.shape, jnp.float32)
    (incoming, sum_qkv, sum_out), _ = lax.scan(
        backward_step, (empty, zero_qkv, zero_out), jnp.arange(total_steps - 1, dtype=jnp.int32)
    )
    _, sum_qkv, sum_out = backward_at(jnp.int32(total_steps - 1), incoming, sum_qkv, sum_out)
    share_qkv, share_out = (
        lax.psum_scatter(sum_qkv, "dp", scatter_dimension=0, tiled=True),
        lax.psum_scatter(sum_out, "dp", scatter_dimension=1, tiled=True),
    )
    return (share_qkv[None], share_out[None])


def nn(a, b):
    return lax.dot_general(a, b, (((1,), (0,)), ((), ())), preferred_element_type=F32)


def nt(a, b):
    return lax.dot_general(a, b, (((1,), (1,)), ((), ())), preferred_element_type=F32)


def block_copies(planes, index, k, refs, out_ref, sems):
    width = refs[0].shape[-1] // (planes * PLANE)
    section, p = index[0], index[2]
    copies = []
    for z in range(planes):
        at = pl.multiple_of((z * PLANE + (p ^ k)) * width, width)
        for half, ref in enumerate(refs):
            copies.append(
                pltpu.make_async_copy(
                    ref.at[section, :, pl.ds(at, width)],
                    out_ref.at[half, :, pl.ds(z * width, width)],
                    sems.at[len(copies)],
                )
            )
    return copies


def mark_kernel(pack_ref, gain_ref, out_ref):
    out_ref[: pack_ref.shape[0], :] = pack_ref[...]
    out_ref[pack_ref.shape[0] :, :] = gain_ref[...]


def blocks_kernel(planes, index, qkv_ref, wout_ref, x_ref, c_ref, pack_ref, *refs):
    out_refs, pack_sems, sems = refs[:-2], refs[-2], refs[-1]
    qkv_rows = qkv_ref.shape[0]
    copies = [
        pltpu.make_async_copy(qkv_ref, pack_ref.at[:qkv_rows], pack_sems.at[0]),
        pltpu.make_async_copy(wout_ref, pack_ref.at[qkv_rows:], pack_sems.at[1]),
    ]
    for k, out_ref in enumerate(out_refs):
        copies += block_copies(planes, index, k, (x_ref, c_ref), out_ref, sems.at[k])
    for copy in copies:
        copy.start()
    for copy in copies:
        copy.wait()


def project_kernel(planes, heads, index, *refs):
    blocks, own, other = refs[:PLANE], refs[PLANE : PLANE + planes], refs[PLANE + planes : PLANE + 2 * planes]
    x_ref, c_ref, vx_ref, gain_ref = refs[PLANE + 2 * planes : PLANE + 2 * planes + 4]
    out_refs = refs[PLANE + 2 * planes + 4 : -4]
    vc_ref, sum_ref, *wide_refs = refs[-4:]
    qkv, width = 3 * heads, vx_ref.shape[-1]
    section, place, p = index[0], index[1], index[2]
    for ref, wide_ref in zip((own[0], other[0]), wide_refs):
        wide_ref[...] = ref[qkv + heads :, :].astype(F32)
    for z in range(planes):
        mine, theirs = (ref[pl.ds(z * PLANE + p, 1), :] for ref in wide_refs)
        gain_ref[z, 0:1, :] = jnp.where(section == 0, mine, theirs)
        gain_ref[z, 1:2, :] = jnp.where(section == 0, theirs, mine)
    for k in range(planes):
        at = place ^ k
        mine, theirs = own[k][: qkv + heads, :], other[k][: qkv + heads, :]
        zero = jnp.where(section == 0, mine, theirs)
        one = jnp.where(section == 0, theirs, mine)
        empty = jnp.zeros((heads, width), BF16)
        vx_ref[at, :qkv, :] = (zero[:qkv].astype(F32) * gain_ref[at, 0:1, :]).astype(BF16)
        vx_ref[at, qkv : qkv + heads, :] = zero[qkv : qkv + heads]
        vx_ref[at, qkv + heads : 2 * qkv + heads, :] = (one[:qkv].astype(F32) * gain_ref[at, 1:2, :]).astype(BF16)
        vx_ref[at, 2 * qkv + heads :, :] = empty
        vc_ref[at, :heads, :] = empty
        vc_ref[at, heads : 2 * heads, :] = one[qkv : qkv + heads]
        vc_ref[at, 2 * heads : 3 * heads, :] = zero[qkv : qkv + heads]
        vc_ref[at, 3 * heads :, :] = empty
    for k in range(PLANE):
        x_ref[p ^ k] = blocks[-k][0]
        c_ref[p ^ k] = blocks[-k][1]
    rows = x_ref.shape[0] * x_ref.shape[1]
    with_x = with_c = squares = products = None
    for z in range(planes):
        cols = slice(z * width, (z + 1) * width)
        x = x_ref[:, :, cols].reshape(rows, width)
        c = c_ref[:, :, cols].reshape(rows, width)
        wide = x.astype(F32)
        out = vx_ref[z, qkv : qkv + heads, :]
        right = jnp.concatenate([vx_ref[z, qkv + heads : 2 * qkv + heads, :], out], axis=0)
        new = nt(x, vx_ref[z]), nt(c, vc_ref[z]), jnp.sum(wide * wide, axis=1, keepdims=True), nt(out, right)
        if with_x is None:
            with_x, with_c, squares, products = new
        else:
            with_x, with_c = with_x + new[0], with_c + new[1]
            squares, products = squares + new[2], products + new[3]
    half = 2 * heads
    lane = lax.broadcasted_iota(jnp.int32, (rows, half), 1)
    high = squares.astype(BF16).astype(F32)
    last = jnp.where(lane == heads, high, jnp.where(lane == heads + 1, squares - high, with_c[:, half:]))
    sum_ref[:, : 3 * half] = with_x[:, : 3 * half].astype(BF16)
    sum_ref[:, 3 * half : 4 * half] = (with_x[:, 3 * half :] + with_c[:, :half]).astype(BF16)
    sum_ref[:, 4 * half :] = last.astype(BF16)
    block = rows // PLANE
    for k in range(PLANE):
        start = pl.multiple_of((p ^ k) * block, block)
        out_refs[k][:, : 5 * half] = sum_ref[pl.ds(start, block), :]
        out_refs[k][:, 5 * half :] = products.astype(BF16)


def attention(qkv, allowed, heads):
    query, keys, values = (qkv[:, i * heads : (i + 1) * heads].astype(BF16) for i in range(3))
    scores = jnp.where(allowed, nt(query, keys) * heads ** (-0.5), -1e30)
    raised = jnp.exp(scores - jnp.max(scores, axis=1, keepdims=True))
    probs = raised / jnp.sum(raised, axis=1, keepdims=True)
    return probs, nn(probs.astype(BF16), values).astype(BF16)


def attention_grad(qkv, probs, att, d_att, heads):
    query, keys, values = (qkv[:, i * heads : (i + 1) * heads].astype(BF16) for i in range(3))
    inner = jnp.sum(att.astype(F32) * d_att.astype(F32), axis=1, keepdims=True)
    d_values = nn(jnp.transpose(probs).astype(BF16), d_att)
    d_scores = probs * (nt(d_att, values) - inner) * heads ** (-0.5)
    d_query = nn(d_scores.astype(BF16), keys)
    d_keys = nn(jnp.transpose(d_scores).astype(BF16), query)
    return jnp.concatenate([d_query, d_keys, d_values], axis=1).astype(BF16).astype(F32)


def summed(parts):
    total = parts[0][...].astype(F32)
    for part in parts[1:]:
        total = total + part[...].astype(F32)
    return total


def chain_kernel(features, heads, index, docs, *refs):
    out_ref = refs[-1]
    qkv, half = 3 * heads, 2 * heads
    total = summed(refs[:-1])
    rows = total.shape[0]
    section = index[0]
    query_at = lax.broadcasted_iota(jnp.int32, (rows, rows), 0)
    key_at = lax.broadcasted_iota(jnp.int32, (rows, rows), 1)
    allowed = query_at >= key_at
    end = 0
    for i in range(docs.shape[2]):
        end = end + docs[section, 0, i]
        allowed = allowed & ((query_at >= end) == (key_at >= end))
    x_out = total[:, qkv : 2 * half]
    x_one = total[:, 2 * half : 2 * half + qkv]
    tail = total[:, 4 * half : 5 * half]
    c_one, c_zero = total[:, 4 * half - heads : 4 * half].astype(BF16), tail[:, :heads]
    lane = lax.broadcasted_iota(jnp.int32, tail.shape, 1)
    squares = jnp.sum(jnp.where((lane == heads) | (lane == heads + 1), tail, 0.0), axis=1, keepdims=True)
    mixed = total[:, 5 * half : 5 * half + qkv].astype(BF16)
    gram = total[:, 5 * half + qkv :].astype(BF16)

    scale0 = lax.rsqrt(squares / features + 1e-05)
    qkv0 = (total[:, :qkv] * scale0).astype(BF16).astype(F32)
    probs0, att0 = attention(qkv0, allowed, heads)
    wide0 = att0.astype(F32)
    y_out = x_out + nn(att0, gram)
    squares = squares + jnp.sum(wide0 * (x_out + y_out), axis=1, keepdims=True)
    scale1 = lax.rsqrt(jnp.maximum(squares, 0.0) / features + 1e-05)
    qkv1 = ((x_one + nn(att0, mixed)) * scale1).astype(BF16).astype(F32)
    probs1, att1 = attention(qkv1, allowed, heads)
    d_qkv1 = attention_grad(qkv1, probs1, att1, c_one, heads)
    inner = jnp.sum(d_qkv1 * qkv1, axis=1, keepdims=True) * scale1 * scale1 / features
    e1 = d_qkv1 * scale1
    d_att0 = c_zero + nt(e1.astype(BF16), mixed) - inner * y_out
    e0 = attention_grad(qkv0, probs0, att0, d_att0.astype(BF16), heads) * scale0
    factors = [e0, wide0, e1, wide0 * inner, att1.astype(F32), jnp.zeros((rows, heads), F32)]
    out_ref[...] = jnp.concatenate(factors, axis=1).astype(BF16)


def grads_kernel(planes, heads, index, *refs):
    factors, (x_ref, c_ref, vx_ref, gain_ref) = refs[:PLANE], refs[PLANE : PLANE + 4]
    keep_ref, send_ref, all_ref = refs[PLANE + 4 :]
    qkv, half, width = 3 * heads, 2 * heads, vx_ref.shape[-1]
    section, p = index[0], index[2]
    for k in range(PLANE):
        all_ref[p ^ k] = factors[k][...]
    rows = x_ref.shape[0] * x_ref.shape[1]
    turned = jnp.transpose(all_ref[...].astype(F32).reshape(rows, 5 * half)).astype(BF16)
    att0, att1 = turned[qkv : qkv + heads], turned[4 * half : 4 * half + heads]
    right = turned[2 * half : 4 * half]
    small = nt(right, att0).astype(BF16)
    small_t = nt(att0, right[:qkv]).astype(BF16)
    for z in range(planes):
        cols = slice(z * width, (z + 1) * width)
        x = x_ref[:, :, cols].reshape(rows, width)
        c = c_ref[:, :, cols].reshape(rows, width)
        out = vx_ref[z, qkv : qkv + heads, :]
        with_x = nn(turned[: 4 * half], x)
        left = with_x[2 * half :] + nn(small, out)
        zero = with_x[:qkv] * gain_ref[z, 0:1, :]
        one = left[:qkv] * gain_ref[z, 1:2, :]
        keep_ref[z, :qkv, :] = jnp.where(section == 0, zero, one)
        send_ref[z, :qkv, :] = jnp.where(section == 0, one, zero).astype(BF16)
        zero = nn(att0, c) + nn(small_t, vx_ref[z, qkv + heads : 2 * qkv + heads, :]) - left[qkv:]
        one = nn(att1, c)
        keep_ref[z, qkv:, :] = jnp.where(section == 0, zero, one)
        send_ref[z, qkv:, :] = jnp.where(section == 0, one, zero).astype(BF16)


def merge_kernel(index, keep_ref, come_ref, *out_refs):
    place = index[1]
    out_refs[0][...] = keep_ref[place] + come_ref[place].astype(F32)
    for k in range(1, len(out_refs)):
        out_refs[k][...] = (keep_ref[place ^ k] + come_ref[place ^ k].astype(F32)).astype(BF16)


def last_kernel(qkv_rows, keep_ref, *refs):
    parts, (qkv_ref, out_ref) = refs[:-2], refs[-2:]
    total = keep_ref[...]
    for part in parts:
        total = total + part[...].astype(F32)
    qkv_ref[...] = total[:qkv_rows]
    out_ref[...] = total[qkv_rows:]


def far_first(value, count, send):
    of = lambda k: value[k] if isinstance(value, (list, tuple)) else value
    got = {k: send(of(k), k) for k in reversed(range(1, count))}
    return [of(0)] + [got[k] for k in range(1, count)]


def call(kernel, outs, *args, scalars=0, scratch=()):
    smem = pl.BlockSpec(memory_space=pltpu.SMEM)
    vmem = pl.BlockSpec(memory_space=pltpu.VMEM)
    return pl.pallas_call(
        kernel,
        out_shape=[jax.ShapeDtypeStruct(shape, dtype) for shape, dtype in outs],
        in_specs=[smem] * scalars + [vmem] * (len(args) - scalars),
        out_specs=[vmem] * len(outs),
        scratch_shapes=[pltpu.VMEM(shape, dtype) for shape, dtype in scratch],
        compiler_params=pltpu.CompilerParams(vmem_limit_bytes=VMEM_LIMIT),
    )(*args)


def planar(inputs, cotangent, doc_lengths, norm_gain, w_qkv, w_out):
    shards = lax.axis_size("dp")
    planes = shards // PLANE
    section, place = lax.axis_index("section"), lax.axis_index("dp")
    z, p = place // PLANE, place % PLANE
    index = jnp.stack([section, z, p]).astype(jnp.int32)
    block, features = inputs.shape[1:]
    rows = PLANE * block
    heads, width = w_out.shape[1:]
    qkv_rows = w_qkv.shape[2]
    cols = planes * width
    def along_z(value, k):
        route = [(a * PLANE + b, (a ^ k) * PLANE + b) for a in range(planes) for b in range(PLANE)]
        return lax.ppermute(value, "dp", route)

    def to_sibling(value):
        return lax.ppermute(value, "section", [(0, 1), (1, 0)])

    def along_plane(value, k):
        route = [(a * PLANE + b, a * PLANE + (b ^ k)) for a in range(planes) for b in range(PLANE)]
        return lax.ppermute(value, "dp", route)

    def exchange(value):
        return far_first(value, PLANE, along_plane)

    smem, vmem = pl.BlockSpec(memory_space=pltpu.SMEM), pl.BlockSpec(memory_space=pltpu.VMEM)
    hbm = pl.BlockSpec(memory_space=pltpu.HBM)
    params = pltpu.CompilerParams(vmem_limit_bytes=VMEM_LIMIT)
    qkv_in, out_in, x_in, c_in = [
        pltpu.with_memory_space_constraint(value, pltpu.HBM)
        for value in (w_qkv[0].T, w_out[0], inputs, cotangent)
    ]
    one_block = jax.ShapeDtypeStruct((2, block, cols), BF16)
    pack, *blocks = pl.pallas_call(
        functools.partial(blocks_kernel, planes),
        out_shape=[jax.ShapeDtypeStruct((qkv_rows + heads, width), BF16)] + [one_block] * PLANE,
        in_specs=[smem] + [hbm] * 4,
        out_specs=[vmem] * (PLANE + 1),
        scratch_shapes=[pltpu.SemaphoreType.DMA((2,)), pltpu.SemaphoreType.DMA((PLANE, 2 * planes))],
        compiler_params=params,
    )(index, qkv_in, out_in, x_in, c_in)
    gain = norm_gain[0].reshape(shards, width)
    blocks = [blocks[0]] + far_first(blocks, PLANE, along_plane)[1:]
    far = {k: along_z(pack, k) for k in reversed(range(2, planes))}
    later, _ = lax.optimization_barrier((pack, blocks[3]))
    near = [along_z(later, 1)] if planes > 1 else []
    mine, late_gain, _ = lax.optimization_barrier((pack, gain, blocks[3]))
    (marked,) = call(mark_kernel, [((qkv_rows + heads + shards, width), BF16)], mine, late_gain)
    own = [marked] + near + [far[k] for k in range(2, planes)]
    other = [to_sibling(piece) for piece in own]

    split = ((PLANE, block, cols), BF16)
    half = 2 * heads
    x, c, vx, gains, *sent = call(
        functools.partial(project_kernel, planes, heads),
        [split, split, ((planes, 4 * half, width), BF16), ((planes, 8, width), F32)]
        + [((block, 7 * half), BF16)] * PLANE,
        index, blocks[0], *blocks[:0:-1], *own, *other, scalars=1,
        scratch=[((planes, 2 * half, width), BF16), ((rows, 5 * half), BF16)] + [((shards, width), F32)] * 2,
    )
    (factors,) = call(
        functools.partial(chain_kernel, features, heads),
        [((block, 5 * half), BF16)],
        index, doc_lengths, *exchange(sent)[::-1], scalars=2,
    )
    grads = (planes, qkv_rows + heads, width)
    keep, send = call(
        functools.partial(grads_kernel, planes, heads),
        [(grads, F32), (grads, BF16)],
        index, *exchange(factors), x, c, vx, gains, scalars=1,
        scratch=[((PLANE, block, 5 * half), BF16)],
    )
    merged = call(
        merge_kernel,
        [(grads[1:], F32)] + [(grads[1:], BF16)] * (planes - 1),
        index, keep, to_sibling(send), scalars=1,
    )
    parts = far_first(merged, planes, along_z)[1:]
    grad_qkv, grad_out = call(
        functools.partial(last_kernel, qkv_rows),
        [((qkv_rows, width), F32), ((heads, width), F32)],
        merged[0], *parts[::-1],
    )
    return (grad_qkv.T[None], grad_out[None])


def solution(mesh):
    sections, shards = mesh.shape["section"], mesh.shape["dp"]
    planes = shards // PLANE

    def body(inputs, *rest):
        fits = shards % PLANE == 0 and planes & (planes - 1) == 0
        if sections == 2 and inputs.shape[0] == 2 and fits:
            return planar(inputs, *rest)
        return pipelined(inputs, *rest)

    return jax.shard_map(
        body,
        mesh=mesh,
        in_specs=(
            P(None, "dp", None),
            P(None, "dp", None),
            P(None, "dp", None),
            P("section", None),
            P("section", "dp", None),
            P("section", None, "dp"),
        ),
        out_specs=(P("section", "dp", None), P("section", None, "dp")),
        check_vma=False,
    )
```

```python
import functools

import jax
import jax.numpy as jnp
from jax import lax
from jax.experimental import pallas as pl
from jax.experimental.pallas import tpu as pltpu
from jax.sharding import PartitionSpec as P

F32 = jnp.float32
BF16 = jnp.bfloat16
PLANE = 4
VMEM_LIMIT = 16 * 1024 * 1024


def passed_along(block, axis, distance):
    devices = range(lax.axis_size(axis))
    route = [(i - distance, i) for i in devices if i - distance in devices]
    return lax.ppermute(block, axis, route)


def segments_of(lengths, count):
    ends = jnp.cumsum(lengths)
    position = jnp.arange(count, dtype=jnp.int32)
    return jnp.sum((position[:, None] >= ends[None, :]).astype(jnp.int32), axis=1)


def layer(x, gain, w_qkv, w_out, seg):
    head = w_out.shape[0]
    x_wide = x.astype(jnp.float32)
    scale = lax.rsqrt(jnp.mean(x_wide * x_wide, axis=-1, keepdims=True) + 1e-05)
    normed = (x_wide * scale * gain.astype(jnp.float32)).astype(jnp.bfloat16)
    qkv = jnp.dot(normed, w_qkv, preferred_element_type=jnp.float32).astype(jnp.bfloat16)
    query = qkv[:, :head]
    keys = qkv[:, head : 2 * head]
    values = qkv[:, 2 * head :]
    scores = jnp.dot(query, keys.T, preferred_element_type=jnp.float32) * head ** (-0.5)
    rows = jnp.arange(x.shape[0], dtype=jnp.int32)
    allowed = (seg[:, None] == seg[None, :]) & (rows[:, None] >= rows[None, :])
    scores = jnp.where(allowed, scores, -1e30)
    probs = jax.nn.softmax(scores, axis=-1).astype(jnp.bfloat16)
    attended = jnp.dot(probs, values, preferred_element_type=jnp.float32).astype(jnp.bfloat16)
    return (x_wide + jnp.dot(attended, w_out, preferred_element_type=jnp.float32)).astype(
        jnp.bfloat16
    )


def pipelined(inputs, cotangent, doc_lengths, norm_gain, w_qkv, w_out):
    sections = lax.axis_size("section")
    section = lax.axis_index("section")
    micro = inputs.shape[0]
    count = inputs.shape[1]
    segs = jax.vmap(lambda lens: segments_of(lens, count))(doc_lengths[:, 0, :])
    gain = norm_gain[0]
    full_qkv, full_out = (
        lax.all_gather(w_qkv[0], "dp", axis=0, tiled=True),
        lax.all_gather(w_out[0], "dp", axis=1, tiled=True),
    )
    total_steps = micro + sections - 1
    empty = jnp.zeros(inputs.shape[1:], inputs.dtype)

    def forward_at(step, incoming, saved):
        index = step - section
        live = (index >= 0) & (index < micro)
        slot = jnp.clip(index, 0, micro - 1)
        first = lax.dynamic_index_in_dim(inputs, slot, 0, keepdims=False)
        x = jnp.where(section == 0, first, incoming)
        seg = lax.dynamic_index_in_dim(segs, slot, 0, keepdims=False)
        out = layer(x, gain, full_qkv, full_out, seg)
        old = lax.dynamic_index_in_dim(saved, slot, 0, keepdims=False)
        saved = lax.dynamic_update_index_in_dim(saved, jnp.where(live, x, old), slot, 0)
        return (out, saved)

    def forward_step(carry, step):
        incoming, saved = carry
        out, saved = forward_at(step, incoming, saved)
        incoming = passed_along(out, "section", 1)
        return ((incoming, saved), None)

    start_saved = jnp.zeros(inputs.shape, inputs.dtype)
    (incoming, saved), _ = lax.scan(
        forward_step, (empty, start_saved), jnp.arange(total_steps - 1, dtype=jnp.int32)
    )
    _, saved = forward_at(jnp.int32(total_steps - 1), incoming, saved)

    def backward_at(step, incoming, sum_qkv, sum_out):
        index = step - (sections - 1 - section)
        live = (index >= 0) & (index < micro)
        slot = jnp.clip(index, 0, micro - 1)
        last = lax.dynamic_index_in_dim(cotangent, slot, 0, keepdims=False)
        grad_y = jnp.where(section == sections - 1, last, incoming)
        x = lax.dynamic_index_in_dim(saved, slot, 0, keepdims=False)
        seg = lax.dynamic_index_in_dim(segs, slot, 0, keepdims=False)
        _, pull = jax.vjp(lambda a, b, c: layer(a, gain, b, c, seg), x, full_qkv, full_out)
        grad_x, grad_q, grad_o = pull(grad_y)
        sum_qkv = sum_qkv + jnp.where(live, grad_q.astype(jnp.float32), 0.0)
        sum_out = sum_out + jnp.where(live, grad_o.astype(jnp.float32), 0.0)
        return (grad_x, sum_qkv, sum_out)

    def backward_step(carry, step):
        incoming, sum_qkv, sum_out = carry
        grad_x, sum_qkv, sum_out = backward_at(step, incoming, sum_qkv, sum_out)
        incoming = passed_along(grad_x, "section", -1)
        return ((incoming, sum_qkv, sum_out), None)

    zero_qkv = jnp.zeros(full_qkv.shape, jnp.float32)
    zero_out = jnp.zeros(full_out.shape, jnp.float32)
    (incoming, sum_qkv, sum_out), _ = lax.scan(
        backward_step, (empty, zero_qkv, zero_out), jnp.arange(total_steps - 1, dtype=jnp.int32)
    )
    _, sum_qkv, sum_out = backward_at(jnp.int32(total_steps - 1), incoming, sum_qkv, sum_out)
    share_qkv, share_out = (
        lax.psum_scatter(sum_qkv, "dp", scatter_dimension=0, tiled=True),
        lax.psum_scatter(sum_out, "dp", scatter_dimension=1, tiled=True),
    )
    return (share_qkv[None], share_out[None])


def nn(a, b):
    return lax.dot_general(a, b, (((1,), (0,)), ((), ())), preferred_element_type=F32)


def nt(a, b):
    return lax.dot_general(a, b, (((1,), (1,)), ((), ())), preferred_element_type=F32)


def block_copies(planes, index, k, refs, out_ref, sems):
    width = refs[0].shape[-1] // (planes * PLANE)
    section, p = index[0], index[2]
    copies = []
    for z in range(planes):
        at = pl.multiple_of((z * PLANE + (p ^ k)) * width, width)
        for half, ref in enumerate(refs):
            copies.append(
                pltpu.make_async_copy(
                    ref.at[section, :, pl.ds(at, width)],
                    out_ref.at[half, :, pl.ds(z * width, width)],
                    sems.at[len(copies)],
                )
            )
    return copies


def mark_kernel(pack_ref, gain_ref, out_ref):
    out_ref[: pack_ref.shape[0], :] = pack_ref[...]
    out_ref[pack_ref.shape[0] :, :] = gain_ref[...]


def blocks_kernel(planes, index, qkv_ref, wout_ref, x_ref, c_ref, pack_ref, *refs):
    out_refs, pack_sems, sems = refs[:-2], refs[-2], refs[-1]
    qkv_rows = qkv_ref.shape[0]
    copies = [
        pltpu.make_async_copy(qkv_ref, pack_ref.at[:qkv_rows], pack_sems.at[0]),
        pltpu.make_async_copy(wout_ref, pack_ref.at[qkv_rows:], pack_sems.at[1]),
    ]
    for k, out_ref in enumerate(out_refs):
        copies += block_copies(planes, index, k, (x_ref, c_ref), out_ref, sems.at[k])
    for copy in copies:
        copy.start()
    for copy in copies:
        copy.wait()


def project_kernel(planes, heads, index, *refs):
    blocks, own, other = refs[:PLANE], refs[PLANE : PLANE + planes], refs[PLANE + planes : PLANE + 2 * planes]
    x_ref, c_ref, vx_ref, gain_ref = refs[PLANE + 2 * planes : PLANE + 2 * planes + 4]
    out_refs = refs[PLANE + 2 * planes + 4 : -4]
    vc_ref, sum_ref, *wide_refs = refs[-4:]
    qkv, width = 3 * heads, vx_ref.shape[-1]
    section, place, p = index[0], index[1], index[2]
    for ref, wide_ref in zip((own[0], other[0]), wide_refs):
        wide_ref[...] = ref[qkv + heads :, :].astype(F32)
    for z in range(planes):
        mine, theirs = (ref[pl.ds(z * PLANE + p, 1), :] for ref in wide_refs)
        gain_ref[z, 0:1, :] = jnp.where(section == 0, mine, theirs)
        gain_ref[z, 1:2, :] = jnp.where(section == 0, theirs, mine)
    for k in range(planes):
        at = place ^ k
        mine, theirs = own[k][: qkv + heads, :], other[k][: qkv + heads, :]
        zero = jnp.where(section == 0, mine, theirs)
        one = jnp.where(section == 0, theirs, mine)
        empty = jnp.zeros((heads, width), BF16)
        vx_ref[at, :qkv, :] = (zero[:qkv].astype(F32) * gain_ref[at, 0:1, :]).astype(BF16)
        vx_ref[at, qkv : qkv + heads, :] = zero[qkv : qkv + heads]
        vx_ref[at, qkv + heads : 2 * qkv + heads, :] = (one[:qkv].astype(F32) * gain_ref[at, 1:2, :]).astype(BF16)
        vx_ref[at, 2 * qkv + heads :, :] = empty
        vc_ref[at, :heads, :] = empty
        vc_ref[at, heads : 2 * heads, :] = one[qkv : qkv + heads]
        vc_ref[at, 2 * heads : 3 * heads, :] = zero[qkv : qkv + heads]
        vc_ref[at, 3 * heads :, :] = empty
    for k in range(PLANE):
        x_ref[p ^ k] = blocks[-k][0]
        c_ref[p ^ k] = blocks[-k][1]
    rows = x_ref.shape[0] * x_ref.shape[1]
    with_x = with_c = squares = products = None
    for z in range(planes):
        cols = slice(z * width, (z + 1) * width)
        x = x_ref[:, :, cols].reshape(rows, width)
        c = c_ref[:, :, cols].reshape(rows, width)
        wide = x.astype(F32)
        out = vx_ref[z, qkv : qkv + heads, :]
        right = jnp.concatenate([vx_ref[z, qkv + heads : 2 * qkv + heads, :], out], axis=0)
        new = nt(x, vx_ref[z]), nt(c, vc_ref[z]), jnp.sum(wide * wide, axis=1, keepdims=True), nt(out, right)
        if with_x is None:
            with_x, with_c, squares, products = new
        else:
            with_x, with_c = with_x + new[0], with_c + new[1]
            squares, products = squares + new[2], products + new[3]
    half = 2 * heads
    lane = lax.broadcasted_iota(jnp.int32, (rows, half), 1)
    high = squares.astype(BF16).astype(F32)
    last = jnp.where(lane == heads, high, jnp.where(lane == heads + 1, squares - high, with_c[:, half:]))
    sum_ref[:, : 3 * half] = with_x[:, : 3 * half].astype(BF16)
    sum_ref[:, 3 * half : 4 * half] = (with_x[:, 3 * half :] + with_c[:, :half]).astype(BF16)
    sum_ref[:, 4 * half :] = last.astype(BF16)
    block = rows // PLANE
    for k in range(PLANE):
        start = pl.multiple_of((p ^ k) * block, block)
        out_refs[k][:, : 5 * half] = sum_ref[pl.ds(start, block), :]
        out_refs[k][:, 5 * half :] = products.astype(BF16)


def attention(qkv, allowed, heads):
    query, keys, values = (qkv[:, i * heads : (i + 1) * heads].astype(BF16) for i in range(3))
    scores = jnp.where(allowed, nt(query, keys) * heads ** (-0.5), -1e30)
    raised = jnp.exp(scores - jnp.max(scores, axis=1, keepdims=True))
    probs = raised / jnp.sum(raised, axis=1, keepdims=True)
    return probs, nn(probs.astype(BF16), values).astype(BF16)


def attention_grad(qkv, probs, att, d_att, heads):
    query, keys, values = (qkv[:, i * heads : (i + 1) * heads].astype(BF16) for i in range(3))
    inner = jnp.sum(att.astype(F32) * d_att.astype(F32), axis=1, keepdims=True)
    d_values = nn(jnp.transpose(probs).astype(BF16), d_att)
    d_scores = probs * (nt(d_att, values) - inner) * heads ** (-0.5)
    d_query = nn(d_scores.astype(BF16), keys)
    d_keys = nn(jnp.transpose(d_scores).astype(BF16), query)
    return jnp.concatenate([d_query, d_keys, d_values], axis=1).astype(BF16).astype(F32)


def summed(parts):
    total = parts[0][...].astype(F32)
    for part in parts[1:]:
        total = total + part[...].astype(F32)
    return total


def chain_kernel(features, heads, index, docs, *refs):
    out_ref = refs[-1]
    qkv, half = 3 * heads, 2 * heads
    total = summed(refs[:-1])
    rows = total.shape[0]
    section = index[0]
    query_at = lax.broadcasted_iota(jnp.int32, (rows, rows), 0)
    key_at = lax.broadcasted_iota(jnp.int32, (rows, rows), 1)
    allowed = query_at >= key_at
    end = 0
    for i in range(docs.shape[2]):
        end = end + docs[section, 0, i]
        allowed = allowed & ((query_at >= end) == (key_at >= end))
    x_out = total[:, qkv : 2 * half]
    x_one = total[:, 2 * half : 2 * half + qkv]
    tail = total[:, 4 * half : 5 * half]
    c_one, c_zero = total[:, 4 * half - heads : 4 * half].astype(BF16), tail[:, :heads]
    lane = lax.broadcasted_iota(jnp.int32, tail.shape, 1)
    squares = jnp.sum(jnp.where((lane == heads) | (lane == heads + 1), tail, 0.0), axis=1, keepdims=True)
    mixed = total[:, 5 * half : 5 * half + qkv].astype(BF16)
    gram = total[:, 5 * half + qkv :].astype(BF16)

    scale0 = lax.rsqrt(squares / features + 1e-05)
    qkv0 = (total[:, :qkv] * scale0).astype(BF16).astype(F32)
    probs0, att0 = attention(qkv0, allowed, heads)
    wide0 = att0.astype(F32)
    y_out = x_out + nn(att0, gram)
    squares = squares + jnp.sum(wide0 * (x_out + y_out), axis=1, keepdims=True)
    scale1 = lax.rsqrt(jnp.maximum(squares, 0.0) / features + 1e-05)
    qkv1 = ((x_one + nn(att0, mixed)) * scale1).astype(BF16).astype(F32)
    probs1, att1 = attention(qkv1, allowed, heads)
    d_qkv1 = attention_grad(qkv1, probs1, att1, c_one, heads)
    inner = jnp.sum(d_qkv1 * qkv1, axis=1, keepdims=True) * scale1 * scale1 / features
    e1 = d_qkv1 * scale1
    d_att0 = c_zero + nt(e1.astype(BF16), mixed) - inner * y_out
    e0 = attention_grad(qkv0, probs0, att0, d_att0.astype(BF16), heads) * scale0
    factors = [e0, wide0, e1, wide0 * inner, att1.astype(F32), jnp.zeros((rows, heads), F32)]
    out_ref[...] = jnp.concatenate(factors, axis=1).astype(BF16)


def grads_kernel(planes, heads, index, *refs):
    factors, (x_ref, c_ref, vx_ref, gain_ref) = refs[:PLANE], refs[PLANE : PLANE + 4]
    keep_ref, send_ref, all_ref = refs[PLANE + 4 :]
    qkv, half, width = 3 * heads, 2 * heads, vx_ref.shape[-1]
    section, p = index[0], index[2]
    for k in range(PLANE):
        all_ref[p ^ k] = factors[k][...]
    rows = x_ref.shape[0] * x_ref.shape[1]
    turned = jnp.transpose(all_ref[...].astype(F32).reshape(rows, 5 * half)).astype(BF16)
    att0, att1 = turned[qkv : qkv + heads], turned[4 * half : 4 * half + heads]
    right = turned[2 * half : 4 * half]
    small = nt(right, att0).astype(BF16)
    small_t = nt(att0, right[:qkv]).astype(BF16)
    for z in range(planes):
        cols = slice(z * width, (z + 1) * width)
        x = x_ref[:, :, cols].reshape(rows, width)
        c = c_ref[:, :, cols].reshape(rows, width)
        out = vx_ref[z, qkv : qkv + heads, :]
        with_x = nn(turned[: 4 * half], x)
        left = with_x[2 * half :] + nn(small, out)
        zero = with_x[:qkv] * gain_ref[z, 0:1, :]
        one = left[:qkv] * gain_ref[z, 1:2, :]
        keep_ref[z, :qkv, :] = jnp.where(section == 0, zero, one)
        send_ref[z, :qkv, :] = jnp.where(section == 0, one, zero).astype(BF16)
        zero = nn(att0, c) + nn(small_t, vx_ref[z, qkv + heads : 2 * qkv + heads, :]) - left[qkv:]
        one = nn(att1, c)
        keep_ref[z, qkv:, :] = jnp.where(section == 0, zero, one)
        send_ref[z, qkv:, :] = jnp.where(section == 0, one, zero).astype(BF16)


def merge_kernel(index, keep_ref, come_ref, *out_refs):
    place = index[1]
    out_refs[0][...] = keep_ref[place] + come_ref[place].astype(F32)
    for k in range(1, len(out_refs)):
        out_refs[k][...] = (keep_ref[place ^ k] + come_ref[place ^ k].astype(F32)).astype(BF16)


def last_kernel(qkv_rows, keep_ref, *refs):
    parts, (qkv_ref, out_ref) = refs[:-2], refs[-2:]
    total = keep_ref[...]
    for part in parts:
        total = total + part[...].astype(F32)
    qkv_ref[...] = total[:qkv_rows]
    out_ref[...] = total[qkv_rows:]


def far_first(value, count, send):
    of = lambda k: value[k] if isinstance(value, (list, tuple)) else value
    got = {k: send(of(k), k) for k in reversed(range(1, count))}
    return [of(0)] + [got[k] for k in range(1, count)]


def call(kernel, outs, *args, scalars=0, scratch=()):
    smem = pl.BlockSpec(memory_space=pltpu.SMEM)
    vmem = pl.BlockSpec(memory_space=pltpu.VMEM)
    return pl.pallas_call(
        kernel,
        out_shape=[jax.ShapeDtypeStruct(shape, dtype) for shape, dtype in outs],
        in_specs=[smem] * scalars + [vmem] * (len(args) - scalars),
        out_specs=[vmem] * len(outs),
        scratch_shapes=[pltpu.VMEM(shape, dtype) for shape, dtype in scratch],
        compiler_params=pltpu.CompilerParams(vmem_limit_bytes=VMEM_LIMIT),
    )(*args)


def planar(inputs, cotangent, doc_lengths, norm_gain, w_qkv, w_out):
    shards = lax.axis_size("dp")
    planes = shards // PLANE
    section, place = lax.axis_index("section"), lax.axis_index("dp")
    z, p = place // PLANE, place % PLANE
    index = jnp.stack([section, z, p]).astype(jnp.int32)
    block, features = inputs.shape[1:]
    rows = PLANE * block
    heads, width = w_out.shape[1:]
    qkv_rows = w_qkv.shape[2]
    cols = planes * width
    def along_z(value, k):
        route = [(a * PLANE + b, (a ^ k) * PLANE + b) for a in range(planes) for b in range(PLANE)]
        return lax.ppermute(value, "dp", route)

    def to_sibling(value):
        return lax.ppermute(value, "section", [(0, 1), (1, 0)])

    def along_plane(value, k):
        route = [(a * PLANE + b, a * PLANE + (b ^ k)) for a in range(planes) for b in range(PLANE)]
        return lax.ppermute(value, "dp", route)

    def exchange(value):
        return far_first(value, PLANE, along_plane)

    smem, vmem = pl.BlockSpec(memory_space=pltpu.SMEM), pl.BlockSpec(memory_space=pltpu.VMEM)
    hbm = pl.BlockSpec(memory_space=pltpu.HBM)
    params = pltpu.CompilerParams(vmem_limit_bytes=VMEM_LIMIT)
    qkv_in, out_in, x_in, c_in = [
        pltpu.with_memory_space_constraint(value, pltpu.HBM)
        for value in (w_qkv[0].T, w_out[0], inputs, cotangent)
    ]
    one_block = jax.ShapeDtypeStruct((2, block, cols), BF16)
    pack, *blocks = pl.pallas_call(
        functools.partial(blocks_kernel, planes),
        out_shape=[jax.ShapeDtypeStruct((qkv_rows + heads, width), BF16)] + [one_block] * PLANE,
        in_specs=[smem] + [hbm] * 4,
        out_specs=[vmem] * (PLANE + 1),
        scratch_shapes=[pltpu.SemaphoreType.DMA((2,)), pltpu.SemaphoreType.DMA((PLANE, 2 * planes))],
        compiler_params=params,
    )(index, qkv_in, out_in, x_in, c_in)
    gain = norm_gain[0].reshape(shards, width)
    blocks = [blocks[0]] + far_first(blocks, PLANE, along_plane)[1:]
    pieces = {0: pack}
    for step in reversed([1 << bit for bit in range(planes.bit_length() - 1)]):
        for k in list(pieces):
            pieces[k ^ step] = along_z(pieces[k], step)
    mine, late_gain, _ = lax.optimization_barrier((pack, gain, blocks[3]))
    (marked,) = call(mark_kernel, [((qkv_rows + heads + shards, width), BF16)], mine, late_gain)
    pieces[planes // 2], _ = lax.optimization_barrier((pieces[planes // 2], blocks[3]))
    own = [marked] + [pieces[k] for k in range(1, planes)]
    other = [to_sibling(piece) for piece in own]

    split = ((PLANE, block, cols), BF16)
    half = 2 * heads
    x, c, vx, gains, *sent = call(
        functools.partial(project_kernel, planes, heads),
        [split, split, ((planes, 4 * half, width), BF16), ((planes, 8, width), F32)]
        + [((block, 7 * half), BF16)] * PLANE,
        index, blocks[0], *blocks[:0:-1], *own, *other, scalars=1,
        scratch=[((planes, 2 * half, width), BF16), ((rows, 5 * half), BF16)] + [((shards, width), F32)] * 2,
    )
    (factors,) = call(
        functools.partial(chain_kernel, features, heads),
        [((block, 5 * half), BF16)],
        index, doc_lengths, *exchange(sent)[::-1], scalars=2,
    )
    grads = (planes, qkv_rows + heads, width)
    keep, send = call(
        functools.partial(grads_kernel, planes, heads),
        [(grads, F32), (grads, BF16)],
        index, *exchange(factors), x, c, vx, gains, scalars=1,
        scratch=[((PLANE, block, 5 * half), BF16)],
    )
    merged = call(
        merge_kernel,
        [(grads[1:], F32)] + [(grads[1:], BF16)] * (planes - 1),
        index, keep, to_sibling(send), scalars=1,
    )
    parts = far_first(merged, planes, along_z)[1:]
    grad_qkv, grad_out = call(
        functools.partial(last_kernel, qkv_rows),
        [((qkv_rows, width), F32), ((heads, width), F32)],
        merged[0], *parts[::-1],
    )
    return (grad_qkv.T[None], grad_out[None])


def solution(mesh):
    sections, shards = mesh.shape["section"], mesh.shape["dp"]
    planes = shards // PLANE

    def body(inputs, *rest):
        fits = shards % PLANE == 0 and planes & (planes - 1) == 0
        if sections == 2 and inputs.shape[0] == 2 and fits:
            return planar(inputs, *rest)
        return pipelined(inputs, *rest)

    return jax.shard_map(
        body,
        mesh=mesh,
        in_specs=(
            P(None, "dp", None),
            P(None, "dp", None),
            P(None, "dp", None),
            P("section", None),
            P("section", "dp", None),
            P("section", None, "dp"),
        ),
        out_specs=(P("section", "dp", None), P("section", None, "dp")),
        check_vma=False,
    )
```

```python
import functools

import jax
import jax.numpy as jnp
from jax import lax
from jax.experimental import pallas as pl
from jax.experimental.pallas import tpu as pltpu
from jax.sharding import PartitionSpec as P

F32 = jnp.float32
BF16 = jnp.bfloat16
PLANE = 4
VMEM_LIMIT = 16 * 1024 * 1024


def passed_along(block, axis, distance):
    devices = range(lax.axis_size(axis))
    route = [(i - distance, i) for i in devices if i - distance in devices]
    return lax.ppermute(block, axis, route)


def segments_of(lengths, count):
    ends = jnp.cumsum(lengths)
    position = jnp.arange(count, dtype=jnp.int32)
    return jnp.sum((position[:, None] >= ends[None, :]).astype(jnp.int32), axis=1)


def layer(x, gain, w_qkv, w_out, seg):
    head = w_out.shape[0]
    x_wide = x.astype(jnp.float32)
    scale = lax.rsqrt(jnp.mean(x_wide * x_wide, axis=-1, keepdims=True) + 1e-05)
    normed = (x_wide * scale * gain.astype(jnp.float32)).astype(jnp.bfloat16)
    qkv = jnp.dot(normed, w_qkv, preferred_element_type=jnp.float32).astype(jnp.bfloat16)
    query = qkv[:, :head]
    keys = qkv[:, head : 2 * head]
    values = qkv[:, 2 * head :]
    scores = jnp.dot(query, keys.T, preferred_element_type=jnp.float32) * head ** (-0.5)
    rows = jnp.arange(x.shape[0], dtype=jnp.int32)
    allowed = (seg[:, None] == seg[None, :]) & (rows[:, None] >= rows[None, :])
    scores = jnp.where(allowed, scores, -1e30)
    probs = jax.nn.softmax(scores, axis=-1).astype(jnp.bfloat16)
    attended = jnp.dot(probs, values, preferred_element_type=jnp.float32).astype(jnp.bfloat16)
    return (x_wide + jnp.dot(attended, w_out, preferred_element_type=jnp.float32)).astype(
        jnp.bfloat16
    )


def pipelined(inputs, cotangent, doc_lengths, norm_gain, w_qkv, w_out):
    sections = lax.axis_size("section")
    section = lax.axis_index("section")
    micro = inputs.shape[0]
    count = inputs.shape[1]
    segs = jax.vmap(lambda lens: segments_of(lens, count))(doc_lengths[:, 0, :])
    gain = norm_gain[0]
    full_qkv, full_out = (
        lax.all_gather(w_qkv[0], "dp", axis=0, tiled=True),
        lax.all_gather(w_out[0], "dp", axis=1, tiled=True),
    )
    total_steps = micro + sections - 1
    empty = jnp.zeros(inputs.shape[1:], inputs.dtype)

    def forward_at(step, incoming, saved):
        index = step - section
        live = (index >= 0) & (index < micro)
        slot = jnp.clip(index, 0, micro - 1)
        first = lax.dynamic_index_in_dim(inputs, slot, 0, keepdims=False)
        x = jnp.where(section == 0, first, incoming)
        seg = lax.dynamic_index_in_dim(segs, slot, 0, keepdims=False)
        out = layer(x, gain, full_qkv, full_out, seg)
        old = lax.dynamic_index_in_dim(saved, slot, 0, keepdims=False)
        saved = lax.dynamic_update_index_in_dim(saved, jnp.where(live, x, old), slot, 0)
        return (out, saved)

    def forward_step(carry, step):
        incoming, saved = carry
        out, saved = forward_at(step, incoming, saved)
        incoming = passed_along(out, "section", 1)
        return ((incoming, saved), None)

    start_saved = jnp.zeros(inputs.shape, inputs.dtype)
    (incoming, saved), _ = lax.scan(
        forward_step, (empty, start_saved), jnp.arange(total_steps - 1, dtype=jnp.int32)
    )
    _, saved = forward_at(jnp.int32(total_steps - 1), incoming, saved)

    def backward_at(step, incoming, sum_qkv, sum_out):
        index = step - (sections - 1 - section)
        live = (index >= 0) & (index < micro)
        slot = jnp.clip(index, 0, micro - 1)
        last = lax.dynamic_index_in_dim(cotangent, slot, 0, keepdims=False)
        grad_y = jnp.where(section == sections - 1, last, incoming)
        x = lax.dynamic_index_in_dim(saved, slot, 0, keepdims=False)
        seg = lax.dynamic_index_in_dim(segs, slot, 0, keepdims=False)
        _, pull = jax.vjp(lambda a, b, c: layer(a, gain, b, c, seg), x, full_qkv, full_out)
        grad_x, grad_q, grad_o = pull(grad_y)
        sum_qkv = sum_qkv + jnp.where(live, grad_q.astype(jnp.float32), 0.0)
        sum_out = sum_out + jnp.where(live, grad_o.astype(jnp.float32), 0.0)
        return (grad_x, sum_qkv, sum_out)

    def backward_step(carry, step):
        incoming, sum_qkv, sum_out = carry
        grad_x, sum_qkv, sum_out = backward_at(step, incoming, sum_qkv, sum_out)
        incoming = passed_along(grad_x, "section", -1)
        return ((incoming, sum_qkv, sum_out), None)

    zero_qkv = jnp.zeros(full_qkv.shape, jnp.float32)
    zero_out = jnp.zeros(full_out.shape, jnp.float32)
    (incoming, sum_qkv, sum_out), _ = lax.scan(
        backward_step, (empty, zero_qkv, zero_out), jnp.arange(total_steps - 1, dtype=jnp.int32)
    )
    _, sum_qkv, sum_out = backward_at(jnp.int32(total_steps - 1), incoming, sum_qkv, sum_out)
    share_qkv, share_out = (
        lax.psum_scatter(sum_qkv, "dp", scatter_dimension=0, tiled=True),
        lax.psum_scatter(sum_out, "dp", scatter_dimension=1, tiled=True),
    )
    return (share_qkv[None], share_out[None])


def nn(a, b):
    return lax.dot_general(a, b, (((1,), (0,)), ((), ())), preferred_element_type=F32)


def nt(a, b):
    return lax.dot_general(a, b, (((1,), (1,)), ((), ())), preferred_element_type=F32)


def block_copies(planes, index, k, refs, out_ref, sems):
    width = refs[0].shape[-1] // (planes * PLANE)
    section, p = index[0], index[2]
    copies = []
    for z in range(planes):
        at = pl.multiple_of((z * PLANE + (p ^ k)) * width, width)
        for half, ref in enumerate(refs):
            copies.append(
                pltpu.make_async_copy(
                    ref.at[section, :, pl.ds(at, width)],
                    out_ref.at[half, :, pl.ds(z * width, width)],
                    sems.at[len(copies)],
                )
            )
    return copies


def mark_kernel(planes, index, pack_ref, gain_ref, x_ref, c_ref, out_ref, block_ref, sems):
    copies = block_copies(planes, index, 0, (x_ref, c_ref), block_ref, sems)
    for copy in copies:
        copy.start()
    out_ref[: pack_ref.shape[0], :] = pack_ref[...]
    out_ref[pack_ref.shape[0] :, :] = gain_ref[...]
    for copy in copies:
        copy.wait()


def blocks_kernel(planes, index, qkv_ref, wout_ref, x_ref, c_ref, pack_ref, *refs):
    out_refs, pack_sems, sems = refs[:-2], refs[-2], refs[-1]
    qkv_rows = qkv_ref.shape[0]
    copies = [
        pltpu.make_async_copy(qkv_ref, pack_ref.at[:qkv_rows], pack_sems.at[0]),
        pltpu.make_async_copy(wout_ref, pack_ref.at[qkv_rows:], pack_sems.at[1]),
    ]
    for k, out_ref in enumerate(out_refs, 1):
        copies += block_copies(planes, index, k, (x_ref, c_ref), out_ref, sems.at[k - 1])
    for copy in copies:
        copy.start()
    for copy in copies:
        copy.wait()


def project_kernel(planes, heads, index, *refs):
    blocks, own, other = refs[:PLANE], refs[PLANE : PLANE + planes], refs[PLANE + planes : PLANE + 2 * planes]
    x_ref, c_ref, vx_ref, gain_ref = refs[PLANE + 2 * planes : PLANE + 2 * planes + 4]
    out_refs = refs[PLANE + 2 * planes + 4 : -4]
    vc_ref, sum_ref, *wide_refs = refs[-4:]
    qkv, width = 3 * heads, vx_ref.shape[-1]
    section, place, p = index[0], index[1], index[2]
    for ref, wide_ref in zip((own[0], other[0]), wide_refs):
        wide_ref[...] = ref[qkv + heads :, :].astype(F32)
    for z in range(planes):
        mine, theirs = (ref[pl.ds(z * PLANE + p, 1), :] for ref in wide_refs)
        gain_ref[z, 0:1, :] = jnp.where(section == 0, mine, theirs)
        gain_ref[z, 1:2, :] = jnp.where(section == 0, theirs, mine)
    for k in range(planes):
        at = place ^ k
        mine, theirs = own[k][: qkv + heads, :], other[k][: qkv + heads, :]
        zero = jnp.where(section == 0, mine, theirs)
        one = jnp.where(section == 0, theirs, mine)
        empty = jnp.zeros((heads, width), BF16)
        vx_ref[at, :qkv, :] = (zero[:qkv].astype(F32) * gain_ref[at, 0:1, :]).astype(BF16)
        vx_ref[at, qkv : qkv + heads, :] = zero[qkv : qkv + heads]
        vx_ref[at, qkv + heads : 2 * qkv + heads, :] = (one[:qkv].astype(F32) * gain_ref[at, 1:2, :]).astype(BF16)
        vx_ref[at, 2 * qkv + heads :, :] = empty
        vc_ref[at, :heads, :] = empty
        vc_ref[at, heads : 2 * heads, :] = one[qkv : qkv + heads]
        vc_ref[at, 2 * heads : 3 * heads, :] = zero[qkv : qkv + heads]
        vc_ref[at, 3 * heads :, :] = empty
    for k in range(PLANE):
        x_ref[p ^ k] = blocks[-k][0]
        c_ref[p ^ k] = blocks[-k][1]
    rows = x_ref.shape[0] * x_ref.shape[1]
    with_x = with_c = squares = products = None
    for z in range(planes):
        cols = slice(z * width, (z + 1) * width)
        x = x_ref[:, :, cols].reshape(rows, width)
        c = c_ref[:, :, cols].reshape(rows, width)
        wide = x.astype(F32)
        out = vx_ref[z, qkv : qkv + heads, :]
        right = jnp.concatenate([vx_ref[z, qkv + heads : 2 * qkv + heads, :], out], axis=0)
        new = nt(x, vx_ref[z]), nt(c, vc_ref[z]), jnp.sum(wide * wide, axis=1, keepdims=True), nt(out, right)
        if with_x is None:
            with_x, with_c, squares, products = new
        else:
            with_x, with_c = with_x + new[0], with_c + new[1]
            squares, products = squares + new[2], products + new[3]
    half = 2 * heads
    lane = lax.broadcasted_iota(jnp.int32, (rows, half), 1)
    high = squares.astype(BF16).astype(F32)
    last = jnp.where(lane == heads, high, jnp.where(lane == heads + 1, squares - high, with_c[:, half:]))
    sum_ref[:, : 3 * half] = with_x[:, : 3 * half].astype(BF16)
    sum_ref[:, 3 * half : 4 * half] = (with_x[:, 3 * half :] + with_c[:, :half]).astype(BF16)
    sum_ref[:, 4 * half :] = last.astype(BF16)
    block = rows // PLANE
    for k in range(PLANE):
        start = pl.multiple_of((p ^ k) * block, block)
        out_refs[k][:, : 5 * half] = sum_ref[pl.ds(start, block), :]
        out_refs[k][:, 5 * half :] = products.astype(BF16)


def attention(qkv, allowed, heads):
    query, keys, values = (qkv[:, i * heads : (i + 1) * heads].astype(BF16) for i in range(3))
    scores = jnp.where(allowed, nt(query, keys) * heads ** (-0.5), -1e30)
    raised = jnp.exp(scores - jnp.max(scores, axis=1, keepdims=True))
    probs = raised / jnp.sum(raised, axis=1, keepdims=True)
    return probs, nn(probs.astype(BF16), values).astype(BF16)


def attention_grad(qkv, probs, att, d_att, heads):
    query, keys, values = (qkv[:, i * heads : (i + 1) * heads].astype(BF16) for i in range(3))
    inner = jnp.sum(att.astype(F32) * d_att.astype(F32), axis=1, keepdims=True)
    d_values = nn(jnp.transpose(probs).astype(BF16), d_att)
    d_scores = probs * (nt(d_att, values) - inner) * heads ** (-0.5)
    d_query = nn(d_scores.astype(BF16), keys)
    d_keys = nn(jnp.transpose(d_scores).astype(BF16), query)
    return jnp.concatenate([d_query, d_keys, d_values], axis=1).astype(BF16).astype(F32)


def summed(parts):
    total = parts[0][...].astype(F32)
    for part in parts[1:]:
        total = total + part[...].astype(F32)
    return total


def chain_kernel(features, heads, index, docs, *refs):
    out_ref = refs[-1]
    qkv, half = 3 * heads, 2 * heads
    total = summed(refs[:-1])
    rows = total.shape[0]
    section = index[0]
    query_at = lax.broadcasted_iota(jnp.int32, (rows, rows), 0)
    key_at = lax.broadcasted_iota(jnp.int32, (rows, rows), 1)
    allowed = query_at >= key_at
    end = 0
    for i in range(docs.shape[2]):
        end = end + docs[section, 0, i]
        allowed = allowed & ((query_at >= end) == (key_at >= end))
    x_out = total[:, qkv : 2 * half]
    x_one = total[:, 2 * half : 2 * half + qkv]
    tail = total[:, 4 * half : 5 * half]
    c_one, c_zero = total[:, 4 * half - heads : 4 * half].astype(BF16), tail[:, :heads]
    lane = lax.broadcasted_iota(jnp.int32, tail.shape, 1)
    squares = jnp.sum(jnp.where((lane == heads) | (lane == heads + 1), tail, 0.0), axis=1, keepdims=True)
    mixed = total[:, 5 * half : 5 * half + qkv].astype(BF16)
    gram = total[:, 5 * half + qkv :].astype(BF16)

    scale0 = lax.rsqrt(squares / features + 1e-05)
    qkv0 = (total[:, :qkv] * scale0).astype(BF16).astype(F32)
    probs0, att0 = attention(qkv0, allowed, heads)
    wide0 = att0.astype(F32)
    y_out = x_out + nn(att0, gram)
    squares = squares + jnp.sum(wide0 * (x_out + y_out), axis=1, keepdims=True)
    scale1 = lax.rsqrt(jnp.maximum(squares, 0.0) / features + 1e-05)
    qkv1 = ((x_one + nn(att0, mixed)) * scale1).astype(BF16).astype(F32)
    probs1, att1 = attention(qkv1, allowed, heads)
    d_qkv1 = attention_grad(qkv1, probs1, att1, c_one, heads)
    inner = jnp.sum(d_qkv1 * qkv1, axis=1, keepdims=True) * scale1 * scale1 / features
    e1 = d_qkv1 * scale1
    d_att0 = c_zero + nt(e1.astype(BF16), mixed) - inner * y_out
    e0 = attention_grad(qkv0, probs0, att0, d_att0.astype(BF16), heads) * scale0
    factors = [e0, wide0, e1, wide0 * inner, att1.astype(F32), jnp.zeros((rows, heads), F32)]
    out_ref[...] = jnp.concatenate(factors, axis=1).astype(BF16)


def grads_kernel(planes, heads, index, *refs):
    factors, (x_ref, c_ref, vx_ref, gain_ref) = refs[:PLANE], refs[PLANE : PLANE + 4]
    keep_ref, send_ref, all_ref = refs[PLANE + 4 :]
    qkv, half, width = 3 * heads, 2 * heads, vx_ref.shape[-1]
    section, p = index[0], index[2]
    for k in range(PLANE):
        all_ref[p ^ k] = factors[k][...]
    rows = x_ref.shape[0] * x_ref.shape[1]
    turned = jnp.transpose(all_ref[...].astype(F32).reshape(rows, 5 * half)).astype(BF16)
    att0, att1 = turned[qkv : qkv + heads], turned[4 * half : 4 * half + heads]
    right = turned[2 * half : 4 * half]
    small = nt(right, att0).astype(BF16)
    small_t = nt(att0, right[:qkv]).astype(BF16)
    for z in range(planes):
        cols = slice(z * width, (z + 1) * width)
        x = x_ref[:, :, cols].reshape(rows, width)
        c = c_ref[:, :, cols].reshape(rows, width)
        out = vx_ref[z, qkv : qkv + heads, :]
        with_x = nn(turned[: 4 * half], x)
        left = with_x[2 * half :] + nn(small, out)
        zero = with_x[:qkv] * gain_ref[z, 0:1, :]
        one = left[:qkv] * gain_ref[z, 1:2, :]
        keep_ref[z, :qkv, :] = jnp.where(section == 0, zero, one)
        send_ref[z, :qkv, :] = jnp.where(section == 0, one, zero).astype(BF16)
        zero = nn(att0, c) + nn(small_t, vx_ref[z, qkv + heads : 2 * qkv + heads, :]) - left[qkv:]
        one = nn(att1, c)
        keep_ref[z, qkv:, :] = jnp.where(section == 0, zero, one)
        send_ref[z, qkv:, :] = jnp.where(section == 0, one, zero).astype(BF16)


def merge_kernel(index, keep_ref, come_ref, *out_refs):
    place, count = index[1], len(out_refs)
    out_refs[0][...] = keep_ref[place] + come_ref[place].astype(F32)
    for k in range(1, count):
        at = (place + k) & (count - 1)
        out_refs[k][...] = (keep_ref[at] + come_ref[at].astype(F32)).astype(BF16)


def last_kernel(qkv_rows, keep_ref, *refs):
    parts, (qkv_ref, out_ref) = refs[:-2], refs[-2:]
    total = keep_ref[...]
    for part in parts:
        total = total + part[...].astype(F32)
    qkv_ref[...] = total[:qkv_rows]
    out_ref[...] = total[qkv_rows:]


def far_first(value, count, send):
    of = lambda k: value[k] if isinstance(value, (list, tuple)) else value
    got = {k: send(of(k), k) for k in reversed(range(1, count))}
    return [of(0)] + [got[k] for k in range(1, count)]


def call(kernel, outs, *args, scalars=0, scratch=()):
    smem = pl.BlockSpec(memory_space=pltpu.SMEM)
    vmem = pl.BlockSpec(memory_space=pltpu.VMEM)
    return pl.pallas_call(
        kernel,
        out_shape=[jax.ShapeDtypeStruct(shape, dtype) for shape, dtype in outs],
        in_specs=[smem] * scalars + [vmem] * (len(args) - scalars),
        out_specs=[vmem] * len(outs),
        scratch_shapes=[pltpu.VMEM(shape, dtype) for shape, dtype in scratch],
        compiler_params=pltpu.CompilerParams(vmem_limit_bytes=VMEM_LIMIT),
    )(*args)


def planar(inputs, cotangent, doc_lengths, norm_gain, w_qkv, w_out):
    shards = lax.axis_size("dp")
    planes = shards // PLANE
    section, place = lax.axis_index("section"), lax.axis_index("dp")
    z, p = place // PLANE, place % PLANE
    index = jnp.stack([section, z, p]).astype(jnp.int32)
    block, features = inputs.shape[1:]
    rows = PLANE * block
    heads, width = w_out.shape[1:]
    qkv_rows = w_qkv.shape[2]
    cols = planes * width
    def along_z(value, k):
        route = [(a * PLANE + b, (a ^ k) * PLANE + b) for a in range(planes) for b in range(PLANE)]
        return lax.ppermute(value, "dp", route)

    def round_z(value, k):
        route = [(a * PLANE + b, (a + k) % planes * PLANE + b) for a in range(planes) for b in range(PLANE)]
        return lax.ppermute(value, "dp", route)

    def to_sibling(value):
        return lax.ppermute(value, "section", [(0, 1), (1, 0)])

    def along_plane(value, k):
        route = [(a * PLANE + b, a * PLANE + (b ^ k)) for a in range(planes) for b in range(PLANE)]
        return lax.ppermute(value, "dp", route)

    def exchange(value):
        return far_first(value, PLANE, along_plane)

    smem, vmem = pl.BlockSpec(memory_space=pltpu.SMEM), pl.BlockSpec(memory_space=pltpu.VMEM)
    hbm = pl.BlockSpec(memory_space=pltpu.HBM)
    params = pltpu.CompilerParams(vmem_limit_bytes=VMEM_LIMIT)
    qkv_in, out_in, x_in, c_in = [
        pltpu.with_memory_space_constraint(value, pltpu.HBM)
        for value in (w_qkv[0].T, w_out[0], inputs, cotangent)
    ]
    one_block = jax.ShapeDtypeStruct((2, block, cols), BF16)
    pack, *blocks = pl.pallas_call(
        functools.partial(blocks_kernel, planes),
        out_shape=[jax.ShapeDtypeStruct((qkv_rows + heads, width), BF16)] + [one_block] * (PLANE - 1),
        in_specs=[smem] + [hbm] * 4,
        out_specs=[vmem] * PLANE,
        scratch_shapes=[pltpu.SemaphoreType.DMA((2,)), pltpu.SemaphoreType.DMA((PLANE - 1, 2 * planes))],
        compiler_params=params,
    )(index, qkv_in, out_in, x_in, c_in)
    gain = norm_gain[0].reshape(shards, width)
    blocks = far_first([None] + blocks, PLANE, along_plane)
    pieces = {0: pack}
    for step in reversed([1 << bit for bit in range(planes.bit_length() - 1)]):
        for k in list(pieces):
            pieces[k ^ step] = along_z(pieces[k], step)
    mine, late_gain, _ = lax.optimization_barrier((pack, gain, blocks[3]))
    marked, blocks[0] = pl.pallas_call(
        functools.partial(mark_kernel, planes),
        out_shape=[jax.ShapeDtypeStruct((qkv_rows + heads + shards, width), BF16), one_block],
        in_specs=[smem] + [vmem] * 2 + [hbm] * 2,
        out_specs=[vmem] * 2,
        scratch_shapes=[pltpu.SemaphoreType.DMA((2 * planes,))],
        compiler_params=params,
    )(index, mine, late_gain, x_in, c_in)
    pieces[planes // 2], _ = lax.optimization_barrier((pieces[planes // 2], blocks[3]))
    own = [marked] + [pieces[k] for k in range(1, planes)]
    other = [to_sibling(piece) for piece in own]

    split = ((PLANE, block, cols), BF16)
    half = 2 * heads
    x, c, vx, gains, *sent = call(
        functools.partial(project_kernel, planes, heads),
        [split, split, ((planes, 4 * half, width), BF16), ((planes, 8, width), F32)]
        + [((block, 7 * half), BF16)] * PLANE,
        index, blocks[0], *blocks[:0:-1], *own, *other, scalars=1,
        scratch=[((planes, 2 * half, width), BF16), ((rows, 5 * half), BF16)] + [((shards, width), F32)] * 2,
    )
    (factors,) = call(
        functools.partial(chain_kernel, features, heads),
        [((block, 5 * half), BF16)],
        index, doc_lengths, *exchange(sent)[::-1], scalars=2,
    )
    grads = (planes, qkv_rows + heads, width)
    keep, send = call(
        functools.partial(grads_kernel, planes, heads),
        [(grads, F32), (grads, BF16)],
        index, *exchange(factors), x, c, vx, gains, scalars=1,
        scratch=[((PLANE, block, 5 * half), BF16)],
    )
    merged = call(
        merge_kernel,
        [(grads[1:], F32)] + [(grads[1:], BF16)] * (planes - 1),
        index, keep, to_sibling(send), scalars=1,
    )
    parts = [round_z(merged[k], k) for k in range(1, planes)]
    grad_qkv, grad_out = call(
        functools.partial(last_kernel, qkv_rows),
        [((qkv_rows, width), F32), ((heads, width), F32)],
        merged[0], *parts,
    )
    return (grad_qkv.T[None], grad_out[None])


def solution(mesh):
    sections, shards = mesh.shape["section"], mesh.shape["dp"]
    planes = shards // PLANE

    def body(inputs, *rest):
        fits = shards % PLANE == 0 and planes & (planes - 1) == 0
        if sections == 2 and inputs.shape[0] == 2 and fits:
            return planar(inputs, *rest)
        return pipelined(inputs, *rest)

    return jax.shard_map(
        body,
        mesh=mesh,
        in_specs=(
            P(None, "dp", None),
            P(None, "dp", None),
            P(None, "dp", None),
            P("section", None),
            P("section", "dp", None),
            P("section", None, "dp"),
        ),
        out_specs=(P("section", "dp", None), P("section", None, "dp")),
        check_vma=False,
    )
```

```python
import functools

import jax
import jax.numpy as jnp
from jax import lax
from jax.experimental import pallas as pl
from jax.experimental.pallas import tpu as pltpu
from jax.sharding import PartitionSpec as P

F32 = jnp.float32
BF16 = jnp.bfloat16
PLANE = 4
VMEM_LIMIT = 16 * 1024 * 1024


def passed_along(block, axis, distance):
    devices = range(lax.axis_size(axis))
    route = [(i - distance, i) for i in devices if i - distance in devices]
    return lax.ppermute(block, axis, route)


def segments_of(lengths, count):
    ends = jnp.cumsum(lengths)
    position = jnp.arange(count, dtype=jnp.int32)
    return jnp.sum((position[:, None] >= ends[None, :]).astype(jnp.int32), axis=1)


def layer(x, gain, w_qkv, w_out, seg):
    head = w_out.shape[0]
    x_wide = x.astype(jnp.float32)
    scale = lax.rsqrt(jnp.mean(x_wide * x_wide, axis=-1, keepdims=True) + 1e-05)
    normed = (x_wide * scale * gain.astype(jnp.float32)).astype(jnp.bfloat16)
    qkv = jnp.dot(normed, w_qkv, preferred_element_type=jnp.float32).astype(jnp.bfloat16)
    query = qkv[:, :head]
    keys = qkv[:, head : 2 * head]
    values = qkv[:, 2 * head :]
    scores = jnp.dot(query, keys.T, preferred_element_type=jnp.float32) * head ** (-0.5)
    rows = jnp.arange(x.shape[0], dtype=jnp.int32)
    allowed = (seg[:, None] == seg[None, :]) & (rows[:, None] >= rows[None, :])
    scores = jnp.where(allowed, scores, -1e30)
    probs = jax.nn.softmax(scores, axis=-1).astype(jnp.bfloat16)
    attended = jnp.dot(probs, values, preferred_element_type=jnp.float32).astype(jnp.bfloat16)
    return (x_wide + jnp.dot(attended, w_out, preferred_element_type=jnp.float32)).astype(
        jnp.bfloat16
    )


def pipelined(inputs, cotangent, doc_lengths, norm_gain, w_qkv, w_out):
    sections = lax.axis_size("section")
    section = lax.axis_index("section")
    micro = inputs.shape[0]
    count = inputs.shape[1]
    segs = jax.vmap(lambda lens: segments_of(lens, count))(doc_lengths[:, 0, :])
    gain = norm_gain[0]
    full_qkv, full_out = (
        lax.all_gather(w_qkv[0], "dp", axis=0, tiled=True),
        lax.all_gather(w_out[0], "dp", axis=1, tiled=True),
    )
    total_steps = micro + sections - 1
    empty = jnp.zeros(inputs.shape[1:], inputs.dtype)

    def forward_at(step, incoming, saved):
        index = step - section
        live = (index >= 0) & (index < micro)
        slot = jnp.clip(index, 0, micro - 1)
        first = lax.dynamic_index_in_dim(inputs, slot, 0, keepdims=False)
        x = jnp.where(section == 0, first, incoming)
        seg = lax.dynamic_index_in_dim(segs, slot, 0, keepdims=False)
        out = layer(x, gain, full_qkv, full_out, seg)
        old = lax.dynamic_index_in_dim(saved, slot, 0, keepdims=False)
        saved = lax.dynamic_update_index_in_dim(saved, jnp.where(live, x, old), slot, 0)
        return (out, saved)

    def forward_step(carry, step):
        incoming, saved = carry
        out, saved = forward_at(step, incoming, saved)
        incoming = passed_along(out, "section", 1)
        return ((incoming, saved), None)

    start_saved = jnp.zeros(inputs.shape, inputs.dtype)
    (incoming, saved), _ = lax.scan(
        forward_step, (empty, start_saved), jnp.arange(total_steps - 1, dtype=jnp.int32)
    )
    _, saved = forward_at(jnp.int32(total_steps - 1), incoming, saved)

    def backward_at(step, incoming, sum_qkv, sum_out):
        index = step - (sections - 1 - section)
        live = (index >= 0) & (index < micro)
        slot = jnp.clip(index, 0, micro - 1)
        last = lax.dynamic_index_in_dim(cotangent, slot, 0, keepdims=False)
        grad_y = jnp.where(section == sections - 1, last, incoming)
        x = lax.dynamic_index_in_dim(saved, slot, 0, keepdims=False)
        seg = lax.dynamic_index_in_dim(segs, slot, 0, keepdims=False)
        _, pull = jax.vjp(lambda a, b, c: layer(a, gain, b, c, seg), x, full_qkv, full_out)
        grad_x, grad_q, grad_o = pull(grad_y)
        sum_qkv = sum_qkv + jnp.where(live, grad_q.astype(jnp.float32), 0.0)
        sum_out = sum_out + jnp.where(live, grad_o.astype(jnp.float32), 0.0)
        return (grad_x, sum_qkv, sum_out)

    def backward_step(carry, step):
        incoming, sum_qkv, sum_out = carry
        grad_x, sum_qkv, sum_out = backward_at(step, incoming, sum_qkv, sum_out)
        incoming = passed_along(grad_x, "section", -1)
        return ((incoming, sum_qkv, sum_out), None)

    zero_qkv = jnp.zeros(full_qkv.shape, jnp.float32)
    zero_out = jnp.zeros(full_out.shape, jnp.float32)
    (incoming, sum_qkv, sum_out), _ = lax.scan(
        backward_step, (empty, zero_qkv, zero_out), jnp.arange(total_steps - 1, dtype=jnp.int32)
    )
    _, sum_qkv, sum_out = backward_at(jnp.int32(total_steps - 1), incoming, sum_qkv, sum_out)
    share_qkv, share_out = (
        lax.psum_scatter(sum_qkv, "dp", scatter_dimension=0, tiled=True),
        lax.psum_scatter(sum_out, "dp", scatter_dimension=1, tiled=True),
    )
    return (share_qkv[None], share_out[None])


def nn(a, b):
    return lax.dot_general(a, b, (((1,), (0,)), ((), ())), preferred_element_type=F32)


def nt(a, b):
    return lax.dot_general(a, b, (((1,), (1,)), ((), ())), preferred_element_type=F32)


def block_copies(planes, index, k, refs, out_ref, sems):
    width = refs[0].shape[-1] // (planes * PLANE)
    section, p = index[0], index[2]
    copies = []
    for z in range(planes):
        at = pl.multiple_of((z * PLANE + (p ^ k)) * width, width)
        for half, ref in enumerate(refs):
            copies.append(
                pltpu.make_async_copy(
                    ref.at[section, :, pl.ds(at, width)],
                    out_ref.at[half, :, pl.ds(z * width, width)],
                    sems.at[len(copies)],
                )
            )
    return copies


def mark_kernel(planes, index, pack_ref, gain_ref, x_ref, c_ref, out_ref, block_ref, sems):
    copies = block_copies(planes, index, 0, (x_ref, c_ref), block_ref, sems)
    for copy in copies:
        copy.start()
    out_ref[: pack_ref.shape[0], :] = pack_ref[...]
    out_ref[pack_ref.shape[0] :, :] = gain_ref[...]
    for copy in copies:
        copy.wait()


def first_kernel(planes, index, qkv_ref, wout_ref, x_ref, c_ref, pack_ref, far_ref, pack_sems, sems):
    qkv_rows = qkv_ref.shape[0]
    copies = [
        pltpu.make_async_copy(qkv_ref, pack_ref.at[:qkv_rows], pack_sems.at[0]),
        pltpu.make_async_copy(wout_ref, pack_ref.at[qkv_rows:], pack_sems.at[1]),
    ] + block_copies(planes, index, PLANE - 1, (x_ref, c_ref), far_ref, sems)
    for copy in copies:
        copy.start()
    for copy in copies:
        copy.wait()


def blocks_kernel(planes, index, x_ref, c_ref, *refs):
    out_refs, sems = refs[:-1], refs[-1]
    copies = []
    for k, out_ref in enumerate(out_refs, 1):
        copies += block_copies(planes, index, k, (x_ref, c_ref), out_ref, sems.at[k - 1])
    for copy in copies:
        copy.start()
    for copy in copies:
        copy.wait()


def project_kernel(planes, heads, index, *refs):
    blocks, own, other = refs[:PLANE], refs[PLANE : PLANE + planes], refs[PLANE + planes : PLANE + 2 * planes]
    x_ref, c_ref, vx_ref, gain_ref = refs[PLANE + 2 * planes : PLANE + 2 * planes + 4]
    out_refs = refs[PLANE + 2 * planes + 4 : -4]
    vc_ref, sum_ref, *wide_refs = refs[-4:]
    qkv, width = 3 * heads, vx_ref.shape[-1]
    section, place, p = index[0], index[1], index[2]
    for ref, wide_ref in zip((own[0], other[0]), wide_refs):
        wide_ref[...] = ref[qkv + heads :, :].astype(F32)
    for z in range(planes):
        mine, theirs = (ref[pl.ds(z * PLANE + p, 1), :] for ref in wide_refs)
        gain_ref[z, 0:1, :] = jnp.where(section == 0, mine, theirs)
        gain_ref[z, 1:2, :] = jnp.where(section == 0, theirs, mine)
    for k in range(planes):
        at = place ^ k
        mine, theirs = own[k][: qkv + heads, :], other[k][: qkv + heads, :]
        zero = jnp.where(section == 0, mine, theirs)
        one = jnp.where(section == 0, theirs, mine)
        empty = jnp.zeros((heads, width), BF16)
        vx_ref[at, :qkv, :] = (zero[:qkv].astype(F32) * gain_ref[at, 0:1, :]).astype(BF16)
        vx_ref[at, qkv : qkv + heads, :] = zero[qkv : qkv + heads]
        vx_ref[at, qkv + heads : 2 * qkv + heads, :] = (one[:qkv].astype(F32) * gain_ref[at, 1:2, :]).astype(BF16)
        vx_ref[at, 2 * qkv + heads :, :] = empty
        vc_ref[at, :heads, :] = empty
        vc_ref[at, heads : 2 * heads, :] = one[qkv : qkv + heads]
        vc_ref[at, 2 * heads : 3 * heads, :] = zero[qkv : qkv + heads]
        vc_ref[at, 3 * heads :, :] = empty
    for k in range(PLANE):
        x_ref[p ^ k] = blocks[-k][0]
        c_ref[p ^ k] = blocks[-k][1]
    rows = x_ref.shape[0] * x_ref.shape[1]
    with_x = with_c = squares = products = None
    for z in range(planes):
        cols = slice(z * width, (z + 1) * width)
        x = x_ref[:, :, cols].reshape(rows, width)
        c = c_ref[:, :, cols].reshape(rows, width)
        wide = x.astype(F32)
        out = vx_ref[z, qkv : qkv + heads, :]
        right = jnp.concatenate([vx_ref[z, qkv + heads : 2 * qkv + heads, :], out], axis=0)
        new = nt(x, vx_ref[z]), nt(c, vc_ref[z]), jnp.sum(wide * wide, axis=1, keepdims=True), nt(out, right)
        if with_x is None:
            with_x, with_c, squares, products = new
        else:
            with_x, with_c = with_x + new[0], with_c + new[1]
            squares, products = squares + new[2], products + new[3]
    half = 2 * heads
    lane = lax.broadcasted_iota(jnp.int32, (rows, half), 1)
    high = squares.astype(BF16).astype(F32)
    last = jnp.where(lane == heads, high, jnp.where(lane == heads + 1, squares - high, with_c[:, half:]))
    sum_ref[:, : 3 * half] = with_x[:, : 3 * half].astype(BF16)
    sum_ref[:, 3 * half : 4 * half] = (with_x[:, 3 * half :] + with_c[:, :half]).astype(BF16)
    sum_ref[:, 4 * half :] = last.astype(BF16)
    block = rows // PLANE
    for k in range(PLANE):
        start = pl.multiple_of((p ^ k) * block, block)
        out_refs[k][:, : 5 * half] = sum_ref[pl.ds(start, block), :]
        out_refs[k][:, 5 * half :] = products.astype(BF16)


def attention(qkv, allowed, heads):
    query, keys, values = (qkv[:, i * heads : (i + 1) * heads].astype(BF16) for i in range(3))
    scores = jnp.where(allowed, nt(query, keys) * heads ** (-0.5), -1e30)
    raised = jnp.exp(scores - jnp.max(scores, axis=1, keepdims=True))
    probs = raised / jnp.sum(raised, axis=1, keepdims=True)
    return probs, nn(probs.astype(BF16), values).astype(BF16)


def attention_grad(qkv, probs, att, d_att, heads):
    query, keys, values = (qkv[:, i * heads : (i + 1) * heads].astype(BF16) for i in range(3))
    inner = jnp.sum(att.astype(F32) * d_att.astype(F32), axis=1, keepdims=True)
    d_values = nn(jnp.transpose(probs).astype(BF16), d_att)
    d_scores = probs * (nt(d_att, values) - inner) * heads ** (-0.5)
    d_query = nn(d_scores.astype(BF16), keys)
    d_keys = nn(jnp.transpose(d_scores).astype(BF16), query)
    return jnp.concatenate([d_query, d_keys, d_values], axis=1).astype(BF16).astype(F32)


def summed(parts):
    total = parts[0][...].astype(F32)
    for part in parts[1:]:
        total = total + part[...].astype(F32)
    return total


def chain_kernel(features, heads, index, docs, *refs):
    out_ref = refs[-1]
    qkv, half = 3 * heads, 2 * heads
    total = summed(refs[:-1])
    rows = total.shape[0]
    section = index[0]
    query_at = lax.broadcasted_iota(jnp.int32, (rows, rows), 0)
    key_at = lax.broadcasted_iota(jnp.int32, (rows, rows), 1)
    allowed = query_at >= key_at
    end = 0
    for i in range(docs.shape[2]):
        end = end + docs[section, 0, i]
        allowed = allowed & ((query_at >= end) == (key_at >= end))
    x_out = total[:, qkv : 2 * half]
    x_one = total[:, 2 * half : 2 * half + qkv]
    tail = total[:, 4 * half : 5 * half]
    c_one, c_zero = total[:, 4 * half - heads : 4 * half].astype(BF16), tail[:, :heads]
    lane = lax.broadcasted_iota(jnp.int32, tail.shape, 1)
    squares = jnp.sum(jnp.where((lane == heads) | (lane == heads + 1), tail, 0.0), axis=1, keepdims=True)
    mixed = total[:, 5 * half : 5 * half + qkv].astype(BF16)
    gram = total[:, 5 * half + qkv :].astype(BF16)

    scale0 = lax.rsqrt(squares / features + 1e-05)
    qkv0 = (total[:, :qkv] * scale0).astype(BF16).astype(F32)
    probs0, att0 = attention(qkv0, allowed, heads)
    wide0 = att0.astype(F32)
    y_out = x_out + nn(att0, gram)
    squares = squares + jnp.sum(wide0 * (x_out + y_out), axis=1, keepdims=True)
    scale1 = lax.rsqrt(jnp.maximum(squares, 0.0) / features + 1e-05)
    qkv1 = ((x_one + nn(att0, mixed)) * scale1).astype(BF16).astype(F32)
    probs1, att1 = attention(qkv1, allowed, heads)
    d_qkv1 = attention_grad(qkv1, probs1, att1, c_one, heads)
    inner = jnp.sum(d_qkv1 * qkv1, axis=1, keepdims=True) * scale1 * scale1 / features
    e1 = d_qkv1 * scale1
    d_att0 = c_zero + nt(e1.astype(BF16), mixed) - inner * y_out
    e0 = attention_grad(qkv0, probs0, att0, d_att0.astype(BF16), heads) * scale0
    factors = [e0, wide0, e1, wide0 * inner, att1.astype(F32), jnp.zeros((rows, heads), F32)]
    out_ref[...] = jnp.concatenate(factors, axis=1).astype(BF16)


def grads_kernel(planes, heads, index, *refs):
    factors, (x_ref, c_ref, vx_ref, gain_ref) = refs[:PLANE], refs[PLANE : PLANE + 4]
    keep_ref, send_ref, all_ref = refs[PLANE + 4 :]
    qkv, half, width = 3 * heads, 2 * heads, vx_ref.shape[-1]
    section, p = index[0], index[2]
    for k in range(PLANE):
        all_ref[p ^ k] = factors[k][...]
    rows = x_ref.shape[0] * x_ref.shape[1]
    turned = jnp.transpose(all_ref[...].astype(F32).reshape(rows, 5 * half)).astype(BF16)
    att0, att1 = turned[qkv : qkv + heads], turned[4 * half : 4 * half + heads]
    right = turned[2 * half : 4 * half]
    small = nt(right, att0).astype(BF16)
    small_t = nt(att0, right[:qkv]).astype(BF16)
    for z in range(planes):
        cols = slice(z * width, (z + 1) * width)
        x = x_ref[:, :, cols].reshape(rows, width)
        c = c_ref[:, :, cols].reshape(rows, width)
        out = vx_ref[z, qkv : qkv + heads, :]
        with_x = nn(turned[: 4 * half], x)
        left = with_x[2 * half :] + nn(small, out)
        zero = with_x[:qkv] * gain_ref[z, 0:1, :]
        one = left[:qkv] * gain_ref[z, 1:2, :]
        keep_ref[z, :qkv, :] = jnp.where(section == 0, zero, one)
        send_ref[z, :qkv, :] = jnp.where(section == 0, one, zero).astype(BF16)
        zero = nn(att0, c) + nn(small_t, vx_ref[z, qkv + heads : 2 * qkv + heads, :]) - left[qkv:]
        one = nn(att1, c)
        keep_ref[z, qkv:, :] = jnp.where(section == 0, zero, one)
        send_ref[z, qkv:, :] = jnp.where(section == 0, one, zero).astype(BF16)


def merge_kernel(index, keep_ref, come_ref, *out_refs):
    place = index[1]
    out_refs[0][...] = keep_ref[place] + come_ref[place].astype(F32)
    for k in range(1, len(out_refs)):
        out_refs[k][...] = (keep_ref[place ^ k] + come_ref[place ^ k].astype(F32)).astype(BF16)


def add_kernel(a_ref, b_ref, out_ref):
    out_ref[...] = (a_ref[...].astype(F32) + b_ref[...].astype(F32)).astype(BF16)


def last_kernel(qkv_rows, keep_ref, *refs):
    parts, (qkv_ref, out_ref) = refs[:-2], refs[-2:]
    total = keep_ref[...]
    for part in parts:
        total = total + part[...].astype(F32)
    qkv_ref[...] = total[:qkv_rows]
    out_ref[...] = total[qkv_rows:]


def far_first(value, count, send):
    of = lambda k: value[k] if isinstance(value, (list, tuple)) else value
    got = {k: send(of(k), k) for k in reversed(range(1, count))}
    return [of(0)] + [got[k] for k in range(1, count)]


def call(kernel, outs, *args, scalars=0, scratch=()):
    smem = pl.BlockSpec(memory_space=pltpu.SMEM)
    vmem = pl.BlockSpec(memory_space=pltpu.VMEM)
    return pl.pallas_call(
        kernel,
        out_shape=[jax.ShapeDtypeStruct(shape, dtype) for shape, dtype in outs],
        in_specs=[smem] * scalars + [vmem] * (len(args) - scalars),
        out_specs=[vmem] * len(outs),
        scratch_shapes=[pltpu.VMEM(shape, dtype) for shape, dtype in scratch],
        compiler_params=pltpu.CompilerParams(vmem_limit_bytes=VMEM_LIMIT),
    )(*args)


def planar(inputs, cotangent, doc_lengths, norm_gain, w_qkv, w_out):
    shards = lax.axis_size("dp")
    planes = shards // PLANE
    section, place = lax.axis_index("section"), lax.axis_index("dp")
    z, p = place // PLANE, place % PLANE
    index = jnp.stack([section, z, p]).astype(jnp.int32)
    block, features = inputs.shape[1:]
    rows = PLANE * block
    heads, width = w_out.shape[1:]
    qkv_rows = w_qkv.shape[2]
    cols = planes * width
    def along_z(value, k):
        route = [(a * PLANE + b, (a ^ k) * PLANE + b) for a in range(planes) for b in range(PLANE)]
        return lax.ppermute(value, "dp", route)

    def to_sibling(value):
        return lax.ppermute(value, "section", [(0, 1), (1, 0)])

    def along_plane(value, k):
        route = [(a * PLANE + b, a * PLANE + (b ^ k)) for a in range(planes) for b in range(PLANE)]
        return lax.ppermute(value, "dp", route)

    def exchange(value):
        return far_first(value, PLANE, along_plane)

    smem, vmem = pl.BlockSpec(memory_space=pltpu.SMEM), pl.BlockSpec(memory_space=pltpu.VMEM)
    hbm = pl.BlockSpec(memory_space=pltpu.HBM)
    params = pltpu.CompilerParams(vmem_limit_bytes=VMEM_LIMIT)
    qkv_in, out_in, x_in, c_in = [
        pltpu.with_memory_space_constraint(value, pltpu.HBM)
        for value in (w_qkv[0].T, w_out[0], inputs, cotangent)
    ]
    one_block = jax.ShapeDtypeStruct((2, block, cols), BF16)
    pack, far_block = pl.pallas_call(
        functools.partial(first_kernel, planes),
        out_shape=[jax.ShapeDtypeStruct((qkv_rows + heads, width), BF16), one_block],
        in_specs=[smem] + [hbm] * 4,
        out_specs=[vmem] * 2,
        scratch_shapes=[pltpu.SemaphoreType.DMA((2,)), pltpu.SemaphoreType.DMA((2 * planes,))],
        compiler_params=params,
    )(index, qkv_in, out_in, x_in, c_in)
    blocks = pl.pallas_call(
        functools.partial(blocks_kernel, planes),
        out_shape=[one_block] * (PLANE - 2),
        in_specs=[smem] + [hbm] * 2,
        out_specs=[vmem] * (PLANE - 2),
        scratch_shapes=[pltpu.SemaphoreType.DMA((PLANE - 2, 2 * planes))],
        compiler_params=params,
    )(index, x_in, c_in)
    blocks = [*blocks, far_block]
    gain = norm_gain[0].reshape(shards, width)
    blocks = far_first([None] + blocks, PLANE, along_plane)
    pieces = {0: pack}
    for step in reversed([1 << bit for bit in range(planes.bit_length() - 1)]):
        for k in list(pieces):
            pieces[k ^ step] = along_z(pieces[k], step)
    mine, late_gain, _ = lax.optimization_barrier((pack, gain, blocks[3]))
    marked, blocks[0] = pl.pallas_call(
        functools.partial(mark_kernel, planes),
        out_shape=[jax.ShapeDtypeStruct((qkv_rows + heads + shards, width), BF16), one_block],
        in_specs=[smem] + [vmem] * 2 + [hbm] * 2,
        out_specs=[vmem] * 2,
        scratch_shapes=[pltpu.SemaphoreType.DMA((2 * planes,))],
        compiler_params=params,
    )(index, mine, late_gain, x_in, c_in)
    pieces[planes // 2], _ = lax.optimization_barrier((pieces[planes // 2], blocks[3]))
    own = [marked] + [pieces[k] for k in range(1, planes)]
    other = [to_sibling(piece) for piece in own]

    split = ((PLANE, block, cols), BF16)
    half = 2 * heads
    x, c, vx, gains, *sent = call(
        functools.partial(project_kernel, planes, heads),
        [split, split, ((planes, 4 * half, width), BF16), ((planes, 8, width), F32)]
        + [((block, 7 * half), BF16)] * PLANE,
        index, blocks[0], *blocks[:0:-1], *own, *other, scalars=1,
        scratch=[((planes, 2 * half, width), BF16), ((rows, 5 * half), BF16)] + [((shards, width), F32)] * 2,
    )
    (factors,) = call(
        functools.partial(chain_kernel, features, heads),
        [((block, 5 * half), BF16)],
        index, doc_lengths, *exchange(sent)[::-1], scalars=2,
    )
    grads = (planes, qkv_rows + heads, width)
    keep, send = call(
        functools.partial(grads_kernel, planes, heads),
        [(grads, F32), (grads, BF16)],
        index, *exchange(factors), x, c, vx, gains, scalars=1,
        scratch=[((PLANE, block, 5 * half), BF16)],
    )
    merged = call(
        merge_kernel,
        [(grads[1:], F32)] + [(grads[1:], BF16)] * (planes - 1),
        index, keep, to_sibling(send), scalars=1,
    )
    pieces, parts = dict(enumerate(merged)), []
    for step in [1 << bit for bit in range(planes.bit_length() - 1)]:
        got = {k ^ step: along_z(pieces.pop(k), step) for k in sorted(pieces, reverse=True) if k & step}
        parts.append(got.pop(0))
        for k, part in got.items():
            (pieces[k],) = call(add_kernel, [(grads[1:], BF16)], pieces[k], part)
    grad_qkv, grad_out = call(
        functools.partial(last_kernel, qkv_rows),
        [((qkv_rows, width), F32), ((heads, width), F32)],
        merged[0], *parts,
    )
    return (grad_qkv.T[None], grad_out[None])


def solution(mesh):
    sections, shards = mesh.shape["section"], mesh.shape["dp"]
    planes = shards // PLANE

    def body(inputs, *rest):
        fits = shards % PLANE == 0 and planes & (planes - 1) == 0
        if sections == 2 and inputs.shape[0] == 2 and fits:
            return planar(inputs, *rest)
        return pipelined(inputs, *rest)

    return jax.shard_map(
        body,
        mesh=mesh,
        in_specs=(
            P(None, "dp", None),
            P(None, "dp", None),
            P(None, "dp", None),
            P("section", None),
            P("section", "dp", None),
            P("section", None, "dp"),
        ),
        out_specs=(P("section", "dp", None), P("section", None, "dp")),
        check_vma=False,
    )
```

```python
import functools

import jax
import jax.numpy as jnp
from jax import lax
from jax.experimental import pallas as pl
from jax.experimental.pallas import tpu as pltpu
from jax.sharding import PartitionSpec as P

F32 = jnp.float32
BF16 = jnp.bfloat16
PLANE = 4
VMEM_LIMIT = 16 * 1024 * 1024


def passed_along(block, axis, distance):
    devices = range(lax.axis_size(axis))
    route = [(i - distance, i) for i in devices if i - distance in devices]
    return lax.ppermute(block, axis, route)


def segments_of(lengths, count):
    ends = jnp.cumsum(lengths)
    position = jnp.arange(count, dtype=jnp.int32)
    return jnp.sum((position[:, None] >= ends[None, :]).astype(jnp.int32), axis=1)


def layer(x, gain, w_qkv, w_out, seg):
    head = w_out.shape[0]
    x_wide = x.astype(jnp.float32)
    scale = lax.rsqrt(jnp.mean(x_wide * x_wide, axis=-1, keepdims=True) + 1e-05)
    normed = (x_wide * scale * gain.astype(jnp.float32)).astype(jnp.bfloat16)
    qkv = jnp.dot(normed, w_qkv, preferred_element_type=jnp.float32).astype(jnp.bfloat16)
    query = qkv[:, :head]
    keys = qkv[:, head : 2 * head]
    values = qkv[:, 2 * head :]
    scores = jnp.dot(query, keys.T, preferred_element_type=jnp.float32) * head ** (-0.5)
    rows = jnp.arange(x.shape[0], dtype=jnp.int32)
    allowed = (seg[:, None] == seg[None, :]) & (rows[:, None] >= rows[None, :])
    scores = jnp.where(allowed, scores, -1e30)
    probs = jax.nn.softmax(scores, axis=-1).astype(jnp.bfloat16)
    attended = jnp.dot(probs, values, preferred_element_type=jnp.float32).astype(jnp.bfloat16)
    return (x_wide + jnp.dot(attended, w_out, preferred_element_type=jnp.float32)).astype(
        jnp.bfloat16
    )


def pipelined(inputs, cotangent, doc_lengths, norm_gain, w_qkv, w_out):
    sections = lax.axis_size("section")
    section = lax.axis_index("section")
    micro = inputs.shape[0]
    count = inputs.shape[1]
    segs = jax.vmap(lambda lens: segments_of(lens, count))(doc_lengths[:, 0, :])
    gain = norm_gain[0]
    full_qkv, full_out = (
        lax.all_gather(w_qkv[0], "dp", axis=0, tiled=True),
        lax.all_gather(w_out[0], "dp", axis=1, tiled=True),
    )
    total_steps = micro + sections - 1
    empty = jnp.zeros(inputs.shape[1:], inputs.dtype)

    def forward_at(step, incoming, saved):
        index = step - section
        live = (index >= 0) & (index < micro)
        slot = jnp.clip(index, 0, micro - 1)
        first = lax.dynamic_index_in_dim(inputs, slot, 0, keepdims=False)
        x = jnp.where(section == 0, first, incoming)
        seg = lax.dynamic_index_in_dim(segs, slot, 0, keepdims=False)
        out = layer(x, gain, full_qkv, full_out, seg)
        old = lax.dynamic_index_in_dim(saved, slot, 0, keepdims=False)
        saved = lax.dynamic_update_index_in_dim(saved, jnp.where(live, x, old), slot, 0)
        return (out, saved)

    def forward_step(carry, step):
        incoming, saved = carry
        out, saved = forward_at(step, incoming, saved)
        incoming = passed_along(out, "section", 1)
        return ((incoming, saved), None)

    start_saved = jnp.zeros(inputs.shape, inputs.dtype)
    (incoming, saved), _ = lax.scan(
        forward_step, (empty, start_saved), jnp.arange(total_steps - 1, dtype=jnp.int32)
    )
    _, saved = forward_at(jnp.int32(total_steps - 1), incoming, saved)

    def backward_at(step, incoming, sum_qkv, sum_out):
        index = step - (sections - 1 - section)
        live = (index >= 0) & (index < micro)
        slot = jnp.clip(index, 0, micro - 1)
        last = lax.dynamic_index_in_dim(cotangent, slot, 0, keepdims=False)
        grad_y = jnp.where(section == sections - 1, last, incoming)
        x = lax.dynamic_index_in_dim(saved, slot, 0, keepdims=False)
        seg = lax.dynamic_index_in_dim(segs, slot, 0, keepdims=False)
        _, pull = jax.vjp(lambda a, b, c: layer(a, gain, b, c, seg), x, full_qkv, full_out)
        grad_x, grad_q, grad_o = pull(grad_y)
        sum_qkv = sum_qkv + jnp.where(live, grad_q.astype(jnp.float32), 0.0)
        sum_out = sum_out + jnp.where(live, grad_o.astype(jnp.float32), 0.0)
        return (grad_x, sum_qkv, sum_out)

    def backward_step(carry, step):
        incoming, sum_qkv, sum_out = carry
        grad_x, sum_qkv, sum_out = backward_at(step, incoming, sum_qkv, sum_out)
        incoming = passed_along(grad_x, "section", -1)
        return ((incoming, sum_qkv, sum_out), None)

    zero_qkv = jnp.zeros(full_qkv.shape, jnp.float32)
    zero_out = jnp.zeros(full_out.shape, jnp.float32)
    (incoming, sum_qkv, sum_out), _ = lax.scan(
        backward_step, (empty, zero_qkv, zero_out), jnp.arange(total_steps - 1, dtype=jnp.int32)
    )
    _, sum_qkv, sum_out = backward_at(jnp.int32(total_steps - 1), incoming, sum_qkv, sum_out)
    share_qkv, share_out = (
        lax.psum_scatter(sum_qkv, "dp", scatter_dimension=0, tiled=True),
        lax.psum_scatter(sum_out, "dp", scatter_dimension=1, tiled=True),
    )
    return (share_qkv[None], share_out[None])


def nn(a, b):
    return lax.dot_general(a, b, (((1,), (0,)), ((), ())), preferred_element_type=F32)


def nt(a, b):
    return lax.dot_general(a, b, (((1,), (1,)), ((), ())), preferred_element_type=F32)


def block_copies(planes, index, k, refs, out_ref, sems):
    width = refs[0].shape[-1] // (planes * PLANE)
    section, p = index[0], index[2]
    copies = []
    for z in range(planes):
        at = pl.multiple_of((z * PLANE + (p ^ k)) * width, width)
        for half, ref in enumerate(refs):
            copies.append(
                pltpu.make_async_copy(
                    ref.at[section, :, pl.ds(at, width)],
                    out_ref.at[half, :, pl.ds(z * width, width)],
                    sems.at[len(copies)],
                )
            )
    return copies


def mark_kernel(planes, index, pack_ref, gain_ref, x_ref, c_ref, out_ref, block_ref, sems):
    copies = block_copies(planes, index, 0, (x_ref, c_ref), block_ref, sems)
    for copy in copies:
        copy.start()
    out_ref[: pack_ref.shape[0], :] = pack_ref[...]
    out_ref[pack_ref.shape[0] :, :] = gain_ref[...]
    for copy in copies:
        copy.wait()


def first_kernel(planes, index, qkv_ref, wout_ref, x_ref, c_ref, pack_ref, far_ref, pack_sems, sems):
    qkv_rows = qkv_ref.shape[0]
    copies = [
        pltpu.make_async_copy(qkv_ref, pack_ref.at[:qkv_rows], pack_sems.at[0]),
        pltpu.make_async_copy(wout_ref, pack_ref.at[qkv_rows:], pack_sems.at[1]),
    ] + block_copies(planes, index, PLANE - 1, (x_ref, c_ref), far_ref, sems)
    for copy in copies:
        copy.start()
    for copy in copies:
        copy.wait()


def blocks_kernel(planes, index, x_ref, c_ref, *refs):
    out_refs, sems = refs[:-1], refs[-1]
    copies = []
    for k, out_ref in enumerate(out_refs, 1):
        copies += block_copies(planes, index, k, (x_ref, c_ref), out_ref, sems.at[k - 1])
    for copy in copies:
        copy.start()
    for copy in copies:
        copy.wait()


def project_kernel(planes, heads, index, *refs):
    blocks, own, other = refs[:PLANE], refs[PLANE : PLANE + planes], refs[PLANE + planes : PLANE + 2 * planes]
    x_ref, c_ref, vx_ref, gain_ref = refs[PLANE + 2 * planes : PLANE + 2 * planes + 4]
    out_refs = refs[PLANE + 2 * planes + 4 : -4]
    vc_ref, sum_ref, *wide_refs = refs[-4:]
    qkv, width = 3 * heads, vx_ref.shape[-1]
    section, place, p = index[0], index[1], index[2]
    for ref, wide_ref in zip((own[0], other[0]), wide_refs):
        wide_ref[...] = ref[qkv + heads :, :].astype(F32)
    for z in range(planes):
        mine, theirs = (ref[pl.ds(z * PLANE + p, 1), :] for ref in wide_refs)
        gain_ref[z, 0:1, :] = jnp.where(section == 0, mine, theirs)
        gain_ref[z, 1:2, :] = jnp.where(section == 0, theirs, mine)
    for k in range(planes):
        at = place ^ k
        mine, theirs = own[k][: qkv + heads, :], other[k][: qkv + heads, :]
        zero = jnp.where(section == 0, mine, theirs)
        one = jnp.where(section == 0, theirs, mine)
        empty = jnp.zeros((heads, width), BF16)
        vx_ref[at, :qkv, :] = (zero[:qkv].astype(F32) * gain_ref[at, 0:1, :]).astype(BF16)
        vx_ref[at, qkv : qkv + heads, :] = zero[qkv : qkv + heads]
        vx_ref[at, qkv + heads : 2 * qkv + heads, :] = (one[:qkv].astype(F32) * gain_ref[at, 1:2, :]).astype(BF16)
        vx_ref[at, 2 * qkv + heads :, :] = empty
        vc_ref[at, :heads, :] = empty
        vc_ref[at, heads : 2 * heads, :] = one[qkv : qkv + heads]
        vc_ref[at, 2 * heads : 3 * heads, :] = zero[qkv : qkv + heads]
        vc_ref[at, 3 * heads :, :] = empty
    for k in range(PLANE):
        x_ref[p ^ k] = blocks[-k][0]
        c_ref[p ^ k] = blocks[-k][1]
    rows = x_ref.shape[0] * x_ref.shape[1]
    with_x = with_c = squares = products = None
    for z in range(planes):
        cols = slice(z * width, (z + 1) * width)
        x = x_ref[:, :, cols].reshape(rows, width)
        c = c_ref[:, :, cols].reshape(rows, width)
        wide = x.astype(F32)
        out = vx_ref[z, qkv : qkv + heads, :]
        right = jnp.concatenate([vx_ref[z, qkv + heads : 2 * qkv + heads, :], out], axis=0)
        new = nt(x, vx_ref[z]), nt(c, vc_ref[z]), jnp.sum(wide * wide, axis=1, keepdims=True), nt(out, right)
        if with_x is None:
            with_x, with_c, squares, products = new
        else:
            with_x, with_c = with_x + new[0], with_c + new[1]
            squares, products = squares + new[2], products + new[3]
    half = 2 * heads
    lane = lax.broadcasted_iota(jnp.int32, (rows, half), 1)
    high = squares.astype(BF16).astype(F32)
    last = jnp.where(lane == heads, high, jnp.where(lane == heads + 1, squares - high, with_c[:, half:]))
    sum_ref[:, : 3 * half] = with_x[:, : 3 * half].astype(BF16)
    sum_ref[:, 3 * half : 4 * half] = (with_x[:, 3 * half :] + with_c[:, :half]).astype(BF16)
    sum_ref[:, 4 * half :] = last.astype(BF16)
    block = rows // PLANE
    for k in range(PLANE):
        start = pl.multiple_of((p ^ k) * block, block)
        out_refs[k][:, : 5 * half] = sum_ref[pl.ds(start, block), :]
        out_refs[k][:, 5 * half :] = products.astype(BF16)


def attention(qkv, allowed, heads):
    query, keys, values = (qkv[:, i * heads : (i + 1) * heads].astype(BF16) for i in range(3))
    scores = jnp.where(allowed, nt(query, keys) * heads ** (-0.5), -1e30)
    raised = jnp.exp(scores - jnp.max(scores, axis=1, keepdims=True))
    scale = 1.0 / jnp.sum(raised, axis=1, keepdims=True)
    return raised * scale, (nn(raised.astype(BF16), values) * scale).astype(BF16)


def attention_grad(qkv, probs, att, d_att, heads):
    query, keys, values = (qkv[:, i * heads : (i + 1) * heads].astype(BF16) for i in range(3))
    inner = jnp.sum(att.astype(F32) * d_att.astype(F32), axis=1, keepdims=True)
    d_values = nn(jnp.transpose(probs).astype(BF16), d_att)
    d_scores = probs * (nt(d_att, values) - inner) * heads ** (-0.5)
    d_query = nn(d_scores.astype(BF16), keys)
    d_keys = nn(jnp.transpose(d_scores).astype(BF16), query)
    return jnp.concatenate([d_query, d_keys, d_values], axis=1).astype(BF16).astype(F32)


def summed(parts):
    total = parts[0][...].astype(F32)
    for part in parts[1:]:
        total = total + part[...].astype(F32)
    return total


def chain_kernel(features, heads, index, docs, *refs):
    out_ref = refs[-1]
    qkv, half = 3 * heads, 2 * heads
    total = summed(refs[:-1])
    rows = total.shape[0]
    section = index[0]
    query_at = lax.broadcasted_iota(jnp.int32, (rows, rows), 0)
    key_at = lax.broadcasted_iota(jnp.int32, (rows, rows), 1)
    allowed = query_at >= key_at
    end = 0
    for i in range(docs.shape[2]):
        end = end + docs[section, 0, i]
        allowed = allowed & ((query_at >= end) == (key_at >= end))
    x_out = total[:, qkv : 2 * half]
    x_one = total[:, 2 * half : 2 * half + qkv]
    tail = total[:, 4 * half : 5 * half]
    c_one, c_zero = total[:, 4 * half - heads : 4 * half].astype(BF16), tail[:, :heads]
    lane = lax.broadcasted_iota(jnp.int32, tail.shape, 1)
    squares = jnp.sum(jnp.where((lane == heads) | (lane == heads + 1), tail, 0.0), axis=1, keepdims=True)
    mixed = total[:, 5 * half : 5 * half + qkv].astype(BF16)
    gram = total[:, 5 * half + qkv :].astype(BF16)

    scale0 = lax.rsqrt(squares / features + 1e-05)
    qkv0 = (total[:, :qkv] * scale0).astype(BF16).astype(F32)
    probs0, att0 = attention(qkv0, allowed, heads)
    wide0 = att0.astype(F32)
    y_out = x_out + nn(att0, gram)
    squares = squares + jnp.sum(wide0 * (x_out + y_out), axis=1, keepdims=True)
    scale1 = lax.rsqrt(jnp.maximum(squares, 0.0) / features + 1e-05)
    qkv1 = ((x_one + nn(att0, mixed)) * scale1).astype(BF16).astype(F32)
    probs1, att1 = attention(qkv1, allowed, heads)
    d_qkv1 = attention_grad(qkv1, probs1, att1, c_one, heads)
    inner = jnp.sum(d_qkv1 * qkv1, axis=1, keepdims=True) * scale1 * scale1 / features
    e1 = d_qkv1 * scale1
    d_att0 = c_zero + nt(e1.astype(BF16), mixed) - inner * y_out
    e0 = attention_grad(qkv0, probs0, att0, d_att0.astype(BF16), heads) * scale0
    factors = [e0, wide0, e1, wide0 * inner, att1.astype(F32), jnp.zeros((rows, heads), F32)]
    out_ref[...] = jnp.concatenate(factors, axis=1).astype(BF16)


def pieces_of(planes, heads, order, index, turned, small, small_t, x_ref, c_ref, vx_ref, gain_ref, keep_ref, send_ref):
    qkv, half, width = 3 * heads, 2 * heads, vx_ref.shape[-1]
    section, place = index[0], index[1]
    rows = x_ref.shape[0] * x_ref.shape[1]
    att0, att1 = turned[qkv : qkv + heads], turned[4 * half : 4 * half + heads]
    for i, k in enumerate(order):
        z = place ^ k
        cols = pl.ds(pl.multiple_of(z * width, width), width)
        x = x_ref[:, :, cols].reshape(rows, width)
        c = c_ref[:, :, cols].reshape(rows, width)
        out = vx_ref[z, qkv : qkv + heads, :]
        with_x = nn(turned[: 4 * half], x)
        left = with_x[2 * half :] + nn(small, out)
        zero = with_x[:qkv] * gain_ref[z, 0:1, :]
        one = left[:qkv] * gain_ref[z, 1:2, :]
        keep_ref[i, :qkv, :] = jnp.where(section == 0, zero, one)
        send_ref[i, :qkv, :] = jnp.where(section == 0, one, zero).astype(BF16)
        zero = nn(att0, c) + nn(small_t, vx_ref[z, qkv + heads : 2 * qkv + heads, :]) - left[qkv:]
        one = nn(att1, c)
        keep_ref[i, qkv:, :] = jnp.where(section == 0, zero, one)
        send_ref[i, qkv:, :] = jnp.where(section == 0, one, zero).astype(BF16)


def far_grads_kernel(planes, heads, order, index, *refs):
    factors, arrays = refs[:PLANE], refs[PLANE : PLANE + 4]
    keep_ref, send_ref, turned_ref, small_ref, small_t_ref, all_ref = refs[PLANE + 4 :]
    qkv, half = 3 * heads, 2 * heads
    p = index[2]
    for k in range(PLANE):
        all_ref[p ^ k] = factors[k][...]
    rows = all_ref.shape[0] * all_ref.shape[1]
    turned = jnp.transpose(all_ref[...].astype(F32).reshape(rows, 5 * half)).astype(BF16)
    att0, right = turned[qkv : qkv + heads], turned[2 * half : 4 * half]
    small = nt(right, att0).astype(BF16)
    small_t = nt(att0, right[:qkv]).astype(BF16)
    turned_ref[...] = turned
    small_ref[...] = small
    small_t_ref[...] = small_t
    pieces_of(planes, heads, order, index, turned, small, small_t, *arrays, keep_ref, send_ref)


def near_grads_kernel(planes, heads, order, index, turned_ref, small_ref, small_t_ref, *refs):
    pieces_of(planes, heads, order, index, turned_ref[...], small_ref[...], small_t_ref[...], *refs)


def merge_kernel(keep_ref, come_ref, *out_refs):
    for i, out_ref in enumerate(out_refs):
        out_ref[...] = (keep_ref[i] + come_ref[i].astype(F32)).astype(out_ref.dtype)


def add_kernel(a_ref, b_ref, out_ref):
    out_ref[...] = (a_ref[...].astype(F32) + b_ref[...].astype(F32)).astype(BF16)


def last_kernel(qkv_rows, keep_ref, *refs):
    parts, (qkv_ref, out_ref) = refs[:-2], refs[-2:]
    total = keep_ref[...]
    for part in parts:
        total = total + part[...].astype(F32)
    qkv_ref[...] = total[:qkv_rows]
    out_ref[...] = total[qkv_rows:]


def far_first(value, count, send):
    of = lambda k: value[k] if isinstance(value, (list, tuple)) else value
    got = {k: send(of(k), k) for k in reversed(range(1, count))}
    return [of(0)] + [got[k] for k in range(1, count)]


def call(kernel, outs, *args, scalars=0, scratch=()):
    smem = pl.BlockSpec(memory_space=pltpu.SMEM)
    vmem = pl.BlockSpec(memory_space=pltpu.VMEM)
    return pl.pallas_call(
        kernel,
        out_shape=[jax.ShapeDtypeStruct(shape, dtype) for shape, dtype in outs],
        in_specs=[smem] * scalars + [vmem] * (len(args) - scalars),
        out_specs=[vmem] * len(outs),
        scratch_shapes=[pltpu.VMEM(shape, dtype) for shape, dtype in scratch],
        compiler_params=pltpu.CompilerParams(vmem_limit_bytes=VMEM_LIMIT),
    )(*args)


def planar(inputs, cotangent, doc_lengths, norm_gain, w_qkv, w_out):
    shards = lax.axis_size("dp")
    planes = shards // PLANE
    section, place = lax.axis_index("section"), lax.axis_index("dp")
    z, p = place // PLANE, place % PLANE
    index = jnp.stack([section, z, p]).astype(jnp.int32)
    block, features = inputs.shape[1:]
    rows = PLANE * block
    heads, width = w_out.shape[1:]
    qkv_rows = w_qkv.shape[2]
    cols = planes * width
    def along_z(value, k):
        route = [(a * PLANE + b, (a ^ k) * PLANE + b) for a in range(planes) for b in range(PLANE)]
        return lax.ppermute(value, "dp", route)

    def to_sibling(value):
        return lax.ppermute(value, "section", [(0, 1), (1, 0)])

    def along_plane(value, k):
        route = [(a * PLANE + b, a * PLANE + (b ^ k)) for a in range(planes) for b in range(PLANE)]
        return lax.ppermute(value, "dp", route)

    def exchange(value):
        return far_first(value, PLANE, along_plane)

    smem, vmem = pl.BlockSpec(memory_space=pltpu.SMEM), pl.BlockSpec(memory_space=pltpu.VMEM)
    hbm = pl.BlockSpec(memory_space=pltpu.HBM)
    params = pltpu.CompilerParams(vmem_limit_bytes=VMEM_LIMIT)
    qkv_in, out_in, x_in, c_in = [
        pltpu.with_memory_space_constraint(value, pltpu.HBM)
        for value in (w_qkv[0].T, w_out[0], inputs, cotangent)
    ]
    one_block = jax.ShapeDtypeStruct((2, block, cols), BF16)
    pack, far_block = pl.pallas_call(
        functools.partial(first_kernel, planes),
        out_shape=[jax.ShapeDtypeStruct((qkv_rows + heads, width), BF16), one_block],
        in_specs=[smem] + [hbm] * 4,
        out_specs=[vmem] * 2,
        scratch_shapes=[pltpu.SemaphoreType.DMA((2,)), pltpu.SemaphoreType.DMA((2 * planes,))],
        compiler_params=params,
    )(index, qkv_in, out_in, x_in, c_in)
    blocks = pl.pallas_call(
        functools.partial(blocks_kernel, planes),
        out_shape=[one_block] * (PLANE - 2),
        in_specs=[smem] + [hbm] * 2,
        out_specs=[vmem] * (PLANE - 2),
        scratch_shapes=[pltpu.SemaphoreType.DMA((PLANE - 2, 2 * planes))],
        compiler_params=params,
    )(index, x_in, c_in)
    blocks = [*blocks, far_block]
    gain = norm_gain[0].reshape(shards, width)
    blocks = far_first([None] + blocks, PLANE, along_plane)
    pieces = {0: pack}
    for step in reversed([1 << bit for bit in range(planes.bit_length() - 1)]):
        for k in list(pieces):
            pieces[k ^ step] = along_z(pieces[k], step)
    mine, late_gain, _ = lax.optimization_barrier((pack, gain, blocks[3]))
    marked, blocks[0] = pl.pallas_call(
        functools.partial(mark_kernel, planes),
        out_shape=[jax.ShapeDtypeStruct((qkv_rows + heads + shards, width), BF16), one_block],
        in_specs=[smem] + [vmem] * 2 + [hbm] * 2,
        out_specs=[vmem] * 2,
        scratch_shapes=[pltpu.SemaphoreType.DMA((2 * planes,))],
        compiler_params=params,
    )(index, mine, late_gain, x_in, c_in)
    pieces[planes // 2], _ = lax.optimization_barrier((pieces[planes // 2], blocks[3]))
    own = [marked] + [pieces[k] for k in range(1, planes)]
    other = [to_sibling(piece) for piece in own]

    split = ((PLANE, block, cols), BF16)
    half = 2 * heads
    x, c, vx, gains, *sent = call(
        functools.partial(project_kernel, planes, heads),
        [split, split, ((planes, 4 * half, width), BF16), ((planes, 8, width), F32)]
        + [((block, 7 * half), BF16)] * PLANE,
        index, blocks[0], *blocks[:0:-1], *own, *other, scalars=1,
        scratch=[((planes, 2 * half, width), BF16), ((rows, 5 * half), BF16)] + [((shards, width), F32)] * 2,
    )
    (factors,) = call(
        functools.partial(chain_kernel, features, heads),
        [((block, 5 * half), BF16)],
        index, doc_lengths, *exchange(sent)[::-1], scalars=2,
    )
    piece = (qkv_rows + heads, width)
    far_order = tuple(reversed(range(planes - planes // 2, planes)))
    near_order = tuple(reversed(range(planes - planes // 2)))

    def swap_and_merge(order, keep, send):
        outs = [(piece, BF16 if k else F32) for k in order]
        return zip(order, call(merge_kernel, outs, keep, to_sibling(send)))

    keep, send, turned, small, small_t = call(
        functools.partial(far_grads_kernel, planes, heads, far_order),
        [((len(far_order),) + piece, F32), ((len(far_order),) + piece, BF16)]
        + [((5 * half, rows), BF16), ((2 * half, heads), BF16), ((heads, qkv_rows), BF16)],
        index, *exchange(factors), x, c, vx, gains, scalars=1,
        scratch=[((PLANE, block, 5 * half), BF16)],
    )
    pieces = dict(swap_and_merge(far_order, keep, send))
    keep, send = call(
        functools.partial(near_grads_kernel, planes, heads, near_order),
        [((len(near_order),) + piece, F32), ((len(near_order),) + piece, BF16)],
        index, turned, small, small_t, x, c, vx, gains, scalars=1,
    )
    pieces.update(swap_and_merge(near_order, keep, send))
    kept, parts = pieces[0], []
    for step in [1 << bit for bit in range(planes.bit_length() - 1)]:
        got = {k ^ step: along_z(pieces.pop(k), step) for k in sorted(pieces, reverse=True) if k & step}
        parts.append(got.pop(0))
        for k, part in got.items():
            (pieces[k],) = call(add_kernel, [(piece, BF16)], pieces[k], part)
    grad_qkv, grad_out = call(
        functools.partial(last_kernel, qkv_rows),
        [((qkv_rows, width), F32), ((heads, width), F32)],
        kept, *parts,
    )
    return (grad_qkv.T[None], grad_out[None])


def solution(mesh):
    sections, shards = mesh.shape["section"], mesh.shape["dp"]
    planes = shards // PLANE

    def body(inputs, *rest):
        fits = shards % PLANE == 0 and planes & (planes - 1) == 0
        if sections == 2 and inputs.shape[0] == 2 and fits:
            return planar(inputs, *rest)
        return pipelined(inputs, *rest)

    return jax.shard_map(
        body,
        mesh=mesh,
        in_specs=(
            P(None, "dp", None),
            P(None, "dp", None),
            P(None, "dp", None),
            P("section", None),
            P("section", "dp", None),
            P("section", None, "dp"),
        ),
        out_specs=(P("section", "dp", None), P("section", None, "dp")),
        check_vma=False,
    )
```

```python
import functools

import jax
import jax.numpy as jnp
from jax import lax
from jax.experimental import pallas as pl
from jax.experimental.pallas import tpu as pltpu
from jax.sharding import PartitionSpec as P

F32 = jnp.float32
BF16 = jnp.bfloat16
PLANE = 4
VMEM_LIMIT = 16 * 1024 * 1024


def passed_along(block, axis, distance):
    devices = range(lax.axis_size(axis))
    route = [(i - distance, i) for i in devices if i - distance in devices]
    return lax.ppermute(block, axis, route)


def segments_of(lengths, count):
    ends = jnp.cumsum(lengths)
    position = jnp.arange(count, dtype=jnp.int32)
    return jnp.sum((position[:, None] >= ends[None, :]).astype(jnp.int32), axis=1)


def layer(x, gain, w_qkv, w_out, seg):
    head = w_out.shape[0]
    x_wide = x.astype(jnp.float32)
    scale = lax.rsqrt(jnp.mean(x_wide * x_wide, axis=-1, keepdims=True) + 1e-05)
    normed = (x_wide * scale * gain.astype(jnp.float32)).astype(jnp.bfloat16)
    qkv = jnp.dot(normed, w_qkv, preferred_element_type=jnp.float32).astype(jnp.bfloat16)
    query = qkv[:, :head]
    keys = qkv[:, head : 2 * head]
    values = qkv[:, 2 * head :]
    scores = jnp.dot(query, keys.T, preferred_element_type=jnp.float32) * head ** (-0.5)
    rows = jnp.arange(x.shape[0], dtype=jnp.int32)
    allowed = (seg[:, None] == seg[None, :]) & (rows[:, None] >= rows[None, :])
    scores = jnp.where(allowed, scores, -1e30)
    probs = jax.nn.softmax(scores, axis=-1).astype(jnp.bfloat16)
    attended = jnp.dot(probs, values, preferred_element_type=jnp.float32).astype(jnp.bfloat16)
    return (x_wide + jnp.dot(attended, w_out, preferred_element_type=jnp.float32)).astype(
        jnp.bfloat16
    )


def pipelined(inputs, cotangent, doc_lengths, norm_gain, w_qkv, w_out):
    sections = lax.axis_size("section")
    section = lax.axis_index("section")
    micro = inputs.shape[0]
    count = inputs.shape[1]
    segs = jax.vmap(lambda lens: segments_of(lens, count))(doc_lengths[:, 0, :])
    gain = norm_gain[0]
    full_qkv, full_out = (
        lax.all_gather(w_qkv[0], "dp", axis=0, tiled=True),
        lax.all_gather(w_out[0], "dp", axis=1, tiled=True),
    )
    total_steps = micro + sections - 1
    empty = jnp.zeros(inputs.shape[1:], inputs.dtype)

    def forward_at(step, incoming, saved):
        index = step - section
        live = (index >= 0) & (index < micro)
        slot = jnp.clip(index, 0, micro - 1)
        first = lax.dynamic_index_in_dim(inputs, slot, 0, keepdims=False)
        x = jnp.where(section == 0, first, incoming)
        seg = lax.dynamic_index_in_dim(segs, slot, 0, keepdims=False)
        out = layer(x, gain, full_qkv, full_out, seg)
        old = lax.dynamic_index_in_dim(saved, slot, 0, keepdims=False)
        saved = lax.dynamic_update_index_in_dim(saved, jnp.where(live, x, old), slot, 0)
        return (out, saved)

    def forward_step(carry, step):
        incoming, saved = carry
        out, saved = forward_at(step, incoming, saved)
        incoming = passed_along(out, "section", 1)
        return ((incoming, saved), None)

    start_saved = jnp.zeros(inputs.shape, inputs.dtype)
    (incoming, saved), _ = lax.scan(
        forward_step, (empty, start_saved), jnp.arange(total_steps - 1, dtype=jnp.int32)
    )
    _, saved = forward_at(jnp.int32(total_steps - 1), incoming, saved)

    def backward_at(step, incoming, sum_qkv, sum_out):
        index = step - (sections - 1 - section)
        live = (index >= 0) & (index < micro)
        slot = jnp.clip(index, 0, micro - 1)
        last = lax.dynamic_index_in_dim(cotangent, slot, 0, keepdims=False)
        grad_y = jnp.where(section == sections - 1, last, incoming)
        x = lax.dynamic_index_in_dim(saved, slot, 0, keepdims=False)
        seg = lax.dynamic_index_in_dim(segs, slot, 0, keepdims=False)
        _, pull = jax.vjp(lambda a, b, c: layer(a, gain, b, c, seg), x, full_qkv, full_out)
        grad_x, grad_q, grad_o = pull(grad_y)
        sum_qkv = sum_qkv + jnp.where(live, grad_q.astype(jnp.float32), 0.0)
        sum_out = sum_out + jnp.where(live, grad_o.astype(jnp.float32), 0.0)
        return (grad_x, sum_qkv, sum_out)

    def backward_step(carry, step):
        incoming, sum_qkv, sum_out = carry
        grad_x, sum_qkv, sum_out = backward_at(step, incoming, sum_qkv, sum_out)
        incoming = passed_along(grad_x, "section", -1)
        return ((incoming, sum_qkv, sum_out), None)

    zero_qkv = jnp.zeros(full_qkv.shape, jnp.float32)
    zero_out = jnp.zeros(full_out.shape, jnp.float32)
    (incoming, sum_qkv, sum_out), _ = lax.scan(
        backward_step, (empty, zero_qkv, zero_out), jnp.arange(total_steps - 1, dtype=jnp.int32)
    )
    _, sum_qkv, sum_out = backward_at(jnp.int32(total_steps - 1), incoming, sum_qkv, sum_out)
    share_qkv, share_out = (
        lax.psum_scatter(sum_qkv, "dp", scatter_dimension=0, tiled=True),
        lax.psum_scatter(sum_out, "dp", scatter_dimension=1, tiled=True),
    )
    return (share_qkv[None], share_out[None])


def nn(a, b):
    return lax.dot_general(a, b, (((1,), (0,)), ((), ())), preferred_element_type=F32)


def nt(a, b):
    return lax.dot_general(a, b, (((1,), (1,)), ((), ())), preferred_element_type=F32)


def block_copies(planes, index, k, refs, out_ref, sems):
    width = refs[0].shape[-1] // (planes * PLANE)
    section, p = index[0], index[2]
    copies = []
    for z in range(planes):
        at = pl.multiple_of((z * PLANE + (p ^ k)) * width, width)
        for half, ref in enumerate(refs):
            copies.append(
                pltpu.make_async_copy(
                    ref.at[section, :, pl.ds(at, width)],
                    out_ref.at[half, :, pl.ds(z * width, width)],
                    sems.at[len(copies)],
                )
            )
    return copies


def mark_kernel(planes, index, pack_ref, gain_ref, x_ref, c_ref, out_ref, block_ref, sems):
    copies = block_copies(planes, index, 0, (x_ref, c_ref), block_ref, sems)
    for copy in copies:
        copy.start()
    out_ref[: pack_ref.shape[0], :] = pack_ref[...]
    out_ref[pack_ref.shape[0] :, :] = gain_ref[...]
    for copy in copies:
        copy.wait()


def first_kernel(planes, index, qkv_ref, wout_ref, x_ref, c_ref, pack_ref, far_ref, pack_sems, sems):
    qkv_rows = qkv_ref.shape[0]
    copies = [
        pltpu.make_async_copy(qkv_ref, pack_ref.at[:qkv_rows], pack_sems.at[0]),
        pltpu.make_async_copy(wout_ref, pack_ref.at[qkv_rows:], pack_sems.at[1]),
    ] + block_copies(planes, index, PLANE - 1, (x_ref, c_ref), far_ref, sems)
    for copy in copies:
        copy.start()
    for copy in copies:
        copy.wait()


def blocks_kernel(planes, index, x_ref, c_ref, *refs):
    out_refs, sems = refs[:-1], refs[-1]
    copies = []
    for k, out_ref in enumerate(out_refs, 1):
        copies += block_copies(planes, index, k, (x_ref, c_ref), out_ref, sems.at[k - 1])
    for copy in copies:
        copy.start()
    for copy in copies:
        copy.wait()


def project_kernel(planes, heads, index, *refs):
    blocks, own, other = refs[:PLANE], refs[PLANE : PLANE + planes], refs[PLANE + planes : PLANE + 2 * planes]
    x_ref, c_ref, vx_ref, gain_ref = refs[PLANE + 2 * planes : PLANE + 2 * planes + 4]
    out_refs = refs[PLANE + 2 * planes + 4 : -4]
    vc_ref, sum_ref, *wide_refs = refs[-4:]
    qkv, width = 3 * heads, vx_ref.shape[-1]
    section, place, p = index[0], index[1], index[2]
    for ref, wide_ref in zip((own[0], other[0]), wide_refs):
        wide_ref[...] = ref[qkv + heads :, :].astype(F32)
    for z in range(planes):
        mine, theirs = (ref[pl.ds(z * PLANE + p, 1), :] for ref in wide_refs)
        gain_ref[z, 0:1, :] = jnp.where(section == 0, mine, theirs)
        gain_ref[z, 1:2, :] = jnp.where(section == 0, theirs, mine)
    for k in range(planes):
        at = place ^ k
        mine, theirs = own[k][: qkv + heads, :], other[k][: qkv + heads, :]
        zero = jnp.where(section == 0, mine, theirs)
        one = jnp.where(section == 0, theirs, mine)
        empty = jnp.zeros((heads, width), BF16)
        vx_ref[at, :qkv, :] = (zero[:qkv].astype(F32) * gain_ref[at, 0:1, :]).astype(BF16)
        vx_ref[at, qkv : qkv + heads, :] = zero[qkv : qkv + heads]
        vx_ref[at, qkv + heads : 2 * qkv + heads, :] = (one[:qkv].astype(F32) * gain_ref[at, 1:2, :]).astype(BF16)
        vx_ref[at, 2 * qkv + heads :, :] = empty
        vc_ref[at, :heads, :] = empty
        vc_ref[at, heads : 2 * heads, :] = one[qkv : qkv + heads]
        vc_ref[at, 2 * heads : 3 * heads, :] = zero[qkv : qkv + heads]
        vc_ref[at, 3 * heads :, :] = empty
    for k in range(PLANE):
        x_ref[p ^ k] = blocks[-k][0]
        c_ref[p ^ k] = blocks[-k][1]
    rows = x_ref.shape[0] * x_ref.shape[1]
    with_x = with_c = squares = products = None
    for z in range(planes):
        cols = slice(z * width, (z + 1) * width)
        x = x_ref[:, :, cols].reshape(rows, width)
        c = c_ref[:, :, cols].reshape(rows, width)
        wide = x.astype(F32)
        out = vx_ref[z, qkv : qkv + heads, :]
        right = jnp.concatenate([vx_ref[z, qkv + heads : 2 * qkv + heads, :], out], axis=0)
        new = nt(x, vx_ref[z]), nt(c, vc_ref[z]), jnp.sum(wide * wide, axis=1, keepdims=True), nt(out, right)
        if with_x is None:
            with_x, with_c, squares, products = new
        else:
            with_x, with_c = with_x + new[0], with_c + new[1]
            squares, products = squares + new[2], products + new[3]
    half = 2 * heads
    lane = lax.broadcasted_iota(jnp.int32, (rows, half), 1)
    high = squares.astype(BF16).astype(F32)
    last = jnp.where(lane == heads, high, jnp.where(lane == heads + 1, squares - high, with_c[:, half:]))
    sum_ref[:, : 3 * half] = with_x[:, : 3 * half].astype(BF16)
    sum_ref[:, 3 * half : 4 * half] = (with_x[:, 3 * half :] + with_c[:, :half]).astype(BF16)
    sum_ref[:, 4 * half :] = last.astype(BF16)
    block = rows // PLANE
    for k in range(PLANE):
        start = pl.multiple_of((p ^ k) * block, block)
        out_refs[k][:, : 5 * half] = sum_ref[pl.ds(start, block), :]
        out_refs[k][:, 5 * half :] = products.astype(BF16)


def attention(qkv, allowed, heads):
    query, keys, values = (qkv[:, i * heads : (i + 1) * heads].astype(BF16) for i in range(3))
    scores = jnp.where(allowed, nt(query, keys) * heads ** (-0.5), -1e30)
    raised = jnp.exp(scores - jnp.max(scores, axis=1, keepdims=True))
    scale = 1.0 / jnp.sum(raised, axis=1, keepdims=True)
    return raised * scale, (nn(raised.astype(BF16), values) * scale).astype(BF16)


def attention_grad(qkv, probs, att, d_att, heads):
    query, keys, values = (qkv[:, i * heads : (i + 1) * heads].astype(BF16) for i in range(3))
    inner = jnp.sum(att.astype(F32) * d_att.astype(F32), axis=1, keepdims=True)
    d_values = nn(jnp.transpose(probs).astype(BF16), d_att)
    d_scores = probs * (nt(d_att, values) - inner) * heads ** (-0.5)
    d_query = nn(d_scores.astype(BF16), keys)
    d_keys = nn(jnp.transpose(d_scores).astype(BF16), query)
    return jnp.concatenate([d_query, d_keys, d_values], axis=1).astype(BF16).astype(F32)


def summed(parts):
    total = parts[0][...].astype(F32)
    for part in parts[1:]:
        total = total + part[...].astype(F32)
    return total


def chain_kernel(features, heads, index, docs, *refs):
    out_ref = refs[-1]
    qkv, half = 3 * heads, 2 * heads
    total = summed(refs[:-1])
    rows = total.shape[0]
    section = index[0]
    query_at = lax.broadcasted_iota(jnp.int32, (rows, rows), 0)
    key_at = lax.broadcasted_iota(jnp.int32, (rows, rows), 1)
    allowed = query_at >= key_at
    end = 0
    for i in range(docs.shape[2]):
        end = end + docs[section, 0, i]
        allowed = allowed & ((query_at >= end) == (key_at >= end))
    x_out = total[:, qkv : 2 * half]
    x_one = total[:, 2 * half : 2 * half + qkv]
    tail = total[:, 4 * half : 5 * half]
    c_one, c_zero = total[:, 4 * half - heads : 4 * half].astype(BF16), tail[:, :heads]
    lane = lax.broadcasted_iota(jnp.int32, tail.shape, 1)
    squares = jnp.sum(jnp.where((lane == heads) | (lane == heads + 1), tail, 0.0), axis=1, keepdims=True)
    mixed = total[:, 5 * half : 5 * half + qkv].astype(BF16)
    gram = total[:, 5 * half + qkv :].astype(BF16)

    scale0 = lax.rsqrt(squares / features + 1e-05)
    qkv0 = (total[:, :qkv] * scale0).astype(BF16).astype(F32)
    probs0, att0 = attention(qkv0, allowed, heads)
    wide0 = att0.astype(F32)
    y_out = x_out + nn(att0, gram)
    squares = squares + jnp.sum(wide0 * (x_out + y_out), axis=1, keepdims=True)
    scale1 = lax.rsqrt(jnp.maximum(squares, 0.0) / features + 1e-05)
    qkv1 = ((x_one + nn(att0, mixed)) * scale1).astype(BF16).astype(F32)
    probs1, att1 = attention(qkv1, allowed, heads)
    d_qkv1 = attention_grad(qkv1, probs1, att1, c_one, heads)
    inner = jnp.sum(d_qkv1 * qkv1, axis=1, keepdims=True) * scale1 * scale1 / features
    e1 = d_qkv1 * scale1
    d_att0 = c_zero + nt(e1.astype(BF16), mixed) - inner * y_out
    e0 = attention_grad(qkv0, probs0, att0, d_att0.astype(BF16), heads) * scale0
    factors = [e0, wide0, e1, wide0 * inner, att1.astype(F32), jnp.zeros((rows, heads), F32)]
    out_ref[...] = jnp.concatenate(factors, axis=1).astype(BF16)


def pieces_of(planes, heads, order, index, turned, small, small_t, x_ref, c_ref, vx_ref, gain_ref, keep_ref, send_ref):
    qkv, half, width = 3 * heads, 2 * heads, vx_ref.shape[-1]
    section, place = index[0], index[1]
    rows = x_ref.shape[0] * x_ref.shape[1]
    att0, att1 = turned[qkv : qkv + heads], turned[4 * half : 4 * half + heads]
    for i, k in enumerate(order):
        z = place ^ k
        cols = pl.ds(pl.multiple_of(z * width, width), width)
        x = x_ref[:, :, cols].reshape(rows, width)
        c = c_ref[:, :, cols].reshape(rows, width)
        out = vx_ref[z, qkv : qkv + heads, :]
        with_x = nn(turned[: 4 * half], x)
        left = with_x[2 * half :] + nn(small, out)
        zero = with_x[:qkv] * gain_ref[z, 0:1, :]
        one = left[:qkv] * gain_ref[z, 1:2, :]
        keep_ref[i, :qkv, :] = jnp.where(section == 0, zero, one)
        send_ref[i, :qkv, :] = jnp.where(section == 0, one, zero).astype(BF16)
        zero = nn(att0, c) + nn(small_t, vx_ref[z, qkv + heads : 2 * qkv + heads, :]) - left[qkv:]
        one = nn(att1, c)
        keep_ref[i, qkv:, :] = jnp.where(section == 0, zero, one)
        send_ref[i, qkv:, :] = jnp.where(section == 0, one, zero).astype(BF16)


def far_grads_kernel(planes, heads, order, index, *refs):
    factors, arrays = refs[:PLANE], refs[PLANE : PLANE + 4]
    keep_ref, send_ref, turned_ref, small_ref, small_t_ref, all_ref = refs[PLANE + 4 :]
    qkv, half = 3 * heads, 2 * heads
    p = index[2]
    for k in range(PLANE):
        all_ref[p ^ k] = factors[k][...]
    rows = all_ref.shape[0] * all_ref.shape[1]
    turned = jnp.transpose(all_ref[...].astype(F32).reshape(rows, 5 * half)).astype(BF16)
    att0, right = turned[qkv : qkv + heads], turned[2 * half : 4 * half]
    small = nt(right, att0).astype(BF16)
    small_t = nt(att0, right[:qkv]).astype(BF16)
    turned_ref[...] = turned
    small_ref[...] = small
    small_t_ref[...] = small_t
    pieces_of(planes, heads, order, index, turned, small, small_t, *arrays, keep_ref, send_ref)


def near_grads_kernel(planes, heads, order, index, turned_ref, small_ref, small_t_ref, *refs):
    pieces_of(planes, heads, order, index, turned_ref[...], small_ref[...], small_t_ref[...], *refs)


def merge_kernel(keep_ref, come_ref, *out_refs):
    for i, out_ref in enumerate(out_refs):
        out_ref[...] = (keep_ref[i] + come_ref[i].astype(F32)).astype(out_ref.dtype)


def wide_add_kernel(a_ref, b_ref, out_ref):
    out_ref[...] = a_ref[...] + b_ref[...].astype(F32)


def add_kernel(a_ref, b_ref, out_ref):
    out_ref[...] = (a_ref[...].astype(F32) + b_ref[...].astype(F32)).astype(BF16)


def last_kernel(qkv_rows, keep_ref, *refs):
    parts, (qkv_ref, out_ref) = refs[:-2], refs[-2:]
    total = keep_ref[...]
    for part in parts:
        total = total + part[...].astype(F32)
    qkv_ref[...] = total[:qkv_rows]
    out_ref[...] = total[qkv_rows:]


def far_first(value, count, send):
    of = lambda k: value[k] if isinstance(value, (list, tuple)) else value
    got = {k: send(of(k), k) for k in reversed(range(1, count))}
    return [of(0)] + [got[k] for k in range(1, count)]


def call(kernel, outs, *args, scalars=0, scratch=()):
    smem = pl.BlockSpec(memory_space=pltpu.SMEM)
    vmem = pl.BlockSpec(memory_space=pltpu.VMEM)
    return pl.pallas_call(
        kernel,
        out_shape=[jax.ShapeDtypeStruct(shape, dtype) for shape, dtype in outs],
        in_specs=[smem] * scalars + [vmem] * (len(args) - scalars),
        out_specs=[vmem] * len(outs),
        scratch_shapes=[pltpu.VMEM(shape, dtype) for shape, dtype in scratch],
        compiler_params=pltpu.CompilerParams(vmem_limit_bytes=VMEM_LIMIT),
    )(*args)


def planar(inputs, cotangent, doc_lengths, norm_gain, w_qkv, w_out):
    shards = lax.axis_size("dp")
    planes = shards // PLANE
    section, place = lax.axis_index("section"), lax.axis_index("dp")
    z, p = place // PLANE, place % PLANE
    index = jnp.stack([section, z, p]).astype(jnp.int32)
    block, features = inputs.shape[1:]
    rows = PLANE * block
    heads, width = w_out.shape[1:]
    qkv_rows = w_qkv.shape[2]
    cols = planes * width
    def along_z(value, k):
        route = [(a * PLANE + b, (a ^ k) * PLANE + b) for a in range(planes) for b in range(PLANE)]
        return lax.ppermute(value, "dp", route)

    def to_sibling(value):
        return lax.ppermute(value, "section", [(0, 1), (1, 0)])

    def along_plane(value, k):
        route = [(a * PLANE + b, a * PLANE + (b ^ k)) for a in range(planes) for b in range(PLANE)]
        return lax.ppermute(value, "dp", route)

    def exchange(value):
        return far_first(value, PLANE, along_plane)

    smem, vmem = pl.BlockSpec(memory_space=pltpu.SMEM), pl.BlockSpec(memory_space=pltpu.VMEM)
    hbm = pl.BlockSpec(memory_space=pltpu.HBM)
    params = pltpu.CompilerParams(vmem_limit_bytes=VMEM_LIMIT)
    qkv_in, out_in, x_in, c_in = [
        pltpu.with_memory_space_constraint(value, pltpu.HBM)
        for value in (w_qkv[0].T, w_out[0], inputs, cotangent)
    ]
    one_block = jax.ShapeDtypeStruct((2, block, cols), BF16)
    pack, far_block = pl.pallas_call(
        functools.partial(first_kernel, planes),
        out_shape=[jax.ShapeDtypeStruct((qkv_rows + heads, width), BF16), one_block],
        in_specs=[smem] + [hbm] * 4,
        out_specs=[vmem] * 2,
        scratch_shapes=[pltpu.SemaphoreType.DMA((2,)), pltpu.SemaphoreType.DMA((2 * planes,))],
        compiler_params=params,
    )(index, qkv_in, out_in, x_in, c_in)
    blocks = pl.pallas_call(
        functools.partial(blocks_kernel, planes),
        out_shape=[one_block] * (PLANE - 2),
        in_specs=[smem] + [hbm] * 2,
        out_specs=[vmem] * (PLANE - 2),
        scratch_shapes=[pltpu.SemaphoreType.DMA((PLANE - 2, 2 * planes))],
        compiler_params=params,
    )(index, x_in, c_in)
    blocks = [*blocks, far_block]
    gain = norm_gain[0].reshape(shards, width)
    blocks = far_first([None] + blocks, PLANE, along_plane)
    pieces = {0: pack}
    for step in reversed([1 << bit for bit in range(planes.bit_length() - 1)]):
        for k in list(pieces):
            pieces[k ^ step] = along_z(pieces[k], step)
    mine, late_gain, _ = lax.optimization_barrier((pack, gain, blocks[3]))
    marked, blocks[0] = pl.pallas_call(
        functools.partial(mark_kernel, planes),
        out_shape=[jax.ShapeDtypeStruct((qkv_rows + heads + shards, width), BF16), one_block],
        in_specs=[smem] + [vmem] * 2 + [hbm] * 2,
        out_specs=[vmem] * 2,
        scratch_shapes=[pltpu.SemaphoreType.DMA((2 * planes,))],
        compiler_params=params,
    )(index, mine, late_gain, x_in, c_in)
    pieces[planes // 2], _ = lax.optimization_barrier((pieces[planes // 2], blocks[3]))
    own = [marked] + [pieces[k] for k in range(1, planes)]
    other = [to_sibling(piece) for piece in own]

    split = ((PLANE, block, cols), BF16)
    half = 2 * heads
    x, c, vx, gains, *sent = call(
        functools.partial(project_kernel, planes, heads),
        [split, split, ((planes, 4 * half, width), BF16), ((planes, 8, width), F32)]
        + [((block, 7 * half), BF16)] * PLANE,
        index, blocks[0], *blocks[:0:-1], *own, *other, scalars=1,
        scratch=[((planes, 2 * half, width), BF16), ((rows, 5 * half), BF16)] + [((shards, width), F32)] * 2,
    )
    (factors,) = call(
        functools.partial(chain_kernel, features, heads),
        [((block, 5 * half), BF16)],
        index, doc_lengths, *exchange(sent)[::-1], scalars=2,
    )
    piece = (qkv_rows + heads, width)
    far_order = tuple(reversed(range(planes - planes // 2, planes)))
    near_order = tuple(reversed(range(planes - planes // 2)))

    def swap_and_merge(order, keep, send):
        outs = [(piece, BF16 if k else F32) for k in order]
        return zip(order, call(merge_kernel, outs, keep, to_sibling(send)))

    keep, send, turned, small, small_t = call(
        functools.partial(far_grads_kernel, planes, heads, far_order),
        [((len(far_order),) + piece, F32), ((len(far_order),) + piece, BF16)]
        + [((5 * half, rows), BF16), ((2 * half, heads), BF16), ((heads, qkv_rows), BF16)],
        index, *exchange(factors), x, c, vx, gains, scalars=1,
        scratch=[((PLANE, block, 5 * half), BF16)],
    )
    pieces = dict(swap_and_merge(far_order, keep, send))
    keep, send = call(
        functools.partial(near_grads_kernel, planes, heads, near_order),
        [((len(near_order),) + piece, F32), ((len(near_order),) + piece, BF16)],
        index, turned, small, small_t, x, c, vx, gains, scalars=1,
    )
    pieces.update(swap_and_merge(near_order, keep, send))
    kept, parts = pieces[0], []
    held = []
    for step in [1 << bit for bit in range(planes.bit_length() - 1)]:
        got = {k ^ step: along_z(pieces.pop(k), step) for k in sorted(pieces, reverse=True) if k & step and k != step}
        if step in pieces:
            held.append((pieces.pop(step), step))
        for k, part in got.items():
            (pieces[k],) = call(add_kernel, [(piece, BF16)], pieces[k], part)
            held = [(lax.optimization_barrier((value, pieces[k]))[0], at) for value, at in held]
    parts = [along_z(value, at) for value, at in reversed(held)]
    for part in parts[:-1]:
        (kept,) = call(wide_add_kernel, [(piece, F32)], kept, part)
    grad_qkv, grad_out = call(
        functools.partial(last_kernel, qkv_rows),
        [((qkv_rows, width), F32), ((heads, width), F32)],
        kept, *parts[-1:],
    )
    return (grad_qkv.T[None], grad_out[None])


def solution(mesh):
    sections, shards = mesh.shape["section"], mesh.shape["dp"]
    planes = shards // PLANE

    def body(inputs, *rest):
        fits = shards % PLANE == 0 and planes & (planes - 1) == 0
        if sections == 2 and inputs.shape[0] == 2 and fits:
            return planar(inputs, *rest)
        return pipelined(inputs, *rest)

    return jax.shard_map(
        body,
        mesh=mesh,
        in_specs=(
            P(None, "dp", None),
            P(None, "dp", None),
            P(None, "dp", None),
            P("section", None),
            P("section", "dp", None),
            P("section", None, "dp"),
        ),
        out_specs=(P("section", "dp", None), P("section", None, "dp")),
        check_vma=False,
    )
```

```python
import functools

import jax
import jax.numpy as jnp
from jax import lax
from jax.experimental import pallas as pl
from jax.experimental.pallas import tpu as pltpu
from jax.sharding import PartitionSpec as P

F32 = jnp.float32
BF16 = jnp.bfloat16
PLANE = 4
VMEM_LIMIT = 16 * 1024 * 1024


def passed_along(block, axis, distance):
    devices = range(lax.axis_size(axis))
    route = [(i - distance, i) for i in devices if i - distance in devices]
    return lax.ppermute(block, axis, route)


def segments_of(lengths, count):
    ends = jnp.cumsum(lengths)
    position = jnp.arange(count, dtype=jnp.int32)
    return jnp.sum((position[:, None] >= ends[None, :]).astype(jnp.int32), axis=1)


def layer(x, gain, w_qkv, w_out, seg):
    head = w_out.shape[0]
    x_wide = x.astype(jnp.float32)
    scale = lax.rsqrt(jnp.mean(x_wide * x_wide, axis=-1, keepdims=True) + 1e-05)
    normed = (x_wide * scale * gain.astype(jnp.float32)).astype(jnp.bfloat16)
    qkv = jnp.dot(normed, w_qkv, preferred_element_type=jnp.float32).astype(jnp.bfloat16)
    query = qkv[:, :head]
    keys = qkv[:, head : 2 * head]
    values = qkv[:, 2 * head :]
    scores = jnp.dot(query, keys.T, preferred_element_type=jnp.float32) * head ** (-0.5)
    rows = jnp.arange(x.shape[0], dtype=jnp.int32)
    allowed = (seg[:, None] == seg[None, :]) & (rows[:, None] >= rows[None, :])
    scores = jnp.where(allowed, scores, -1e30)
    probs = jax.nn.softmax(scores, axis=-1).astype(jnp.bfloat16)
    attended = jnp.dot(probs, values, preferred_element_type=jnp.float32).astype(jnp.bfloat16)
    return (x_wide + jnp.dot(attended, w_out, preferred_element_type=jnp.float32)).astype(
        jnp.bfloat16
    )


def pipelined(inputs, cotangent, doc_lengths, norm_gain, w_qkv, w_out):
    sections = lax.axis_size("section")
    section = lax.axis_index("section")
    micro = inputs.shape[0]
    count = inputs.shape[1]
    segs = jax.vmap(lambda lens: segments_of(lens, count))(doc_lengths[:, 0, :])
    gain = norm_gain[0]
    full_qkv, full_out = (
        lax.all_gather(w_qkv[0], "dp", axis=0, tiled=True),
        lax.all_gather(w_out[0], "dp", axis=1, tiled=True),
    )
    total_steps = micro + sections - 1
    empty = jnp.zeros(inputs.shape[1:], inputs.dtype)

    def forward_at(step, incoming, saved):
        index = step - section
        live = (index >= 0) & (index < micro)
        slot = jnp.clip(index, 0, micro - 1)
        first = lax.dynamic_index_in_dim(inputs, slot, 0, keepdims=False)
        x = jnp.where(section == 0, first, incoming)
        seg = lax.dynamic_index_in_dim(segs, slot, 0, keepdims=False)
        out = layer(x, gain, full_qkv, full_out, seg)
        old = lax.dynamic_index_in_dim(saved, slot, 0, keepdims=False)
        saved = lax.dynamic_update_index_in_dim(saved, jnp.where(live, x, old), slot, 0)
        return (out, saved)

    def forward_step(carry, step):
        incoming, saved = carry
        out, saved = forward_at(step, incoming, saved)
        incoming = passed_along(out, "section", 1)
        return ((incoming, saved), None)

    start_saved = jnp.zeros(inputs.shape, inputs.dtype)
    (incoming, saved), _ = lax.scan(
        forward_step, (empty, start_saved), jnp.arange(total_steps - 1, dtype=jnp.int32)
    )
    _, saved = forward_at(jnp.int32(total_steps - 1), incoming, saved)

    def backward_at(step, incoming, sum_qkv, sum_out):
        index = step - (sections - 1 - section)
        live = (index >= 0) & (index < micro)
        slot = jnp.clip(index, 0, micro - 1)
        last = lax.dynamic_index_in_dim(cotangent, slot, 0, keepdims=False)
        grad_y = jnp.where(section == sections - 1, last, incoming)
        x = lax.dynamic_index_in_dim(saved, slot, 0, keepdims=False)
        seg = lax.dynamic_index_in_dim(segs, slot, 0, keepdims=False)
        _, pull = jax.vjp(lambda a, b, c: layer(a, gain, b, c, seg), x, full_qkv, full_out)
        grad_x, grad_q, grad_o = pull(grad_y)
        sum_qkv = sum_qkv + jnp.where(live, grad_q.astype(jnp.float32), 0.0)
        sum_out = sum_out + jnp.where(live, grad_o.astype(jnp.float32), 0.0)
        return (grad_x, sum_qkv, sum_out)

    def backward_step(carry, step):
        incoming, sum_qkv, sum_out = carry
        grad_x, sum_qkv, sum_out = backward_at(step, incoming, sum_qkv, sum_out)
        incoming = passed_along(grad_x, "section", -1)
        return ((incoming, sum_qkv, sum_out), None)

    zero_qkv = jnp.zeros(full_qkv.shape, jnp.float32)
    zero_out = jnp.zeros(full_out.shape, jnp.float32)
    (incoming, sum_qkv, sum_out), _ = lax.scan(
        backward_step, (empty, zero_qkv, zero_out), jnp.arange(total_steps - 1, dtype=jnp.int32)
    )
    _, sum_qkv, sum_out = backward_at(jnp.int32(total_steps - 1), incoming, sum_qkv, sum_out)
    share_qkv, share_out = (
        lax.psum_scatter(sum_qkv, "dp", scatter_dimension=0, tiled=True),
        lax.psum_scatter(sum_out, "dp", scatter_dimension=1, tiled=True),
    )
    return (share_qkv[None], share_out[None])


def nn(a, b):
    return lax.dot_general(a, b, (((1,), (0,)), ((), ())), preferred_element_type=F32)


def nt(a, b):
    return lax.dot_general(a, b, (((1,), (1,)), ((), ())), preferred_element_type=F32)


def block_copies(planes, index, k, refs, out_ref, sems):
    width = refs[0].shape[-1] // (planes * PLANE)
    section, p = index[0], index[2]
    copies = []
    for z in range(planes):
        at = pl.multiple_of((z * PLANE + (p ^ k)) * width, width)
        for half, ref in enumerate(refs):
            copies.append(
                pltpu.make_async_copy(
                    ref.at[section, :, pl.ds(at, width)],
                    out_ref.at[half, :, pl.ds(z * width, width)],
                    sems.at[len(copies)],
                )
            )
    return copies


def mark_kernel(planes, index, pack_ref, gain_ref, x_ref, c_ref, out_ref, block_ref, sems):
    copies = block_copies(planes, index, 0, (x_ref, c_ref), block_ref, sems)
    for copy in copies:
        copy.start()
    out_ref[: pack_ref.shape[0], :] = pack_ref[...]
    out_ref[pack_ref.shape[0] :, :] = gain_ref[...]
    for copy in copies:
        copy.wait()


def first_kernel(planes, index, qkv_ref, wout_ref, x_ref, c_ref, pack_ref, far_ref, pack_sems, sems):
    qkv_rows = qkv_ref.shape[0]
    copies = [
        pltpu.make_async_copy(qkv_ref, pack_ref.at[:qkv_rows], pack_sems.at[0]),
        pltpu.make_async_copy(wout_ref, pack_ref.at[qkv_rows:], pack_sems.at[1]),
    ] + block_copies(planes, index, PLANE - 1, (x_ref, c_ref), far_ref, sems)
    for copy in copies:
        copy.start()
    for copy in copies:
        copy.wait()


def blocks_kernel(planes, index, x_ref, c_ref, *refs):
    out_refs, sems = refs[:-1], refs[-1]
    copies = []
    for k, out_ref in enumerate(out_refs, 1):
        copies += block_copies(planes, index, k, (x_ref, c_ref), out_ref, sems.at[k - 1])
    for copy in copies:
        copy.start()
    for copy in copies:
        copy.wait()


def weights_of(heads, index, at, own, other, gain_refs, vx_ref, vc_ref, gain_ref, i):
    qkv, width = 3 * heads, vx_ref.shape[-1]
    section, p = index[0], index[2]
    mine, theirs = (ref[pl.ds(at * PLANE + p, 1), :] for ref in gain_refs)
    gain0, gain1 = jnp.where(section == 0, mine, theirs), jnp.where(section == 0, theirs, mine)
    gain_ref[i, 0:1, :] = gain0
    gain_ref[i, 1:2, :] = gain1
    zero, one = jnp.where(section == 0, own, other), jnp.where(section == 0, other, own)
    empty = jnp.zeros((heads, width), BF16)
    vx_ref[i, :qkv, :] = (zero[:qkv].astype(F32) * gain0).astype(BF16)
    vx_ref[i, qkv : qkv + heads, :] = zero[qkv:]
    vx_ref[i, qkv + heads : 2 * qkv + heads, :] = (one[:qkv].astype(F32) * gain1).astype(BF16)
    vx_ref[i, 2 * qkv + heads :, :] = empty
    vc_ref[i, :heads, :] = empty
    vc_ref[i, heads : 2 * heads, :] = one[qkv:]
    vc_ref[i, 2 * heads : 3 * heads, :] = zero[qkv:]
    vc_ref[i, 3 * heads :, :] = empty


def products_of(heads, x, c, vx_ref, vc_ref, i):
    qkv = 3 * heads
    wide = x.astype(F32)
    out = vx_ref[i, qkv : qkv + heads, :]
    right = jnp.concatenate([vx_ref[i, qkv + heads : 2 * qkv + heads, :], out], axis=0)
    return nt(x, vx_ref[i]), nt(c, vc_ref[i]), jnp.sum(wide * wide, axis=1, keepdims=True), nt(out, right)


def columns(ref, at, width):
    cols = pl.ds(pl.multiple_of(at * width, width), width)
    return ref[:, :, cols].reshape(ref.shape[0] * ref.shape[1], width)


def early_kernel(planes, heads, index, *refs):
    count = planes - 1
    blocks, own, other = refs[:PLANE], refs[PLANE : PLANE + count], refs[PLANE + count : PLANE + 2 * count]
    x_ref, c_ref, vx_ref, gain_ref, wide_ref, *sum_refs = refs[PLANE + 2 * count : -1]
    vc_ref = refs[-1]
    size, width = 4 * heads, vx_ref.shape[-1]
    place, p = index[1], index[2]
    rows_of_gain = planes * PLANE
    for i, ref in enumerate((own[0], other[0])):
        wide_ref[i * rows_of_gain : (i + 1) * rows_of_gain, :] = ref[size:, :].astype(F32)
    gain_refs = [wide_ref.at[i * rows_of_gain : (i + 1) * rows_of_gain] for i in range(2)]
    for k in range(PLANE):
        x_ref[p ^ k] = blocks[-k][0]
        c_ref[p ^ k] = blocks[-k][1]
    totals = None
    for k in range(count):
        at = place ^ k
        weights_of(heads, index, at, own[k][:size, :], other[k][:size, :], gain_refs, vx_ref, vc_ref, gain_ref, k)
        new = products_of(heads, columns(x_ref, at, width), columns(c_ref, at, width), vx_ref, vc_ref, k)
        totals = new if totals is None else [a + b for a, b in zip(totals, new)]
    for ref, total in zip(sum_refs, totals):
        ref[...] = jnp.broadcast_to(total, ref.shape)


def project_kernel(planes, heads, index, own, other, x_ref, c_ref, wide_ref, *refs):
    sums, (vx_ref, gain_ref) = refs[:4], refs[4:6]
    out_refs, (vc_ref, sum_ref) = refs[6:-2], refs[-2:]
    width = vx_ref.shape[-1]
    place, p = index[1], index[2]
    at = place ^ (planes - 1)
    rows_of_gain = planes * PLANE
    gain_refs = [wide_ref.at[i * rows_of_gain : (i + 1) * rows_of_gain] for i in range(2)]
    weights_of(heads, index, at, own[...], other[...], gain_refs, vx_ref, vc_ref, gain_ref, 0)
    new = products_of(heads, columns(x_ref, at, width), columns(c_ref, at, width), vx_ref, vc_ref, 0)
    with_x, with_c, products = (sums[i][...] + new[i] for i in (0, 1, 3))
    squares = sums[2][:, 0:1] + new[2]
    rows, half = with_x.shape[0], 2 * heads
    lane = lax.broadcasted_iota(jnp.int32, (rows, half), 1)
    high = squares.astype(BF16).astype(F32)
    last = jnp.where(lane == heads, high, jnp.where(lane == heads + 1, squares - high, with_c[:, half:]))
    sum_ref[:, : 3 * half] = with_x[:, : 3 * half].astype(BF16)
    sum_ref[:, 3 * half : 4 * half] = (with_x[:, 3 * half :] + with_c[:, :half]).astype(BF16)
    sum_ref[:, 4 * half :] = last.astype(BF16)
    block = rows // PLANE
    for k in range(PLANE):
        start = pl.multiple_of((p ^ k) * block, block)
        out_refs[k][:, : 5 * half] = sum_ref[pl.ds(start, block), :]
        out_refs[k][:, 5 * half :] = products.astype(BF16)


def attention(qkv, allowed, heads):
    query, keys, values = (qkv[:, i * heads : (i + 1) * heads].astype(BF16) for i in range(3))
    scores = jnp.where(allowed, nt(query, keys) * heads ** (-0.5), -1e30)
    raised = jnp.exp(scores - jnp.max(scores, axis=1, keepdims=True))
    scale = 1.0 / jnp.sum(raised, axis=1, keepdims=True)
    return raised * scale, (nn(raised.astype(BF16), values) * scale).astype(BF16)


def attention_grad(qkv, probs, att, d_att, heads):
    query, keys, values = (qkv[:, i * heads : (i + 1) * heads].astype(BF16) for i in range(3))
    inner = jnp.sum(att.astype(F32) * d_att.astype(F32), axis=1, keepdims=True)
    d_values = nn(jnp.transpose(probs).astype(BF16), d_att)
    d_scores = probs * (nt(d_att, values) - inner) * heads ** (-0.5)
    d_query = nn(d_scores.astype(BF16), keys)
    d_keys = nn(jnp.transpose(d_scores).astype(BF16), query)
    return jnp.concatenate([d_query, d_keys, d_values], axis=1).astype(BF16).astype(F32)


def summed(parts):
    total = parts[0][...].astype(F32)
    for part in parts[1:]:
        total = total + part[...].astype(F32)
    return total


def chain_kernel(features, heads, index, docs, *refs):
    out_ref = refs[-1]
    qkv, half = 3 * heads, 2 * heads
    total = summed(refs[:-1])
    rows = total.shape[0]
    section = index[0]
    query_at = lax.broadcasted_iota(jnp.int32, (rows, rows), 0)
    key_at = lax.broadcasted_iota(jnp.int32, (rows, rows), 1)
    allowed = query_at >= key_at
    end = 0
    for i in range(docs.shape[2]):
        end = end + docs[section, 0, i]
        allowed = allowed & ((query_at >= end) == (key_at >= end))
    x_out = total[:, qkv : 2 * half]
    x_one = total[:, 2 * half : 2 * half + qkv]
    tail = total[:, 4 * half : 5 * half]
    c_one, c_zero = total[:, 4 * half - heads : 4 * half].astype(BF16), tail[:, :heads]
    lane = lax.broadcasted_iota(jnp.int32, tail.shape, 1)
    squares = jnp.sum(jnp.where((lane == heads) | (lane == heads + 1), tail, 0.0), axis=1, keepdims=True)
    mixed = total[:, 5 * half : 5 * half + qkv].astype(BF16)
    gram = total[:, 5 * half + qkv :].astype(BF16)

    scale0 = lax.rsqrt(squares / features + 1e-05)
    qkv0 = (total[:, :qkv] * scale0).astype(BF16).astype(F32)
    probs0, att0 = attention(qkv0, allowed, heads)
    wide0 = att0.astype(F32)
    y_out = x_out + nn(att0, gram)
    squares = squares + jnp.sum(wide0 * (x_out + y_out), axis=1, keepdims=True)
    scale1 = lax.rsqrt(jnp.maximum(squares, 0.0) / features + 1e-05)
    qkv1 = ((x_one + nn(att0, mixed)) * scale1).astype(BF16).astype(F32)
    probs1, att1 = attention(qkv1, allowed, heads)
    d_qkv1 = attention_grad(qkv1, probs1, att1, c_one, heads)
    inner = jnp.sum(d_qkv1 * qkv1, axis=1, keepdims=True) * scale1 * scale1 / features
    e1 = d_qkv1 * scale1
    d_att0 = c_zero + nt(e1.astype(BF16), mixed) - inner * y_out
    e0 = attention_grad(qkv0, probs0, att0, d_att0.astype(BF16), heads) * scale0
    factors = [e0, wide0, e1, wide0 * inner, att1.astype(F32), jnp.zeros((rows, heads), F32)]
    out_ref[...] = jnp.concatenate(factors, axis=1).astype(BF16)


def pieces_of(heads, order, index, turned, small, small_t, x_ref, c_ref, weights, keep_ref, send_ref):
    qkv, half = 3 * heads, 2 * heads
    section, place = index[0], index[1]
    att0, att1 = turned[qkv : qkv + heads], turned[4 * half : 4 * half + heads]
    early_vx, late_vx, early_gain, late_gain = weights
    count = early_vx.shape[0]
    for i, k in enumerate(order):
        vx, gain = (early_vx.at[k], early_gain.at[k]) if k < count else (late_vx.at[0], late_gain.at[0])
        x = columns(x_ref, place ^ k, vx.shape[-1])
        c = columns(c_ref, place ^ k, vx.shape[-1])
        out = vx[qkv : qkv + heads, :]
        with_x = nn(turned[: 4 * half], x)
        left = with_x[2 * half :] + nn(small, out)
        zero = with_x[:qkv] * gain[0:1, :]
        one = left[:qkv] * gain[1:2, :]
        keep_ref[i, :qkv, :] = jnp.where(section == 0, zero, one)
        send_ref[i, :qkv, :] = jnp.where(section == 0, one, zero).astype(BF16)
        zero = nn(att0, c) + nn(small_t, vx[qkv + heads : 2 * qkv + heads, :]) - left[qkv:]
        one = nn(att1, c)
        keep_ref[i, qkv:, :] = jnp.where(section == 0, zero, one)
        send_ref[i, qkv:, :] = jnp.where(section == 0, one, zero).astype(BF16)


def far_grads_kernel(heads, order, index, *refs):
    factors, (x_ref, c_ref, *weights) = refs[:PLANE], refs[PLANE : PLANE + 6]
    keep_ref, send_ref, turned_ref, small_ref, small_t_ref, all_ref = refs[PLANE + 6 :]
    qkv, half = 3 * heads, 2 * heads
    p = index[2]
    for k in range(PLANE):
        all_ref[p ^ k] = factors[-k][...]
    rows = all_ref.shape[0] * all_ref.shape[1]
    turned = jnp.transpose(all_ref[...].astype(F32).reshape(rows, 5 * half)).astype(BF16)
    att0, right = turned[qkv : qkv + heads], turned[2 * half : 4 * half]
    small = nt(right, att0).astype(BF16)
    small_t = nt(att0, right[:qkv]).astype(BF16)
    turned_ref[...] = turned
    small_ref[...] = small
    small_t_ref[...] = small_t
    pieces_of(heads, order, index, turned, small, small_t, x_ref, c_ref, weights, keep_ref, send_ref)


def near_grads_kernel(heads, order, index, turned_ref, small_ref, small_t_ref, x_ref, c_ref, *refs):
    factors = turned_ref[...], small_ref[...], small_t_ref[...]
    pieces_of(heads, order, index, *factors, x_ref, c_ref, refs[:4], *refs[4:])


def merge_kernel(keep_ref, come_ref, *out_refs):
    for i, out_ref in enumerate(out_refs):
        out_ref[...] = (keep_ref[i] + come_ref[i].astype(F32)).astype(out_ref.dtype)


def wide_add_kernel(a_ref, b_ref, out_ref):
    out_ref[...] = a_ref[...] + b_ref[...].astype(F32)


def add_kernel(a_ref, b_ref, out_ref):
    out_ref[...] = (a_ref[...].astype(F32) + b_ref[...].astype(F32)).astype(BF16)


def last_kernel(qkv_rows, keep_ref, *refs):
    parts, (qkv_ref, out_ref) = refs[:-2], refs[-2:]
    total = keep_ref[...]
    for part in parts:
        total = total + part[...].astype(F32)
    qkv_ref[...] = total[:qkv_rows]
    out_ref[...] = total[qkv_rows:]


def far_first(value, count, send):
    of = lambda k: value[k] if isinstance(value, (list, tuple)) else value
    got = {k: send(of(k), k) for k in reversed(range(1, count))}
    return [of(0)] + [got[k] for k in range(1, count)]


def turned_round(values):
    return [values[0], *values[:0:-1]]


def call(kernel, outs, *args, scalars=0, scratch=()):
    smem = pl.BlockSpec(memory_space=pltpu.SMEM)
    vmem = pl.BlockSpec(memory_space=pltpu.VMEM)
    return pl.pallas_call(
        kernel,
        out_shape=[jax.ShapeDtypeStruct(shape, dtype) for shape, dtype in outs],
        in_specs=[smem] * scalars + [vmem] * (len(args) - scalars),
        out_specs=[vmem] * len(outs),
        scratch_shapes=[pltpu.VMEM(shape, dtype) for shape, dtype in scratch],
        compiler_params=pltpu.CompilerParams(vmem_limit_bytes=VMEM_LIMIT),
    )(*args)


def planar(inputs, cotangent, doc_lengths, norm_gain, w_qkv, w_out):
    shards = lax.axis_size("dp")
    planes = shards // PLANE
    section, place = lax.axis_index("section"), lax.axis_index("dp")
    z, p = place // PLANE, place % PLANE
    index = jnp.stack([section, z, p]).astype(jnp.int32)
    block, features = inputs.shape[1:]
    rows = PLANE * block
    heads, width = w_out.shape[1:]
    qkv_rows = w_qkv.shape[2]
    cols = planes * width
    def along_z(value, k):
        route = [(a * PLANE + b, (a ^ k) * PLANE + b) for a in range(planes) for b in range(PLANE)]
        return lax.ppermute(value, "dp", route)

    def to_sibling(value):
        return lax.ppermute(value, "section", [(0, 1), (1, 0)])

    def along_plane(value, k):
        route = [(a * PLANE + b, a * PLANE + (b ^ k)) for a in range(planes) for b in range(PLANE)]
        return lax.ppermute(value, "dp", route)

    def exchange(value):
        return far_first(value, PLANE, along_plane)

    smem, vmem = pl.BlockSpec(memory_space=pltpu.SMEM), pl.BlockSpec(memory_space=pltpu.VMEM)
    hbm = pl.BlockSpec(memory_space=pltpu.HBM)
    params = pltpu.CompilerParams(vmem_limit_bytes=VMEM_LIMIT)
    qkv_in, out_in, x_in, c_in = [
        pltpu.with_memory_space_constraint(value, pltpu.HBM)
        for value in (w_qkv[0].T, w_out[0], inputs, cotangent)
    ]
    one_block = jax.ShapeDtypeStruct((2, block, cols), BF16)
    pack, far_block = pl.pallas_call(
        functools.partial(first_kernel, planes),
        out_shape=[jax.ShapeDtypeStruct((qkv_rows + heads, width), BF16), one_block],
        in_specs=[smem] + [hbm] * 4,
        out_specs=[vmem] * 2,
        scratch_shapes=[pltpu.SemaphoreType.DMA((2,)), pltpu.SemaphoreType.DMA((2 * planes,))],
        compiler_params=params,
    )(index, qkv_in, out_in, x_in, c_in)
    blocks = pl.pallas_call(
        functools.partial(blocks_kernel, planes),
        out_shape=[one_block] * (PLANE - 2),
        in_specs=[smem] + [hbm] * 2,
        out_specs=[vmem] * (PLANE - 2),
        scratch_shapes=[pltpu.SemaphoreType.DMA((PLANE - 2, 2 * planes))],
        compiler_params=params,
    )(index, x_in, c_in)
    blocks = [*blocks, far_block]
    gain = norm_gain[0].reshape(shards, width)
    blocks = far_first([None] + blocks, PLANE, along_plane)
    pieces = {0: pack}
    for step in reversed([1 << bit for bit in range(planes.bit_length() - 1)]):
        for k in list(pieces):
            pieces[k ^ step] = along_z(pieces[k], step)
    mine, late_gain, _ = lax.optimization_barrier((pack, gain, blocks[3]))
    marked, blocks[0] = pl.pallas_call(
        functools.partial(mark_kernel, planes),
        out_shape=[jax.ShapeDtypeStruct((qkv_rows + heads + shards, width), BF16), one_block],
        in_specs=[smem] + [vmem] * 2 + [hbm] * 2,
        out_specs=[vmem] * 2,
        scratch_shapes=[pltpu.SemaphoreType.DMA((2 * planes,))],
        compiler_params=params,
    )(index, mine, late_gain, x_in, c_in)
    pieces[planes // 2], _ = lax.optimization_barrier((pieces[planes // 2], pieces[1]))
    own = [marked] + [pieces[k] for k in range(1, planes)]
    other = [to_sibling(piece) for piece in own]

    split = ((PLANE, block, cols), BF16)
    half = 2 * heads
    sums = [((rows, 4 * half), F32), ((rows, 2 * half), F32), ((rows, 2 * heads), F32), ((heads, 2 * half), F32)]

    def weights(count):
        return [((count, 4 * half, width), BF16), ((count, 8, width), F32)]

    x, c, early_vx, early_gain, wide, *totals = call(
        functools.partial(early_kernel, planes, heads),
        [split, split] + weights(planes - 1) + [((2 * shards, width), F32)] + sums,
        index, blocks[0], *blocks[:0:-1], *own[:-1], *other[:-1], scalars=1,
        scratch=[((planes - 1, 2 * half, width), BF16)],
    )
    late_vx, late_gain, *sent = call(
        functools.partial(project_kernel, planes, heads),
        weights(1) + [((block, 7 * half), BF16)] * PLANE,
        index, own[-1], other[-1], x, c, wide, *totals, scalars=1,
        scratch=[((1, 2 * half, width), BF16), ((rows, 5 * half), BF16)],
    )
    arrays = x, c, early_vx, late_vx, early_gain, late_gain
    (factors,) = call(
        functools.partial(chain_kernel, features, heads),
        [((block, 5 * half), BF16)],
        index, doc_lengths, *exchange(sent)[::-1], scalars=2,
    )
    piece = (qkv_rows + heads, width)
    far_order = tuple(reversed(range(planes - planes // 2, planes)))
    near_order = tuple(reversed(range(planes - planes // 2)))

    def swap_and_merge(order, keep, send):
        outs = [(piece, BF16 if k else F32) for k in order]
        return zip(order, call(merge_kernel, outs, keep, to_sibling(send)))

    keep, send, turned, small, small_t = call(
        functools.partial(far_grads_kernel, heads, far_order),
        [((len(far_order),) + piece, F32), ((len(far_order),) + piece, BF16)]
        + [((5 * half, rows), BF16), ((2 * half, heads), BF16), ((heads, qkv_rows), BF16)],
        index, *turned_round(exchange(factors)), *arrays, scalars=1,
        scratch=[((PLANE, block, 5 * half), BF16)],
    )
    pieces = dict(swap_and_merge(far_order, keep, send))
    keep, send = call(
        functools.partial(near_grads_kernel, heads, near_order),
        [((len(near_order),) + piece, F32), ((len(near_order),) + piece, BF16)],
        index, turned, small, small_t, *arrays, scalars=1,
    )
    pieces.update(swap_and_merge(near_order, keep, send))
    kept, parts = pieces[0], []
    held = []
    for step in [1 << bit for bit in range(planes.bit_length() - 1)]:
        got = {k ^ step: along_z(pieces.pop(k), step) for k in sorted(pieces, reverse=True) if k & step and k != step}
        if step in pieces:
            held.append((pieces.pop(step), step))
        for k, part in got.items():
            (pieces[k],) = call(add_kernel, [(piece, BF16)], pieces[k], part)
            held = [(lax.optimization_barrier((value, pieces[k]))[0], at) for value, at in held]
    parts = [along_z(value, at) for value, at in reversed(held)]
    for part in parts[:-1]:
        (kept,) = call(wide_add_kernel, [(piece, F32)], kept, part)
    grad_qkv, grad_out = call(
        functools.partial(last_kernel, qkv_rows),
        [((qkv_rows, width), F32), ((heads, width), F32)],
        kept, *parts[-1:],
    )
    return (grad_qkv.T[None], grad_out[None])


def solution(mesh):
    sections, shards = mesh.shape["section"], mesh.shape["dp"]
    planes = shards // PLANE

    def body(inputs, *rest):
        fits = shards % PLANE == 0 and planes & (planes - 1) == 0
        if sections == 2 and inputs.shape[0] == 2 and fits:
            return planar(inputs, *rest)
        return pipelined(inputs, *rest)

    return jax.shard_map(
        body,
        mesh=mesh,
        in_specs=(
            P(None, "dp", None),
            P(None, "dp", None),
            P(None, "dp", None),
            P("section", None),
            P("section", "dp", None),
            P("section", None, "dp"),
        ),
        out_specs=(P("section", "dp", None), P("section", None, "dp")),
        check_vma=False,
    )
```

```python
import functools

import jax
import jax.numpy as jnp
from jax import lax
from jax.experimental import pallas as pl
from jax.experimental.pallas import tpu as pltpu
from jax.sharding import PartitionSpec as P

F32 = jnp.float32
BF16 = jnp.bfloat16
PLANE = 4
VMEM_LIMIT = 16 * 1024 * 1024


def passed_along(block, axis, distance):
    devices = range(lax.axis_size(axis))
    route = [(i - distance, i) for i in devices if i - distance in devices]
    return lax.ppermute(block, axis, route)


def segments_of(lengths, count):
    ends = jnp.cumsum(lengths)
    position = jnp.arange(count, dtype=jnp.int32)
    return jnp.sum((position[:, None] >= ends[None, :]).astype(jnp.int32), axis=1)


def layer(x, gain, w_qkv, w_out, seg):
    head = w_out.shape[0]
    x_wide = x.astype(jnp.float32)
    scale = lax.rsqrt(jnp.mean(x_wide * x_wide, axis=-1, keepdims=True) + 1e-05)
    normed = (x_wide * scale * gain.astype(jnp.float32)).astype(jnp.bfloat16)
    qkv = jnp.dot(normed, w_qkv, preferred_element_type=jnp.float32).astype(jnp.bfloat16)
    query = qkv[:, :head]
    keys = qkv[:, head : 2 * head]
    values = qkv[:, 2 * head :]
    scores = jnp.dot(query, keys.T, preferred_element_type=jnp.float32) * head ** (-0.5)
    rows = jnp.arange(x.shape[0], dtype=jnp.int32)
    allowed = (seg[:, None] == seg[None, :]) & (rows[:, None] >= rows[None, :])
    scores = jnp.where(allowed, scores, -1e30)
    probs = jax.nn.softmax(scores, axis=-1).astype(jnp.bfloat16)
    attended = jnp.dot(probs, values, preferred_element_type=jnp.float32).astype(jnp.bfloat16)
    return (x_wide + jnp.dot(attended, w_out, preferred_element_type=jnp.float32)).astype(
        jnp.bfloat16
    )


def pipelined(inputs, cotangent, doc_lengths, norm_gain, w_qkv, w_out):
    sections = lax.axis_size("section")
    section = lax.axis_index("section")
    micro = inputs.shape[0]
    count = inputs.shape[1]
    segs = jax.vmap(lambda lens: segments_of(lens, count))(doc_lengths[:, 0, :])
    gain = norm_gain[0]
    full_qkv, full_out = (
        lax.all_gather(w_qkv[0], "dp", axis=0, tiled=True),
        lax.all_gather(w_out[0], "dp", axis=1, tiled=True),
    )
    total_steps = micro + sections - 1
    empty = jnp.zeros(inputs.shape[1:], inputs.dtype)

    def forward_at(step, incoming, saved):
        index = step - section
        live = (index >= 0) & (index < micro)
        slot = jnp.clip(index, 0, micro - 1)
        first = lax.dynamic_index_in_dim(inputs, slot, 0, keepdims=False)
        x = jnp.where(section == 0, first, incoming)
        seg = lax.dynamic_index_in_dim(segs, slot, 0, keepdims=False)
        out = layer(x, gain, full_qkv, full_out, seg)
        old = lax.dynamic_index_in_dim(saved, slot, 0, keepdims=False)
        saved = lax.dynamic_update_index_in_dim(saved, jnp.where(live, x, old), slot, 0)
        return (out, saved)

    def forward_step(carry, step):
        incoming, saved = carry
        out, saved = forward_at(step, incoming, saved)
        incoming = passed_along(out, "section", 1)
        return ((incoming, saved), None)

    start_saved = jnp.zeros(inputs.shape, inputs.dtype)
    (incoming, saved), _ = lax.scan(
        forward_step, (empty, start_saved), jnp.arange(total_steps - 1, dtype=jnp.int32)
    )
    _, saved = forward_at(jnp.int32(total_steps - 1), incoming, saved)

    def backward_at(step, incoming, sum_qkv, sum_out):
        index = step - (sections - 1 - section)
        live = (index >= 0) & (index < micro)
        slot = jnp.clip(index, 0, micro - 1)
        last = lax.dynamic_index_in_dim(cotangent, slot, 0, keepdims=False)
        grad_y = jnp.where(section == sections - 1, last, incoming)
        x = lax.dynamic_index_in_dim(saved, slot, 0, keepdims=False)
        seg = lax.dynamic_index_in_dim(segs, slot, 0, keepdims=False)
        _, pull = jax.vjp(lambda a, b, c: layer(a, gain, b, c, seg), x, full_qkv, full_out)
        grad_x, grad_q, grad_o = pull(grad_y)
        sum_qkv = sum_qkv + jnp.where(live, grad_q.astype(jnp.float32), 0.0)
        sum_out = sum_out + jnp.where(live, grad_o.astype(jnp.float32), 0.0)
        return (grad_x, sum_qkv, sum_out)

    def backward_step(carry, step):
        incoming, sum_qkv, sum_out = carry
        grad_x, sum_qkv, sum_out = backward_at(step, incoming, sum_qkv, sum_out)
        incoming = passed_along(grad_x, "section", -1)
        return ((incoming, sum_qkv, sum_out), None)

    zero_qkv = jnp.zeros(full_qkv.shape, jnp.float32)
    zero_out = jnp.zeros(full_out.shape, jnp.float32)
    (incoming, sum_qkv, sum_out), _ = lax.scan(
        backward_step, (empty, zero_qkv, zero_out), jnp.arange(total_steps - 1, dtype=jnp.int32)
    )
    _, sum_qkv, sum_out = backward_at(jnp.int32(total_steps - 1), incoming, sum_qkv, sum_out)
    share_qkv, share_out = (
        lax.psum_scatter(sum_qkv, "dp", scatter_dimension=0, tiled=True),
        lax.psum_scatter(sum_out, "dp", scatter_dimension=1, tiled=True),
    )
    return (share_qkv[None], share_out[None])


def nn(a, b):
    return lax.dot_general(a, b, (((1,), (0,)), ((), ())), preferred_element_type=F32)


def nt(a, b):
    return lax.dot_general(a, b, (((1,), (1,)), ((), ())), preferred_element_type=F32)


def block_copies(planes, index, k, refs, out_ref, sems):
    width = refs[0].shape[-1] // (planes * PLANE)
    section, p = index[0], index[2]
    copies = []
    for z in range(planes):
        at = pl.multiple_of((z * PLANE + (p ^ k)) * width, width)
        for half, ref in enumerate(refs):
            copies.append(
                pltpu.make_async_copy(
                    ref.at[section, :, pl.ds(at, width)],
                    out_ref.at[half, :, pl.ds(z * width, width)],
                    sems.at[len(copies)],
                )
            )
    return copies


def mark_kernel(planes, index, pack_ref, gain_ref, x_ref, c_ref, out_ref, block_ref, sems):
    copies = block_copies(planes, index, 0, (x_ref, c_ref), block_ref, sems)
    for copy in copies:
        copy.start()
    out_ref[: pack_ref.shape[0], :] = pack_ref[...]
    out_ref[pack_ref.shape[0] :, :] = gain_ref[...]
    for copy in copies:
        copy.wait()


def first_kernel(planes, index, qkv_ref, wout_ref, x_ref, c_ref, pack_ref, far_ref, pack_sems, sems):
    qkv_rows = qkv_ref.shape[0]
    copies = [
        pltpu.make_async_copy(qkv_ref, pack_ref.at[:qkv_rows], pack_sems.at[0]),
        pltpu.make_async_copy(wout_ref, pack_ref.at[qkv_rows:], pack_sems.at[1]),
    ] + block_copies(planes, index, PLANE - 1, (x_ref, c_ref), far_ref, sems)
    for copy in copies:
        copy.start()
    for copy in copies:
        copy.wait()


def blocks_kernel(planes, index, x_ref, c_ref, *refs):
    out_refs, sems = refs[:-1], refs[-1]
    copies = []
    for k, out_ref in enumerate(out_refs, 1):
        copies += block_copies(planes, index, k, (x_ref, c_ref), out_ref, sems.at[k - 1])
    for copy in copies:
        copy.start()
    for copy in copies:
        copy.wait()


def project_kernel(planes, heads, index, *refs):
    blocks, own, other = refs[:PLANE], refs[PLANE : PLANE + planes], refs[PLANE + planes : PLANE + 2 * planes]
    x_ref, c_ref, vx_ref, gain_ref = refs[PLANE + 2 * planes : PLANE + 2 * planes + 4]
    out_refs = refs[PLANE + 2 * planes + 4 : -4]
    vc_ref, sum_ref, *wide_refs = refs[-4:]
    qkv, width = 3 * heads, vx_ref.shape[-1]
    section, place, p = index[0], index[1], index[2]
    for ref, wide_ref in zip((own[0], other[0]), wide_refs):
        wide_ref[...] = ref[qkv + heads :, :].astype(F32)
    for z in range(planes):
        mine, theirs = (ref[pl.ds(z * PLANE + p, 1), :] for ref in wide_refs)
        gain_ref[z, 0:1, :] = jnp.where(section == 0, mine, theirs)
        gain_ref[z, 1:2, :] = jnp.where(section == 0, theirs, mine)
    for k in range(planes):
        at = place ^ k
        mine, theirs = own[k][: qkv + heads, :], other[k][: qkv + heads, :]
        zero = jnp.where(section == 0, mine, theirs)
        one = jnp.where(section == 0, theirs, mine)
        empty = jnp.zeros((heads, width), BF16)
        vx_ref[at, :qkv, :] = (zero[:qkv].astype(F32) * gain_ref[at, 0:1, :]).astype(BF16)
        vx_ref[at, qkv : qkv + heads, :] = zero[qkv : qkv + heads]
        vx_ref[at, qkv + heads : 2 * qkv + heads, :] = (one[:qkv].astype(F32) * gain_ref[at, 1:2, :]).astype(BF16)
        vx_ref[at, 2 * qkv + heads :, :] = empty
        vc_ref[at, :heads, :] = one[qkv : qkv + heads]
        vc_ref[at, heads:, :] = zero[qkv : qkv + heads]
    for k in range(PLANE):
        x_ref[p ^ k] = blocks[-k][0]
        c_ref[p ^ k] = blocks[-k][1]
    rows = x_ref.shape[0] * x_ref.shape[1]
    with_x = with_c = squares = products = None
    for z in range(planes):
        cols = slice(z * width, (z + 1) * width)
        x = x_ref[:, :, cols].reshape(rows, width)
        c = c_ref[:, :, cols].reshape(rows, width)
        wide = x.astype(F32)
        out = vx_ref[z, qkv : qkv + heads, :]
        right = jnp.concatenate([vx_ref[z, qkv + heads : 2 * qkv + heads, :], out], axis=0)
        new = nt(x, vx_ref[z]), nt(c, vc_ref[z]), jnp.sum(wide * wide, axis=1, keepdims=True), nt(out, right)
        if with_x is None:
            with_x, with_c, squares, products = new
        else:
            with_x, with_c = with_x + new[0], with_c + new[1]
            squares, products = squares + new[2], products + new[3]
    half = 2 * heads
    lane = lax.broadcasted_iota(jnp.int32, (rows, half), 1)
    high = squares.astype(BF16).astype(F32)
    last = jnp.where(lane == heads, high, jnp.where(lane == heads + 1, squares - high, with_x[:, 3 * half :]))
    sum_ref[:, : 3 * half] = with_x[:, : 3 * half].astype(BF16)
    sum_ref[:, 3 * half : 4 * half] = last.astype(BF16)
    sum_ref[:, 4 * half :] = with_c.astype(BF16)
    block = rows // PLANE
    for k in range(PLANE):
        start = pl.multiple_of((p ^ k) * block, block)
        out_refs[k][:, : 5 * half] = sum_ref[pl.ds(start, block), :]
        out_refs[k][:, 5 * half :] = products.astype(BF16)


def attention(qkv, allowed, heads):
    query, keys, values = (qkv[:, i * heads : (i + 1) * heads].astype(BF16) for i in range(3))
    scores = jnp.where(allowed, nt(query, keys) * heads ** (-0.5), -1e30)
    raised = jnp.exp(scores - jnp.max(scores, axis=1, keepdims=True))
    scale = 1.0 / jnp.sum(raised, axis=1, keepdims=True)
    return raised * scale, (nn(raised.astype(BF16), values) * scale).astype(BF16)


def attention_grad(qkv, probs, att, d_att, heads):
    query, keys, values = (qkv[:, i * heads : (i + 1) * heads].astype(BF16) for i in range(3))
    inner = jnp.sum(att.astype(F32) * d_att.astype(F32), axis=1, keepdims=True)
    d_values = nn(jnp.transpose(probs).astype(BF16), d_att)
    d_scores = probs * (nt(d_att, values) - inner) * heads ** (-0.5)
    d_query = nn(d_scores.astype(BF16), keys)
    d_keys = nn(jnp.transpose(d_scores).astype(BF16), query)
    return jnp.concatenate([d_query, d_keys, d_values], axis=1).astype(BF16).astype(F32)


def summed(parts):
    total = parts[0][...].astype(F32)
    for part in parts[1:]:
        total = total + part[...].astype(F32)
    return total


def chain_kernel(features, heads, index, docs, *refs):
    out_ref = refs[-1]
    qkv, half = 3 * heads, 2 * heads
    total = summed(refs[:-1])
    rows = total.shape[0]
    section = index[0]
    query_at = lax.broadcasted_iota(jnp.int32, (rows, rows), 0)
    key_at = lax.broadcasted_iota(jnp.int32, (rows, rows), 1)
    allowed = query_at >= key_at
    end = 0
    for i in range(docs.shape[2]):
        end = end + docs[section, 0, i]
        allowed = allowed & ((query_at >= end) == (key_at >= end))
    x_out = total[:, qkv : 2 * half]
    x_one = total[:, 2 * half : 2 * half + qkv]
    tail = total[:, 3 * half : 4 * half]
    c_one, c_zero = total[:, 4 * half : 4 * half + heads].astype(BF16), total[:, 4 * half + heads : 5 * half]
    lane = lax.broadcasted_iota(jnp.int32, tail.shape, 1)
    squares = jnp.sum(jnp.where((lane == heads) | (lane == heads + 1), tail, 0.0), axis=1, keepdims=True)
    mixed = total[:, 5 * half : 5 * half + qkv].astype(BF16)
    gram = total[:, 5 * half + qkv :].astype(BF16)

    scale0 = lax.rsqrt(squares / features + 1e-05)
    qkv0 = (total[:, :qkv] * scale0).astype(BF16).astype(F32)
    probs0, att0 = attention(qkv0, allowed, heads)
    wide0 = att0.astype(F32)
    y_out = x_out + nn(att0, gram)
    squares = squares + jnp.sum(wide0 * (x_out + y_out), axis=1, keepdims=True)
    scale1 = lax.rsqrt(jnp.maximum(squares, 0.0) / features + 1e-05)
    qkv1 = ((x_one + nn(att0, mixed)) * scale1).astype(BF16).astype(F32)
    probs1, att1 = attention(qkv1, allowed, heads)
    d_qkv1 = attention_grad(qkv1, probs1, att1, c_one, heads)
    inner = jnp.sum(d_qkv1 * qkv1, axis=1, keepdims=True) * scale1 * scale1 / features
    e1 = d_qkv1 * scale1
    d_att0 = c_zero + nt(e1.astype(BF16), mixed) - inner * y_out
    e0 = attention_grad(qkv0, probs0, att0, d_att0.astype(BF16), heads) * scale0
    factors = jnp.concatenate([e0, wide0, e1, wide0 * inner], axis=1).astype(BF16)
    for g in range(4):
        out_ref[g * rows : (g + 1) * rows, :] = factors[:, g * half : (g + 1) * half]
    wide1 = att1.astype(F32)
    out_ref[4 * rows :, :] = jnp.concatenate([wide1[: rows // 2], wide1[rows // 2 :]], axis=1).astype(BF16)


def pieces_of(planes, heads, order, index, turned, small, small_t, x_ref, c_ref, vx_ref, gain_ref, keep_ref, send_ref):
    qkv, half, width = 3 * heads, 2 * heads, vx_ref.shape[-1]
    section, place = index[0], index[1]
    rows = x_ref.shape[0] * x_ref.shape[1]
    att0, att1 = turned[qkv : qkv + heads], turned[4 * half : 4 * half + heads]
    for i, k in enumerate(order):
        z = place ^ k
        cols = pl.ds(pl.multiple_of(z * width, width), width)
        x = x_ref[:, :, cols].reshape(rows, width)
        c = c_ref[:, :, cols].reshape(rows, width)
        out = vx_ref[z, qkv : qkv + heads, :]
        with_x = nn(turned[: 4 * half], x)
        left = with_x[2 * half :] + nn(small, out)
        zero = with_x[:qkv] * gain_ref[z, 0:1, :]
        one = left[:qkv] * gain_ref[z, 1:2, :]
        keep_ref[i, :qkv, :] = jnp.where(section == 0, zero, one)
        send_ref[i, :qkv, :] = jnp.where(section == 0, one, zero).astype(BF16)
        zero = nn(att0, c) + nn(small_t, vx_ref[z, qkv + heads : 2 * qkv + heads, :]) - left[qkv:]
        one = nn(att1, c)
        keep_ref[i, qkv:, :] = jnp.where(section == 0, zero, one)
        send_ref[i, qkv:, :] = jnp.where(section == 0, one, zero).astype(BF16)


def far_grads_kernel(planes, heads, order, index, *refs):
    factors, arrays = refs[:PLANE], refs[PLANE : PLANE + 4]
    keep_ref, send_ref, turned_ref, small_ref, small_t_ref, all_ref = refs[PLANE + 4 :]
    qkv, half = 3 * heads, 2 * heads
    p = index[2]
    block = all_ref.shape[1]
    for k in range(PLANE):
        for g in range(4):
            all_ref[p ^ k, :, g * half : (g + 1) * half] = factors[k][g * block : (g + 1) * block, :]
        folded = factors[k][4 * block :, :]
        last = jnp.concatenate([folded[:, :heads].astype(F32), folded[:, heads:].astype(F32)], axis=0)
        all_ref[p ^ k, :, 4 * half :] = jnp.concatenate([last, jnp.zeros_like(last)], axis=1).astype(BF16)
    rows = all_ref.shape[0] * block
    turned = jnp.transpose(all_ref[...].astype(F32).reshape(rows, 5 * half)).astype(BF16)
    att0, right = turned[qkv : qkv + heads], turned[2 * half : 4 * half]
    small = nt(right, att0).astype(BF16)
    small_t = nt(att0, right[:qkv]).astype(BF16)
    turned_ref[...] = turned
    small_ref[...] = small
    small_t_ref[...] = small_t
    pieces_of(planes, heads, order, index, turned, small, small_t, *arrays, keep_ref, send_ref)


def near_grads_kernel(planes, heads, order, index, turned_ref, small_ref, small_t_ref, *refs):
    pieces_of(planes, heads, order, index, turned_ref[...], small_ref[...], small_t_ref[...], *refs)


def merge_kernel(keep_ref, come_ref, *out_refs):
    for i, out_ref in enumerate(out_refs):
        out_ref[...] = (keep_ref[i] + come_ref[i].astype(F32)).astype(out_ref.dtype)


def wide_add_kernel(a_ref, b_ref, out_ref):
    out_ref[...] = a_ref[...] + b_ref[...].astype(F32)


def add_kernel(a_ref, b_ref, out_ref):
    out_ref[...] = (a_ref[...].astype(F32) + b_ref[...].astype(F32)).astype(BF16)


def last_kernel(qkv_rows, keep_ref, *refs):
    parts, (qkv_ref, out_ref) = refs[:-2], refs[-2:]
    total = keep_ref[...]
    for part in parts:
        total = total + part[...].astype(F32)
    qkv_ref[...] = total[:qkv_rows]
    out_ref[...] = total[qkv_rows:]


def far_first(value, count, send):
    of = lambda k: value[k] if isinstance(value, (list, tuple)) else value
    got = {k: send(of(k), k) for k in reversed(range(1, count))}
    return [of(0)] + [got[k] for k in range(1, count)]


def call(kernel, outs, *args, scalars=0, scratch=()):
    smem = pl.BlockSpec(memory_space=pltpu.SMEM)
    vmem = pl.BlockSpec(memory_space=pltpu.VMEM)
    return pl.pallas_call(
        kernel,
        out_shape=[jax.ShapeDtypeStruct(shape, dtype) for shape, dtype in outs],
        in_specs=[smem] * scalars + [vmem] * (len(args) - scalars),
        out_specs=[vmem] * len(outs),
        scratch_shapes=[pltpu.VMEM(shape, dtype) for shape, dtype in scratch],
        compiler_params=pltpu.CompilerParams(vmem_limit_bytes=VMEM_LIMIT),
    )(*args)


def planar(inputs, cotangent, doc_lengths, norm_gain, w_qkv, w_out):
    shards = lax.axis_size("dp")
    planes = shards // PLANE
    section, place = lax.axis_index("section"), lax.axis_index("dp")
    z, p = place // PLANE, place % PLANE
    index = jnp.stack([section, z, p]).astype(jnp.int32)
    block, features = inputs.shape[1:]
    rows = PLANE * block
    heads, width = w_out.shape[1:]
    qkv_rows = w_qkv.shape[2]
    cols = planes * width
    def along_z(value, k):
        route = [(a * PLANE + b, (a ^ k) * PLANE + b) for a in range(planes) for b in range(PLANE)]
        return lax.ppermute(value, "dp", route)

    def to_sibling(value):
        return lax.ppermute(value, "section", [(0, 1), (1, 0)])

    def along_plane(value, k):
        route = [(a * PLANE + b, a * PLANE + (b ^ k)) for a in range(planes) for b in range(PLANE)]
        return lax.ppermute(value, "dp", route)

    def exchange(value):
        return far_first(value, PLANE, along_plane)

    smem, vmem = pl.BlockSpec(memory_space=pltpu.SMEM), pl.BlockSpec(memory_space=pltpu.VMEM)
    hbm = pl.BlockSpec(memory_space=pltpu.HBM)
    params = pltpu.CompilerParams(vmem_limit_bytes=VMEM_LIMIT)
    qkv_in, out_in, x_in, c_in = [
        pltpu.with_memory_space_constraint(value, pltpu.HBM)
        for value in (w_qkv[0].T, w_out[0], inputs, cotangent)
    ]
    one_block = jax.ShapeDtypeStruct((2, block, cols), BF16)
    pack, far_block = pl.pallas_call(
        functools.partial(first_kernel, planes),
        out_shape=[jax.ShapeDtypeStruct((qkv_rows + heads, width), BF16), one_block],
        in_specs=[smem] + [hbm] * 4,
        out_specs=[vmem] * 2,
        scratch_shapes=[pltpu.SemaphoreType.DMA((2,)), pltpu.SemaphoreType.DMA((2 * planes,))],
        compiler_params=params,
    )(index, qkv_in, out_in, x_in, c_in)
    blocks = pl.pallas_call(
        functools.partial(blocks_kernel, planes),
        out_shape=[one_block] * (PLANE - 2),
        in_specs=[smem] + [hbm] * 2,
        out_specs=[vmem] * (PLANE - 2),
        scratch_shapes=[pltpu.SemaphoreType.DMA((PLANE - 2, 2 * planes))],
        compiler_params=params,
    )(index, x_in, c_in)
    blocks = [*blocks, far_block]
    gain = norm_gain[0].reshape(shards, width)
    blocks = far_first([None] + blocks, PLANE, along_plane)
    pieces = {0: pack}
    for step in reversed([1 << bit for bit in range(planes.bit_length() - 1)]):
        for k in list(pieces):
            pieces[k ^ step] = along_z(pieces[k], step)
    mine, late_gain, _ = lax.optimization_barrier((pack, gain, blocks[3]))
    marked, blocks[0] = pl.pallas_call(
        functools.partial(mark_kernel, planes),
        out_shape=[jax.ShapeDtypeStruct((qkv_rows + heads + shards, width), BF16), one_block],
        in_specs=[smem] + [vmem] * 2 + [hbm] * 2,
        out_specs=[vmem] * 2,
        scratch_shapes=[pltpu.SemaphoreType.DMA((2 * planes,))],
        compiler_params=params,
    )(index, mine, late_gain, x_in, c_in)
    pieces[planes // 2], _ = lax.optimization_barrier((pieces[planes // 2], blocks[3]))
    own = [marked] + [pieces[k] for k in range(1, planes)]
    other = [to_sibling(piece) for piece in own]

    split = ((PLANE, block, cols), BF16)
    half = 2 * heads
    x, c, vx, gains, *sent = call(
        functools.partial(project_kernel, planes, heads),
        [split, split, ((planes, 4 * half, width), BF16), ((planes, 8, width), F32)]
        + [((block, 7 * half), BF16)] * PLANE,
        index, blocks[0], *blocks[:0:-1], *own, *other, scalars=1,
        scratch=[((planes, half, width), BF16), ((rows, 5 * half), BF16)] + [((shards, width), F32)] * 2,
    )
    (factors,) = call(
        functools.partial(chain_kernel, features, heads),
        [((9 * block // 2, half), BF16)],
        index, doc_lengths, *exchange(sent)[::-1], scalars=2,
    )
    piece = (qkv_rows + heads, width)
    far_order = tuple(reversed(range(planes - planes // 2, planes)))
    near_order = tuple(reversed(range(planes - planes // 2)))

    def swap_and_merge(order, keep, send):
        outs = [(piece, BF16 if k else F32) for k in order]
        return zip(order, call(merge_kernel, outs, keep, to_sibling(send)))

    keep, send, turned, small, small_t = call(
        functools.partial(far_grads_kernel, planes, heads, far_order),
        [((len(far_order),) + piece, F32), ((len(far_order),) + piece, BF16)]
        + [((5 * half, rows), BF16), ((2 * half, heads), BF16), ((heads, qkv_rows), BF16)],
        index, *exchange(factors), x, c, vx, gains, scalars=1,
        scratch=[((PLANE, block, 5 * half), BF16)],
    )
    pieces = dict(swap_and_merge(far_order, keep, send))
    keep, send = call(
        functools.partial(near_grads_kernel, planes, heads, near_order),
        [((len(near_order),) + piece, F32), ((len(near_order),) + piece, BF16)],
        index, turned, small, small_t, x, c, vx, gains, scalars=1,
    )
    pieces.update(swap_and_merge(near_order, keep, send))
    kept, parts = pieces[0], []
    held = []
    for step in [1 << bit for bit in range(planes.bit_length() - 1)]:
        got = {k ^ step: along_z(pieces.pop(k), step) for k in sorted(pieces, reverse=True) if k & step and k != step}
        if step in pieces:
            held.append((pieces.pop(step), step))
        for k, part in got.items():
            (pieces[k],) = call(add_kernel, [(piece, BF16)], pieces[k], part)
            held = [(lax.optimization_barrier((value, pieces[k]))[0], at) for value, at in held]
    parts = [along_z(value, at) for value, at in reversed(held)]
    for part in parts[:-1]:
        (kept,) = call(wide_add_kernel, [(piece, F32)], kept, part)
    grad_qkv, grad_out = call(
        functools.partial(last_kernel, qkv_rows),
        [((qkv_rows, width), F32), ((heads, width), F32)],
        kept, *parts[-1:],
    )
    return (grad_qkv.T[None], grad_out[None])


def solution(mesh):
    sections, shards = mesh.shape["section"], mesh.shape["dp"]
    planes = shards // PLANE

    def body(inputs, *rest):
        fits = shards % PLANE == 0 and planes & (planes - 1) == 0
        if sections == 2 and inputs.shape[0] == 2 and fits:
            return planar(inputs, *rest)
        return pipelined(inputs, *rest)

    return jax.shard_map(
        body,
        mesh=mesh,
        in_specs=(
            P(None, "dp", None),
            P(None, "dp", None),
            P(None, "dp", None),
            P("section", None),
            P("section", "dp", None),
            P("section", None, "dp"),
        ),
        out_specs=(P("section", "dp", None), P("section", None, "dp")),
        check_vma=False,
    )
```

```python
import functools

import jax
import jax.numpy as jnp
from jax import lax
from jax.experimental import pallas as pl
from jax.experimental.pallas import tpu as pltpu
from jax.sharding import PartitionSpec as P

F32 = jnp.float32
BF16 = jnp.bfloat16
PLANE = 4
VMEM_LIMIT = 16 * 1024 * 1024


def passed_along(block, axis, distance):
    devices = range(lax.axis_size(axis))
    route = [(i - distance, i) for i in devices if i - distance in devices]
    return lax.ppermute(block, axis, route)


def segments_of(lengths, count):
    ends = jnp.cumsum(lengths)
    position = jnp.arange(count, dtype=jnp.int32)
    return jnp.sum((position[:, None] >= ends[None, :]).astype(jnp.int32), axis=1)


def layer(x, gain, w_qkv, w_out, seg):
    head = w_out.shape[0]
    x_wide = x.astype(jnp.float32)
    scale = lax.rsqrt(jnp.mean(x_wide * x_wide, axis=-1, keepdims=True) + 1e-05)
    normed = (x_wide * scale * gain.astype(jnp.float32)).astype(jnp.bfloat16)
    qkv = jnp.dot(normed, w_qkv, preferred_element_type=jnp.float32).astype(jnp.bfloat16)
    query = qkv[:, :head]
    keys = qkv[:, head : 2 * head]
    values = qkv[:, 2 * head :]
    scores = jnp.dot(query, keys.T, preferred_element_type=jnp.float32) * head ** (-0.5)
    rows = jnp.arange(x.shape[0], dtype=jnp.int32)
    allowed = (seg[:, None] == seg[None, :]) & (rows[:, None] >= rows[None, :])
    scores = jnp.where(allowed, scores, -1e30)
    probs = jax.nn.softmax(scores, axis=-1).astype(jnp.bfloat16)
    attended = jnp.dot(probs, values, preferred_element_type=jnp.float32).astype(jnp.bfloat16)
    return (x_wide + jnp.dot(attended, w_out, preferred_element_type=jnp.float32)).astype(
        jnp.bfloat16
    )


def pipelined(inputs, cotangent, doc_lengths, norm_gain, w_qkv, w_out):
    sections = lax.axis_size("section")
    section = lax.axis_index("section")
    micro = inputs.shape[0]
    count = inputs.shape[1]
    segs = jax.vmap(lambda lens: segments_of(lens, count))(doc_lengths[:, 0, :])
    gain = norm_gain[0]
    full_qkv, full_out = (
        lax.all_gather(w_qkv[0], "dp", axis=0, tiled=True),
        lax.all_gather(w_out[0], "dp", axis=1, tiled=True),
    )
    total_steps = micro + sections - 1
    empty = jnp.zeros(inputs.shape[1:], inputs.dtype)

    def forward_at(step, incoming, saved):
        index = step - section
        live = (index >= 0) & (index < micro)
        slot = jnp.clip(index, 0, micro - 1)
        first = lax.dynamic_index_in_dim(inputs, slot, 0, keepdims=False)
        x = jnp.where(section == 0, first, incoming)
        seg = lax.dynamic_index_in_dim(segs, slot, 0, keepdims=False)
        out = layer(x, gain, full_qkv, full_out, seg)
        old = lax.dynamic_index_in_dim(saved, slot, 0, keepdims=False)
        saved = lax.dynamic_update_index_in_dim(saved, jnp.where(live, x, old), slot, 0)
        return (out, saved)

    def forward_step(carry, step):
        incoming, saved = carry
        out, saved = forward_at(step, incoming, saved)
        incoming = passed_along(out, "section", 1)
        return ((incoming, saved), None)

    start_saved = jnp.zeros(inputs.shape, inputs.dtype)
    (incoming, saved), _ = lax.scan(
        forward_step, (empty, start_saved), jnp.arange(total_steps - 1, dtype=jnp.int32)
    )
    _, saved = forward_at(jnp.int32(total_steps - 1), incoming, saved)

    def backward_at(step, incoming, sum_qkv, sum_out):
        index = step - (sections - 1 - section)
        live = (index >= 0) & (index < micro)
        slot = jnp.clip(index, 0, micro - 1)
        last = lax.dynamic_index_in_dim(cotangent, slot, 0, keepdims=False)
        grad_y = jnp.where(section == sections - 1, last, incoming)
        x = lax.dynamic_index_in_dim(saved, slot, 0, keepdims=False)
        seg = lax.dynamic_index_in_dim(segs, slot, 0, keepdims=False)
        _, pull = jax.vjp(lambda a, b, c: layer(a, gain, b, c, seg), x, full_qkv, full_out)
        grad_x, grad_q, grad_o = pull(grad_y)
        sum_qkv = sum_qkv + jnp.where(live, grad_q.astype(jnp.float32), 0.0)
        sum_out = sum_out + jnp.where(live, grad_o.astype(jnp.float32), 0.0)
        return (grad_x, sum_qkv, sum_out)

    def backward_step(carry, step):
        incoming, sum_qkv, sum_out = carry
        grad_x, sum_qkv, sum_out = backward_at(step, incoming, sum_qkv, sum_out)
        incoming = passed_along(grad_x, "section", -1)
        return ((incoming, sum_qkv, sum_out), None)

    zero_qkv = jnp.zeros(full_qkv.shape, jnp.float32)
    zero_out = jnp.zeros(full_out.shape, jnp.float32)
    (incoming, sum_qkv, sum_out), _ = lax.scan(
        backward_step, (empty, zero_qkv, zero_out), jnp.arange(total_steps - 1, dtype=jnp.int32)
    )
    _, sum_qkv, sum_out = backward_at(jnp.int32(total_steps - 1), incoming, sum_qkv, sum_out)
    share_qkv, share_out = (
        lax.psum_scatter(sum_qkv, "dp", scatter_dimension=0, tiled=True),
        lax.psum_scatter(sum_out, "dp", scatter_dimension=1, tiled=True),
    )
    return (share_qkv[None], share_out[None])


def nn(a, b):
    return lax.dot_general(a, b, (((1,), (0,)), ((), ())), preferred_element_type=F32)


def nt(a, b):
    return lax.dot_general(a, b, (((1,), (1,)), ((), ())), preferred_element_type=F32)


def block_copies(planes, index, k, refs, out_ref, sems):
    width = refs[0].shape[-1] // (planes * PLANE)
    section, p = index[0], index[2]
    copies = []
    for z in range(planes):
        at = pl.multiple_of((z * PLANE + (p ^ k)) * width, width)
        for half, ref in enumerate(refs):
            copies.append(
                pltpu.make_async_copy(
                    ref.at[section, :, pl.ds(at, width)],
                    out_ref.at[half, :, pl.ds(z * width, width)],
                    sems.at[len(copies)],
                )
            )
    return copies


def mark_kernel(planes, index, pack_ref, gain_ref, x_ref, c_ref, out_ref, block_ref, sems):
    copies = block_copies(planes, index, 0, (x_ref, c_ref), block_ref, sems)
    for copy in copies:
        copy.start()
    out_ref[: pack_ref.shape[0], :] = pack_ref[...]
    out_ref[pack_ref.shape[0] :, :] = gain_ref[...]
    for copy in copies:
        copy.wait()


def first_kernel(planes, index, qkv_ref, wout_ref, x_ref, c_ref, pack_ref, far_ref, pack_sems, sems):
    qkv_rows = qkv_ref.shape[0]
    copies = [
        pltpu.make_async_copy(qkv_ref, pack_ref.at[:qkv_rows], pack_sems.at[0]),
        pltpu.make_async_copy(wout_ref, pack_ref.at[qkv_rows:], pack_sems.at[1]),
    ] + block_copies(planes, index, PLANE - 1, (x_ref, c_ref), far_ref, sems)
    for copy in copies:
        copy.start()
    for copy in copies:
        copy.wait()


def blocks_kernel(planes, index, x_ref, c_ref, *refs):
    out_refs, sems = refs[:-1], refs[-1]
    copies = []
    for k, out_ref in enumerate(out_refs, 1):
        copies += block_copies(planes, index, k, (x_ref, c_ref), out_ref, sems.at[k - 1])
    for copy in copies:
        copy.start()
    for copy in copies:
        copy.wait()


def weights_of(heads, index, at, own, other, gain_refs, vx_ref, vc_ref, gain_ref, i):
    qkv, width = 3 * heads, vx_ref.shape[-1]
    section, p = index[0], index[2]
    mine, theirs = (ref[pl.ds(at * PLANE + p, 1), :] for ref in gain_refs)
    gain0, gain1 = jnp.where(section == 0, mine, theirs), jnp.where(section == 0, theirs, mine)
    gain_ref[i, 0:1, :] = gain0
    gain_ref[i, 1:2, :] = gain1
    zero, one = jnp.where(section == 0, own, other), jnp.where(section == 0, other, own)
    empty = jnp.zeros((heads, width), BF16)
    vx_ref[i, :qkv, :] = (zero[:qkv].astype(F32) * gain0).astype(BF16)
    vx_ref[i, qkv : qkv + heads, :] = zero[qkv:]
    vx_ref[i, qkv + heads : 2 * qkv + heads, :] = (one[:qkv].astype(F32) * gain1).astype(BF16)
    vx_ref[i, 2 * qkv + heads :, :] = empty
    vc_ref[i, :heads, :] = empty
    vc_ref[i, heads : 2 * heads, :] = one[qkv:]
    vc_ref[i, 2 * heads : 3 * heads, :] = zero[qkv:]
    vc_ref[i, 3 * heads :, :] = empty


def products_of(heads, x, c, vx_ref, vc_ref, i):
    qkv = 3 * heads
    wide = x.astype(F32)
    out = vx_ref[i, qkv : qkv + heads, :]
    right = jnp.concatenate([vx_ref[i, qkv + heads : 2 * qkv + heads, :], out], axis=0)
    return nt(x, vx_ref[i]), nt(c, vc_ref[i]), jnp.sum(wide * wide, axis=1, keepdims=True), nt(out, right)


def columns(ref, at, width):
    cols = pl.ds(pl.multiple_of(at * width, width), width)
    return ref[:, :, cols].reshape(ref.shape[0] * ref.shape[1], width)


def early_kernel(planes, heads, index, *refs):
    count = planes - 1
    blocks, own, other = refs[:PLANE], refs[PLANE : PLANE + count], refs[PLANE + count : PLANE + 2 * count]
    x_ref, c_ref, vx_ref, gain_ref, wide_ref, *sum_refs = refs[PLANE + 2 * count : -1]
    vc_ref = refs[-1]
    size, width = 4 * heads, vx_ref.shape[-1]
    place, p = index[1], index[2]
    rows_of_gain = planes * PLANE
    for i, ref in enumerate((own[0], other[0])):
        wide_ref[i * rows_of_gain : (i + 1) * rows_of_gain, :] = ref[size:, :].astype(F32)
    gain_refs = [wide_ref.at[i * rows_of_gain : (i + 1) * rows_of_gain] for i in range(2)]
    for k in range(PLANE):
        x_ref[p ^ k] = blocks[-k][0]
        c_ref[p ^ k] = blocks[-k][1]
    totals = None
    for k in range(count):
        at = place ^ k
        weights_of(heads, index, at, own[k][:size, :], other[k][:size, :], gain_refs, vx_ref, vc_ref, gain_ref, k)
        new = products_of(heads, columns(x_ref, at, width), columns(c_ref, at, width), vx_ref, vc_ref, k)
        totals = new if totals is None else [a + b for a, b in zip(totals, new)]
    for ref, total in zip(sum_refs, totals):
        ref[...] = jnp.broadcast_to(total, ref.shape)


def project_kernel(planes, heads, index, own, other, x_ref, c_ref, wide_ref, *refs):
    sums, (vx_ref, gain_ref) = refs[:4], refs[4:6]
    out_refs, (vc_ref, sum_ref) = refs[6:-2], refs[-2:]
    width = vx_ref.shape[-1]
    place, p = index[1], index[2]
    at = place ^ (planes - 1)
    rows_of_gain = planes * PLANE
    gain_refs = [wide_ref.at[i * rows_of_gain : (i + 1) * rows_of_gain] for i in range(2)]
    weights_of(heads, index, at, own[...], other[...], gain_refs, vx_ref, vc_ref, gain_ref, 0)
    new = products_of(heads, columns(x_ref, at, width), columns(c_ref, at, width), vx_ref, vc_ref, 0)
    with_x, with_c, products = (sums[i][...] + new[i] for i in (0, 1, 3))
    squares = sums[2][:, 0:1] + new[2]
    rows, half = with_x.shape[0], 2 * heads
    lane = lax.broadcasted_iota(jnp.int32, (rows, half), 1)
    high = squares.astype(BF16).astype(F32)
    last = jnp.where(lane == heads, high, jnp.where(lane == heads + 1, squares - high, with_c[:, half:]))
    sum_ref[:, : 3 * half] = with_x[:, : 3 * half].astype(BF16)
    sum_ref[:, 3 * half : 4 * half] = (with_x[:, 3 * half :] + with_c[:, :half]).astype(BF16)
    sum_ref[:, 4 * half :] = last.astype(BF16)
    block = rows // PLANE
    for k in range(PLANE):
        start = pl.multiple_of((p ^ k) * block, block)
        out_refs[k][:, : 5 * half] = sum_ref[pl.ds(start, block), :]
        out_refs[k][:, 5 * half :] = products.astype(BF16)


def attention(qkv, allowed, heads):
    query, keys, values = (qkv[:, i * heads : (i + 1) * heads].astype(BF16) for i in range(3))
    scores = jnp.where(allowed, nt(query, keys) * heads ** (-0.5), -1e30)
    raised = jnp.exp(scores - jnp.max(scores, axis=1, keepdims=True))
    scale = 1.0 / jnp.sum(raised, axis=1, keepdims=True)
    return raised * scale, (nn(raised.astype(BF16), values) * scale).astype(BF16)


def attention_grad(qkv, probs, att, d_att, heads):
    query, keys, values = (qkv[:, i * heads : (i + 1) * heads].astype(BF16) for i in range(3))
    inner = jnp.sum(att.astype(F32) * d_att.astype(F32), axis=1, keepdims=True)
    d_values = nn(jnp.transpose(probs).astype(BF16), d_att)
    d_scores = probs * (nt(d_att, values) - inner) * heads ** (-0.5)
    d_query = nn(d_scores.astype(BF16), keys)
    d_keys = nn(jnp.transpose(d_scores).astype(BF16), query)
    return jnp.concatenate([d_query, d_keys, d_values], axis=1).astype(BF16).astype(F32)


def summed(parts):
    total = parts[0][...].astype(F32)
    for part in parts[1:]:
        total = total + part[...].astype(F32)
    return total


def chain_kernel(features, heads, index, docs, *refs):
    out_ref = refs[-1]
    qkv, half = 3 * heads, 2 * heads
    total = summed(refs[:-1])
    rows = total.shape[0]
    section = index[0]
    query_at = lax.broadcasted_iota(jnp.int32, (rows, rows), 0)
    key_at = lax.broadcasted_iota(jnp.int32, (rows, rows), 1)
    allowed = query_at >= key_at
    end = 0
    for i in range(docs.shape[2]):
        end = end + docs[section, 0, i]
        allowed = allowed & ((query_at >= end) == (key_at >= end))
    x_out = total[:, qkv : 2 * half]
    x_one = total[:, 2 * half : 2 * half + qkv]
    tail = total[:, 4 * half : 5 * half]
    c_one, c_zero = total[:, 4 * half - heads : 4 * half].astype(BF16), tail[:, :heads]
    lane = lax.broadcasted_iota(jnp.int32, tail.shape, 1)
    squares = jnp.sum(jnp.where((lane == heads) | (lane == heads + 1), tail, 0.0), axis=1, keepdims=True)
    mixed = total[:, 5 * half : 5 * half + qkv].astype(BF16)
    gram = total[:, 5 * half + qkv :].astype(BF16)

    scale0 = lax.rsqrt(squares / features + 1e-05)
    qkv0 = (total[:, :qkv] * scale0).astype(BF16).astype(F32)
    probs0, att0 = attention(qkv0, allowed, heads)
    wide0 = att0.astype(F32)
    y_out = x_out + nn(att0, gram)
    squares = squares + jnp.sum(wide0 * (x_out + y_out), axis=1, keepdims=True)
    scale1 = lax.rsqrt(jnp.maximum(squares, 0.0) / features + 1e-05)
    qkv1 = ((x_one + nn(att0, mixed)) * scale1).astype(BF16).astype(F32)
    probs1, att1 = attention(qkv1, allowed, heads)
    d_qkv1 = attention_grad(qkv1, probs1, att1, c_one, heads)
    inner = jnp.sum(d_qkv1 * qkv1, axis=1, keepdims=True) * scale1 * scale1 / features
    e1 = d_qkv1 * scale1
    d_att0 = c_zero + nt(e1.astype(BF16), mixed) - inner * y_out
    e0 = attention_grad(qkv0, probs0, att0, d_att0.astype(BF16), heads) * scale0
    factors = [e0, wide0, e1, wide0 * inner, att1.astype(F32), jnp.zeros((rows, heads), F32)]
    out_ref[...] = jnp.concatenate(factors, axis=1).astype(BF16)


def pieces_of(heads, order, index, turned, small, small_t, x_ref, c_ref, weights, keep_ref, send_ref):
    qkv, half = 3 * heads, 2 * heads
    section, place = index[0], index[1]
    att0, att1 = turned[qkv : qkv + heads], turned[4 * half : 4 * half + heads]
    early_vx, late_vx, early_gain, late_gain = weights
    count = early_vx.shape[0]
    for i, k in enumerate(order):
        vx, gain = (early_vx.at[k], early_gain.at[k]) if k < count else (late_vx.at[0], late_gain.at[0])
        x = columns(x_ref, place ^ k, vx.shape[-1])
        c = columns(c_ref, place ^ k, vx.shape[-1])
        out = vx[qkv : qkv + heads, :]
        with_x = nn(turned[: 4 * half], x)
        left = with_x[2 * half :] + nn(small, out)
        zero = with_x[:qkv] * gain[0:1, :]
        one = left[:qkv] * gain[1:2, :]
        keep_ref[i, :qkv, :] = jnp.where(section == 0, zero, one)
        send_ref[i, :qkv, :] = jnp.where(section == 0, one, zero).astype(BF16)
        zero = nn(att0, c) + nn(small_t, vx[qkv + heads : 2 * qkv + heads, :]) - left[qkv:]
        one = nn(att1, c)
        keep_ref[i, qkv:, :] = jnp.where(section == 0, zero, one)
        send_ref[i, qkv:, :] = jnp.where(section == 0, one, zero).astype(BF16)


def far_grads_kernel(heads, order, index, *refs):
    factors, (x_ref, c_ref, *weights) = refs[:PLANE], refs[PLANE : PLANE + 6]
    keep_ref, send_ref, turned_ref, small_ref, small_t_ref, all_ref = refs[PLANE + 6 :]
    qkv, half = 3 * heads, 2 * heads
    p = index[2]
    for k in range(PLANE):
        all_ref[p ^ k] = factors[-k][...]
    rows = all_ref.shape[0] * all_ref.shape[1]
    turned = jnp.transpose(all_ref[...].astype(F32).reshape(rows, 5 * half)).astype(BF16)
    att0, right = turned[qkv : qkv + heads], turned[2 * half : 4 * half]
    small = nt(right, att0).astype(BF16)
    small_t = nt(att0, right[:qkv]).astype(BF16)
    turned_ref[...] = turned
    small_ref[...] = small
    small_t_ref[...] = small_t
    pieces_of(heads, order, index, turned, small, small_t, x_ref, c_ref, weights, keep_ref, send_ref)


def near_grads_kernel(heads, order, index, turned_ref, small_ref, small_t_ref, x_ref, c_ref, *refs):
    factors = turned_ref[...], small_ref[...], small_t_ref[...]
    pieces_of(heads, order, index, *factors, x_ref, c_ref, refs[:4], *refs[4:])


def merge_kernel(keep_ref, come_ref, *out_refs):
    for i, out_ref in enumerate(out_refs):
        out_ref[...] = (keep_ref[i] + come_ref[i].astype(F32)).astype(out_ref.dtype)


def wide_add_kernel(a_ref, b_ref, out_ref):
    out_ref[...] = a_ref[...] + b_ref[...].astype(F32)


def add_kernel(a_ref, b_ref, out_ref):
    out_ref[...] = (a_ref[...].astype(F32) + b_ref[...].astype(F32)).astype(BF16)


def last_kernel(qkv_rows, keep_ref, *refs):
    parts, (qkv_ref, out_ref) = refs[:-2], refs[-2:]
    total = keep_ref[...]
    for part in parts:
        total = total + part[...].astype(F32)
    qkv_ref[...] = total[:qkv_rows]
    out_ref[...] = total[qkv_rows:]


def far_first(value, count, send):
    of = lambda k: value[k] if isinstance(value, (list, tuple)) else value
    got = {k: send(of(k), k) for k in reversed(range(1, count))}
    return [of(0)] + [got[k] for k in range(1, count)]


def turned_round(values):
    return [values[0], *values[:0:-1]]


def call(kernel, outs, *args, scalars=0, scratch=()):
    smem = pl.BlockSpec(memory_space=pltpu.SMEM)
    vmem = pl.BlockSpec(memory_space=pltpu.VMEM)
    return pl.pallas_call(
        kernel,
        out_shape=[jax.ShapeDtypeStruct(shape, dtype) for shape, dtype in outs],
        in_specs=[smem] * scalars + [vmem] * (len(args) - scalars),
        out_specs=[vmem] * len(outs),
        scratch_shapes=[pltpu.VMEM(shape, dtype) for shape, dtype in scratch],
        compiler_params=pltpu.CompilerParams(vmem_limit_bytes=VMEM_LIMIT),
    )(*args)


def planar(inputs, cotangent, doc_lengths, norm_gain, w_qkv, w_out):
    shards = lax.axis_size("dp")
    planes = shards // PLANE
    section, place = lax.axis_index("section"), lax.axis_index("dp")
    z, p = place // PLANE, place % PLANE
    index = jnp.stack([section, z, p]).astype(jnp.int32)
    block, features = inputs.shape[1:]
    rows = PLANE * block
    heads, width = w_out.shape[1:]
    qkv_rows = w_qkv.shape[2]
    cols = planes * width
    def along_z(value, k):
        route = [(a * PLANE + b, (a ^ k) * PLANE + b) for a in range(planes) for b in range(PLANE)]
        return lax.ppermute(value, "dp", route)

    def to_sibling(value):
        return lax.ppermute(value, "section", [(0, 1), (1, 0)])

    def along_plane(value, k):
        route = [(a * PLANE + b, a * PLANE + (b ^ k)) for a in range(planes) for b in range(PLANE)]
        return lax.ppermute(value, "dp", route)

    def exchange(value):
        return far_first(value, PLANE, along_plane)

    smem, vmem = pl.BlockSpec(memory_space=pltpu.SMEM), pl.BlockSpec(memory_space=pltpu.VMEM)
    hbm = pl.BlockSpec(memory_space=pltpu.HBM)
    params = pltpu.CompilerParams(vmem_limit_bytes=VMEM_LIMIT)
    qkv_in, out_in, x_in, c_in = [
        pltpu.with_memory_space_constraint(value, pltpu.HBM)
        for value in (w_qkv[0].T, w_out[0], inputs, cotangent)
    ]
    one_block = jax.ShapeDtypeStruct((2, block, cols), BF16)
    pack, far_block = pl.pallas_call(
        functools.partial(first_kernel, planes),
        out_shape=[jax.ShapeDtypeStruct((qkv_rows + heads, width), BF16), one_block],
        in_specs=[smem] + [hbm] * 4,
        out_specs=[vmem] * 2,
        scratch_shapes=[pltpu.SemaphoreType.DMA((2,)), pltpu.SemaphoreType.DMA((2 * planes,))],
        compiler_params=params,
    )(index, qkv_in, out_in, x_in, c_in)
    blocks = pl.pallas_call(
        functools.partial(blocks_kernel, planes),
        out_shape=[one_block] * (PLANE - 2),
        in_specs=[smem] + [hbm] * 2,
        out_specs=[vmem] * (PLANE - 2),
        scratch_shapes=[pltpu.SemaphoreType.DMA((PLANE - 2, 2 * planes))],
        compiler_params=params,
    )(index, x_in, c_in)
    blocks = [*blocks, far_block]
    gain = norm_gain[0].reshape(shards, width)
    blocks = far_first([None] + blocks, PLANE, along_plane)
    pieces = {0: pack}
    for step in reversed([1 << bit for bit in range(planes.bit_length() - 1)]):
        for k in list(pieces):
            pieces[k ^ step] = along_z(pieces[k], step)
    mine, late_gain, _ = lax.optimization_barrier((pack, gain, pieces[1]))
    marked, blocks[0] = pl.pallas_call(
        functools.partial(mark_kernel, planes),
        out_shape=[jax.ShapeDtypeStruct((qkv_rows + heads + shards, width), BF16), one_block],
        in_specs=[smem] + [vmem] * 2 + [hbm] * 2,
        out_specs=[vmem] * 2,
        scratch_shapes=[pltpu.SemaphoreType.DMA((2 * planes,))],
        compiler_params=params,
    )(index, mine, late_gain, x_in, c_in)
    pieces[planes // 2], _ = lax.optimization_barrier((pieces[planes // 2], pieces[3]))
    pieces[1], _ = lax.optimization_barrier((pieces[1], blocks[3]))
    own = [marked] + [pieces[k] for k in range(1, planes)]
    other = [to_sibling(piece) for piece in own]

    split = ((PLANE, block, cols), BF16)
    half = 2 * heads
    sums = [((rows, 4 * half), F32), ((rows, 2 * half), F32), ((rows, 2 * heads), F32), ((heads, 2 * half), F32)]

    def weights(count):
        return [((count, 4 * half, width), BF16), ((count, 8, width), F32)]

    x, c, early_vx, early_gain, wide, *totals = call(
        functools.partial(early_kernel, planes, heads),
        [split, split] + weights(planes - 1) + [((2 * shards, width), F32)] + sums,
        index, blocks[0], *blocks[:0:-1], *own[:-1], *other[:-1], scalars=1,
        scratch=[((planes - 1, 2 * half, width), BF16)],
    )
    late_vx, late_gain, *sent = call(
        functools.partial(project_kernel, planes, heads),
        weights(1) + [((block, 7 * half), BF16)] * PLANE,
        index, own[-1], other[-1], x, c, wide, *totals, scalars=1,
        scratch=[((1, 2 * half, width), BF16), ((rows, 5 * half), BF16)],
    )
    arrays = x, c, early_vx, late_vx, early_gain, late_gain
    (factors,) = call(
        functools.partial(chain_kernel, features, heads),
        [((block, 5 * half), BF16)],
        index, doc_lengths, *exchange(sent)[::-1], scalars=2,
    )
    piece = (qkv_rows + heads, width)
    far_order = tuple(reversed(range(planes - planes // 2, planes)))
    near_order = tuple(reversed(range(planes - planes // 2)))

    def swap_and_merge(order, keep, send):
        outs = [(piece, BF16 if k else F32) for k in order]
        return zip(order, call(merge_kernel, outs, keep, to_sibling(send)))

    keep, send, turned, small, small_t = call(
        functools.partial(far_grads_kernel, heads, far_order),
        [((len(far_order),) + piece, F32), ((len(far_order),) + piece, BF16)]
        + [((5 * half, rows), BF16), ((2 * half, heads), BF16), ((heads, qkv_rows), BF16)],
        index, *turned_round(exchange(factors)), *arrays, scalars=1,
        scratch=[((PLANE, block, 5 * half), BF16)],
    )
    pieces = dict(swap_and_merge(far_order, keep, send))
    keep, send = call(
        functools.partial(near_grads_kernel, heads, near_order),
        [((len(near_order),) + piece, F32), ((len(near_order),) + piece, BF16)],
        index, turned, small, small_t, *arrays, scalars=1,
    )
    pieces.update(swap_and_merge(near_order, keep, send))
    kept, parts = pieces[0], []
    held = []
    for step in [1 << bit for bit in range(planes.bit_length() - 1)]:
        got = {k ^ step: along_z(pieces.pop(k), step) for k in sorted(pieces, reverse=True) if k & step and k != step}
        if step in pieces:
            held.append((pieces.pop(step), step))
        for k, part in got.items():
            (pieces[k],) = call(add_kernel, [(piece, BF16)], pieces[k], part)
            held = [(lax.optimization_barrier((value, pieces[k]))[0], at) for value, at in held]
    parts = [along_z(value, at) for value, at in reversed(held)]
    for part in parts[:-1]:
        (kept,) = call(wide_add_kernel, [(piece, F32)], kept, part)
    grad_qkv, grad_out = call(
        functools.partial(last_kernel, qkv_rows),
        [((qkv_rows, width), F32), ((heads, width), F32)],
        kept, *parts[-1:],
    )
    return (grad_qkv.T[None], grad_out[None])


def solution(mesh):
    sections, shards = mesh.shape["section"], mesh.shape["dp"]
    planes = shards // PLANE

    def body(inputs, *rest):
        fits = shards % PLANE == 0 and planes & (planes - 1) == 0
        if sections == 2 and inputs.shape[0] == 2 and fits:
            return planar(inputs, *rest)
        return pipelined(inputs, *rest)

    return jax.shard_map(
        body,
        mesh=mesh,
        in_specs=(
            P(None, "dp", None),
            P(None, "dp", None),
            P(None, "dp", None),
            P("section", None),
            P("section", "dp", None),
            P("section", None, "dp"),
        ),
        out_specs=(P("section", "dp", None), P("section", None, "dp")),
        check_vma=False,
    )
```

```python
import functools

import jax
import jax.numpy as jnp
from jax import lax
from jax.experimental import pallas as pl
from jax.experimental.pallas import tpu as pltpu
from jax.sharding import PartitionSpec as P

F32 = jnp.float32
BF16 = jnp.bfloat16
PLANE = 4
VMEM_LIMIT = 16 * 1024 * 1024


def passed_along(block, axis, distance):
    devices = range(lax.axis_size(axis))
    route = [(i - distance, i) for i in devices if i - distance in devices]
    return lax.ppermute(block, axis, route)


def segments_of(lengths, count):
    ends = jnp.cumsum(lengths)
    position = jnp.arange(count, dtype=jnp.int32)
    return jnp.sum((position[:, None] >= ends[None, :]).astype(jnp.int32), axis=1)


def layer(x, gain, w_qkv, w_out, seg):
    head = w_out.shape[0]
    x_wide = x.astype(jnp.float32)
    scale = lax.rsqrt(jnp.mean(x_wide * x_wide, axis=-1, keepdims=True) + 1e-05)
    normed = (x_wide * scale * gain.astype(jnp.float32)).astype(jnp.bfloat16)
    qkv = jnp.dot(normed, w_qkv, preferred_element_type=jnp.float32).astype(jnp.bfloat16)
    query = qkv[:, :head]
    keys = qkv[:, head : 2 * head]
    values = qkv[:, 2 * head :]
    scores = jnp.dot(query, keys.T, preferred_element_type=jnp.float32) * head ** (-0.5)
    rows = jnp.arange(x.shape[0], dtype=jnp.int32)
    allowed = (seg[:, None] == seg[None, :]) & (rows[:, None] >= rows[None, :])
    scores = jnp.where(allowed, scores, -1e30)
    probs = jax.nn.softmax(scores, axis=-1).astype(jnp.bfloat16)
    attended = jnp.dot(probs, values, preferred_element_type=jnp.float32).astype(jnp.bfloat16)
    return (x_wide + jnp.dot(attended, w_out, preferred_element_type=jnp.float32)).astype(
        jnp.bfloat16
    )


def pipelined(inputs, cotangent, doc_lengths, norm_gain, w_qkv, w_out):
    sections = lax.axis_size("section")
    section = lax.axis_index("section")
    micro = inputs.shape[0]
    count = inputs.shape[1]
    segs = jax.vmap(lambda lens: segments_of(lens, count))(doc_lengths[:, 0, :])
    gain = norm_gain[0]
    full_qkv, full_out = (
        lax.all_gather(w_qkv[0], "dp", axis=0, tiled=True),
        lax.all_gather(w_out[0], "dp", axis=1, tiled=True),
    )
    total_steps = micro + sections - 1
    empty = jnp.zeros(inputs.shape[1:], inputs.dtype)

    def forward_at(step, incoming, saved):
        index = step - section
        live = (index >= 0) & (index < micro)
        slot = jnp.clip(index, 0, micro - 1)
        first = lax.dynamic_index_in_dim(inputs, slot, 0, keepdims=False)
        x = jnp.where(section == 0, first, incoming)
        seg = lax.dynamic_index_in_dim(segs, slot, 0, keepdims=False)
        out = layer(x, gain, full_qkv, full_out, seg)
        old = lax.dynamic_index_in_dim(saved, slot, 0, keepdims=False)
        saved = lax.dynamic_update_index_in_dim(saved, jnp.where(live, x, old), slot, 0)
        return (out, saved)

    def forward_step(carry, step):
        incoming, saved = carry
        out, saved = forward_at(step, incoming, saved)
        incoming = passed_along(out, "section", 1)
        return ((incoming, saved), None)

    start_saved = jnp.zeros(inputs.shape, inputs.dtype)
    (incoming, saved), _ = lax.scan(
        forward_step, (empty, start_saved), jnp.arange(total_steps - 1, dtype=jnp.int32)
    )
    _, saved = forward_at(jnp.int32(total_steps - 1), incoming, saved)

    def backward_at(step, incoming, sum_qkv, sum_out):
        index = step - (sections - 1 - section)
        live = (index >= 0) & (index < micro)
        slot = jnp.clip(index, 0, micro - 1)
        last = lax.dynamic_index_in_dim(cotangent, slot, 0, keepdims=False)
        grad_y = jnp.where(section == sections - 1, last, incoming)
        x = lax.dynamic_index_in_dim(saved, slot, 0, keepdims=False)
        seg = lax.dynamic_index_in_dim(segs, slot, 0, keepdims=False)
        _, pull = jax.vjp(lambda a, b, c: layer(a, gain, b, c, seg), x, full_qkv, full_out)
        grad_x, grad_q, grad_o = pull(grad_y)
        sum_qkv = sum_qkv + jnp.where(live, grad_q.astype(jnp.float32), 0.0)
        sum_out = sum_out + jnp.where(live, grad_o.astype(jnp.float32), 0.0)
        return (grad_x, sum_qkv, sum_out)

    def backward_step(carry, step):
        incoming, sum_qkv, sum_out = carry
        grad_x, sum_qkv, sum_out = backward_at(step, incoming, sum_qkv, sum_out)
        incoming = passed_along(grad_x, "section", -1)
        return ((incoming, sum_qkv, sum_out), None)

    zero_qkv = jnp.zeros(full_qkv.shape, jnp.float32)
    zero_out = jnp.zeros(full_out.shape, jnp.float32)
    (incoming, sum_qkv, sum_out), _ = lax.scan(
        backward_step, (empty, zero_qkv, zero_out), jnp.arange(total_steps - 1, dtype=jnp.int32)
    )
    _, sum_qkv, sum_out = backward_at(jnp.int32(total_steps - 1), incoming, sum_qkv, sum_out)
    share_qkv, share_out = (
        lax.psum_scatter(sum_qkv, "dp", scatter_dimension=0, tiled=True),
        lax.psum_scatter(sum_out, "dp", scatter_dimension=1, tiled=True),
    )
    return (share_qkv[None], share_out[None])


def nn(a, b):
    return lax.dot_general(a, b, (((1,), (0,)), ((), ())), preferred_element_type=F32)


def nt(a, b):
    return lax.dot_general(a, b, (((1,), (1,)), ((), ())), preferred_element_type=F32)


def block_copies(planes, index, k, refs, out_ref, sems):
    width = refs[0].shape[-1] // (planes * PLANE)
    section, p = index[0], index[2]
    copies = []
    for z in range(planes):
        at = pl.multiple_of((z * PLANE + (p ^ k)) * width, width)
        for half, ref in enumerate(refs):
            copies.append(
                pltpu.make_async_copy(
                    ref.at[section, :, pl.ds(at, width)],
                    out_ref.at[half, :, pl.ds(z * width, width)],
                    sems.at[len(copies)],
                )
            )
    return copies


def mark_kernel(planes, index, pack_ref, gain_ref, x_ref, c_ref, out_ref, block_ref, sems):
    copies = block_copies(planes, index, 0, (x_ref, c_ref), block_ref, sems)
    for copy in copies:
        copy.start()
    out_ref[: pack_ref.shape[0], :] = pack_ref[...]
    out_ref[pack_ref.shape[0] :, :] = gain_ref[...]
    for copy in copies:
        copy.wait()


def first_kernel(planes, index, qkv_ref, wout_ref, x_ref, c_ref, pack_ref, far_ref, pack_sems, sems):
    qkv_rows = qkv_ref.shape[0]
    copies = [
        pltpu.make_async_copy(qkv_ref, pack_ref.at[:qkv_rows], pack_sems.at[0]),
        pltpu.make_async_copy(wout_ref, pack_ref.at[qkv_rows:], pack_sems.at[1]),
    ] + block_copies(planes, index, PLANE - 1, (x_ref, c_ref), far_ref, sems)
    for copy in copies:
        copy.start()
    for copy in copies:
        copy.wait()


def blocks_kernel(planes, index, x_ref, c_ref, *refs):
    out_refs, sems = refs[:-1], refs[-1]
    copies = []
    for k, out_ref in enumerate(out_refs, 1):
        copies += block_copies(planes, index, k, (x_ref, c_ref), out_ref, sems.at[k - 1])
    for copy in copies:
        copy.start()
    for copy in copies:
        copy.wait()


def project_kernel(planes, heads, index, *refs):
    blocks, own, other = refs[:PLANE], refs[PLANE : PLANE + planes], refs[PLANE + planes : PLANE + 2 * planes]
    x_ref, c_ref, vx_ref, gain_ref = refs[PLANE + 2 * planes : PLANE + 2 * planes + 4]
    out_refs = refs[PLANE + 2 * planes + 4 : -4]
    vc_ref, sum_ref, *wide_refs = refs[-4:]
    qkv, width = 3 * heads, vx_ref.shape[-1]
    section, place, p = index[0], index[1], index[2]
    for ref, wide_ref in zip((own[0], other[0]), wide_refs):
        wide_ref[...] = ref[qkv + heads :, :].astype(F32)
    for z in range(planes):
        mine, theirs = (ref[pl.ds(z * PLANE + p, 1), :] for ref in wide_refs)
        gain_ref[z, 0:1, :] = jnp.where(section == 0, mine, theirs)
        gain_ref[z, 1:2, :] = jnp.where(section == 0, theirs, mine)
    for k in range(planes):
        at = place ^ k
        mine, theirs = own[k][: qkv + heads, :], other[k][: qkv + heads, :]
        zero = jnp.where(section == 0, mine, theirs)
        one = jnp.where(section == 0, theirs, mine)
        empty = jnp.zeros((heads, width), BF16)
        vx_ref[at, :qkv, :] = (zero[:qkv].astype(F32) * gain_ref[at, 0:1, :]).astype(BF16)
        vx_ref[at, qkv : qkv + heads, :] = zero[qkv : qkv + heads]
        vx_ref[at, qkv + heads : 2 * qkv + heads, :] = (one[:qkv].astype(F32) * gain_ref[at, 1:2, :]).astype(BF16)
        vx_ref[at, 2 * qkv + heads :, :] = empty
        vc_ref[at, :heads, :] = one[qkv : qkv + heads]
        vc_ref[at, heads:, :] = zero[qkv : qkv + heads]
    for k in range(PLANE):
        x_ref[p ^ k] = blocks[-k][0]
        c_ref[p ^ k] = blocks[-k][1]
    rows = x_ref.shape[0] * x_ref.shape[1]
    with_x = with_c = squares = products = None
    for z in range(planes):
        cols = slice(z * width, (z + 1) * width)
        x = x_ref[:, :, cols].reshape(rows, width)
        c = c_ref[:, :, cols].reshape(rows, width)
        wide = x.astype(F32)
        out = vx_ref[z, qkv : qkv + heads, :]
        right = jnp.concatenate([vx_ref[z, qkv + heads : 2 * qkv + heads, :], out], axis=0)
        new = nt(x, vx_ref[z]), nt(c, vc_ref[z]), jnp.sum(wide * wide, axis=1, keepdims=True), nt(out, right)
        if with_x is None:
            with_x, with_c, squares, products = new
        else:
            with_x, with_c = with_x + new[0], with_c + new[1]
            squares, products = squares + new[2], products + new[3]
    half = 2 * heads
    lane = lax.broadcasted_iota(jnp.int32, (rows, half), 1)
    high = squares.astype(BF16).astype(F32)
    last = jnp.where(lane == heads, high, jnp.where(lane == heads + 1, squares - high, with_x[:, 3 * half :]))
    sum_ref[:, : 3 * half] = with_x[:, : 3 * half].astype(BF16)
    sum_ref[:, 3 * half : 4 * half] = last.astype(BF16)
    sum_ref[:, 4 * half :] = with_c.astype(BF16)
    block = rows // PLANE
    for k in range(PLANE):
        start = pl.multiple_of((p ^ k) * block, block)
        out_refs[k][:, : 5 * half] = sum_ref[pl.ds(start, block), :]
        out_refs[k][:, 5 * half :] = products.astype(BF16)


def attention(qkv, allowed, heads):
    query, keys, values = (qkv[:, i * heads : (i + 1) * heads].astype(BF16) for i in range(3))
    scores = jnp.where(allowed, nt(query, keys) * heads ** (-0.5), -1e30)
    raised = jnp.exp(scores - jnp.max(scores, axis=1, keepdims=True))
    scale = 1.0 / jnp.sum(raised, axis=1, keepdims=True)
    return raised * scale, (nn(raised.astype(BF16), values) * scale).astype(BF16)


def attention_grad(qkv, probs, att, d_att, heads):
    query, keys, values = (qkv[:, i * heads : (i + 1) * heads].astype(BF16) for i in range(3))
    inner = jnp.sum(att.astype(F32) * d_att.astype(F32), axis=1, keepdims=True)
    d_values = nn(jnp.transpose(probs).astype(BF16), d_att)
    d_scores = probs * (nt(d_att, values) - inner) * heads ** (-0.5)
    d_query = nn(d_scores.astype(BF16), keys)
    d_keys = nn(jnp.transpose(d_scores).astype(BF16), query)
    return jnp.concatenate([d_query, d_keys, d_values], axis=1).astype(BF16).astype(F32)


def summed(parts):
    total = parts[0][...].astype(F32)
    for part in parts[1:]:
        total = total + part[...].astype(F32)
    return total


def chain_kernel(features, heads, index, docs, *refs):
    out_ref = refs[-1]
    qkv, half = 3 * heads, 2 * heads
    total = summed(refs[:-1])
    rows = total.shape[0]
    section = index[0]
    query_at = lax.broadcasted_iota(jnp.int32, (rows, rows), 0)
    key_at = lax.broadcasted_iota(jnp.int32, (rows, rows), 1)
    allowed = query_at >= key_at
    end = 0
    for i in range(docs.shape[2]):
        end = end + docs[section, 0, i]
        allowed = allowed & ((query_at >= end) == (key_at >= end))
    x_out = total[:, qkv : 2 * half]
    x_one = total[:, 2 * half : 2 * half + qkv]
    tail = total[:, 3 * half : 4 * half]
    c_one, c_zero = total[:, 4 * half : 4 * half + heads].astype(BF16), total[:, 4 * half + heads : 5 * half]
    lane = lax.broadcasted_iota(jnp.int32, tail.shape, 1)
    squares = jnp.sum(jnp.where((lane == heads) | (lane == heads + 1), tail, 0.0), axis=1, keepdims=True)
    mixed = total[:, 5 * half : 5 * half + qkv].astype(BF16)
    gram = total[:, 5 * half + qkv :].astype(BF16)

    scale0 = lax.rsqrt(squares / features + 1e-05)
    qkv0 = (total[:, :qkv] * scale0).astype(BF16).astype(F32)
    probs0, att0 = attention(qkv0, allowed, heads)
    wide0 = att0.astype(F32)
    y_out = x_out + nn(att0, gram)
    squares = squares + jnp.sum(wide0 * (x_out + y_out), axis=1, keepdims=True)
    scale1 = lax.rsqrt(jnp.maximum(squares, 0.0) / features + 1e-05)
    qkv1 = ((x_one + nn(att0, mixed)) * scale1).astype(BF16).astype(F32)
    probs1, att1 = attention(qkv1, allowed, heads)
    d_qkv1 = attention_grad(qkv1, probs1, att1, c_one, heads)
    inner = jnp.sum(d_qkv1 * qkv1, axis=1, keepdims=True) * scale1 * scale1 / features
    e1 = d_qkv1 * scale1
    d_att0 = c_zero + nt(e1.astype(BF16), mixed) - inner * y_out
    e0 = attention_grad(qkv0, probs0, att0, d_att0.astype(BF16), heads) * scale0
    factors = jnp.concatenate([e0, wide0, e1, wide0 * inner], axis=1).astype(BF16)
    for g in range(4):
        out_ref[g * rows : (g + 1) * rows, :] = factors[:, g * half : (g + 1) * half]
    wide1 = att1.astype(F32)
    out_ref[4 * rows :, :] = jnp.concatenate([wide1[: rows // 2], wide1[rows // 2 :]], axis=1).astype(BF16)


def pieces_of(planes, heads, order, index, turned, small, small_t, x_ref, c_ref, vx_ref, gain_ref, keep_ref, send_ref):
    qkv, half, width = 3 * heads, 2 * heads, vx_ref.shape[-1]
    section, place = index[0], index[1]
    rows = x_ref.shape[0] * x_ref.shape[1]
    att0, att1 = turned[qkv : qkv + heads], turned[4 * half : 4 * half + heads]
    for i, k in enumerate(order):
        z = place ^ k
        cols = pl.ds(pl.multiple_of(z * width, width), width)
        x = x_ref[:, :, cols].reshape(rows, width)
        c = c_ref[:, :, cols].reshape(rows, width)
        out = vx_ref[z, qkv : qkv + heads, :]
        with_x = nn(turned[: 4 * half], x)
        left = with_x[2 * half :] + nn(small, out)
        zero = with_x[:qkv] * gain_ref[z, 0:1, :]
        one = left[:qkv] * gain_ref[z, 1:2, :]
        keep_ref[i, :qkv, :] = jnp.where(section == 0, zero, one)
        send_ref[i, :qkv, :] = jnp.where(section == 0, one, zero).astype(BF16)
        zero = nn(att0, c) + nn(small_t, vx_ref[z, qkv + heads : 2 * qkv + heads, :]) - left[qkv:]
        one = nn(att1, c)
        keep_ref[i, qkv:, :] = jnp.where(section == 0, zero, one)
        send_ref[i, qkv:, :] = jnp.where(section == 0, one, zero).astype(BF16)


def far_grads_kernel(planes, heads, order, index, *refs):
    factors, arrays = refs[:PLANE], refs[PLANE : PLANE + 4]
    keep_ref, send_ref, turned_ref, small_ref, small_t_ref, all_ref = refs[PLANE + 4 :]
    qkv, half = 3 * heads, 2 * heads
    p = index[2]
    block = all_ref.shape[1]
    for k in range(PLANE):
        for g in range(4):
            all_ref[p ^ k, :, g * half : (g + 1) * half] = factors[k][g * block : (g + 1) * block, :]
        folded = factors[k][4 * block :, :]
        last = jnp.concatenate([folded[:, :heads].astype(F32), folded[:, heads:].astype(F32)], axis=0)
        all_ref[p ^ k, :, 4 * half :] = jnp.concatenate([last, jnp.zeros_like(last)], axis=1).astype(BF16)
    rows = all_ref.shape[0] * block
    turned = jnp.transpose(all_ref[...].astype(F32).reshape(rows, 5 * half)).astype(BF16)
    att0, right = turned[qkv : qkv + heads], turned[2 * half : 4 * half]
    small = nt(right, att0).astype(BF16)
    small_t = nt(att0, right[:qkv]).astype(BF16)
    turned_ref[...] = turned
    small_ref[...] = small
    small_t_ref[...] = small_t
    pieces_of(planes, heads, order, index, turned, small, small_t, *arrays, keep_ref, send_ref)


def near_grads_kernel(planes, heads, order, index, turned_ref, small_ref, small_t_ref, *refs):
    pieces_of(planes, heads, order, index, turned_ref[...], small_ref[...], small_t_ref[...], *refs)


def merge_kernel(cuts, keep_ref, come_ref, *out_refs):
    rows = keep_ref.shape[1] // cuts
    for j, out_ref in enumerate(out_refs):
        here = slice(j % cuts * rows, (j % cuts + 1) * rows)
        out_ref[...] = (keep_ref[j // cuts, here] + come_ref[j // cuts, here].astype(F32)).astype(out_ref.dtype)


def wide_add_kernel(at, a_ref, part_ref, out_ref):
    rows = slice(at, at + part_ref.shape[0])
    out_ref[...] = a_ref[...]
    out_ref[rows, :] = a_ref[rows, :] + part_ref[...].astype(F32)


def add_kernel(a_ref, b_ref, out_ref):
    out_ref[...] = (a_ref[...].astype(F32) + b_ref[...].astype(F32)).astype(BF16)


def last_kernel(qkv_rows, keep_ref, *refs):
    parts, (qkv_ref, out_ref) = refs[:-2], refs[-2:]
    total = keep_ref[...]
    for part in parts:
        total = total + part[...].astype(F32)
    qkv_ref[...] = total[:qkv_rows]
    out_ref[...] = total[qkv_rows:]


def far_first(value, count, send):
    of = lambda k: value[k] if isinstance(value, (list, tuple)) else value
    got = {k: send(of(k), k) for k in reversed(range(1, count))}
    return [of(0)] + [got[k] for k in range(1, count)]


def call(kernel, outs, *args, scalars=0, scratch=()):
    smem = pl.BlockSpec(memory_space=pltpu.SMEM)
    vmem = pl.BlockSpec(memory_space=pltpu.VMEM)
    return pl.pallas_call(
        kernel,
        out_shape=[jax.ShapeDtypeStruct(shape, dtype) for shape, dtype in outs],
        in_specs=[smem] * scalars + [vmem] * (len(args) - scalars),
        out_specs=[vmem] * len(outs),
        scratch_shapes=[pltpu.VMEM(shape, dtype) for shape, dtype in scratch],
        compiler_params=pltpu.CompilerParams(vmem_limit_bytes=VMEM_LIMIT),
    )(*args)


def planar(inputs, cotangent, doc_lengths, norm_gain, w_qkv, w_out):
    shards = lax.axis_size("dp")
    planes = shards // PLANE
    section, place = lax.axis_index("section"), lax.axis_index("dp")
    z, p = place // PLANE, place % PLANE
    index = jnp.stack([section, z, p]).astype(jnp.int32)
    block, features = inputs.shape[1:]
    rows = PLANE * block
    heads, width = w_out.shape[1:]
    qkv_rows = w_qkv.shape[2]
    cols = planes * width
    def along_z(value, k):
        route = [(a * PLANE + b, (a ^ k) * PLANE + b) for a in range(planes) for b in range(PLANE)]
        return lax.ppermute(value, "dp", route)

    def to_sibling(value):
        return lax.ppermute(value, "section", [(0, 1), (1, 0)])

    def along_plane(value, k):
        route = [(a * PLANE + b, a * PLANE + (b ^ k)) for a in range(planes) for b in range(PLANE)]
        return lax.ppermute(value, "dp", route)

    def exchange(value):
        return far_first(value, PLANE, along_plane)

    smem, vmem = pl.BlockSpec(memory_space=pltpu.SMEM), pl.BlockSpec(memory_space=pltpu.VMEM)
    hbm = pl.BlockSpec(memory_space=pltpu.HBM)
    params = pltpu.CompilerParams(vmem_limit_bytes=VMEM_LIMIT)
    qkv_in, out_in, x_in, c_in = [
        pltpu.with_memory_space_constraint(value, pltpu.HBM)
        for value in (w_qkv[0].T, w_out[0], inputs, cotangent)
    ]
    one_block = jax.ShapeDtypeStruct((2, block, cols), BF16)
    pack, far_block = pl.pallas_call(
        functools.partial(first_kernel, planes),
        out_shape=[jax.ShapeDtypeStruct((qkv_rows + heads, width), BF16), one_block],
        in_specs=[smem] + [hbm] * 4,
        out_specs=[vmem] * 2,
        scratch_shapes=[pltpu.SemaphoreType.DMA((2,)), pltpu.SemaphoreType.DMA((2 * planes,))],
        compiler_params=params,
    )(index, qkv_in, out_in, x_in, c_in)
    blocks = pl.pallas_call(
        functools.partial(blocks_kernel, planes),
        out_shape=[one_block] * (PLANE - 2),
        in_specs=[smem] + [hbm] * 2,
        out_specs=[vmem] * (PLANE - 2),
        scratch_shapes=[pltpu.SemaphoreType.DMA((PLANE - 2, 2 * planes))],
        compiler_params=params,
    )(index, x_in, c_in)
    blocks = [*blocks, far_block]
    gain = norm_gain[0].reshape(shards, width)
    blocks = far_first([None] + blocks, PLANE, along_plane)
    pieces = {0: pack}
    for step in reversed([1 << bit for bit in range(planes.bit_length() - 1)]):
        for k in list(pieces):
            pieces[k ^ step] = along_z(pieces[k], step)
    mine, late_gain, _ = lax.optimization_barrier((pack, gain, blocks[3]))
    marked, blocks[0] = pl.pallas_call(
        functools.partial(mark_kernel, planes),
        out_shape=[jax.ShapeDtypeStruct((qkv_rows + heads + shards, width), BF16), one_block],
        in_specs=[smem] + [vmem] * 2 + [hbm] * 2,
        out_specs=[vmem] * 2,
        scratch_shapes=[pltpu.SemaphoreType.DMA((2 * planes,))],
        compiler_params=params,
    )(index, mine, late_gain, x_in, c_in)
    pieces[planes // 2], _ = lax.optimization_barrier((pieces[planes // 2], blocks[3]))
    own = [marked] + [pieces[k] for k in range(1, planes)]
    other = [to_sibling(piece) for piece in own]

    split = ((PLANE, block, cols), BF16)
    half = 2 * heads
    x, c, vx, gains, *sent = call(
        functools.partial(project_kernel, planes, heads),
        [split, split, ((planes, 4 * half, width), BF16), ((planes, 8, width), F32)]
        + [((block, 7 * half), BF16)] * PLANE,
        index, blocks[0], *blocks[:0:-1], *own, *other, scalars=1,
        scratch=[((planes, half, width), BF16), ((rows, 5 * half), BF16)] + [((shards, width), F32)] * 2,
    )
    (factors,) = call(
        functools.partial(chain_kernel, features, heads),
        [((9 * block // 2, half), BF16)],
        index, doc_lengths, *exchange(sent)[::-1], scalars=2,
    )
    piece = (qkv_rows + heads, width)
    far_order = tuple(reversed(range(planes - planes // 2, planes)))
    near_order = tuple(reversed(range(planes - planes // 2)))

    def swap_and_merge(order, keep, send, cuts):
        outs = [((piece[0] // cuts, width), BF16 if k else F32) for k in order for _ in range(cuts)]
        cut = call(functools.partial(merge_kernel, cuts), outs, keep, to_sibling(send))
        return {k: list(cut[i * cuts : (i + 1) * cuts]) for i, k in enumerate(order)}

    keep, send, turned, small, small_t = call(
        functools.partial(far_grads_kernel, planes, heads, far_order),
        [((len(far_order),) + piece, F32), ((len(far_order),) + piece, BF16)]
        + [((5 * half, rows), BF16), ((2 * half, heads), BF16), ((heads, qkv_rows), BF16)],
        index, *exchange(factors), x, c, vx, gains, scalars=1,
        scratch=[((PLANE, block, 5 * half), BF16)],
    )
    pieces = swap_and_merge(far_order, keep, send, 2)
    keep, send = call(
        functools.partial(near_grads_kernel, planes, heads, near_order),
        [((len(near_order),) + piece, F32), ((len(near_order),) + piece, BF16)],
        index, turned, small, small_t, x, c, vx, gains, scalars=1,
    )
    pieces.update(swap_and_merge(near_order, keep, send, 1))
    (kept,), held = pieces[0], []
    for step in [1 << bit for bit in range(planes.bit_length() - 1)]:
        senders = [k for k in sorted(pieces, reverse=True) if k & step and k != step]
        got = {k ^ step: [along_z(part, step) for part in pieces.pop(k)] for k in senders}
        if step in pieces:
            held.append((pieces.pop(step), step))
        for k, come in got.items():
            pieces[k] = [call(add_kernel, [(a.shape, BF16)], a, b)[0] for a, b in zip(pieces[k], come)]
            held = [
                (parts, at) for parts, at in held
            ]
    parts = [[along_z(part, at) for part in value] for value, at in reversed(held)]
    for come in parts[:-1]:
        for i, part in enumerate(come):
            (kept,) = call(functools.partial(wide_add_kernel, i * part.shape[0]), [(piece, F32)], kept, part)
    grad_qkv, grad_out = call(
        functools.partial(last_kernel, qkv_rows),
        [((qkv_rows, width), F32), ((heads, width), F32)],
        kept, *(parts[-1] if parts else []),
    )
    return (grad_qkv.T[None], grad_out[None])


def solution(mesh):
    sections, shards = mesh.shape["section"], mesh.shape["dp"]
    planes = shards // PLANE

    def body(inputs, *rest):
        fits = shards % PLANE == 0 and planes & (planes - 1) == 0
        if sections == 2 and inputs.shape[0] == 2 and fits:
            return planar(inputs, *rest)
        return pipelined(inputs, *rest)

    return jax.shard_map(
        body,
        mesh=mesh,
        in_specs=(
            P(None, "dp", None),
            P(None, "dp", None),
            P(None, "dp", None),
            P("section", None),
            P("section", "dp", None),
            P("section", None, "dp"),
        ),
        out_specs=(P("section", "dp", None), P("section", None, "dp")),
        check_vma=False,
    )
```

```python
import functools

import jax
import jax.numpy as jnp
from jax import lax
from jax.experimental import pallas as pl
from jax.experimental.pallas import tpu as pltpu
from jax.sharding import PartitionSpec as P

F32 = jnp.float32
BF16 = jnp.bfloat16
PLANE = 4
VMEM_LIMIT = 16 * 1024 * 1024


def passed_along(block, axis, distance):
    devices = range(lax.axis_size(axis))
    route = [(i - distance, i) for i in devices if i - distance in devices]
    return lax.ppermute(block, axis, route)


def segments_of(lengths, count):
    ends = jnp.cumsum(lengths)
    position = jnp.arange(count, dtype=jnp.int32)
    return jnp.sum((position[:, None] >= ends[None, :]).astype(jnp.int32), axis=1)


def layer(x, gain, w_qkv, w_out, seg):
    head = w_out.shape[0]
    x_wide = x.astype(jnp.float32)
    scale = lax.rsqrt(jnp.mean(x_wide * x_wide, axis=-1, keepdims=True) + 1e-05)
    normed = (x_wide * scale * gain.astype(jnp.float32)).astype(jnp.bfloat16)
    qkv = jnp.dot(normed, w_qkv, preferred_element_type=jnp.float32).astype(jnp.bfloat16)
    query = qkv[:, :head]
    keys = qkv[:, head : 2 * head]
    values = qkv[:, 2 * head :]
    scores = jnp.dot(query, keys.T, preferred_element_type=jnp.float32) * head ** (-0.5)
    rows = jnp.arange(x.shape[0], dtype=jnp.int32)
    allowed = (seg[:, None] == seg[None, :]) & (rows[:, None] >= rows[None, :])
    scores = jnp.where(allowed, scores, -1e30)
    probs = jax.nn.softmax(scores, axis=-1).astype(jnp.bfloat16)
    attended = jnp.dot(probs, values, preferred_element_type=jnp.float32).astype(jnp.bfloat16)
    return (x_wide + jnp.dot(attended, w_out, preferred_element_type=jnp.float32)).astype(
        jnp.bfloat16
    )


def pipelined(inputs, cotangent, doc_lengths, norm_gain, w_qkv, w_out):
    sections = lax.axis_size("section")
    section = lax.axis_index("section")
    micro = inputs.shape[0]
    count = inputs.shape[1]
    segs = jax.vmap(lambda lens: segments_of(lens, count))(doc_lengths[:, 0, :])
    gain = norm_gain[0]
    full_qkv, full_out = (
        lax.all_gather(w_qkv[0], "dp", axis=0, tiled=True),
        lax.all_gather(w_out[0], "dp", axis=1, tiled=True),
    )
    total_steps = micro + sections - 1
    empty = jnp.zeros(inputs.shape[1:], inputs.dtype)

    def forward_at(step, incoming, saved):
        index = step - section
        live = (index >= 0) & (index < micro)
        slot = jnp.clip(index, 0, micro - 1)
        first = lax.dynamic_index_in_dim(inputs, slot, 0, keepdims=False)
        x = jnp.where(section == 0, first, incoming)
        seg = lax.dynamic_index_in_dim(segs, slot, 0, keepdims=False)
        out = layer(x, gain, full_qkv, full_out, seg)
        old = lax.dynamic_index_in_dim(saved, slot, 0, keepdims=False)
        saved = lax.dynamic_update_index_in_dim(saved, jnp.where(live, x, old), slot, 0)
        return (out, saved)

    def forward_step(carry, step):
        incoming, saved = carry
        out, saved = forward_at(step, incoming, saved)
        incoming = passed_along(out, "section", 1)
        return ((incoming, saved), None)

    start_saved = jnp.zeros(inputs.shape, inputs.dtype)
    (incoming, saved), _ = lax.scan(
        forward_step, (empty, start_saved), jnp.arange(total_steps - 1, dtype=jnp.int32)
    )
    _, saved = forward_at(jnp.int32(total_steps - 1), incoming, saved)

    def backward_at(step, incoming, sum_qkv, sum_out):
        index = step - (sections - 1 - section)
        live = (index >= 0) & (index < micro)
        slot = jnp.clip(index, 0, micro - 1)
        last = lax.dynamic_index_in_dim(cotangent, slot, 0, keepdims=False)
        grad_y = jnp.where(section == sections - 1, last, incoming)
        x = lax.dynamic_index_in_dim(saved, slot, 0, keepdims=False)
        seg = lax.dynamic_index_in_dim(segs, slot, 0, keepdims=False)
        _, pull = jax.vjp(lambda a, b, c: layer(a, gain, b, c, seg), x, full_qkv, full_out)
        grad_x, grad_q, grad_o = pull(grad_y)
        sum_qkv = sum_qkv + jnp.where(live, grad_q.astype(jnp.float32), 0.0)
        sum_out = sum_out + jnp.where(live, grad_o.astype(jnp.float32), 0.0)
        return (grad_x, sum_qkv, sum_out)

    def backward_step(carry, step):
        incoming, sum_qkv, sum_out = carry
        grad_x, sum_qkv, sum_out = backward_at(step, incoming, sum_qkv, sum_out)
        incoming = passed_along(grad_x, "section", -1)
        return ((incoming, sum_qkv, sum_out), None)

    zero_qkv = jnp.zeros(full_qkv.shape, jnp.float32)
    zero_out = jnp.zeros(full_out.shape, jnp.float32)
    (incoming, sum_qkv, sum_out), _ = lax.scan(
        backward_step, (empty, zero_qkv, zero_out), jnp.arange(total_steps - 1, dtype=jnp.int32)
    )
    _, sum_qkv, sum_out = backward_at(jnp.int32(total_steps - 1), incoming, sum_qkv, sum_out)
    share_qkv, share_out = (
        lax.psum_scatter(sum_qkv, "dp", scatter_dimension=0, tiled=True),
        lax.psum_scatter(sum_out, "dp", scatter_dimension=1, tiled=True),
    )
    return (share_qkv[None], share_out[None])


def nn(a, b):
    return lax.dot_general(a, b, (((1,), (0,)), ((), ())), preferred_element_type=F32)


def nt(a, b):
    return lax.dot_general(a, b, (((1,), (1,)), ((), ())), preferred_element_type=F32)


def block_copies(planes, index, k, refs, out_ref, sems):
    width = refs[0].shape[-1] // (planes * PLANE)
    section, p = index[0], index[2]
    copies = []
    for z in range(planes):
        at = pl.multiple_of((z * PLANE + (p ^ k)) * width, width)
        for half, ref in enumerate(refs):
            copies.append(
                pltpu.make_async_copy(
                    ref.at[section, :, pl.ds(at, width)],
                    out_ref.at[half, :, pl.ds(z * width, width)],
                    sems.at[len(copies)],
                )
            )
    return copies


def mark_kernel(planes, index, pack_ref, gain_ref, x_ref, c_ref, out_ref, block_ref, sems):
    copies = block_copies(planes, index, 0, (x_ref, c_ref), block_ref, sems)
    for copy in copies:
        copy.start()
    out_ref[: pack_ref.shape[0], :] = pack_ref[...]
    out_ref[pack_ref.shape[0] :, :] = gain_ref[...]
    for copy in copies:
        copy.wait()


def first_kernel(planes, index, qkv_ref, wout_ref, x_ref, c_ref, pack_ref, near_ref, pack_sems, sems):
    qkv_rows = qkv_ref.shape[0]
    copies = [
        pltpu.make_async_copy(qkv_ref, pack_ref.at[:qkv_rows], pack_sems.at[0]),
        pltpu.make_async_copy(wout_ref, pack_ref.at[qkv_rows:], pack_sems.at[1]),
    ] + block_copies(planes, index, 1, (x_ref, c_ref), near_ref, sems)
    for copy in copies:
        copy.start()
    for copy in copies:
        copy.wait()


def blocks_kernel(planes, index, x_ref, c_ref, *refs):
    out_refs, sems = refs[:-1], refs[-1]
    copies = []
    for k, out_ref in enumerate(out_refs, 2):
        copies += block_copies(planes, index, k, (x_ref, c_ref), out_ref, sems.at[k - 2])
    for copy in copies:
        copy.start()
    for copy in copies:
        copy.wait()


def project_kernel(planes, heads, index, *refs):
    blocks, own, other = refs[:PLANE], refs[PLANE : PLANE + planes], refs[PLANE + planes : PLANE + 2 * planes]
    x_ref, c_ref, vx_ref, gain_ref = refs[PLANE + 2 * planes : PLANE + 2 * planes + 4]
    out_refs = refs[PLANE + 2 * planes + 4 : -4]
    vc_ref, sum_ref, *wide_refs = refs[-4:]
    qkv, width = 3 * heads, vx_ref.shape[-1]
    section, place, p = index[0], index[1], index[2]
    for ref, wide_ref in zip((own[0], other[0]), wide_refs):
        wide_ref[...] = ref[qkv + heads :, :].astype(F32)
    for z in range(planes):
        mine, theirs = (ref[pl.ds(z * PLANE + p, 1), :] for ref in wide_refs)
        gain_ref[z, 0:1, :] = jnp.where(section == 0, mine, theirs)
        gain_ref[z, 1:2, :] = jnp.where(section == 0, theirs, mine)
    for k in range(planes):
        at = place ^ k
        mine, theirs = own[k][: qkv + heads, :], other[k][: qkv + heads, :]
        zero = jnp.where(section == 0, mine, theirs)
        one = jnp.where(section == 0, theirs, mine)
        empty = jnp.zeros((heads, width), BF16)
        vx_ref[at, :qkv, :] = (zero[:qkv].astype(F32) * gain_ref[at, 0:1, :]).astype(BF16)
        vx_ref[at, qkv : qkv + heads, :] = zero[qkv : qkv + heads]
        vx_ref[at, qkv + heads : 2 * qkv + heads, :] = (one[:qkv].astype(F32) * gain_ref[at, 1:2, :]).astype(BF16)
        vx_ref[at, 2 * qkv + heads :, :] = empty
        vc_ref[at, :heads, :] = one[qkv : qkv + heads]
        vc_ref[at, heads:, :] = zero[qkv : qkv + heads]
    for k in range(PLANE):
        x_ref[p ^ k] = blocks[-k][0]
        c_ref[p ^ k] = blocks[-k][1]
    rows = x_ref.shape[0] * x_ref.shape[1]
    with_x = with_c = squares = products = None
    for z in range(planes):
        cols = slice(z * width, (z + 1) * width)
        x = x_ref[:, :, cols].reshape(rows, width)
        c = c_ref[:, :, cols].reshape(rows, width)
        wide = x.astype(F32)
        out = vx_ref[z, qkv : qkv + heads, :]
        right = jnp.concatenate([vx_ref[z, qkv + heads : 2 * qkv + heads, :], out], axis=0)
        new = nt(x, vx_ref[z]), nt(c, vc_ref[z]), jnp.sum(wide * wide, axis=1, keepdims=True), nt(out, right)
        if with_x is None:
            with_x, with_c, squares, products = new
        else:
            with_x, with_c = with_x + new[0], with_c + new[1]
            squares, products = squares + new[2], products + new[3]
    half = 2 * heads
    lane = lax.broadcasted_iota(jnp.int32, (rows, half), 1)
    high = squares.astype(BF16).astype(F32)
    last = jnp.where(lane == heads, high, jnp.where(lane == heads + 1, squares - high, with_x[:, 3 * half :]))
    sum_ref[:, : 3 * half] = with_x[:, : 3 * half].astype(BF16)
    sum_ref[:, 3 * half : 4 * half] = last.astype(BF16)
    sum_ref[:, 4 * half :] = with_c.astype(BF16)
    block = rows // PLANE
    for k in range(PLANE):
        start = pl.multiple_of((p ^ k) * block, block)
        out_refs[k][:, : 5 * half] = sum_ref[pl.ds(start, block), :]
        out_refs[k][:, 5 * half :] = products.astype(BF16)


def attention(qkv, allowed, heads):
    query, keys, values = (qkv[:, i * heads : (i + 1) * heads].astype(BF16) for i in range(3))
    scores = jnp.where(allowed, nt(query, keys) * heads ** (-0.5), -1e30)
    raised = jnp.exp(scores - jnp.max(scores, axis=1, keepdims=True))
    scale = 1.0 / jnp.sum(raised, axis=1, keepdims=True)
    return raised * scale, (nn(raised.astype(BF16), values) * scale).astype(BF16)


def attention_grad(qkv, probs, att, d_att, heads):
    query, keys, values = (qkv[:, i * heads : (i + 1) * heads].astype(BF16) for i in range(3))
    inner = jnp.sum(att.astype(F32) * d_att.astype(F32), axis=1, keepdims=True)
    d_values = nn(jnp.transpose(probs).astype(BF16), d_att)
    d_scores = probs * (nt(d_att, values) - inner) * heads ** (-0.5)
    d_query = nn(d_scores.astype(BF16), keys)
    d_keys = nn(jnp.transpose(d_scores).astype(BF16), query)
    return jnp.concatenate([d_query, d_keys, d_values], axis=1).astype(BF16).astype(F32)


def summed(parts):
    total = parts[0][...].astype(F32)
    for part in parts[1:]:
        total = total + part[...].astype(F32)
    return total


def chain_kernel(features, heads, index, docs, *refs):
    out_ref = refs[-1]
    qkv, half = 3 * heads, 2 * heads
    total = summed(refs[:-1])
    rows = total.shape[0]
    section = index[0]
    query_at = lax.broadcasted_iota(jnp.int32, (rows, rows), 0)
    key_at = lax.broadcasted_iota(jnp.int32, (rows, rows), 1)
    allowed = query_at >= key_at
    end = 0
    for i in range(docs.shape[2]):
        end = end + docs[section, 0, i]
        allowed = allowed & ((query_at >= end) == (key_at >= end))
    x_out = total[:, qkv : 2 * half]
    x_one = total[:, 2 * half : 2 * half + qkv]
    tail = total[:, 3 * half : 4 * half]
    c_one, c_zero = total[:, 4 * half : 4 * half + heads].astype(BF16), total[:, 4 * half + heads : 5 * half]
    lane = lax.broadcasted_iota(jnp.int32, tail.shape, 1)
    squares = jnp.sum(jnp.where((lane == heads) | (lane == heads + 1), tail, 0.0), axis=1, keepdims=True)
    mixed = total[:, 5 * half : 5 * half + qkv].astype(BF16)
    gram = total[:, 5 * half + qkv :].astype(BF16)

    scale0 = lax.rsqrt(squares / features + 1e-05)
    qkv0 = (total[:, :qkv] * scale0).astype(BF16).astype(F32)
    probs0, att0 = attention(qkv0, allowed, heads)
    wide0 = att0.astype(F32)
    y_out = x_out + nn(att0, gram)
    squares = squares + jnp.sum(wide0 * (x_out + y_out), axis=1, keepdims=True)
    scale1 = lax.rsqrt(jnp.maximum(squares, 0.0) / features + 1e-05)
    qkv1 = ((x_one + nn(att0, mixed)) * scale1).astype(BF16).astype(F32)
    probs1, att1 = attention(qkv1, allowed, heads)
    d_qkv1 = attention_grad(qkv1, probs1, att1, c_one, heads)
    inner = jnp.sum(d_qkv1 * qkv1, axis=1, keepdims=True) * scale1 * scale1 / features
    e1 = d_qkv1 * scale1
    d_att0 = c_zero + nt(e1.astype(BF16), mixed) - inner * y_out
    e0 = attention_grad(qkv0, probs0, att0, d_att0.astype(BF16), heads) * scale0
    factors = jnp.concatenate([e0, wide0, e1, wide0 * inner], axis=1).astype(BF16)
    for g in range(4):
        out_ref[g * rows : (g + 1) * rows, :] = factors[:, g * half : (g + 1) * half]
    wide1 = att1.astype(F32)
    out_ref[4 * rows :, :] = jnp.concatenate([wide1[: rows // 2], wide1[rows // 2 :]], axis=1).astype(BF16)


def pieces_of(planes, heads, order, index, turned, small, small_t, x_ref, c_ref, vx_ref, gain_ref, keep_ref, send_ref):
    qkv, half, width = 3 * heads, 2 * heads, vx_ref.shape[-1]
    section, place = index[0], index[1]
    rows = x_ref.shape[0] * x_ref.shape[1]
    att0, att1 = turned[qkv : qkv + heads], turned[4 * half : 4 * half + heads]
    for i, k in enumerate(order):
        z = place ^ k
        cols = pl.ds(pl.multiple_of(z * width, width), width)
        x = x_ref[:, :, cols].reshape(rows, width)
        c = c_ref[:, :, cols].reshape(rows, width)
        out = vx_ref[z, qkv : qkv + heads, :]
        with_x = nn(turned[: 4 * half], x)
        left = with_x[2 * half :] + nn(small, out)
        zero = with_x[:qkv] * gain_ref[z, 0:1, :]
        one = left[:qkv] * gain_ref[z, 1:2, :]
        keep_ref[i, :qkv, :] = jnp.where(section == 0, zero, one)
        send_ref[i, :qkv, :] = jnp.where(section == 0, one, zero).astype(BF16)
        zero = nn(att0, c) + nn(small_t, vx_ref[z, qkv + heads : 2 * qkv + heads, :]) - left[qkv:]
        one = nn(att1, c)
        keep_ref[i, qkv:, :] = jnp.where(section == 0, zero, one)
        send_ref[i, qkv:, :] = jnp.where(section == 0, one, zero).astype(BF16)


def far_grads_kernel(planes, heads, order, index, *refs):
    factors, arrays = refs[:PLANE], refs[PLANE : PLANE + 4]
    keep_ref, send_ref, turned_ref, small_ref, small_t_ref, all_ref = refs[PLANE + 4 :]
    qkv, half = 3 * heads, 2 * heads
    p = index[2]
    block = all_ref.shape[1]
    for k in range(PLANE):
        for g in range(4):
            all_ref[p ^ k, :, g * half : (g + 1) * half] = factors[k][g * block : (g + 1) * block, :]
        folded = factors[k][4 * block :, :]
        last = jnp.concatenate([folded[:, :heads].astype(F32), folded[:, heads:].astype(F32)], axis=0)
        all_ref[p ^ k, :, 4 * half :] = jnp.concatenate([last, jnp.zeros_like(last)], axis=1).astype(BF16)
    rows = all_ref.shape[0] * block
    turned = jnp.transpose(all_ref[...].astype(F32).reshape(rows, 5 * half)).astype(BF16)
    att0, right = turned[qkv : qkv + heads], turned[2 * half : 4 * half]
    small = nt(right, att0).astype(BF16)
    small_t = nt(att0, right[:qkv]).astype(BF16)
    turned_ref[...] = turned
    small_ref[...] = small
    small_t_ref[...] = small_t
    pieces_of(planes, heads, order, index, turned, small, small_t, *arrays, keep_ref, send_ref)


def near_grads_kernel(planes, heads, order, index, turned_ref, small_ref, small_t_ref, *refs):
    pieces_of(planes, heads, order, index, turned_ref[...], small_ref[...], small_t_ref[...], *refs)


def merge_kernel(cuts, keep_ref, come_ref, *out_refs):
    rows = keep_ref.shape[1] // cuts
    for j, out_ref in enumerate(out_refs):
        here = slice(j % cuts * rows, (j % cuts + 1) * rows)
        out_ref[...] = (keep_ref[j // cuts, here] + come_ref[j // cuts, here].astype(F32)).astype(out_ref.dtype)


def wide_add_kernel(at, a_ref, part_ref, out_ref):
    rows = slice(at, at + part_ref.shape[0])
    out_ref[...] = a_ref[...]
    out_ref[rows, :] = a_ref[rows, :] + part_ref[...].astype(F32)


def add_kernel(a_ref, b_ref, out_ref):
    out_ref[...] = (a_ref[...].astype(F32) + b_ref[...].astype(F32)).astype(BF16)


def last_kernel(qkv_rows, keep_ref, *refs):
    parts, (qkv_ref, out_ref) = refs[:-2], refs[-2:]
    total = keep_ref[...]
    for part in parts:
        total = total + part[...].astype(F32)
    qkv_ref[...] = total[:qkv_rows]
    out_ref[...] = total[qkv_rows:]


def far_first(value, count, send):
    of = lambda k: value[k] if isinstance(value, (list, tuple)) else value
    got = {k: send(of(k), k) for k in reversed(range(1, count))}
    return [of(0)] + [got[k] for k in range(1, count)]


def call(kernel, outs, *args, scalars=0, scratch=()):
    smem = pl.BlockSpec(memory_space=pltpu.SMEM)
    vmem = pl.BlockSpec(memory_space=pltpu.VMEM)
    return pl.pallas_call(
        kernel,
        out_shape=[jax.ShapeDtypeStruct(shape, dtype) for shape, dtype in outs],
        in_specs=[smem] * scalars + [vmem] * (len(args) - scalars),
        out_specs=[vmem] * len(outs),
        scratch_shapes=[pltpu.VMEM(shape, dtype) for shape, dtype in scratch],
        compiler_params=pltpu.CompilerParams(vmem_limit_bytes=VMEM_LIMIT),
    )(*args)


def planar(inputs, cotangent, doc_lengths, norm_gain, w_qkv, w_out):
    shards = lax.axis_size("dp")
    planes = shards // PLANE
    section, place = lax.axis_index("section"), lax.axis_index("dp")
    z, p = place // PLANE, place % PLANE
    index = jnp.stack([section, z, p]).astype(jnp.int32)
    block, features = inputs.shape[1:]
    rows = PLANE * block
    heads, width = w_out.shape[1:]
    qkv_rows = w_qkv.shape[2]
    cols = planes * width
    def along_z(value, k):
        route = [(a * PLANE + b, (a ^ k) * PLANE + b) for a in range(planes) for b in range(PLANE)]
        return lax.ppermute(value, "dp", route)

    def to_sibling(value):
        return lax.ppermute(value, "section", [(0, 1), (1, 0)])

    def along_plane(value, k):
        route = [(a * PLANE + b, a * PLANE + (b ^ k)) for a in range(planes) for b in range(PLANE)]
        return lax.ppermute(value, "dp", route)

    def exchange(value):
        return far_first(value, PLANE, along_plane)

    smem, vmem = pl.BlockSpec(memory_space=pltpu.SMEM), pl.BlockSpec(memory_space=pltpu.VMEM)
    hbm = pl.BlockSpec(memory_space=pltpu.HBM)
    params = pltpu.CompilerParams(vmem_limit_bytes=VMEM_LIMIT)
    qkv_in, out_in, x_in, c_in = [
        pltpu.with_memory_space_constraint(value, pltpu.HBM)
        for value in (w_qkv[0].T, w_out[0], inputs, cotangent)
    ]
    one_block = jax.ShapeDtypeStruct((2, block, cols), BF16)
    pack, near_block = pl.pallas_call(
        functools.partial(first_kernel, planes),
        out_shape=[jax.ShapeDtypeStruct((qkv_rows + heads, width), BF16), one_block],
        in_specs=[smem] + [hbm] * 4,
        out_specs=[vmem] * 2,
        scratch_shapes=[pltpu.SemaphoreType.DMA((2,)), pltpu.SemaphoreType.DMA((2 * planes,))],
        compiler_params=params,
    )(index, qkv_in, out_in, x_in, c_in)
    blocks = pl.pallas_call(
        functools.partial(blocks_kernel, planes),
        out_shape=[one_block] * (PLANE - 2),
        in_specs=[smem] + [hbm] * 2,
        out_specs=[vmem] * (PLANE - 2),
        scratch_shapes=[pltpu.SemaphoreType.DMA((PLANE - 2, 2 * planes))],
        compiler_params=params,
    )(index, x_in, c_in)
    blocks = [near_block, *blocks]
    gain = norm_gain[0].reshape(shards, width)
    blocks = far_first([None] + blocks, PLANE, along_plane)
    pieces = {0: pack}
    for step in reversed([1 << bit for bit in range(planes.bit_length() - 1)]):
        for k in list(pieces):
            pieces[k ^ step] = along_z(pieces[k], step)
    mine, late_gain, _ = lax.optimization_barrier((pack, gain, blocks[1]))
    marked, blocks[0] = pl.pallas_call(
        functools.partial(mark_kernel, planes),
        out_shape=[jax.ShapeDtypeStruct((qkv_rows + heads + shards, width), BF16), one_block],
        in_specs=[smem] + [vmem] * 2 + [hbm] * 2,
        out_specs=[vmem] * 2,
        scratch_shapes=[pltpu.SemaphoreType.DMA((2 * planes,))],
        compiler_params=params,
    )(index, mine, late_gain, x_in, c_in)
    pieces[planes // 2], _ = lax.optimization_barrier((pieces[planes // 2], blocks[1]))
    own = [marked] + [pieces[k] for k in range(1, planes)]
    other = [to_sibling(piece) for piece in own]

    split = ((PLANE, block, cols), BF16)
    half = 2 * heads
    x, c, vx, gains, *sent = call(
        functools.partial(project_kernel, planes, heads),
        [split, split, ((planes, 4 * half, width), BF16), ((planes, 8, width), F32)]
        + [((block, 7 * half), BF16)] * PLANE,
        index, blocks[0], *blocks[:0:-1], *own, *other, scalars=1,
        scratch=[((planes, half, width), BF16), ((rows, 5 * half), BF16)] + [((shards, width), F32)] * 2,
    )
    (factors,) = call(
        functools.partial(chain_kernel, features, heads),
        [((9 * block // 2, half), BF16)],
        index, doc_lengths, *exchange(sent)[::-1], scalars=2,
    )
    piece = (qkv_rows + heads, width)
    far_order = tuple(reversed(range(planes - planes // 2, planes)))
    near_order = tuple(reversed(range(planes - planes // 2)))

    def swap_and_merge(order, keep, send, cuts):
        outs = [((piece[0] // cuts, width), BF16 if k else F32) for k in order for _ in range(cuts)]
        cut = call(functools.partial(merge_kernel, cuts), outs, keep, to_sibling(send))
        return {k: list(cut[i * cuts : (i + 1) * cuts]) for i, k in enumerate(order)}

    keep, send, turned, small, small_t = call(
        functools.partial(far_grads_kernel, planes, heads, far_order),
        [((len(far_order),) + piece, F32), ((len(far_order),) + piece, BF16)]
        + [((5 * half, rows), BF16), ((2 * half, heads), BF16), ((heads, qkv_rows), BF16)],
        index, *exchange(factors), x, c, vx, gains, scalars=1,
        scratch=[((PLANE, block, 5 * half), BF16)],
    )
    pieces = swap_and_merge(far_order, keep, send, 2)
    keep, send = call(
        functools.partial(near_grads_kernel, planes, heads, near_order),
        [((len(near_order),) + piece, F32), ((len(near_order),) + piece, BF16)],
        index, turned, small, small_t, x, c, vx, gains, scalars=1,
    )
    pieces.update(swap_and_merge(near_order, keep, send, 1))
    (kept,), held = pieces[0], []
    for step in [1 << bit for bit in range(planes.bit_length() - 1)]:
        senders = [k for k in sorted(pieces, reverse=True) if k & step and k != step]
        got = {k ^ step: [along_z(part, step) for part in pieces.pop(k)] for k in senders}
        if step in pieces:
            held.append((pieces.pop(step), step))
        for k, come in got.items():
            pieces[k] = [call(add_kernel, [(a.shape, BF16)], a, b)[0] for a, b in zip(pieces[k], come)]
            held = [
                (parts, at) for parts, at in held
            ]
    parts = [[along_z(part, at) for part in value] for value, at in reversed(held)]
    for come in parts[:-1]:
        for i, part in enumerate(come):
            (kept,) = call(functools.partial(wide_add_kernel, i * part.shape[0]), [(piece, F32)], kept, part)
    grad_qkv, grad_out = call(
        functools.partial(last_kernel, qkv_rows),
        [((qkv_rows, width), F32), ((heads, width), F32)],
        kept, *(parts[-1] if parts else []),
    )
    return (grad_qkv.T[None], grad_out[None])


def solution(mesh):
    sections, shards = mesh.shape["section"], mesh.shape["dp"]
    planes = shards // PLANE

    def body(inputs, *rest):
        fits = shards % PLANE == 0 and planes & (planes - 1) == 0
        if sections == 2 and inputs.shape[0] == 2 and fits:
            return planar(inputs, *rest)
        return pipelined(inputs, *rest)

    return jax.shard_map(
        body,
        mesh=mesh,
        in_specs=(
            P(None, "dp", None),
            P(None, "dp", None),
            P(None, "dp", None),
            P("section", None),
            P("section", "dp", None),
            P("section", None, "dp"),
        ),
        out_specs=(P("section", "dp", None), P("section", None, "dp")),
        check_vma=False,
    )
```

```python
import functools

import jax
import jax.numpy as jnp
from jax import lax
from jax.experimental import pallas as pl
from jax.experimental.pallas import tpu as pltpu
from jax.sharding import PartitionSpec as P

F32 = jnp.float32
BF16 = jnp.bfloat16
PLANE = 4
VMEM_LIMIT = 16 * 1024 * 1024


def passed_along(block, axis, distance):
    devices = range(lax.axis_size(axis))
    route = [(i - distance, i) for i in devices if i - distance in devices]
    return lax.ppermute(block, axis, route)


def segments_of(lengths, count):
    ends = jnp.cumsum(lengths)
    position = jnp.arange(count, dtype=jnp.int32)
    return jnp.sum((position[:, None] >= ends[None, :]).astype(jnp.int32), axis=1)


def layer(x, gain, w_qkv, w_out, seg):
    head = w_out.shape[0]
    x_wide = x.astype(jnp.float32)
    scale = lax.rsqrt(jnp.mean(x_wide * x_wide, axis=-1, keepdims=True) + 1e-05)
    normed = (x_wide * scale * gain.astype(jnp.float32)).astype(jnp.bfloat16)
    qkv = jnp.dot(normed, w_qkv, preferred_element_type=jnp.float32).astype(jnp.bfloat16)
    query = qkv[:, :head]
    keys = qkv[:, head : 2 * head]
    values = qkv[:, 2 * head :]
    scores = jnp.dot(query, keys.T, preferred_element_type=jnp.float32) * head ** (-0.5)
    rows = jnp.arange(x.shape[0], dtype=jnp.int32)
    allowed = (seg[:, None] == seg[None, :]) & (rows[:, None] >= rows[None, :])
    scores = jnp.where(allowed, scores, -1e30)
    probs = jax.nn.softmax(scores, axis=-1).astype(jnp.bfloat16)
    attended = jnp.dot(probs, values, preferred_element_type=jnp.float32).astype(jnp.bfloat16)
    return (x_wide + jnp.dot(attended, w_out, preferred_element_type=jnp.float32)).astype(
        jnp.bfloat16
    )


def pipelined(inputs, cotangent, doc_lengths, norm_gain, w_qkv, w_out):
    sections = lax.axis_size("section")
    section = lax.axis_index("section")
    micro = inputs.shape[0]
    count = inputs.shape[1]
    segs = jax.vmap(lambda lens: segments_of(lens, count))(doc_lengths[:, 0, :])
    gain = norm_gain[0]
    full_qkv, full_out = (
        lax.all_gather(w_qkv[0], "dp", axis=0, tiled=True),
        lax.all_gather(w_out[0], "dp", axis=1, tiled=True),
    )
    total_steps = micro + sections - 1
    empty = jnp.zeros(inputs.shape[1:], inputs.dtype)

    def forward_at(step, incoming, saved):
        index = step - section
        live = (index >= 0) & (index < micro)
        slot = jnp.clip(index, 0, micro - 1)
        first = lax.dynamic_index_in_dim(inputs, slot, 0, keepdims=False)
        x = jnp.where(section == 0, first, incoming)
        seg = lax.dynamic_index_in_dim(segs, slot, 0, keepdims=False)
        out = layer(x, gain, full_qkv, full_out, seg)
        old = lax.dynamic_index_in_dim(saved, slot, 0, keepdims=False)
        saved = lax.dynamic_update_index_in_dim(saved, jnp.where(live, x, old), slot, 0)
        return (out, saved)

    def forward_step(carry, step):
        incoming, saved = carry
        out, saved = forward_at(step, incoming, saved)
        incoming = passed_along(out, "section", 1)
        return ((incoming, saved), None)

    start_saved = jnp.zeros(inputs.shape, inputs.dtype)
    (incoming, saved), _ = lax.scan(
        forward_step, (empty, start_saved), jnp.arange(total_steps - 1, dtype=jnp.int32)
    )
    _, saved = forward_at(jnp.int32(total_steps - 1), incoming, saved)

    def backward_at(step, incoming, sum_qkv, sum_out):
        index = step - (sections - 1 - section)
        live = (index >= 0) & (index < micro)
        slot = jnp.clip(index, 0, micro - 1)
        last = lax.dynamic_index_in_dim(cotangent, slot, 0, keepdims=False)
        grad_y = jnp.where(section == sections - 1, last, incoming)
        x = lax.dynamic_index_in_dim(saved, slot, 0, keepdims=False)
        seg = lax.dynamic_index_in_dim(segs, slot, 0, keepdims=False)
        _, pull = jax.vjp(lambda a, b, c: layer(a, gain, b, c, seg), x, full_qkv, full_out)
        grad_x, grad_q, grad_o = pull(grad_y)
        sum_qkv = sum_qkv + jnp.where(live, grad_q.astype(jnp.float32), 0.0)
        sum_out = sum_out + jnp.where(live, grad_o.astype(jnp.float32), 0.0)
        return (grad_x, sum_qkv, sum_out)

    def backward_step(carry, step):
        incoming, sum_qkv, sum_out = carry
        grad_x, sum_qkv, sum_out = backward_at(step, incoming, sum_qkv, sum_out)
        incoming = passed_along(grad_x, "section", -1)
        return ((incoming, sum_qkv, sum_out), None)

    zero_qkv = jnp.zeros(full_qkv.shape, jnp.float32)
    zero_out = jnp.zeros(full_out.shape, jnp.float32)
    (incoming, sum_qkv, sum_out), _ = lax.scan(
        backward_step, (empty, zero_qkv, zero_out), jnp.arange(total_steps - 1, dtype=jnp.int32)
    )
    _, sum_qkv, sum_out = backward_at(jnp.int32(total_steps - 1), incoming, sum_qkv, sum_out)
    share_qkv, share_out = (
        lax.psum_scatter(sum_qkv, "dp", scatter_dimension=0, tiled=True),
        lax.psum_scatter(sum_out, "dp", scatter_dimension=1, tiled=True),
    )
    return (share_qkv[None], share_out[None])


def nn(a, b):
    return lax.dot_general(a, b, (((1,), (0,)), ((), ())), preferred_element_type=F32)


def nt(a, b):
    return lax.dot_general(a, b, (((1,), (1,)), ((), ())), preferred_element_type=F32)


def block_copies(planes, index, k, refs, out_ref, sems):
    width = refs[0].shape[-1] // (planes * PLANE)
    section, p = index[0], index[2]
    copies = []
    for z in range(planes):
        at = pl.multiple_of((z * PLANE + (p ^ k)) * width, width)
        for half, ref in enumerate(refs):
            copies.append(
                pltpu.make_async_copy(
                    ref.at[section, :, pl.ds(at, width)],
                    out_ref.at[half, :, pl.ds(z * width, width)],
                    sems.at[len(copies)],
                )
            )
    return copies


def mark_kernel(planes, index, pack_ref, gain_ref, x_ref, c_ref, out_ref, block_ref, sems):
    copies = block_copies(planes, index, 0, (x_ref, c_ref), block_ref, sems)
    for copy in copies:
        copy.start()
    out_ref[: pack_ref.shape[0], :] = pack_ref[...]
    out_ref[pack_ref.shape[0] :, :] = gain_ref[...]
    for copy in copies:
        copy.wait()


def first_kernel(planes, index, qkv_ref, wout_ref, x_ref, c_ref, pack_ref, far_ref, pack_sems, sems):
    qkv_rows = qkv_ref.shape[0]
    copies = [
        pltpu.make_async_copy(qkv_ref, pack_ref.at[:qkv_rows], pack_sems.at[0]),
        pltpu.make_async_copy(wout_ref, pack_ref.at[qkv_rows:], pack_sems.at[1]),
    ] + block_copies(planes, index, PLANE - 1, (x_ref, c_ref), far_ref, sems)
    for copy in copies:
        copy.start()
    for copy in copies:
        copy.wait()


def blocks_kernel(planes, index, x_ref, c_ref, *refs):
    out_refs, sems = refs[:-1], refs[-1]
    copies = []
    for k, out_ref in enumerate(out_refs, 1):
        copies += block_copies(planes, index, k, (x_ref, c_ref), out_ref, sems.at[k - 1])
    for copy in copies:
        copy.start()
    for copy in copies:
        copy.wait()


def project_kernel(planes, heads, index, *refs):
    blocks, own, other = refs[:PLANE], refs[PLANE : PLANE + planes], refs[PLANE + planes : PLANE + 2 * planes]
    x_ref, c_ref, vx_ref, gain_ref = refs[PLANE + 2 * planes : PLANE + 2 * planes + 4]
    out_refs = refs[PLANE + 2 * planes + 4 : -4]
    vc_ref, sum_ref, *wide_refs = refs[-4:]
    qkv, width = 3 * heads, vx_ref.shape[-1]
    section, place, p = index[0], index[1], index[2]
    for ref, wide_ref in zip((own[0], other[0]), wide_refs):
        wide_ref[...] = ref[qkv + heads :, :].astype(F32)
    for z in range(planes):
        mine, theirs = (ref[pl.ds(z * PLANE + p, 1), :] for ref in wide_refs)
        gain_ref[z, 0:1, :] = jnp.where(section == 0, mine, theirs)
        gain_ref[z, 1:2, :] = jnp.where(section == 0, theirs, mine)
    for k in range(planes):
        at = place ^ k
        mine, theirs = own[k][: qkv + heads, :], other[k][: qkv + heads, :]
        zero = jnp.where(section == 0, mine, theirs)
        one = jnp.where(section == 0, theirs, mine)
        empty = jnp.zeros((heads, width), BF16)
        vx_ref[at, :qkv, :] = (zero[:qkv].astype(F32) * gain_ref[at, 0:1, :]).astype(BF16)
        vx_ref[at, qkv : qkv + heads, :] = zero[qkv : qkv + heads]
        vx_ref[at, qkv + heads : 2 * qkv + heads, :] = (one[:qkv].astype(F32) * gain_ref[at, 1:2, :]).astype(BF16)
        vx_ref[at, 2 * qkv + heads :, :] = empty
        vc_ref[at, :heads, :] = one[qkv : qkv + heads]
        vc_ref[at, heads:, :] = zero[qkv : qkv + heads]
    for k in range(PLANE):
        x_ref[p ^ k] = blocks[-k][0]
        c_ref[p ^ k] = blocks[-k][1]
    rows = x_ref.shape[0] * x_ref.shape[1]
    with_x = with_c = squares = products = None
    for z in range(planes):
        cols = slice(z * width, (z + 1) * width)
        x = x_ref[:, :, cols].reshape(rows, width)
        c = c_ref[:, :, cols].reshape(rows, width)
        wide = x.astype(F32)
        out = vx_ref[z, qkv : qkv + heads, :]
        right = jnp.concatenate([vx_ref[z, qkv + heads : 2 * qkv + heads, :], out], axis=0)
        new = nt(x, vx_ref[z]), nt(c, vc_ref[z]), jnp.sum(wide * wide, axis=1, keepdims=True), nt(out, right)
        if with_x is None:
            with_x, with_c, squares, products = new
        else:
            with_x, with_c = with_x + new[0], with_c + new[1]
            squares, products = squares + new[2], products + new[3]
    half = 2 * heads
    lane = lax.broadcasted_iota(jnp.int32, (rows, half), 1)
    high = squares.astype(BF16).astype(F32)
    last = jnp.where(lane == heads, high, jnp.where(lane == heads + 1, squares - high, with_x[:, 3 * half :]))
    sum_ref[:, : 3 * half] = with_x[:, : 3 * half].astype(BF16)
    sum_ref[:, 3 * half : 4 * half] = last.astype(BF16)
    sum_ref[:, 4 * half :] = with_c.astype(BF16)
    block = rows // PLANE
    for k in range(PLANE):
        start = pl.multiple_of((p ^ k) * block, block)
        out_refs[k][:, : 5 * half] = sum_ref[pl.ds(start, block), :]
        out_refs[k][:, 5 * half :] = products.astype(BF16)


def attention(qkv, allowed, heads):
    query, keys, values = (qkv[:, i * heads : (i + 1) * heads].astype(BF16) for i in range(3))
    scores = jnp.where(allowed, nt(query, keys) * heads ** (-0.5), -1e30)
    raised = jnp.exp(scores - jnp.max(scores, axis=1, keepdims=True))
    scale = 1.0 / jnp.sum(raised, axis=1, keepdims=True)
    return raised * scale, (nn(raised.astype(BF16), values) * scale).astype(BF16)


def attention_grad(qkv, probs, att, d_att, heads):
    query, keys, values = (qkv[:, i * heads : (i + 1) * heads].astype(BF16) for i in range(3))
    inner = jnp.sum(att.astype(F32) * d_att.astype(F32), axis=1, keepdims=True)
    d_values = nn(jnp.transpose(probs).astype(BF16), d_att)
    d_scores = probs * (nt(d_att, values) - inner) * heads ** (-0.5)
    d_query = nn(d_scores.astype(BF16), keys)
    d_keys = nn(jnp.transpose(d_scores).astype(BF16), query)
    return jnp.concatenate([d_query, d_keys, d_values], axis=1).astype(BF16).astype(F32)


def summed(parts):
    total = parts[0][...].astype(F32)
    for part in parts[1:]:
        total = total + part[...].astype(F32)
    return total


def chain_kernel(features, heads, index, docs, *refs):
    out_ref = refs[-1]
    qkv, half = 3 * heads, 2 * heads
    total = summed(refs[:-1])
    rows = total.shape[0]
    section = index[0]
    query_at = lax.broadcasted_iota(jnp.int32, (rows, rows), 0)
    key_at = lax.broadcasted_iota(jnp.int32, (rows, rows), 1)
    allowed = query_at >= key_at
    end = 0
    for i in range(docs.shape[2]):
        end = end + docs[section, 0, i]
        allowed = allowed & ((query_at >= end) == (key_at >= end))
    x_out = total[:, qkv : 2 * half]
    x_one = total[:, 2 * half : 2 * half + qkv]
    tail = total[:, 3 * half : 4 * half]
    c_one, c_zero = total[:, 4 * half : 4 * half + heads].astype(BF16), total[:, 4 * half + heads : 5 * half]
    lane = lax.broadcasted_iota(jnp.int32, tail.shape, 1)
    squares = jnp.sum(jnp.where((lane == heads) | (lane == heads + 1), tail, 0.0), axis=1, keepdims=True)
    mixed = total[:, 5 * half : 5 * half + qkv].astype(BF16)
    gram = total[:, 5 * half + qkv :].astype(BF16)

    scale0 = lax.rsqrt(squares / features + 1e-05)
    qkv0 = (total[:, :qkv] * scale0).astype(BF16).astype(F32)
    probs0, att0 = attention(qkv0, allowed, heads)
    wide0 = att0.astype(F32)
    y_out = x_out + nn(att0, gram)
    squares = squares + jnp.sum(wide0 * (x_out + y_out), axis=1, keepdims=True)
    scale1 = lax.rsqrt(jnp.maximum(squares, 0.0) / features + 1e-05)
    qkv1 = ((x_one + nn(att0, mixed)) * scale1).astype(BF16).astype(F32)
    probs1, att1 = attention(qkv1, allowed, heads)
    d_qkv1 = attention_grad(qkv1, probs1, att1, c_one, heads)
    inner = jnp.sum(d_qkv1 * qkv1, axis=1, keepdims=True) * scale1 * scale1 / features
    e1 = d_qkv1 * scale1
    d_att0 = c_zero + nt(e1.astype(BF16), mixed) - inner * y_out
    e0 = attention_grad(qkv0, probs0, att0, d_att0.astype(BF16), heads) * scale0
    factors = jnp.concatenate([e0, wide0, e1, wide0 * inner], axis=1).astype(BF16)
    for g in range(4):
        out_ref[g * rows : (g + 1) * rows, :] = factors[:, g * half : (g + 1) * half]
    wide1 = att1.astype(F32)
    out_ref[4 * rows :, :] = jnp.concatenate([wide1[: rows // 2], wide1[rows // 2 :]], axis=1).astype(BF16)


def pieces_of(planes, heads, order, index, turned, small, small_t, x_ref, c_ref, vx_ref, gain_ref, keep_ref, send_ref):
    qkv, half, width = 3 * heads, 2 * heads, vx_ref.shape[-1]
    section, place = index[0], index[1]
    rows = x_ref.shape[0] * x_ref.shape[1]
    att0, att1 = turned[qkv : qkv + heads], turned[4 * half : 4 * half + heads]
    for i, k in enumerate(order):
        z = place ^ k
        cols = pl.ds(pl.multiple_of(z * width, width), width)
        x = x_ref[:, :, cols].reshape(rows, width)
        c = c_ref[:, :, cols].reshape(rows, width)
        out = vx_ref[z, qkv : qkv + heads, :]
        with_x = nn(turned[: 4 * half], x)
        left = with_x[2 * half :] + nn(small, out)
        zero = with_x[:qkv] * gain_ref[z, 0:1, :]
        one = left[:qkv] * gain_ref[z, 1:2, :]
        keep_ref[i, :qkv, :] = jnp.where(section == 0, zero, one)
        send_ref[i, :qkv, :] = jnp.where(section == 0, one, zero).astype(BF16)
        zero = nn(att0, c) + nn(small_t, vx_ref[z, qkv + heads : 2 * qkv + heads, :]) - left[qkv:]
        one = nn(att1, c)
        keep_ref[i, qkv:, :] = jnp.where(section == 0, zero, one)
        send_ref[i, qkv:, :] = jnp.where(section == 0, one, zero).astype(BF16)


def far_grads_kernel(planes, heads, order, index, *refs):
    factors, arrays = refs[:PLANE], refs[PLANE : PLANE + 4]
    keep_ref, send_ref, turned_ref, small_ref, small_t_ref, all_ref = refs[PLANE + 4 :]
    qkv, half = 3 * heads, 2 * heads
    p = index[2]
    block = all_ref.shape[1]
    for k in range(PLANE):
        for g in range(4):
            all_ref[p ^ k, :, g * half : (g + 1) * half] = factors[k][g * block : (g + 1) * block, :]
        folded = factors[k][4 * block :, :]
        last = jnp.concatenate([folded[:, :heads].astype(F32), folded[:, heads:].astype(F32)], axis=0)
        all_ref[p ^ k, :, 4 * half :] = jnp.concatenate([last, jnp.zeros_like(last)], axis=1).astype(BF16)
    rows = all_ref.shape[0] * block
    turned = jnp.transpose(all_ref[...].astype(F32).reshape(rows, 5 * half)).astype(BF16)
    att0, right = turned[qkv : qkv + heads], turned[2 * half : 4 * half]
    small = nt(right, att0).astype(BF16)
    small_t = nt(att0, right[:qkv]).astype(BF16)
    turned_ref[...] = turned
    small_ref[...] = small
    small_t_ref[...] = small_t
    pieces_of(planes, heads, order, index, turned, small, small_t, *arrays, keep_ref, send_ref)


def near_grads_kernel(planes, heads, order, index, turned_ref, small_ref, small_t_ref, *refs):
    pieces_of(planes, heads, order, index, turned_ref[...], small_ref[...], small_t_ref[...], *refs)


def merge_kernel(cuts, keep_ref, come_ref, *out_refs):
    rows = keep_ref.shape[1] // cuts
    for j, out_ref in enumerate(out_refs):
        here = slice(j % cuts * rows, (j % cuts + 1) * rows)
        out_ref[...] = (keep_ref[j // cuts, here] + come_ref[j // cuts, here].astype(F32)).astype(out_ref.dtype)


def wide_add_kernel(at, a_ref, part_ref, out_ref):
    rows = slice(at, at + part_ref.shape[0])
    out_ref[...] = a_ref[...]
    out_ref[rows, :] = a_ref[rows, :] + part_ref[...].astype(F32)


def add_kernel(a_ref, b_ref, out_ref):
    out_ref[...] = (a_ref[...].astype(F32) + b_ref[...].astype(F32)).astype(BF16)


def last_kernel(qkv_rows, keep_ref, *refs):
    parts, (qkv_ref, out_ref) = refs[:-2], refs[-2:]
    total = keep_ref[...]
    for part in parts:
        total = total + part[...].astype(F32)
    qkv_ref[...] = total[:qkv_rows]
    out_ref[...] = total[qkv_rows:]


def far_first(value, count, send):
    of = lambda k: value[k] if isinstance(value, (list, tuple)) else value
    got = {k: send(of(k), k) for k in reversed(range(1, count))}
    return [of(0)] + [got[k] for k in range(1, count)]


def call(kernel, outs, *args, scalars=0, scratch=()):
    smem = pl.BlockSpec(memory_space=pltpu.SMEM)
    vmem = pl.BlockSpec(memory_space=pltpu.VMEM)
    return pl.pallas_call(
        kernel,
        out_shape=[jax.ShapeDtypeStruct(shape, dtype) for shape, dtype in outs],
        in_specs=[smem] * scalars + [vmem] * (len(args) - scalars),
        out_specs=[vmem] * len(outs),
        scratch_shapes=[pltpu.VMEM(shape, dtype) for shape, dtype in scratch],
        compiler_params=pltpu.CompilerParams(vmem_limit_bytes=VMEM_LIMIT),
    )(*args)


def planar(inputs, cotangent, doc_lengths, norm_gain, w_qkv, w_out):
    shards = lax.axis_size("dp")
    planes = shards // PLANE
    section, place = lax.axis_index("section"), lax.axis_index("dp")
    z, p = place // PLANE, place % PLANE
    index = jnp.stack([section, z, p]).astype(jnp.int32)
    block, features = inputs.shape[1:]
    rows = PLANE * block
    heads, width = w_out.shape[1:]
    qkv_rows = w_qkv.shape[2]
    cols = planes * width
    def along_z(value, k):
        route = [(a * PLANE + b, (a ^ k) * PLANE + b) for a in range(planes) for b in range(PLANE)]
        return lax.ppermute(value, "dp", route)

    def to_sibling(value):
        return lax.ppermute(value, "section", [(0, 1), (1, 0)])

    def along_plane(value, k):
        route = [(a * PLANE + b, a * PLANE + (b ^ k)) for a in range(planes) for b in range(PLANE)]
        return lax.ppermute(value, "dp", route)

    def exchange(value):
        return far_first(value, PLANE, along_plane)

    smem, vmem = pl.BlockSpec(memory_space=pltpu.SMEM), pl.BlockSpec(memory_space=pltpu.VMEM)
    hbm = pl.BlockSpec(memory_space=pltpu.HBM)
    params = pltpu.CompilerParams(vmem_limit_bytes=VMEM_LIMIT)
    qkv_in, out_in, x_in, c_in = [
        pltpu.with_memory_space_constraint(value, pltpu.HBM)
        for value in (w_qkv[0].T, w_out[0], inputs, cotangent)
    ]
    one_block = jax.ShapeDtypeStruct((2, block, cols), BF16)
    pack, far_block = pl.pallas_call(
        functools.partial(first_kernel, planes),
        out_shape=[jax.ShapeDtypeStruct((qkv_rows + heads, width), BF16), one_block],
        in_specs=[smem] + [hbm] * 4,
        out_specs=[vmem] * 2,
        scratch_shapes=[pltpu.SemaphoreType.DMA((2,)), pltpu.SemaphoreType.DMA((2 * planes,))],
        compiler_params=params,
    )(index, qkv_in, out_in, x_in, c_in)
    blocks = pl.pallas_call(
        functools.partial(blocks_kernel, planes),
        out_shape=[one_block] * (PLANE - 2),
        in_specs=[smem] + [hbm] * 2,
        out_specs=[vmem] * (PLANE - 2),
        scratch_shapes=[pltpu.SemaphoreType.DMA((PLANE - 2, 2 * planes))],
        compiler_params=params,
    )(index, x_in, c_in)
    blocks = [*blocks, far_block]
    gain = norm_gain[0].reshape(shards, width)
    blocks = far_first([None] + blocks, PLANE, along_plane)
    pieces = {0: pack}
    for step in reversed([1 << bit for bit in range(planes.bit_length() - 1)]):
        for k in list(pieces):
            pieces[k ^ step] = along_z(pieces[k], step)
    mine, late_gain, _ = lax.optimization_barrier((pack, gain, blocks[3]))
    marked, blocks[0] = pl.pallas_call(
        functools.partial(mark_kernel, planes),
        out_shape=[jax.ShapeDtypeStruct((qkv_rows + heads + shards, width), BF16), one_block],
        in_specs=[smem] + [vmem] * 2 + [hbm] * 2,
        out_specs=[vmem] * 2,
        scratch_shapes=[pltpu.SemaphoreType.DMA((2 * planes,))],
        compiler_params=params,
    )(index, mine, late_gain, x_in, c_in)
    pieces[planes // 2], _ = lax.optimization_barrier((pieces[planes // 2], blocks[3]))
    own = [marked] + [pieces[k] for k in range(1, planes)]
    other = [to_sibling(piece) for piece in own]

    split = ((PLANE, block, cols), BF16)
    half = 2 * heads
    x, c, vx, gains, *sent = call(
        functools.partial(project_kernel, planes, heads),
        [split, split, ((planes, 4 * half, width), BF16), ((planes, 8, width), F32)]
        + [((block, 7 * half), BF16)] * PLANE,
        index, blocks[0], *blocks[:0:-1], *own, *other, scalars=1,
        scratch=[((planes, half, width), BF16), ((rows, 5 * half), BF16)] + [((shards, width), F32)] * 2,
    )
    (factors,) = call(
        functools.partial(chain_kernel, features, heads),
        [((9 * block // 2, half), BF16)],
        index, doc_lengths, *exchange(sent)[::-1], scalars=2,
    )
    piece = (qkv_rows + heads, width)
    far_order = tuple(reversed(range(planes - planes // 2, planes)))
    near_order = tuple(reversed(range(planes - planes // 2)))

    def swap_and_merge(order, keep, send, cuts):
        outs = [((piece[0] // cuts, width), BF16 if k else F32) for k in order for _ in range(cuts)]
        cut = call(functools.partial(merge_kernel, cuts), outs, keep, to_sibling(send))
        return {k: list(cut[i * cuts : (i + 1) * cuts]) for i, k in enumerate(order)}

    keep, send, turned, small, small_t = call(
        functools.partial(far_grads_kernel, planes, heads, far_order),
        [((len(far_order),) + piece, F32), ((len(far_order),) + piece, BF16)]
        + [((5 * half, rows), BF16), ((2 * half, heads), BF16), ((heads, qkv_rows), BF16)],
        index, *exchange(factors), x, c, vx, gains, scalars=1,
        scratch=[((PLANE, block, 5 * half), BF16)],
    )
    pieces = swap_and_merge(far_order, keep, send, 2)
    keep, send = call(
        functools.partial(near_grads_kernel, planes, heads, near_order),
        [((len(near_order),) + piece, F32), ((len(near_order),) + piece, BF16)],
        index, turned, small, small_t, x, c, vx, gains, scalars=1,
    )
    pieces.update(swap_and_merge(near_order, keep, send, 1))
    (kept,), held = pieces[0], []
    for step in [1 << bit for bit in range(planes.bit_length() - 1)]:
        senders = [k for k in sorted(pieces, reverse=True) if k & step and k != step]
        got = {k ^ step: [along_z(part, step) for part in pieces.pop(k)] for k in senders}
        if step in pieces:
            held.append((pieces.pop(step), step))
        for k, come in got.items():
            pieces[k] = [call(add_kernel, [(a.shape, BF16)], a, b)[0] for a, b in zip(pieces[k], come)]
            held = [
                ([lax.optimization_barrier((part, pieces[k][0]))[0] for part in parts], at) for parts, at in held
            ]
    parts = [[along_z(part, at) for part in value] for value, at in reversed(held)]
    for come in parts[:-1]:
        for i, part in enumerate(come):
            (kept,) = call(functools.partial(wide_add_kernel, i * part.shape[0]), [(piece, F32)], kept, part)
    grad_qkv, grad_out = call(
        functools.partial(last_kernel, qkv_rows),
        [((qkv_rows, width), F32), ((heads, width), F32)],
        kept, *(parts[-1] if parts else []),
    )
    return (grad_qkv.T[None], grad_out[None])


def solution(mesh):
    sections, shards = mesh.shape["section"], mesh.shape["dp"]
    planes = shards // PLANE

    def body(inputs, *rest):
        fits = shards % PLANE == 0 and planes & (planes - 1) == 0
        if sections == 2 and inputs.shape[0] == 2 and fits:
            return planar(inputs, *rest)
        return pipelined(inputs, *rest)

    return jax.shard_map(
        body,
        mesh=mesh,
        in_specs=(
            P(None, "dp", None),
            P(None, "dp", None),
            P(None, "dp", None),
            P("section", None),
            P("section", "dp", None),
            P("section", None, "dp"),
        ),
        out_specs=(P("section", "dp", None), P("section", None, "dp")),
        check_vma=False,
    )
```

```python
import functools

import jax
import jax.numpy as jnp
from jax import lax
from jax.experimental import pallas as pl
from jax.experimental.pallas import tpu as pltpu
from jax.sharding import PartitionSpec as P

F32 = jnp.float32
BF16 = jnp.bfloat16
PLANE = 4
VMEM_LIMIT = 16 * 1024 * 1024


def passed_along(block, axis, distance):
    devices = range(lax.axis_size(axis))
    route = [(i - distance, i) for i in devices if i - distance in devices]
    return lax.ppermute(block, axis, route)


def segments_of(lengths, count):
    ends = jnp.cumsum(lengths)
    position = jnp.arange(count, dtype=jnp.int32)
    return jnp.sum((position[:, None] >= ends[None, :]).astype(jnp.int32), axis=1)


def layer(x, gain, w_qkv, w_out, seg):
    head = w_out.shape[0]
    x_wide = x.astype(jnp.float32)
    scale = lax.rsqrt(jnp.mean(x_wide * x_wide, axis=-1, keepdims=True) + 1e-05)
    normed = (x_wide * scale * gain.astype(jnp.float32)).astype(jnp.bfloat16)
    qkv = jnp.dot(normed, w_qkv, preferred_element_type=jnp.float32).astype(jnp.bfloat16)
    query = qkv[:, :head]
    keys = qkv[:, head : 2 * head]
    values = qkv[:, 2 * head :]
    scores = jnp.dot(query, keys.T, preferred_element_type=jnp.float32) * head ** (-0.5)
    rows = jnp.arange(x.shape[0], dtype=jnp.int32)
    allowed = (seg[:, None] == seg[None, :]) & (rows[:, None] >= rows[None, :])
    scores = jnp.where(allowed, scores, -1e30)
    probs = jax.nn.softmax(scores, axis=-1).astype(jnp.bfloat16)
    attended = jnp.dot(probs, values, preferred_element_type=jnp.float32).astype(jnp.bfloat16)
    return (x_wide + jnp.dot(attended, w_out, preferred_element_type=jnp.float32)).astype(
        jnp.bfloat16
    )


def pipelined(inputs, cotangent, doc_lengths, norm_gain, w_qkv, w_out):
    sections = lax.axis_size("section")
    section = lax.axis_index("section")
    micro = inputs.shape[0]
    count = inputs.shape[1]
    segs = jax.vmap(lambda lens: segments_of(lens, count))(doc_lengths[:, 0, :])
    gain = norm_gain[0]
    full_qkv, full_out = (
        lax.all_gather(w_qkv[0], "dp", axis=0, tiled=True),
        lax.all_gather(w_out[0], "dp", axis=1, tiled=True),
    )
    total_steps = micro + sections - 1
    empty = jnp.zeros(inputs.shape[1:], inputs.dtype)

    def forward_at(step, incoming, saved):
        index = step - section
        live = (index >= 0) & (index < micro)
        slot = jnp.clip(index, 0, micro - 1)
        first = lax.dynamic_index_in_dim(inputs, slot, 0, keepdims=False)
        x = jnp.where(section == 0, first, incoming)
        seg = lax.dynamic_index_in_dim(segs, slot, 0, keepdims=False)
        out = layer(x, gain, full_qkv, full_out, seg)
        old = lax.dynamic_index_in_dim(saved, slot, 0, keepdims=False)
        saved = lax.dynamic_update_index_in_dim(saved, jnp.where(live, x, old), slot, 0)
        return (out, saved)

    def forward_step(carry, step):
        incoming, saved = carry
        out, saved = forward_at(step, incoming, saved)
        incoming = passed_along(out, "section", 1)
        return ((incoming, saved), None)

    start_saved = jnp.zeros(inputs.shape, inputs.dtype)
    (incoming, saved), _ = lax.scan(
        forward_step, (empty, start_saved), jnp.arange(total_steps - 1, dtype=jnp.int32)
    )
    _, saved = forward_at(jnp.int32(total_steps - 1), incoming, saved)

    def backward_at(step, incoming, sum_qkv, sum_out):
        index = step - (sections - 1 - section)
        live = (index >= 0) & (index < micro)
        slot = jnp.clip(index, 0, micro - 1)
        last = lax.dynamic_index_in_dim(cotangent, slot, 0, keepdims=False)
        grad_y = jnp.where(section == sections - 1, last, incoming)
        x = lax.dynamic_index_in_dim(saved, slot, 0, keepdims=False)
        seg = lax.dynamic_index_in_dim(segs, slot, 0, keepdims=False)
        _, pull = jax.vjp(lambda a, b, c: layer(a, gain, b, c, seg), x, full_qkv, full_out)
        grad_x, grad_q, grad_o = pull(grad_y)
        sum_qkv = sum_qkv + jnp.where(live, grad_q.astype(jnp.float32), 0.0)
        sum_out = sum_out + jnp.where(live, grad_o.astype(jnp.float32), 0.0)
        return (grad_x, sum_qkv, sum_out)

    def backward_step(carry, step):
        incoming, sum_qkv, sum_out = carry
        grad_x, sum_qkv, sum_out = backward_at(step, incoming, sum_qkv, sum_out)
        incoming = passed_along(grad_x, "section", -1)
        return ((incoming, sum_qkv, sum_out), None)

    zero_qkv = jnp.zeros(full_qkv.shape, jnp.float32)
    zero_out = jnp.zeros(full_out.shape, jnp.float32)
    (incoming, sum_qkv, sum_out), _ = lax.scan(
        backward_step, (empty, zero_qkv, zero_out), jnp.arange(total_steps - 1, dtype=jnp.int32)
    )
    _, sum_qkv, sum_out = backward_at(jnp.int32(total_steps - 1), incoming, sum_qkv, sum_out)
    share_qkv, share_out = (
        lax.psum_scatter(sum_qkv, "dp", scatter_dimension=0, tiled=True),
        lax.psum_scatter(sum_out, "dp", scatter_dimension=1, tiled=True),
    )
    return (share_qkv[None], share_out[None])


def nn(a, b):
    return lax.dot_general(a, b, (((1,), (0,)), ((), ())), preferred_element_type=F32)


def nt(a, b):
    return lax.dot_general(a, b, (((1,), (1,)), ((), ())), preferred_element_type=F32)


def block_copies(planes, index, k, refs, out_ref, sems):
    width = refs[0].shape[-1] // (planes * PLANE)
    section, p = index[0], index[2]
    copies = []
    for z in range(planes):
        at = pl.multiple_of((z * PLANE + (p ^ k)) * width, width)
        for half, ref in enumerate(refs):
            copies.append(
                pltpu.make_async_copy(
                    ref.at[section, :, pl.ds(at, width)],
                    out_ref.at[half, :, pl.ds(z * width, width)],
                    sems.at[len(copies)],
                )
            )
    return copies


def mark_kernel(planes, index, pack_ref, gain_ref, x_ref, c_ref, out_ref, block_ref, sems):
    copies = block_copies(planes, index, 0, (x_ref, c_ref), block_ref, sems)
    for copy in copies:
        copy.start()
    out_ref[: pack_ref.shape[0], :] = pack_ref[...]
    out_ref[pack_ref.shape[0] :, :] = gain_ref[...]
    for copy in copies:
        copy.wait()


def first_kernel(planes, index, qkv_ref, wout_ref, x_ref, c_ref, pack_ref, far_ref, pack_sems, sems):
    qkv_rows = qkv_ref.shape[0]
    copies = [
        pltpu.make_async_copy(qkv_ref, pack_ref.at[:qkv_rows], pack_sems.at[0]),
        pltpu.make_async_copy(wout_ref, pack_ref.at[qkv_rows:], pack_sems.at[1]),
    ] + block_copies(planes, index, PLANE - 1, (x_ref, c_ref), far_ref, sems)
    for copy in copies:
        copy.start()
    for copy in copies:
        copy.wait()


def blocks_kernel(planes, index, x_ref, c_ref, *refs):
    out_refs, sems = refs[:-1], refs[-1]
    copies = []
    for k, out_ref in enumerate(out_refs, 1):
        copies += block_copies(planes, index, k, (x_ref, c_ref), out_ref, sems.at[k - 1])
    for copy in copies:
        copy.start()
    for copy in copies:
        copy.wait()


def project_kernel(planes, heads, index, *refs):
    blocks, own, other = refs[:PLANE], refs[PLANE : PLANE + planes], refs[PLANE + planes : PLANE + 2 * planes]
    x_ref, c_ref, vx_ref, gain_ref = refs[PLANE + 2 * planes : PLANE + 2 * planes + 4]
    out_refs = refs[PLANE + 2 * planes + 4 : -4]
    vc_ref, sum_ref, *wide_refs = refs[-4:]
    qkv, width = 3 * heads, vx_ref.shape[-1]
    section, place, p = index[0], index[1], index[2]
    for ref, wide_ref in zip((own[0], other[0]), wide_refs):
        wide_ref[...] = ref[qkv + heads :, :].astype(F32)
    for z in range(planes):
        mine, theirs = (ref[pl.ds(z * PLANE + p, 1), :] for ref in wide_refs)
        gain_ref[z, 0:1, :] = jnp.where(section == 0, mine, theirs)
        gain_ref[z, 1:2, :] = jnp.where(section == 0, theirs, mine)
    for k in range(planes):
        at = place ^ k
        mine, theirs = own[k][: qkv + heads, :], other[k][: qkv + heads, :]
        zero = jnp.where(section == 0, mine, theirs)
        one = jnp.where(section == 0, theirs, mine)
        empty = jnp.zeros((heads, width), BF16)
        vx_ref[at, :qkv, :] = (zero[:qkv].astype(F32) * gain_ref[at, 0:1, :]).astype(BF16)
        vx_ref[at, qkv : qkv + heads, :] = zero[qkv : qkv + heads]
        vx_ref[at, qkv + heads : 2 * qkv + heads, :] = (one[:qkv].astype(F32) * gain_ref[at, 1:2, :]).astype(BF16)
        vx_ref[at, 2 * qkv + heads :, :] = empty
        vc_ref[at, :heads, :] = one[qkv : qkv + heads]
        vc_ref[at, heads:, :] = zero[qkv : qkv + heads]
    for k in range(PLANE):
        x_ref[p ^ k] = blocks[-k][0]
        c_ref[p ^ k] = blocks[-k][1]
    rows = x_ref.shape[0] * x_ref.shape[1]
    with_x = with_c = squares = products = None
    for z in range(planes):
        cols = slice(z * width, (z + 1) * width)
        x = x_ref[:, :, cols].reshape(rows, width)
        c = c_ref[:, :, cols].reshape(rows, width)
        wide = x.astype(F32)
        out = vx_ref[z, qkv : qkv + heads, :]
        right = jnp.concatenate([vx_ref[z, qkv + heads : 2 * qkv + heads, :], out], axis=0)
        new = nt(x, vx_ref[z]), nt(c, vc_ref[z]), jnp.sum(wide * wide, axis=1, keepdims=True), nt(out, right)
        if with_x is None:
            with_x, with_c, squares, products = new
        else:
            with_x, with_c = with_x + new[0], with_c + new[1]
            squares, products = squares + new[2], products + new[3]
    half = 2 * heads
    lane = lax.broadcasted_iota(jnp.int32, (rows, half), 1)
    high = squares.astype(BF16).astype(F32)
    last = jnp.where(lane == heads, high, jnp.where(lane == heads + 1, squares - high, with_x[:, 3 * half :]))
    sum_ref[:, : 3 * half] = with_x[:, : 3 * half].astype(BF16)
    sum_ref[:, 3 * half : 4 * half] = last.astype(BF16)
    sum_ref[:, 4 * half :] = with_c.astype(BF16)
    block = rows // PLANE
    for k in range(PLANE):
        start = pl.multiple_of((p ^ k) * block, block)
        out_refs[k][:, : 5 * half] = sum_ref[pl.ds(start, block), :]
        out_refs[k][:, 5 * half :] = products.astype(BF16)


def attention(qkv, allowed, heads):
    query, keys, values = (qkv[:, i * heads : (i + 1) * heads].astype(BF16) for i in range(3))
    scores = jnp.where(allowed, nt(query, keys) * heads ** (-0.5), -1e30)
    raised = jnp.exp(scores - jnp.max(scores, axis=1, keepdims=True))
    scale = 1.0 / jnp.sum(raised, axis=1, keepdims=True)
    return raised * scale, (nn(raised.astype(BF16), values) * scale).astype(BF16)


def attention_grad(qkv, probs, att, d_att, heads):
    query, keys, values = (qkv[:, i * heads : (i + 1) * heads].astype(BF16) for i in range(3))
    inner = jnp.sum(att.astype(F32) * d_att.astype(F32), axis=1, keepdims=True)
    d_values = nn(jnp.transpose(probs).astype(BF16), d_att)
    d_scores = probs * (nt(d_att, values) - inner) * heads ** (-0.5)
    d_query = nn(d_scores.astype(BF16), keys)
    d_keys = nn(jnp.transpose(d_scores).astype(BF16), query)
    return jnp.concatenate([d_query, d_keys, d_values], axis=1).astype(BF16).astype(F32)


def summed(parts):
    total = parts[0][...].astype(F32)
    for part in parts[1:]:
        total = total + part[...].astype(F32)
    return total


def chain_kernel(features, heads, index, docs, *refs):
    out_ref = refs[-1]
    qkv, half = 3 * heads, 2 * heads
    total = summed(refs[:-1])
    rows = total.shape[0]
    section = index[0]
    query_at = lax.broadcasted_iota(jnp.int32, (rows, rows), 0)
    key_at = lax.broadcasted_iota(jnp.int32, (rows, rows), 1)
    allowed = query_at >= key_at
    end = 0
    for i in range(docs.shape[2]):
        end = end + docs[section, 0, i]
        allowed = allowed & ((query_at >= end) == (key_at >= end))
    x_out = total[:, qkv : 2 * half]
    x_one = total[:, 2 * half : 2 * half + qkv]
    tail = total[:, 3 * half : 4 * half]
    c_one, c_zero = total[:, 4 * half : 4 * half + heads].astype(BF16), total[:, 4 * half + heads : 5 * half]
    lane = lax.broadcasted_iota(jnp.int32, tail.shape, 1)
    squares = jnp.sum(jnp.where((lane == heads) | (lane == heads + 1), tail, 0.0), axis=1, keepdims=True)
    mixed = total[:, 5 * half : 5 * half + qkv].astype(BF16)
    gram = total[:, 5 * half + qkv :].astype(BF16)

    scale0 = lax.rsqrt(squares / features + 1e-05)
    qkv0 = (total[:, :qkv] * scale0).astype(BF16).astype(F32)
    probs0, att0 = attention(qkv0, allowed, heads)
    wide0 = att0.astype(F32)
    y_out = x_out + nn(att0, gram)
    squares = squares + jnp.sum(wide0 * (x_out + y_out), axis=1, keepdims=True)
    scale1 = lax.rsqrt(jnp.maximum(squares, 0.0) / features + 1e-05)
    qkv1 = ((x_one + nn(att0, mixed)) * scale1).astype(BF16).astype(F32)
    probs1, att1 = attention(qkv1, allowed, heads)
    d_qkv1 = attention_grad(qkv1, probs1, att1, c_one, heads)
    inner = jnp.sum(d_qkv1 * qkv1, axis=1, keepdims=True) * scale1 * scale1 / features
    e1 = d_qkv1 * scale1
    d_att0 = c_zero + nt(e1.astype(BF16), mixed) - inner * y_out
    e0 = attention_grad(qkv0, probs0, att0, d_att0.astype(BF16), heads) * scale0
    factors = jnp.concatenate([e0, wide0, e1, wide0 * inner], axis=1).astype(BF16)
    for g in range(4):
        out_ref[g * rows : (g + 1) * rows, :] = factors[:, g * half : (g + 1) * half]
    wide1 = att1.astype(F32)
    out_ref[4 * rows :, :] = jnp.concatenate([wide1[: rows // 2], wide1[rows // 2 :]], axis=1).astype(BF16)


def pieces_of(planes, heads, order, index, turned, small, small_t, x_ref, c_ref, vx_ref, gain_ref, keep_ref, send_ref):
    qkv, half, width = 3 * heads, 2 * heads, vx_ref.shape[-1]
    section, place = index[0], index[1]
    rows = x_ref.shape[0] * x_ref.shape[1]
    att0, att1 = turned[qkv : qkv + heads], turned[4 * half : 4 * half + heads]
    for i, k in enumerate(order):
        z = place ^ k
        cols = pl.ds(pl.multiple_of(z * width, width), width)
        x = x_ref[:, :, cols].reshape(rows, width)
        c = c_ref[:, :, cols].reshape(rows, width)
        out = vx_ref[z, qkv : qkv + heads, :]
        with_x = nn(turned[: 4 * half], x)
        left = with_x[2 * half :] + nn(small, out)
        zero = with_x[:qkv] * gain_ref[z, 0:1, :]
        one = left[:qkv] * gain_ref[z, 1:2, :]
        keep_ref[i, :qkv, :] = jnp.where(section == 0, zero, one)
        send_ref[i, :qkv, :] = jnp.where(section == 0, one, zero).astype(BF16)
        zero = nn(att0, c) + nn(small_t, vx_ref[z, qkv + heads : 2 * qkv + heads, :]) - left[qkv:]
        one = nn(att1, c)
        keep_ref[i, qkv:, :] = jnp.where(section == 0, zero, one)
        send_ref[i, qkv:, :] = jnp.where(section == 0, one, zero).astype(BF16)


def far_grads_kernel(planes, heads, order, index, *refs):
    factors, arrays = refs[:PLANE], refs[PLANE : PLANE + 4]
    keep_ref, send_ref, turned_ref, small_ref, small_t_ref, all_ref = refs[PLANE + 4 :]
    qkv, half = 3 * heads, 2 * heads
    p = index[2]
    block = all_ref.shape[1]
    for k in range(PLANE):
        for g in range(4):
            all_ref[p ^ k, :, g * half : (g + 1) * half] = factors[k][g * block : (g + 1) * block, :]
        folded = factors[k][4 * block :, :]
        last = jnp.concatenate([folded[:, :heads].astype(F32), folded[:, heads:].astype(F32)], axis=0)
        all_ref[p ^ k, :, 4 * half :] = jnp.concatenate([last, jnp.zeros_like(last)], axis=1).astype(BF16)
    rows = all_ref.shape[0] * block
    turned = jnp.transpose(all_ref[...].astype(F32).reshape(rows, 5 * half)).astype(BF16)
    att0, right = turned[qkv : qkv + heads], turned[2 * half : 4 * half]
    small = nt(right, att0).astype(BF16)
    small_t = nt(att0, right[:qkv]).astype(BF16)
    turned_ref[...] = turned
    small_ref[...] = small
    small_t_ref[...] = small_t
    pieces_of(planes, heads, order, index, turned, small, small_t, *arrays, keep_ref, send_ref)


def near_grads_kernel(planes, heads, order, index, turned_ref, small_ref, small_t_ref, *refs):
    pieces_of(planes, heads, order, index, turned_ref[...], small_ref[...], small_t_ref[...], *refs)


def merge_kernel(cuts, keep_ref, come_ref, *out_refs):
    rows = keep_ref.shape[1] // cuts
    for j, out_ref in enumerate(out_refs):
        here = slice(j % cuts * rows, (j % cuts + 1) * rows)
        out_ref[...] = (keep_ref[j // cuts, here] + come_ref[j // cuts, here].astype(F32)).astype(out_ref.dtype)


def wide_add_kernel(at, a_ref, part_ref, out_ref):
    rows = slice(at, at + part_ref.shape[0])
    out_ref[...] = a_ref[...]
    out_ref[rows, :] = a_ref[rows, :] + part_ref[...].astype(F32)


def add_kernel(a_ref, b_ref, out_ref):
    out_ref[...] = (a_ref[...].astype(F32) + b_ref[...].astype(F32)).astype(BF16)


def last_kernel(qkv_rows, keep_ref, *refs):
    parts, (qkv_ref, out_ref) = refs[:-2], refs[-2:]
    total = keep_ref[...]
    for part in parts:
        total = total + part[...].astype(F32)
    qkv_ref[...] = total[:qkv_rows]
    out_ref[...] = total[qkv_rows:]


def far_first(value, count, send):
    of = lambda k: value[k] if isinstance(value, (list, tuple)) else value
    got = {k: send(of(k), k) for k in reversed(range(1, count))}
    return [of(0)] + [got[k] for k in range(1, count)]


def call(kernel, outs, *args, scalars=0, scratch=()):
    smem = pl.BlockSpec(memory_space=pltpu.SMEM)
    vmem = pl.BlockSpec(memory_space=pltpu.VMEM)
    return pl.pallas_call(
        kernel,
        out_shape=[jax.ShapeDtypeStruct(shape, dtype) for shape, dtype in outs],
        in_specs=[smem] * scalars + [vmem] * (len(args) - scalars),
        out_specs=[vmem] * len(outs),
        scratch_shapes=[pltpu.VMEM(shape, dtype) for shape, dtype in scratch],
        compiler_params=pltpu.CompilerParams(vmem_limit_bytes=VMEM_LIMIT),
    )(*args)


def planar(inputs, cotangent, doc_lengths, norm_gain, w_qkv, w_out):
    shards = lax.axis_size("dp")
    planes = shards // PLANE
    section, place = lax.axis_index("section"), lax.axis_index("dp")
    z, p = place // PLANE, place % PLANE
    index = jnp.stack([section, z, p]).astype(jnp.int32)
    block, features = inputs.shape[1:]
    rows = PLANE * block
    heads, width = w_out.shape[1:]
    qkv_rows = w_qkv.shape[2]
    cols = planes * width
    def along_z(value, k):
        route = [(a * PLANE + b, (a ^ k) * PLANE + b) for a in range(planes) for b in range(PLANE)]
        return lax.ppermute(value, "dp", route)

    def to_sibling(value):
        return lax.ppermute(value, "section", [(0, 1), (1, 0)])

    def along_plane(value, k):
        route = [(a * PLANE + b, a * PLANE + (b ^ k)) for a in range(planes) for b in range(PLANE)]
        return lax.ppermute(value, "dp", route)

    def exchange(value):
        return far_first(value, PLANE, along_plane)

    smem, vmem = pl.BlockSpec(memory_space=pltpu.SMEM), pl.BlockSpec(memory_space=pltpu.VMEM)
    hbm = pl.BlockSpec(memory_space=pltpu.HBM)
    params = pltpu.CompilerParams(vmem_limit_bytes=VMEM_LIMIT)
    qkv_in, out_in, x_in, c_in = [
        pltpu.with_memory_space_constraint(value, pltpu.HBM)
        for value in (w_qkv[0].T, w_out[0], inputs, cotangent)
    ]
    one_block = jax.ShapeDtypeStruct((2, block, cols), BF16)
    pack, far_block = pl.pallas_call(
        functools.partial(first_kernel, planes),
        out_shape=[jax.ShapeDtypeStruct((qkv_rows + heads, width), BF16), one_block],
        in_specs=[smem] + [hbm] * 4,
        out_specs=[vmem] * 2,
        scratch_shapes=[pltpu.SemaphoreType.DMA((2,)), pltpu.SemaphoreType.DMA((2 * planes,))],
        compiler_params=params,
    )(index, qkv_in, out_in, x_in, c_in)
    blocks = pl.pallas_call(
        functools.partial(blocks_kernel, planes),
        out_shape=[one_block] * (PLANE - 2),
        in_specs=[smem] + [hbm] * 2,
        out_specs=[vmem] * (PLANE - 2),
        scratch_shapes=[pltpu.SemaphoreType.DMA((PLANE - 2, 2 * planes))],
        compiler_params=params,
    )(index, x_in, c_in)
    blocks = [*blocks, far_block]
    gain = norm_gain[0].reshape(shards, width)
    blocks = far_first([None] + blocks, PLANE, along_plane)
    pieces = {0: pack}
    for step in reversed([1 << bit for bit in range(planes.bit_length() - 1)]):
        for k in list(pieces):
            pieces[k ^ step] = along_z(pieces[k], step)
    mine, late_gain, _ = lax.optimization_barrier((pack, gain, blocks[3]))
    marked, blocks[0] = pl.pallas_call(
        functools.partial(mark_kernel, planes),
        out_shape=[jax.ShapeDtypeStruct((qkv_rows + heads + shards, width), BF16), one_block],
        in_specs=[smem] + [vmem] * 2 + [hbm] * 2,
        out_specs=[vmem] * 2,
        scratch_shapes=[pltpu.SemaphoreType.DMA((2 * planes,))],
        compiler_params=params,
    )(index, mine, late_gain, x_in, c_in)
    pieces[planes // 2], _ = lax.optimization_barrier((pieces[planes // 2], blocks[3]))
    own = [marked] + [pieces[k] for k in range(1, planes)]
    other = [to_sibling(piece) for piece in own]

    split = ((PLANE, block, cols), BF16)
    half = 2 * heads
    x, c, vx, gains, *sent = call(
        functools.partial(project_kernel, planes, heads),
        [split, split, ((planes, 4 * half, width), BF16), ((planes, 8, width), F32)]
        + [((block, 7 * half), BF16)] * PLANE,
        index, blocks[0], *blocks[:0:-1], *own, *other, scalars=1,
        scratch=[((planes, half, width), BF16), ((rows, 5 * half), BF16)] + [((shards, width), F32)] * 2,
    )
    (factors,) = call(
        functools.partial(chain_kernel, features, heads),
        [((9 * block // 2, half), BF16)],
        index, doc_lengths, *exchange(sent), scalars=2,
    )
    piece = (qkv_rows + heads, width)
    far_order = tuple(reversed(range(planes - planes // 2, planes)))
    near_order = tuple(reversed(range(planes - planes // 2)))

    def swap_and_merge(order, keep, send, cuts):
        outs = [((piece[0] // cuts, width), BF16 if k else F32) for k in order for _ in range(cuts)]
        cut = call(functools.partial(merge_kernel, cuts), outs, keep, to_sibling(send))
        return {k: list(cut[i * cuts : (i + 1) * cuts]) for i, k in enumerate(order)}

    keep, send, turned, small, small_t = call(
        functools.partial(far_grads_kernel, planes, heads, far_order),
        [((len(far_order),) + piece, F32), ((len(far_order),) + piece, BF16)]
        + [((5 * half, rows), BF16), ((2 * half, heads), BF16), ((heads, qkv_rows), BF16)],
        index, *exchange(factors), x, c, vx, gains, scalars=1,
        scratch=[((PLANE, block, 5 * half), BF16)],
    )
    pieces = swap_and_merge(far_order, keep, send, 2)
    keep, send = call(
        functools.partial(near_grads_kernel, planes, heads, near_order),
        [((len(near_order),) + piece, F32), ((len(near_order),) + piece, BF16)],
        index, turned, small, small_t, x, c, vx, gains, scalars=1,
    )
    pieces.update(swap_and_merge(near_order, keep, send, 1))
    (kept,), held = pieces[0], []
    for step in [1 << bit for bit in range(planes.bit_length() - 1)]:
        senders = [k for k in sorted(pieces, reverse=True) if k & step and k != step]
        got = {k ^ step: [along_z(part, step) for part in pieces.pop(k)] for k in senders}
        if step in pieces:
            held.append((pieces.pop(step), step))
        for k, come in got.items():
            pieces[k] = [call(add_kernel, [(a.shape, BF16)], a, b)[0] for a, b in zip(pieces[k], come)]
            held = [
                (parts, at) for parts, at in held
            ]
    parts = [[along_z(part, at) for part in value] for value, at in reversed(held)]
    for come in parts[:-1]:
        for i, part in enumerate(come):
            (kept,) = call(functools.partial(wide_add_kernel, i * part.shape[0]), [(piece, F32)], kept, part)
    grad_qkv, grad_out = call(
        functools.partial(last_kernel, qkv_rows),
        [((qkv_rows, width), F32), ((heads, width), F32)],
        kept, *(parts[-1] if parts else []),
    )
    return (grad_qkv.T[None], grad_out[None])


def solution(mesh):
    sections, shards = mesh.shape["section"], mesh.shape["dp"]
    planes = shards // PLANE

    def body(inputs, *rest):
        fits = shards % PLANE == 0 and planes & (planes - 1) == 0
        if sections == 2 and inputs.shape[0] == 2 and fits:
            return planar(inputs, *rest)
        return pipelined(inputs, *rest)

    return jax.shard_map(
        body,
        mesh=mesh,
        in_specs=(
            P(None, "dp", None),
            P(None, "dp", None),
            P(None, "dp", None),
            P("section", None),
            P("section", "dp", None),
            P("section", None, "dp"),
        ),
        out_specs=(P("section", "dp", None), P("section", None, "dp")),
        check_vma=False,
    )
```
